32 devices in a mesh: seq: 16 (over z, x, core), tp: 2 (over y).
Axes of the slice: x: 2, y: 2, z: 4, core: 2. Of those that a mesh axis runs over, the one named last changes fastest.
Arguments:
- features: bfloat16 [2048, 8192], P('seq', 'tp'), may hold values from -6 to 6
- in_proj: bfloat16 [3, 8192, 1024], P(None, 'seq', 'tp'), may hold values from -0.0625 to 0.0625
- short_taps: float32 [3, 3, 1024], P(None, None, 'tp'), may hold values from -3 to 3
- long_filter: float32 [2048, 1024], P('seq', 'tp'), may hold values from -1.8 to 1.8
- skip_gain: float32 [1024], P('tp'), may hold values from -4 to 4
- out_proj: bfloat16 [1024, 8192], P('tp', 'seq'), may hold values from -0.1875 to 0.1875
Outputs:
- mixed: bfloat16 [2048, 8192], P('seq', 'tp')
The draws below stay inside these ranges and needn't reach their ends.
All inputs are finite; a program needn't handle non-finite values.
Results may differ from the reference program's by a relative error of at most 0.007.
Values may be sent and summed in bfloat16 or wider, within the bound.
No kernel may reach another device: no remote copies, remote signals or barrier semaphores. Data moves between devices by JAX's collectives and lax.ppermute only.
A program may use at most 128 MiB of HBM per device.

```python
import jax
import jax.numpy as jnp

D = 1024
D_MODEL = 8192
SHORT = 3
TOKENS = 2048


def draw_long_filter(key, part):
    position = jnp.arange(TOKENS, dtype=jnp.float32)[:, None]
    envelope = 0.3 * (1.0 + position) ** (-0.5)
    values = jnp.clip(jax.random.normal(key, (TOKENS, D), jnp.float32), -6.0, 6.0)
    return (values * envelope).astype(jnp.float32)


def levels(own_key, dims, cuts, least, top_value):
    factor_of = 1.0
    for dim, blocks in cuts:
        steps = jax.random.uniform(jax.random.fold_in(jax.random.fold_in(own_key, 6), dim), (blocks,), jnp.float32, least / len(cuts), top_value / len(cuts))
        factor_of = factor_of * jnp.repeat(jnp.exp(steps), dims[dim] // blocks).reshape((-1,) + (1,) * (len(dims) - 1 - dim))
    return factor_of


def bell_draw(key, extent, width, limit, split=(), kind=jnp.bfloat16):
    entries = jax.random.normal(key, extent, jnp.float32) * width
    if len(split) > 0:
        entries = levels(key, extent, split, -0.22, 0.18) * entries
    return jnp.clip(entries, min=-limit, max=limit).astype(kind)


def setup_inputs(seed: int = 0) -> dict:
    key_list = jax.random.split(jax.random.key(seed), 7)
    return {
        "features": bell_draw(key_list[0], (TOKENS, D_MODEL), 1.0, 6.0, ((0, 16), (1, 2))),
        "in_proj": bell_draw(key_list[1], (3, D_MODEL, D), D_MODEL ** -0.5, 0.0625, ((1, 16), (2, 2))),
        "short_taps": bell_draw(key_list[2], (3, SHORT, D), 0.5, 3.0, ((2, 2),), jnp.float32),
        "long_filter": draw_long_filter(jax.random.fold_in(key_list[6], 71), 0),
        "skip_gain": bell_draw(key_list[4], (D,), 1.0, 4.0, ((0, 2),), jnp.float32),
        "out_proj": bell_draw(key_list[5], (D, D_MODEL), D ** -0.5, 0.1875, ((0, 2), (1, 16))),
    }


def reference(features, in_proj, short_taps, long_filter, skip_gain, out_proj):
    projected = jnp.stack([jnp.dot(features, in_proj[stream], preferred_element_type=jnp.float32) for stream in range(3)]).astype(jnp.bfloat16)
    widened = projected.astype(jnp.float32)
    padded = jnp.pad(widened, ((0, 0), (SHORT - 1, 0), (0, 0)))
    filtered = jnp.zeros_like(widened)
    for offset in range(SHORT):
        begin = SHORT - 1 - offset
        filtered = filtered + short_taps[:, offset, None, :] * padded[:, begin:begin + TOKENS, :]
    query = filtered[0]
    inner = filtered[1] * filtered[2]
    pieces = []
    block = min(128, D)
    for start in range(0, D, block):
        spec_inner = jnp.fft.rfft(inner[:, start:start + block], n=2 * TOKENS, axis=0)
        spec_filter = jnp.fft.rfft(long_filter[:, start:start + block], n=2 * TOKENS, axis=0)
        pieces.append(jnp.fft.irfft(spec_inner * spec_filter, n=2 * TOKENS, axis=0)[:TOKENS].astype(jnp.float32))
    long_mix = jnp.concatenate(pieces, axis=1)
    gated = (query * (long_mix + skip_gain[None, :] * inner)).astype(jnp.bfloat16)
    return jnp.dot(gated, out_proj, preferred_element_type=jnp.float32).astype(jnp.bfloat16)
```

```python
import functools
import math

import jax
import jax.numpy as jnp
import numpy as np
from jax import lax
from jax.experimental import pallas as pl
from jax.experimental.pallas import tpu as pltpu
from jax.sharding import PartitionSpec as P

HIGHEST = lax.Precision.HIGHEST
UNROLL = 16


def outer_factor(seq_parts):
    outer = 1
    while 4 * outer * outer <= seq_parts and seq_parts % (2 * outer) == 0:
        outer *= 2
    return outer


def match_rounds(edges, nodes, degree):
    left = list(edges)
    rounds = []
    for _ in range(degree):
        by_source = {}
        for edge in left:
            by_source.setdefault(edge[0], []).append(edge)
        taken = {}

        def place(source, seen):
            for edge in by_source[source]:
                target = edge[1]
                if target in seen:
                    continue
                seen.add(target)
                if target not in taken or place(taken[target][0], seen):
                    taken[target] = edge
                    return True
            return False

        for source in range(nodes):
            place(source, set())
        chosen = sorted(taken.values())
        rounds.append(chosen)
        for edge in chosen:
            left.remove(edge)
    return rounds


def feature_routes(outer, tp_parts):
    groups = max(1, outer // tp_parts)
    shares = max(1, tp_parts // outer)
    edges = []
    for src_outer in range(outer):
        for src_tp in range(tp_parts):
            for group in range(groups):
                for dst_tp in range(tp_parts):
                    dst_outer = src_tp * groups + group if groups > 1 else src_tp // shares
                    slot = src_outer * shares + (src_tp % shares)
                    edges.append(
                        (
                            src_outer * tp_parts + src_tp,
                            dst_outer * tp_parts + dst_tp,
                            group * tp_parts + dst_tp,
                            slot,
                        )
                    )
    return match_rounds(edges, outer * tp_parts, groups * tp_parts)


def spread_features(features, outer, inner_parts, tp_parts):
    rows, cols = features.shape
    groups = max(1, outer // tp_parts)
    shares = max(1, tp_parts // outer)
    width = cols // (groups * tp_parts)
    node = (lax.axis_index("seq") // inner_parts) * tp_parts + lax.axis_index("tp")
    buffer = jnp.zeros((outer * shares, rows, width), features.dtype)
    for chosen in feature_routes(outer, tp_parts):
        send = np.zeros(outer * tp_parts, np.int32)
        fill = np.zeros(outer * tp_parts, np.int32)
        pairs = []
        for source, target, block, slot in chosen:
            send[source] = block
            fill[target] = slot
            for inner in range(inner_parts):
                pairs.append(
                    (
                        ((source // tp_parts) * inner_parts + inner) * tp_parts + source % tp_parts,
                        ((target // tp_parts) * inner_parts + inner) * tp_parts + target % tp_parts,
                    )
                )
        piece = lax.dynamic_slice_in_dim(features, jnp.asarray(send)[node] * width, width, axis=1)
        piece = lax.ppermute(piece, ("seq", "tp"), pairs)
        buffer = lax.dynamic_update_slice_in_dim(buffer, piece[None], jnp.asarray(fill)[node], axis=0)
    return buffer.reshape(outer, shares, rows, width)


def share_over_tp(part, tp_parts):
    position = lax.axis_index("tp")
    full = jnp.zeros((tp_parts,) + part.shape, part.dtype)
    for step in range(tp_parts):
        pairs = [(i, (i + step) % tp_parts) for i in range(tp_parts)]
        piece = lax.ppermute(part, "tp", pairs) if step else part
        full = lax.dynamic_update_slice_in_dim(
            full, piece[None], lax.rem(position - step + tp_parts, tp_parts), axis=0
        )
    return full


def tables(block):
    place = np.arange(block)
    angle = 2.0 * math.pi * np.outer(place, place + 0.5) / (2 * block)
    forward = np.concatenate([np.cos(angle), -np.sin(angle)], 1)
    place = np.arange(2 * block)
    angle = 2.0 * math.pi * np.outer(np.arange(block) + 0.5, place) / (2 * block)
    backward = np.concatenate([np.cos(angle), -np.sin(angle)], 0) / block
    return forward.astype(np.float32), backward.astype(np.float32)


def each(count, body):
    if isinstance(count, int) and count <= UNROLL:
        for index in range(count):
            body(index)
    else:
        lax.fori_loop(0, count, lambda index, carry: (body(index), carry)[1], 0)


def total(count, term, zero):
    if isinstance(count, int) and count <= UNROLL:
        result = zero
        for index in range(count):
            result = jax.tree.map(jnp.add, result, term(index))
        return result
    return lax.fori_loop(
        0, count, lambda index, sums: jax.tree.map(jnp.add, sums, term(index)), zero
    )


def conv_kernel(
    outer, parts_ref, filter_ref, taps_ref, skip_ref, fwd_ref, bwd_ref, out_ref,
    proj, query, inner, spec, filter_spec, product, back
):
    blocks, streams, chans, _ = parts_ref.shape
    rows = filter_ref.shape[2]
    inner_parts = blocks // outer
    taps_count = taps_ref.shape[1]
    lane = lax.broadcasted_iota(jnp.int32, (chans, rows), 1)

    def add_up(index, stream, slot):
        sums = jnp.zeros((chans, rows), jnp.float32)
        column = pl.ds(pl.multiple_of(slot * rows, rows), rows)
        for part in range(outer):
            sums = sums + parts_ref[part * inner_parts + index % inner_parts, stream, :, column].astype(jnp.float32)
        return sums.astype(jnp.bfloat16).astype(jnp.float32)

    for stream in range(streams):
        proj[0, stream] = jnp.zeros((chans, rows), jnp.float32)

    def first(index):
        filtered = []
        for stream in range(streams):
            proj[index + 1, stream] = add_up(index, stream, index // inner_parts)
        for stream in range(streams):
            now, past = proj[index + 1, stream], proj[index, stream]
            value = taps_ref[stream, 0] * now
            for offset in range(1, taps_count):
                moved = jnp.where(
                    lane < offset, pltpu.roll(past, offset, 1), pltpu.roll(now, offset, 1)
                )
                value = value + taps_ref[stream, offset] * moved
            filtered.append(value)
        query[index] = filtered[0]
        inner[index] = filtered[1] * filtered[2]

    each(blocks, first)

    def apply(source, table_ref, target):
        if chans % 8 == 0:
            flat = source[...].reshape(blocks * chans, source.shape[2])
            done = jnp.dot(flat, table_ref[...], precision=HIGHEST, preferred_element_type=jnp.float32)
            target[...] = done.reshape(target.shape)
        else:

            def one(index):
                target[index] = jnp.dot(
                    source[index], table_ref[...], precision=HIGHEST, preferred_element_type=jnp.float32
                )

            each(blocks, one)

    apply(filter_ref, fwd_ref, filter_spec)
    apply(inner, fwd_ref, spec)

    def multiply(index):
        def term(step):
            left, right = spec[step], filter_spec[index - step]
            left_real, left_imag = left[:, :rows], left[:, rows:]
            right_real, right_imag = right[:, :rows], right[:, rows:]
            return (
                left_real * right_real - left_imag * right_imag,
                left_real * right_imag + left_imag * right_real,
            )

        zero = jnp.zeros((chans, rows), jnp.float32)
        real, imag = total(index + 1, term, (zero, zero))
        product[index, :, :rows] = real
        product[index, :, rows:] = imag

    each(blocks, multiply)
    apply(product, bwd_ref, back)

    def last(index, carried):
        long_mix = back[index, :, :rows] + carried
        gated = query[index] * (long_mix + skip_ref[...] * inner[index])
        out_ref[index] = gated.astype(out_ref.dtype)

    last(0, jnp.zeros((chans, rows), jnp.float32))
    each(blocks - 1, lambda index: last(index + 1, back[index, :, rows:]))


def convolve(parts, filter_blocks, taps, skip, outer):
    blocks, streams, chans, _ = parts.shape
    rows = filter_blocks.shape[2]
    forward, backward = tables(rows)
    wide = (blocks, chans, 2 * rows)
    narrow = (blocks, chans, rows)
    vmem = pl.BlockSpec(memory_space=pltpu.VMEM)
    return pl.pallas_call(
        functools.partial(conv_kernel, outer),
        out_shape=jax.ShapeDtypeStruct(narrow, jnp.bfloat16),
        in_specs=[vmem] * 6,
        out_specs=vmem,
        scratch_shapes=[
            pltpu.VMEM((blocks + 1, streams, chans, rows), jnp.float32),
            pltpu.VMEM(narrow, jnp.float32),
            pltpu.VMEM(narrow, jnp.float32),
            pltpu.VMEM(wide, jnp.float32),
            pltpu.VMEM(wide, jnp.float32),
            pltpu.VMEM(wide, jnp.float32),
            pltpu.VMEM(wide, jnp.float32),
        ],
        compiler_params=pltpu.CompilerParams(vmem_limit_bytes=40 * 2**20),
        cost_estimate=pl.CostEstimate(flops=10**9, bytes_accessed=4 * 2**20, transcendentals=0),
    )(parts, filter_blocks, taps, skip, jnp.asarray(forward), jnp.asarray(backward))


def out_kernel(gated_ref, weight_ref, out_ref):
    shares, _, depth, _ = weight_ref.shape
    sums = jnp.zeros(out_ref.shape, jnp.float32)
    for share in range(shares):
        left = gated_ref[:, share * depth : (share + 1) * depth]
        sums = sums + jnp.dot(left, weight_ref[share, 0], preferred_element_type=jnp.float32)
    out_ref[...] = sums.astype(out_ref.dtype)


def project_out(gated, weight):
    rows, depth_all = gated.shape
    shares, ranges, depth, width = weight.shape
    return pl.pallas_call(
        out_kernel,
        grid=(ranges,),
        out_shape=jax.ShapeDtypeStruct((rows, ranges * width), jnp.bfloat16),
        in_specs=[
            pl.BlockSpec((rows, depth_all), lambda r: (0, 0)),
            pl.BlockSpec((shares, 1, depth, width), lambda r: (0, r, 0, 0)),
        ],
        out_specs=pl.BlockSpec((rows, width), lambda r: (0, r)),
        compiler_params=pltpu.CompilerParams(vmem_limit_bytes=24 * 2**20),
        cost_estimate=pl.CostEstimate(
            flops=2 * rows * depth_all * ranges * width,
            bytes_accessed=2 * (weight.size + gated.size + rows * ranges * width),
            transcendentals=0,
        ),
    )(gated, weight)


def per_device(features, in_proj, short_taps, long_filter, skip_gain, out_proj):
    rows = features.shape[0]
    seq_parts = lax.axis_size("seq")
    tp_parts = lax.axis_size("tp")
    outer = outer_factor(seq_parts)
    inner_parts = seq_parts // outer
    streams, _, chan_tp = in_proj.shape
    chans = chan_tp // seq_parts
    position = lax.axis_index("seq")

    inner_groups = [[a * inner_parts + b for b in range(inner_parts)] for a in range(outer)]
    weight = lax.all_gather(in_proj, "seq", axis=1, tiled=True, axis_index_groups=inner_groups)

    part = spread_features(features, outer, inner_parts, tp_parts)
    full = share_over_tp(part, tp_parts)
    tokens = jnp.transpose(full, (1, 3, 2, 0, 4)).reshape(outer * rows, -1)

    filter_blocks = lax.all_to_all(
        long_filter.T.reshape(seq_parts, chans, rows), "seq", split_axis=0, concat_axis=0, tiled=True
    )
    taps = lax.dynamic_slice_in_dim(short_taps, position * chans, chans, axis=2)
    taps = jnp.broadcast_to(taps[..., None], taps.shape + (rows,))
    skip = lax.dynamic_slice_in_dim(skip_gain, position * chans, chans, axis=0)
    skip = jnp.broadcast_to(skip[:, None], (chans, rows))

    ranges = seq_parts // tp_parts
    pairs = []
    for seq in range(seq_parts):
        for tp in range(tp_parts):
            target = (tp * ranges + seq % ranges) * tp_parts + seq // ranges
            pairs.append((seq * tp_parts + tp, target))
    out_weight = lax.all_gather(lax.ppermute(out_proj, ("seq", "tp"), pairs), "seq")
    out_weight = out_weight.reshape((tp_parts, ranges) + out_proj.shape)

    partial = jnp.einsum("tk,skc->sct", tokens, weight, preferred_element_type=jnp.float32)
    partial = partial.astype(jnp.bfloat16).reshape(streams, seq_parts, chans, outer * rows)
    partial = jnp.transpose(partial, (1, 0, 2, 3))
    parts = lax.all_to_all(partial, "seq", split_axis=0, concat_axis=0, tiled=True)

    gated = convolve(parts, filter_blocks, taps, skip, outer)
    gated = jnp.broadcast_to(gated[None], (tp_parts,) + gated.shape).reshape(-1, chans, rows)
    gated = lax.all_to_all(gated, ("tp", "seq"), split_axis=0, concat_axis=0, tiled=True)
    gated = gated.reshape(tp_parts * chan_tp, rows).T
    return project_out(gated, out_weight)


def solution(mesh):
    return jax.shard_map(
        per_device,
        mesh=mesh,
        in_specs=(
            P("seq", "tp"),
            P(None, "seq", "tp"),
            P(None, None, "tp"),
            P("seq", "tp"),
            P("tp"),
            P("tp", "seq"),
        ),
        out_specs=P("seq", "tp"),
        check_vma=False,
    )
```

```python
import functools
import math

import jax
import jax.numpy as jnp
import numpy as np
from jax import lax
from jax.experimental import pallas as pl
from jax.experimental.pallas import tpu as pltpu
from jax.sharding import PartitionSpec as P

HIGHEST = lax.Precision.HIGHEST
UNROLL = 16


def outer_factor(seq_parts):
    outer = 1
    while 4 * outer * outer <= seq_parts and seq_parts % (2 * outer) == 0:
        outer *= 2
    return outer


def match_rounds(edges, nodes, degree):
    left = list(edges)
    rounds = []
    for _ in range(degree):
        by_source = {}
        for edge in left:
            by_source.setdefault(edge[0], []).append(edge)
        taken = {}

        def place(source, seen):
            for edge in by_source[source]:
                target = edge[1]
                if target in seen:
                    continue
                seen.add(target)
                if target not in taken or place(taken[target][0], seen):
                    taken[target] = edge
                    return True
            return False

        for source in range(nodes):
            place(source, set())
        chosen = sorted(taken.values())
        rounds.append(chosen)
        for edge in chosen:
            left.remove(edge)
    return rounds


def feature_routes(outer, tp_parts):
    groups = max(1, outer // tp_parts)
    shares = max(1, tp_parts // outer)
    edges = []
    for src_outer in range(outer):
        for src_tp in range(tp_parts):
            for group in range(groups):
                for dst_tp in range(tp_parts):
                    dst_outer = src_tp * groups + group if groups > 1 else src_tp // shares
                    slot = src_outer * shares + (src_tp % shares)
                    edges.append(
                        (
                            src_outer * tp_parts + src_tp,
                            dst_outer * tp_parts + dst_tp,
                            group * tp_parts + dst_tp,
                            slot,
                        )
                    )
    return match_rounds(edges, outer * tp_parts, groups * tp_parts)


def spread_features(features, outer, inner_parts, tp_parts):
    rows, cols = features.shape
    groups = max(1, outer // tp_parts)
    shares = max(1, tp_parts // outer)
    width = cols // (groups * tp_parts)
    node = (lax.axis_index("seq") // inner_parts) * tp_parts + lax.axis_index("tp")
    buffer = jnp.zeros((outer * shares, rows, width), features.dtype)
    for chosen in feature_routes(outer, tp_parts):
        send = np.zeros(outer * tp_parts, np.int32)
        fill = np.zeros(outer * tp_parts, np.int32)
        pairs = []
        for source, target, block, slot in chosen:
            send[source] = block
            fill[target] = slot
            for inner in range(inner_parts):
                pairs.append(
                    (
                        ((source // tp_parts) * inner_parts + inner) * tp_parts + source % tp_parts,
                        ((target // tp_parts) * inner_parts + inner) * tp_parts + target % tp_parts,
                    )
                )
        piece = lax.dynamic_slice_in_dim(features, jnp.asarray(send)[node] * width, width, axis=1)
        piece = lax.ppermute(piece, ("seq", "tp"), pairs)
        buffer = lax.dynamic_update_slice_in_dim(buffer, piece[None], jnp.asarray(fill)[node], axis=0)
    return buffer.reshape(outer, shares, rows, width)


def share_over_tp(part, tp_parts):
    pieces = [part]
    for step in range(1, tp_parts):
        pairs = [(i, (i + step) % tp_parts) for i in range(tp_parts)]
        pieces.append(lax.ppermute(part, "tp", pairs))
    return pieces


def project_kernel(place_ref, *refs):
    *share_refs, weight_ref, out_ref = refs
    tp_parts = len(share_refs)
    outer, shares, rows, width = share_refs[0].shape
    seq_parts, _, chans, count = out_ref.shape
    sums = jnp.zeros((count, seq_parts * chans), jnp.float32)
    for step, share_ref in enumerate(share_refs):
        which = lax.rem(place_ref[0] - step + tp_parts, tp_parts)
        for share in range(shares):
            sums = sums + jnp.dot(
                share_ref[:, share].reshape(count, width),
                weight_ref[0, share, which],
                preferred_element_type=jnp.float32,
            )
    turned = sums.T.astype(out_ref.dtype)
    for seq in range(seq_parts):
        out_ref[seq, 0] = turned[seq * chans : (seq + 1) * chans]


def project_in(pieces, weight, seq_parts):
    tp_parts = len(pieces)
    outer, shares, rows, width = pieces[0].shape
    streams, _, chan_tp = weight.shape
    weight = weight.reshape(streams, shares, tp_parts, width, chan_tp)
    chans = chan_tp // seq_parts
    count = outer * rows
    place = lax.axis_index("tp").astype(jnp.int32)[None]
    whole = pl.BlockSpec((outer, shares, rows, width), lambda i, place: (0, 0, 0, 0))
    return pl.pallas_call(
        project_kernel,
        grid_spec=pltpu.PrefetchScalarGridSpec(
            num_scalar_prefetch=1,
            grid=(streams,),
            in_specs=[whole] * tp_parts
            + [
                pl.BlockSpec(
                    (1, shares, tp_parts, width, chan_tp), lambda i, place: (i, 0, 0, 0, 0)
                )
            ],
            out_specs=pl.BlockSpec((seq_parts, 1, chans, count), lambda i, place: (0, i, 0, 0)),
        ),
        out_shape=jax.ShapeDtypeStruct((seq_parts, streams, chans, count), jnp.bfloat16),
        compiler_params=pltpu.CompilerParams(vmem_limit_bytes=56 * 2**20),
        cost_estimate=pl.CostEstimate(
            flops=2 * count * weight.size,
            bytes_accessed=2 * (weight.size + tp_parts * pieces[0].size) + 2 * streams * count * chan_tp,
            transcendentals=0,
        ),
    )(place, *pieces, weight)


def tables(block):
    place = np.arange(block)
    angle = 2.0 * math.pi * np.outer(place, place + 0.5) / (2 * block)
    forward = np.concatenate([np.cos(angle), -np.sin(angle)], 1)
    place = np.arange(2 * block)
    angle = 2.0 * math.pi * np.outer(np.arange(block) + 0.5, place) / (2 * block)
    backward = np.concatenate([np.cos(angle), -np.sin(angle)], 0) / block
    return forward.astype(np.float32), backward.astype(np.float32)


def each(count, body):
    if isinstance(count, int) and count <= UNROLL:
        for index in range(count):
            body(index)
    else:
        lax.fori_loop(0, count, lambda index, carry: (body(index), carry)[1], 0)


def total(count, term, zero):
    if isinstance(count, int) and count <= UNROLL:
        result = zero
        for index in range(count):
            result = jax.tree.map(jnp.add, result, term(index))
        return result
    return lax.fori_loop(
        0, count, lambda index, sums: jax.tree.map(jnp.add, sums, term(index)), zero
    )


def conv_kernel(
    outer, parts_ref, filter_ref, taps_ref, skip_ref, fwd_ref, bwd_ref, out_ref,
    proj, query, inner, spec, filter_spec, product, back
):
    blocks, streams, chans, _ = parts_ref.shape
    rows = filter_ref.shape[2]
    inner_parts = blocks // outer
    taps_count = taps_ref.shape[1]
    lane = lax.broadcasted_iota(jnp.int32, (chans, rows), 1)

    def add_up(index, stream, slot):
        sums = jnp.zeros((chans, rows), jnp.float32)
        column = pl.ds(pl.multiple_of(slot * rows, rows), rows)
        for part in range(outer):
            sums = sums + parts_ref[part * inner_parts + index % inner_parts, stream, :, column].astype(jnp.float32)
        return sums

    for stream in range(streams):
        proj[0, stream] = jnp.zeros((chans, rows), jnp.float32)

    def first(index):
        filtered = []
        for stream in range(streams):
            proj[index + 1, stream] = add_up(index, stream, index // inner_parts)
        for stream in range(streams):
            now, past = proj[index + 1, stream], proj[index, stream]
            value = taps_ref[stream, 0] * now
            for offset in range(1, taps_count):
                moved = jnp.where(
                    lane < offset, pltpu.roll(past, offset, 1), pltpu.roll(now, offset, 1)
                )
                value = value + taps_ref[stream, offset] * moved
            filtered.append(value)
        query[index] = filtered[0]
        inner[index] = filtered[1] * filtered[2]

    each(blocks, first)

    def apply(source, table_ref, target):
        if chans % 8 == 0:
            flat = source[...].reshape(blocks * chans, source.shape[2])
            done = jnp.dot(flat, table_ref[...], precision=HIGHEST, preferred_element_type=jnp.float32)
            target[...] = done.reshape(target.shape)
        else:

            def one(index):
                target[index] = jnp.dot(
                    source[index], table_ref[...], precision=HIGHEST, preferred_element_type=jnp.float32
                )

            each(blocks, one)

    apply(filter_ref, fwd_ref, filter_spec)
    apply(inner, fwd_ref, spec)

    def multiply(index):
        def term(step):
            left, right = spec[step], filter_spec[index - step]
            left_real, left_imag = left[:, :rows], left[:, rows:]
            right_real, right_imag = right[:, :rows], right[:, rows:]
            return (
                left_real * right_real - left_imag * right_imag,
                left_real * right_imag + left_imag * right_real,
            )

        zero = jnp.zeros((chans, rows), jnp.float32)
        real, imag = total(index + 1, term, (zero, zero))
        product[index, :, :rows] = real
        product[index, :, rows:] = imag

    each(blocks, multiply)
    apply(product, bwd_ref, back)

    def last(index, carried):
        long_mix = back[index, :, :rows] + carried
        gated = query[index] * (long_mix + skip_ref[...] * inner[index])
        out_ref[index] = gated.astype(out_ref.dtype)

    last(0, jnp.zeros((chans, rows), jnp.float32))
    each(blocks - 1, lambda index: last(index + 1, back[index, :, rows:]))


def convolve(parts, filter_blocks, taps, skip, outer):
    blocks, streams, chans, _ = parts.shape
    rows = filter_blocks.shape[2]
    forward, backward = tables(rows)
    wide = (blocks, chans, 2 * rows)
    narrow = (blocks, chans, rows)
    vmem = pl.BlockSpec(memory_space=pltpu.VMEM)
    return pl.pallas_call(
        functools.partial(conv_kernel, outer),
        out_shape=jax.ShapeDtypeStruct(narrow, jnp.bfloat16),
        in_specs=[vmem] * 6,
        out_specs=vmem,
        scratch_shapes=[
            pltpu.VMEM((blocks + 1, streams, chans, rows), jnp.float32),
            pltpu.VMEM(narrow, jnp.float32),
            pltpu.VMEM(narrow, jnp.float32),
            pltpu.VMEM(wide, jnp.float32),
            pltpu.VMEM(wide, jnp.float32),
            pltpu.VMEM(wide, jnp.float32),
            pltpu.VMEM(wide, jnp.float32),
        ],
        compiler_params=pltpu.CompilerParams(vmem_limit_bytes=40 * 2**20),
        cost_estimate=pl.CostEstimate(flops=10**9, bytes_accessed=4 * 2**20, transcendentals=0),
    )(parts, filter_blocks, taps, skip, jnp.asarray(forward), jnp.asarray(backward))


def lay_out(out_proj, seq_parts, tp_parts):
    ranges = seq_parts // tp_parts
    pairs = []
    for seq in range(seq_parts):
        for tp in range(tp_parts):
            target = (tp * ranges + seq % ranges) * tp_parts + seq // ranges
            pairs.append((seq * tp_parts + tp, target))
    return lax.ppermute(out_proj, ("seq", "tp"), pairs)


def out_kernel(gated_ref, weight_ref, out_ref):
    shares, _, depth, _ = weight_ref.shape
    sums = jnp.zeros(out_ref.shape, jnp.float32)
    for share in range(shares):
        left = gated_ref[:, share * depth : (share + 1) * depth]
        sums = sums + jnp.dot(left, weight_ref[share, 0], preferred_element_type=jnp.float32)
    out_ref[...] = sums.astype(out_ref.dtype)


def project_out(gated, weight):
    rows, depth_all = gated.shape
    shares, ranges, depth, width = weight.shape
    columns = ranges * width
    return pl.pallas_call(
        out_kernel,
        grid=(ranges,),
        out_shape=jax.ShapeDtypeStruct((rows, columns), jnp.bfloat16),
        in_specs=[
            pl.BlockSpec((rows, depth_all), lambda r: (0, 0)),
            pl.BlockSpec((shares, 1, depth, width), lambda r: (0, r, 0, 0)),
        ],
        out_specs=pl.BlockSpec((rows, width), lambda r: (0, r)),
        compiler_params=pltpu.CompilerParams(vmem_limit_bytes=56 * 2**20),
        cost_estimate=pl.CostEstimate(
            flops=2 * rows * depth_all * columns,
            bytes_accessed=2 * (weight.size + gated.size + rows * columns),
            transcendentals=0,
        ),
    )(gated, weight)


def per_device(features, in_proj, short_taps, long_filter, skip_gain, out_proj):
    rows = features.shape[0]
    seq_parts = lax.axis_size("seq")
    tp_parts = lax.axis_size("tp")
    outer = outer_factor(seq_parts)
    inner_parts = seq_parts // outer
    streams, _, chan_tp = in_proj.shape
    chans = chan_tp // seq_parts
    position = lax.axis_index("seq")

    inner_groups = [[a * inner_parts + b for b in range(inner_parts)] for a in range(outer)]
    weight = lax.all_gather(in_proj, "seq", axis=1, tiled=True, axis_index_groups=inner_groups)

    part = spread_features(features, outer, inner_parts, tp_parts)
    part, out_proj, long_filter = lax.optimization_barrier((part, out_proj, long_filter))
    pieces = share_over_tp(part, tp_parts)
    out_block = lay_out(out_proj, seq_parts, tp_parts)
    filter_blocks = lax.all_to_all(
        long_filter.T.reshape(seq_parts, chans, rows), "seq", split_axis=0, concat_axis=0, tiled=True
    )
    pieces, weight, out_block, filter_blocks = lax.optimization_barrier(
        (pieces, weight, out_block, filter_blocks)
    )
    out_weight = lax.all_gather(out_block, "seq")
    out_weight = out_weight.reshape((tp_parts, seq_parts // tp_parts) + out_proj.shape)

    taps = lax.dynamic_slice_in_dim(short_taps, position * chans, chans, axis=2)
    taps = jnp.broadcast_to(taps[..., None], taps.shape + (rows,))
    skip = lax.dynamic_slice_in_dim(skip_gain, position * chans, chans, axis=0)
    skip = jnp.broadcast_to(skip[:, None], (chans, rows))

    partial = project_in(pieces, weight, seq_parts)
    parts = lax.all_to_all(partial, "seq", split_axis=0, concat_axis=0, tiled=True)

    gated = convolve(parts, filter_blocks, taps, skip, outer)
    gated = jnp.broadcast_to(gated[None], (tp_parts,) + gated.shape).reshape(-1, chans, rows)
    gated = lax.all_to_all(gated, ("tp", "seq"), split_axis=0, concat_axis=0, tiled=True)
    gated = gated.reshape(tp_parts * chan_tp, rows).T
    return project_out(gated, out_weight)


def solution(mesh):
    return jax.shard_map(
        per_device,
        mesh=mesh,
        in_specs=(
            P("seq", "tp"),
            P(None, "seq", "tp"),
            P(None, None, "tp"),
            P("seq", "tp"),
            P("tp"),
            P("tp", "seq"),
        ),
        out_specs=P("seq", "tp"),
        check_vma=False,
    )
```

```python
import functools
import math

import jax
import jax.numpy as jnp
import numpy as np
from jax import lax
from jax.experimental import pallas as pl
from jax.experimental.pallas import tpu as pltpu
from jax.sharding import PartitionSpec as P

HIGHEST = lax.Precision.HIGHEST
UNROLL = 16
CHUNKS = 2


def outer_factor(seq_parts):
    return 2 if seq_parts % 2 == 0 else 1


def spread_features(features, outer, inner_parts, tp_parts):
    rows, cols = features.shape
    groups = max(1, outer // tp_parts)
    shares = max(1, tp_parts // outer)
    width = cols // (groups * tp_parts)
    tp_place = lax.axis_index("tp")
    outer_place = lax.axis_index("seq") // inner_parts
    blocks = features.reshape(rows, groups, tp_parts, width)
    held = []
    for step in range(tp_parts):
        which = lax.rem(tp_place + step, tp_parts)
        piece = lax.dynamic_index_in_dim(blocks, which, axis=2, keepdims=False)
        if step:
            piece = lax.ppermute(piece, "tp", [(i, (i + step) % tp_parts) for i in range(tp_parts)])
        held.append(jnp.transpose(piece, (1, 0, 2)))
    held = jnp.stack(held)
    order = lax.rem(tp_place - jnp.arange(tp_parts) + tp_parts, tp_parts)
    ranges = held[order].reshape(outer, shares, rows, width)
    seq_parts = outer * inner_parts
    arrived = []
    for step in range(outer):
        which = lax.rem(outer_place + step, outer)
        piece = lax.dynamic_index_in_dim(ranges, which, axis=0, keepdims=False)
        if step:
            far = step * inner_parts
            piece = lax.ppermute(piece, "seq", [(i, (i + far) % seq_parts) for i in range(seq_parts)])
        arrived.append(piece)
    order = lax.rem(outer_place - jnp.arange(outer) + outer, outer)
    return jnp.stack(arrived)[order]


def share_over_tp(part, tp_parts):
    pieces = [part]
    for step in range(1, tp_parts):
        pairs = [(i, (i + step) % tp_parts) for i in range(tp_parts)]
        pieces.append(lax.ppermute(part, "tp", pairs))
    return pieces


def project_kernel(tp_parts, place_ref, *refs):
    *share_refs, weight_ref, out_ref = refs
    seq_parts, _, chans, count = out_ref.shape
    done = []
    for first in range(0, len(share_refs), tp_parts):
        outer, shares, rows, width = share_refs[first].shape
        sums = jnp.zeros((outer * rows, seq_parts * chans), jnp.float32)
        for step in range(tp_parts):
            which = lax.rem(place_ref[0] - step + tp_parts, tp_parts)
            for share in range(shares):
                sums = sums + jnp.dot(
                    share_refs[first + step][:, share].reshape(outer * rows, width),
                    weight_ref[0, share, which],
                    preferred_element_type=jnp.float32,
                )
        done.append(sums.reshape(outer, rows, seq_parts * chans))
    turned = jnp.concatenate(done, 1).reshape(count, seq_parts * chans).T.astype(out_ref.dtype)
    for seq in range(seq_parts):
        out_ref[seq, 0] = turned[seq * chans : (seq + 1) * chans]


def project_in(chunks, weight, seq_parts):
    tp_parts = len(chunks[0])
    outer, shares, rows, width = chunks[0][0].shape
    streams, _, chan_tp = weight.shape
    weight = weight.reshape(streams, shares, tp_parts, width, chan_tp)
    chans = chan_tp // seq_parts
    count = outer * rows * len(chunks)
    pieces = [piece for chunk in chunks for piece in chunk]
    place = lax.axis_index("tp").astype(jnp.int32)[None]
    whole = pl.BlockSpec((outer, shares, rows, width), lambda i, place: (0, 0, 0, 0))
    return pl.pallas_call(
        functools.partial(project_kernel, tp_parts),
        grid_spec=pltpu.PrefetchScalarGridSpec(
            num_scalar_prefetch=1,
            grid=(streams,),
            in_specs=[whole] * len(pieces)
            + [
                pl.BlockSpec(
                    (1, shares, tp_parts, width, chan_tp), lambda i, place: (i, 0, 0, 0, 0)
                )
            ],
            out_specs=pl.BlockSpec((seq_parts, 1, chans, count), lambda i, place: (0, i, 0, 0)),
        ),
        out_shape=jax.ShapeDtypeStruct((seq_parts, streams, chans, count), jnp.bfloat16),
        compiler_params=pltpu.CompilerParams(vmem_limit_bytes=56 * 2**20),
        cost_estimate=pl.CostEstimate(
            flops=2 * count * weight.size,
            bytes_accessed=2 * (weight.size + len(pieces) * pieces[0].size)
            + 2 * streams * count * chan_tp,
            transcendentals=0,
        ),
    )(place, *pieces, weight)


def tables(block):
    place = np.arange(block)
    angle = 2.0 * math.pi * np.outer(place, place + 0.5) / (2 * block)
    forward = np.concatenate([np.cos(angle), -np.sin(angle)], 1)
    place = np.arange(2 * block)
    angle = 2.0 * math.pi * np.outer(np.arange(block) + 0.5, place) / (2 * block)
    backward = np.concatenate([np.cos(angle), -np.sin(angle)], 0) / block
    return forward.astype(np.float32), backward.astype(np.float32)


def each(count, body):
    if isinstance(count, int) and count <= UNROLL:
        for index in range(count):
            body(index)
    else:
        lax.fori_loop(0, count, lambda index, carry: (body(index), carry)[1], 0)


def total(count, term, zero):
    if isinstance(count, int) and count <= UNROLL:
        result = zero
        for index in range(count):
            result = jax.tree.map(jnp.add, result, term(index))
        return result
    return lax.fori_loop(
        0, count, lambda index, sums: jax.tree.map(jnp.add, sums, term(index)), zero
    )


def conv_kernel(
    outer, parts_ref, filter_ref, taps_ref, skip_ref, fwd_ref, bwd_ref, out_ref,
    proj, query, inner, spec, filter_spec, product, back
):
    blocks, streams, chans, _ = parts_ref.shape
    rows = filter_ref.shape[2]
    inner_parts = blocks // outer
    taps_count = taps_ref.shape[1]
    lane = lax.broadcasted_iota(jnp.int32, (chans, rows), 1)

    def add_up(index, stream, slot):
        sums = jnp.zeros((chans, rows), jnp.float32)
        column = pl.ds(pl.multiple_of(slot * rows, rows), rows)
        for part in range(outer):
            sums = sums + parts_ref[part * inner_parts + index % inner_parts, stream, :, column].astype(jnp.float32)
        return sums

    for stream in range(streams):
        proj[0, stream] = jnp.zeros((chans, rows), jnp.float32)

    def first(index):
        filtered = []
        for stream in range(streams):
            proj[index + 1, stream] = add_up(index, stream, index // inner_parts)
        for stream in range(streams):
            now, past = proj[index + 1, stream], proj[index, stream]
            value = taps_ref[stream, 0] * now
            for offset in range(1, taps_count):
                moved = jnp.where(
                    lane < offset, pltpu.roll(past, offset, 1), pltpu.roll(now, offset, 1)
                )
                value = value + taps_ref[stream, offset] * moved
            filtered.append(value)
        query[index] = filtered[0]
        inner[index] = filtered[1] * filtered[2]

    each(blocks, first)

    def apply(source, table_ref, target):
        if chans % 8 == 0:
            flat = source[...].reshape(blocks * chans, source.shape[2])
            done = jnp.dot(flat, table_ref[...], precision=HIGHEST, preferred_element_type=jnp.float32)
            target[...] = done.reshape(target.shape)
        else:

            def one(index):
                target[index] = jnp.dot(
                    source[index], table_ref[...], precision=HIGHEST, preferred_element_type=jnp.float32
                )

            each(blocks, one)

    apply(filter_ref, fwd_ref, filter_spec)
    apply(inner, fwd_ref, spec)

    def multiply(index):
        def term(step):
            left, right = spec[step], filter_spec[index - step]
            left_real, left_imag = left[:, :rows], left[:, rows:]
            right_real, right_imag = right[:, :rows], right[:, rows:]
            return (
                left_real * right_real - left_imag * right_imag,
                left_real * right_imag + left_imag * right_real,
            )

        zero = jnp.zeros((chans, rows), jnp.float32)
        real, imag = total(index + 1, term, (zero, zero))
        product[index, :, :rows] = real
        product[index, :, rows:] = imag

    each(blocks, multiply)
    apply(product, bwd_ref, back)

    def last(index, carried):
        long_mix = back[index, :, :rows] + carried
        gated = query[index] * (long_mix + skip_ref[...] * inner[index])
        out_ref[index] = gated.astype(out_ref.dtype)

    last(0, jnp.zeros((chans, rows), jnp.float32))
    each(blocks - 1, lambda index: last(index + 1, back[index, :, rows:]))


def convolve(parts, filter_blocks, taps, skip, outer):
    blocks, streams, chans, _ = parts.shape
    rows = filter_blocks.shape[2]
    forward, backward = tables(rows)
    wide = (blocks, chans, 2 * rows)
    narrow = (blocks, chans, rows)
    vmem = pl.BlockSpec(memory_space=pltpu.VMEM)
    return pl.pallas_call(
        functools.partial(conv_kernel, outer),
        out_shape=jax.ShapeDtypeStruct(narrow, jnp.bfloat16),
        in_specs=[vmem] * 6,
        out_specs=vmem,
        scratch_shapes=[
            pltpu.VMEM((blocks + 1, streams, chans, rows), jnp.float32),
            pltpu.VMEM(narrow, jnp.float32),
            pltpu.VMEM(narrow, jnp.float32),
            pltpu.VMEM(wide, jnp.float32),
            pltpu.VMEM(wide, jnp.float32),
            pltpu.VMEM(wide, jnp.float32),
            pltpu.VMEM(wide, jnp.float32),
        ],
        compiler_params=pltpu.CompilerParams(vmem_limit_bytes=40 * 2**20),
        cost_estimate=pl.CostEstimate(flops=10**9, bytes_accessed=4 * 2**20, transcendentals=0),
    )(parts, filter_blocks, taps, skip, jnp.asarray(forward), jnp.asarray(backward))


def lay_out(out_proj, seq_parts, tp_parts):
    ranges = seq_parts // tp_parts
    pairs = []
    for seq in range(seq_parts):
        for tp in range(tp_parts):
            target = (tp * ranges + seq % ranges) * tp_parts + seq // ranges
            pairs.append((seq * tp_parts + tp, target))
    return lax.ppermute(out_proj, ("seq", "tp"), pairs)


def out_kernel(gated_ref, weight_ref, out_ref):
    shares, _, depth, _ = weight_ref.shape
    sums = jnp.zeros(out_ref.shape, jnp.float32)
    for share in range(shares):
        left = gated_ref[:, share * depth : (share + 1) * depth]
        sums = sums + jnp.dot(left, weight_ref[share, 0], preferred_element_type=jnp.float32)
    out_ref[...] = sums.astype(out_ref.dtype)


def project_out(gated, weight):
    rows, depth_all = gated.shape
    shares, ranges, depth, width = weight.shape
    columns = ranges * width
    return pl.pallas_call(
        out_kernel,
        grid=(ranges,),
        out_shape=jax.ShapeDtypeStruct((rows, columns), jnp.bfloat16),
        in_specs=[
            pl.BlockSpec((rows, depth_all), lambda r: (0, 0)),
            pl.BlockSpec((shares, 1, depth, width), lambda r: (0, r, 0, 0)),
        ],
        out_specs=pl.BlockSpec((rows, width), lambda r: (0, r)),
        compiler_params=pltpu.CompilerParams(vmem_limit_bytes=56 * 2**20),
        cost_estimate=pl.CostEstimate(
            flops=2 * rows * depth_all * columns,
            bytes_accessed=2 * (weight.size + gated.size + rows * columns),
            transcendentals=0,
        ),
    )(gated, weight)


def per_device(features, in_proj, short_taps, long_filter, skip_gain, out_proj):
    rows = features.shape[0]
    seq_parts = lax.axis_size("seq")
    tp_parts = lax.axis_size("tp")
    outer = outer_factor(seq_parts)
    inner_parts = seq_parts // outer
    streams, _, chan_tp = in_proj.shape
    chans = chan_tp // seq_parts
    position = lax.axis_index("seq")

    inner_groups = [[a * inner_parts + b for b in range(inner_parts)] for a in range(outer)]
    weight = lax.all_gather(in_proj, "seq", axis=1, tiled=True, axis_index_groups=inner_groups)

    chunk_rows = rows // CHUNKS
    parts = [
        spread_features(
            features[index * chunk_rows : (index + 1) * chunk_rows], outer, inner_parts, tp_parts
        )
        for index in range(CHUNKS)
    ]
    chunks = [share_over_tp(part, tp_parts) for part in parts]
    _, out_proj, long_filter = lax.optimization_barrier((parts, out_proj, long_filter))
    out_block = lay_out(out_proj, seq_parts, tp_parts)
    filter_blocks = lax.all_to_all(
        long_filter.T.reshape(seq_parts, chans, rows), "seq", split_axis=0, concat_axis=0, tiled=True
    )
    chunks, weight, out_block, filter_blocks = lax.optimization_barrier(
        (chunks, weight, out_block, filter_blocks)
    )
    out_weight = lax.all_gather(out_block, "seq")
    out_weight = out_weight.reshape((tp_parts, seq_parts // tp_parts) + out_proj.shape)

    taps = lax.dynamic_slice_in_dim(short_taps, position * chans, chans, axis=2)
    taps = jnp.broadcast_to(taps[..., None], taps.shape + (rows,))
    skip = lax.dynamic_slice_in_dim(skip_gain, position * chans, chans, axis=0)
    skip = jnp.broadcast_to(skip[:, None], (chans, rows))

    partial = project_in(chunks, weight, seq_parts)
    parts = lax.all_to_all(partial, "seq", split_axis=0, concat_axis=0, tiled=True)

    gated = convolve(parts, filter_blocks, taps, skip, outer)
    gated = jnp.broadcast_to(gated[None], (tp_parts,) + gated.shape).reshape(-1, chans, rows)
    gated = lax.all_to_all(gated, ("tp", "seq"), split_axis=0, concat_axis=0, tiled=True)
    gated = gated.reshape(tp_parts * chan_tp, rows).T
    return project_out(gated, out_weight)


def solution(mesh):
    return jax.shard_map(
        per_device,
        mesh=mesh,
        in_specs=(
            P("seq", "tp"),
            P(None, "seq", "tp"),
            P(None, None, "tp"),
            P("seq", "tp"),
            P("tp"),
            P("tp", "seq"),
        ),
        out_specs=P("seq", "tp"),
        check_vma=False,
    )
```

```python
import functools
import math

import jax
import jax.numpy as jnp
import numpy as np
from jax import lax
from jax.experimental import pallas as pl
from jax.experimental.pallas import tpu as pltpu
from jax.sharding import PartitionSpec as P

HIGHEST = lax.Precision.HIGHEST
UNROLL = 16
CHUNKS = 2


def outer_factor(seq_parts, tp_parts):
    outer = tp_parts
    while 4 * outer * outer <= seq_parts and seq_parts % (2 * outer) == 0:
        outer *= 2
    return outer


def match_rounds(edges, nodes, degree):
    left = list(edges)
    rounds = []
    for _ in range(degree):
        by_source = {}
        for edge in left:
            by_source.setdefault(edge[0], []).append(edge)
        taken = {}

        def place(source, seen):
            for edge in by_source[source]:
                target = edge[1]
                if target in seen:
                    continue
                seen.add(target)
                if target not in taken or place(taken[target][0], seen):
                    taken[target] = edge
                    return True
            return False

        for source in range(nodes):
            place(source, set())
        chosen = sorted(taken.values())
        rounds.append(chosen)
        for edge in chosen:
            left.remove(edge)
    return rounds


def return_output(out, outer, inner_parts, tp_parts):
    _, part_rows, width = out.shape
    per_tp = outer // tp_parts
    edges = []
    for src in range(outer):
        for tp in range(tp_parts):
            for dst in range(outer):
                edges.append((src * tp_parts + tp, dst * tp_parts + src // per_tp, dst, tp, src % per_tp))
    node = (lax.axis_index("seq") // inner_parts) * tp_parts + lax.axis_index("tp")
    result = jnp.zeros((tp_parts * part_rows, per_tp * width), out.dtype)
    for chosen in match_rounds(edges, outer * tp_parts, outer):
        send, row, column = (np.zeros(outer * tp_parts, np.int32) for _ in range(3))
        pairs = []
        for source, target, block, row_part, column_part in chosen:
            send[source], row[target], column[target] = block, row_part, column_part
            for inner in range(inner_parts):
                pairs.append(
                    tuple(
                        ((end // tp_parts) * inner_parts + inner) * tp_parts + end % tp_parts
                        for end in (source, target)
                    )
                )
        piece = lax.dynamic_index_in_dim(out, jnp.asarray(send)[node], axis=0, keepdims=False)
        piece = lax.ppermute(piece, ("seq", "tp"), pairs)
        result = lax.dynamic_update_slice(
            result, piece, (jnp.asarray(row)[node] * part_rows, jnp.asarray(column)[node] * width)
        )
    return result


def share_columns(features, outer, tp_parts):
    rows, cols = features.shape
    groups = outer // tp_parts
    blocks = features.reshape(rows, groups, tp_parts, cols // outer)
    blocks = jnp.transpose(blocks, (2, 1, 0, 3))
    blocks = lax.all_to_all(blocks, "tp", split_axis=0, concat_axis=0, tiled=True)
    return blocks.reshape(outer, rows, -1)


def share_over_tp(part, tp_parts):
    pieces = [part]
    for step in range(1, tp_parts):
        pairs = [(i, (i + step) % tp_parts) for i in range(tp_parts)]
        pieces.append(lax.ppermute(part, "tp", pairs))
    return pieces


def project_kernel(tp_parts, place_ref, *refs):
    *share_refs, weight_ref, out_ref = refs
    seq_parts, _, chans, count = out_ref.shape
    done = []
    for first in range(0, len(share_refs), tp_parts):
        outer, rows, width = share_refs[first].shape
        sums = jnp.zeros((outer * rows, seq_parts * chans), jnp.float32)
        for step in range(tp_parts):
            which = lax.rem(place_ref[0] - step + tp_parts, tp_parts)
            sums = sums + jnp.dot(
                share_refs[first + step][...].reshape(outer * rows, width),
                weight_ref[0, which],
                preferred_element_type=jnp.float32,
            )
        done.append(sums.reshape(outer, rows, seq_parts * chans))
    turned = jnp.concatenate(done, 1).reshape(count, seq_parts * chans).T.astype(out_ref.dtype)
    for seq in range(seq_parts):
        out_ref[seq, 0] = turned[seq * chans : (seq + 1) * chans]


def project_in(chunks, weight, seq_parts):
    tp_parts = len(chunks[0])
    outer, rows, width = chunks[0][0].shape
    streams, _, chan_tp = weight.shape
    weight = weight.reshape(streams, tp_parts, width, chan_tp)
    chans = chan_tp // seq_parts
    count = outer * rows * len(chunks)
    pieces = [piece for chunk in chunks for piece in chunk]
    place = lax.axis_index("tp").astype(jnp.int32)[None]
    whole = pl.BlockSpec((outer, rows, width), lambda i, place: (0, 0, 0))
    return pl.pallas_call(
        functools.partial(project_kernel, tp_parts),
        grid_spec=pltpu.PrefetchScalarGridSpec(
            num_scalar_prefetch=1,
            grid=(streams,),
            in_specs=[whole] * len(pieces)
            + [pl.BlockSpec((1, tp_parts, width, chan_tp), lambda i, place: (i, 0, 0, 0))],
            out_specs=pl.BlockSpec((seq_parts, 1, chans, count), lambda i, place: (0, i, 0, 0)),
        ),
        out_shape=jax.ShapeDtypeStruct((seq_parts, streams, chans, count), jnp.bfloat16),
        compiler_params=pltpu.CompilerParams(vmem_limit_bytes=56 * 2**20),
        cost_estimate=pl.CostEstimate(
            flops=2 * count * weight.size,
            bytes_accessed=2 * (weight.size + len(pieces) * pieces[0].size)
            + 2 * streams * count * chan_tp,
            transcendentals=0,
        ),
    )(place, *pieces, weight)


def tables(block):
    place = np.arange(block)
    angle = 2.0 * math.pi * np.outer(place, place + 0.5) / (2 * block)
    forward = np.concatenate([np.cos(angle), -np.sin(angle)], 1)
    place = np.arange(2 * block)
    angle = 2.0 * math.pi * np.outer(np.arange(block) + 0.5, place) / (2 * block)
    backward = np.concatenate([np.cos(angle), -np.sin(angle)], 0) / block
    return forward.astype(np.float32), backward.astype(np.float32)


def each(count, body):
    if isinstance(count, int) and count <= UNROLL:
        for index in range(count):
            body(index)
    else:
        lax.fori_loop(0, count, lambda index, carry: (body(index), carry)[1], 0)


def total(count, term, zero):
    if isinstance(count, int) and count <= UNROLL:
        result = zero
        for index in range(count):
            result = jax.tree.map(jnp.add, result, term(index))
        return result
    return lax.fori_loop(
        0, count, lambda index, sums: jax.tree.map(jnp.add, sums, term(index)), zero
    )


def conv_kernel(
    outer, parts_ref, filter_ref, taps_ref, skip_ref, fwd_ref, bwd_ref, out_ref,
    proj, query, inner, spec, filter_spec, product, back
):
    blocks, streams, chans, _ = parts_ref.shape
    rows = filter_ref.shape[2]
    inner_parts = blocks // outer
    taps_count = taps_ref.shape[1]
    lane = lax.broadcasted_iota(jnp.int32, (chans, rows), 1)

    def add_up(index, stream, slot):
        sums = jnp.zeros((chans, rows), jnp.float32)
        column = pl.ds(pl.multiple_of(slot * rows, rows), rows)
        for part in range(outer):
            sums = sums + parts_ref[part * inner_parts + index % inner_parts, stream, :, column].astype(jnp.float32)
        return sums

    for stream in range(streams):
        proj[0, stream] = jnp.zeros((chans, rows), jnp.float32)

    def first(index):
        filtered = []
        for stream in range(streams):
            proj[index + 1, stream] = add_up(index, stream, index // inner_parts)
        for stream in range(streams):
            now, past = proj[index + 1, stream], proj[index, stream]
            value = taps_ref[stream, 0] * now
            for offset in range(1, taps_count):
                moved = jnp.where(
                    lane < offset, pltpu.roll(past, offset, 1), pltpu.roll(now, offset, 1)
                )
                value = value + taps_ref[stream, offset] * moved
            filtered.append(value)
        query[index] = filtered[0]
        inner[index] = filtered[1] * filtered[2]

    each(blocks, first)

    def apply(source, table_ref, target):
        if chans % 8 == 0:
            flat = source[...].reshape(blocks * chans, source.shape[2])
            done = jnp.dot(flat, table_ref[...], precision=HIGHEST, preferred_element_type=jnp.float32)
            target[...] = done.reshape(target.shape)
        else:

            def one(index):
                target[index] = jnp.dot(
                    source[index], table_ref[...], precision=HIGHEST, preferred_element_type=jnp.float32
                )

            each(blocks, one)

    apply(filter_ref, fwd_ref, filter_spec)
    apply(inner, fwd_ref, spec)

    def multiply(index):
        def term(step):
            left, right = spec[step], filter_spec[index - step]
            left_real, left_imag = left[:, :rows], left[:, rows:]
            right_real, right_imag = right[:, :rows], right[:, rows:]
            return (
                left_real * right_real - left_imag * right_imag,
                left_real * right_imag + left_imag * right_real,
            )

        zero = jnp.zeros((chans, rows), jnp.float32)
        real, imag = total(index + 1, term, (zero, zero))
        product[index, :, :rows] = real
        product[index, :, rows:] = imag

    each(blocks, multiply)
    apply(product, bwd_ref, back)

    def last(index, carried):
        long_mix = back[index, :, :rows] + carried
        query[index] = query[index] * (long_mix + skip_ref[...] * inner[index])

    last(0, jnp.zeros((chans, rows), jnp.float32))
    each(blocks - 1, lambda index: last(index + 1, back[index, :, rows:]))

    tp_parts = out_ref.shape[0]
    part_rows = rows // tp_parts

    def spread(inner_index):
        for part in range(tp_parts):
            for group in range(outer // tp_parts):
                packed = jnp.zeros((chans, rows), jnp.float32)
                for place in range(tp_parts):
                    block = query[(group * tp_parts + place) * inner_parts + inner_index]
                    shift = (place - part) * part_rows % rows
                    block = pltpu.roll(block, shift, 1) if shift else block
                    packed = jnp.where(lane // part_rows == place, block, packed)
                out_ref[part, inner_index, :, group * rows : (group + 1) * rows] = packed.astype(out_ref.dtype)

    each(inner_parts, spread)


def convolve(parts, filter_blocks, taps, skip, outer, tp_parts):
    blocks, streams, chans, _ = parts.shape
    rows = filter_blocks.shape[2]
    forward, backward = tables(rows)
    wide = (blocks, chans, 2 * rows)
    narrow = (blocks, chans, rows)
    vmem = pl.BlockSpec(memory_space=pltpu.VMEM)
    return pl.pallas_call(
        functools.partial(conv_kernel, outer),
        out_shape=jax.ShapeDtypeStruct(
            (tp_parts, blocks // outer, chans, outer // tp_parts * rows), jnp.bfloat16
        ),
        in_specs=[vmem] * 6,
        out_specs=vmem,
        scratch_shapes=[
            pltpu.VMEM((blocks + 1, streams, chans, rows), jnp.float32),
            pltpu.VMEM(narrow, jnp.float32),
            pltpu.VMEM(narrow, jnp.float32),
            pltpu.VMEM(wide, jnp.float32),
            pltpu.VMEM(wide, jnp.float32),
            pltpu.VMEM(wide, jnp.float32),
            pltpu.VMEM(wide, jnp.float32),
        ],
        compiler_params=pltpu.CompilerParams(vmem_limit_bytes=40 * 2**20),
        cost_estimate=pl.CostEstimate(flops=10**9, bytes_accessed=4 * 2**20, transcendentals=0),
    )(parts, filter_blocks, taps, skip, jnp.asarray(forward), jnp.asarray(backward))


def out_kernel(place_ref, gated_ref, weight_ref, out_ref):
    tp_parts = gated_ref.shape[0]
    sums = jnp.zeros(out_ref.shape, jnp.float32)
    for step in range(tp_parts):
        which = lax.rem(place_ref[0] - step + tp_parts, tp_parts)
        sums = sums + jnp.dot(gated_ref[which], weight_ref[0, step], preferred_element_type=jnp.float32)
    out_ref[...] = sums.astype(out_ref.dtype)


def project_out(gated, weight):
    tp_parts, rows, depth = gated.shape
    inner_parts, _, _, width = weight.shape
    columns = inner_parts * width
    place = lax.axis_index("tp").astype(jnp.int32)[None]
    return pl.pallas_call(
        out_kernel,
        grid_spec=pltpu.PrefetchScalarGridSpec(
            num_scalar_prefetch=1,
            grid=(inner_parts,),
            in_specs=[
                pl.BlockSpec((tp_parts, rows, depth), lambda b, place: (0, 0, 0)),
                pl.BlockSpec((1, tp_parts, depth, width), lambda b, place: (b, 0, 0, 0)),
            ],
            out_specs=pl.BlockSpec((rows, width), lambda b, place: (0, b)),
        ),
        out_shape=jax.ShapeDtypeStruct((rows, columns), jnp.bfloat16),
        compiler_params=pltpu.CompilerParams(vmem_limit_bytes=56 * 2**20),
        cost_estimate=pl.CostEstimate(
            flops=2 * gated.size * columns,
            bytes_accessed=2 * (weight.size + gated.size + rows * columns),
            transcendentals=0,
        ),
    )(place, gated, weight)


def per_device(features, in_proj, short_taps, long_filter, skip_gain, out_proj):
    rows = features.shape[0]
    seq_parts = lax.axis_size("seq")
    tp_parts = lax.axis_size("tp")
    outer = outer_factor(seq_parts, tp_parts)
    inner_parts = seq_parts // outer
    streams, _, chan_tp = in_proj.shape
    chans = chan_tp // seq_parts
    position = lax.axis_index("seq")
    inner_groups = [[a * inner_parts + b for b in range(inner_parts)] for a in range(outer)]
    outer_groups = [[a * inner_parts + b for a in range(outer)] for b in range(inner_parts)]

    weight = lax.all_gather(in_proj, "seq", axis=1, tiled=True, axis_index_groups=inner_groups)

    chunk_rows = rows // CHUNKS
    shared = [
        share_columns(features[index * chunk_rows : (index + 1) * chunk_rows], outer, tp_parts)
        for index in range(CHUNKS)
    ]
    crossed = [
        lax.all_to_all(
            part, "seq", split_axis=0, concat_axis=0, tiled=True, axis_index_groups=outer_groups
        )
        for part in shared
    ]
    chunks = [share_over_tp(part, tp_parts) for part in crossed]

    _, out_proj = lax.optimization_barrier((shared, out_proj))
    out_block = jnp.stack(share_over_tp(out_proj, tp_parts))
    out_weight = lax.all_gather(out_block, "seq", axis_index_groups=inner_groups)

    _, long_filter = lax.optimization_barrier((crossed, long_filter))
    filter_blocks = lax.all_to_all(
        long_filter.T.reshape(seq_parts, chans, rows), "seq", split_axis=0, concat_axis=0, tiled=True
    )
    taps = lax.dynamic_slice_in_dim(short_taps, position * chans, chans, axis=2)
    taps = jnp.broadcast_to(taps[..., None], taps.shape + (rows,))
    skip = lax.dynamic_slice_in_dim(skip_gain, position * chans, chans, axis=0)
    skip = jnp.broadcast_to(skip[:, None], (chans, rows))
    chunks, filter_blocks, taps, skip = lax.optimization_barrier((chunks, filter_blocks, taps, skip))

    partial = project_in(chunks, weight, seq_parts)
    parts = lax.all_to_all(partial, "seq", split_axis=0, concat_axis=0, tiled=True)

    gated = convolve(parts, filter_blocks, taps, skip, outer, tp_parts)
    gated = jnp.broadcast_to(gated[:, None], (tp_parts, outer) + gated.shape[1:])
    gated = lax.all_to_all(
        gated.reshape((-1,) + gated.shape[3:]), ("tp", "seq"), split_axis=0, concat_axis=0, tiled=True
    )
    gated = jnp.swapaxes(gated.reshape(tp_parts, chan_tp, -1), 1, 2)
    out = project_out(gated, out_weight)
    return return_output(out.reshape(outer, rows // tp_parts, -1), outer, inner_parts, tp_parts)


def solution(mesh):
    return jax.shard_map(
        per_device,
        mesh=mesh,
        in_specs=(
            P("seq", "tp"),
            P(None, "seq", "tp"),
            P(None, None, "tp"),
            P("seq", "tp"),
            P("tp"),
            P("tp", "seq"),
        ),
        out_specs=P("seq", "tp"),
        check_vma=False,
    )
```

```python
import functools
import math

import jax
import jax.numpy as jnp
import numpy as np
from jax import lax
from jax.experimental import pallas as pl
from jax.experimental.pallas import tpu as pltpu
from jax.sharding import PartitionSpec as P

HIGHEST = lax.Precision.HIGHEST
UNROLL = 16
CHUNKS = 2


def outer_factor(seq_parts, tp_parts):
    outer = tp_parts
    while 4 * outer * outer <= seq_parts and seq_parts % (2 * outer) == 0:
        outer *= 2
    return outer


def assemble_kernel(place_ref, *refs):
    *piece_refs, out_ref, sems = refs
    part_rows, width = piece_refs[0].shape
    copies = []
    for index, piece_ref in enumerate(piece_refs):
        row = pl.multiple_of(place_ref[2 * index] * part_rows, part_rows)
        column = pl.multiple_of(place_ref[2 * index + 1] * width, width)
        copies.append(
            pltpu.make_async_copy(
                piece_ref,
                out_ref.at[pl.ds(row, part_rows), pl.ds(column, width)],
                sems.at[index],
            )
        )
    for copy in copies:
        copy.start()
    for copy in copies:
        copy.wait()


def assemble(pieces, places, shape):
    anywhere = pl.BlockSpec(memory_space=pl.ANY)
    return pl.pallas_call(
        assemble_kernel,
        out_shape=jax.ShapeDtypeStruct(shape, pieces[0].dtype),
        in_specs=[pl.BlockSpec(memory_space=pltpu.SMEM)] + [anywhere] * len(pieces),
        out_specs=anywhere,
        scratch_shapes=[pltpu.SemaphoreType.DMA((len(pieces),))],
        cost_estimate=pl.CostEstimate(
            flops=0, bytes_accessed=4 * shape[0] * shape[1], transcendentals=0
        ),
    )(jnp.stack(places).astype(jnp.int32), *pieces)


def return_output(out, outer, inner_parts, tp_parts):
    _, part_rows, width = out.shape
    per_tp = outer // tp_parts
    tp_place = lax.axis_index("tp")
    outer_place = lax.axis_index("seq") // inner_parts
    pieces, places = [], []
    for far in range(tp_parts):
        for near in range(per_tp):

            def target(seq, tp):
                src = seq // inner_parts
                dst = (tp + far) % tp_parts * per_tp + (src % per_tp + near) % per_tp
                return (dst * inner_parts + seq % inner_parts) * tp_parts + src // per_tp

            pairs = [
                (seq * tp_parts + tp, target(seq, tp))
                for seq in range(outer * inner_parts)
                for tp in range(tp_parts)
            ]
            block = (tp_place + far) % tp_parts * per_tp + (outer_place % per_tp + near) % per_tp
            piece = lax.dynamic_index_in_dim(out, block, axis=0, keepdims=False)
            pieces.append(lax.ppermute(piece, ("seq", "tp"), pairs))
            places.append((outer_place // per_tp - far + tp_parts) % tp_parts)
            places.append((outer_place % per_tp - near + per_tp) % per_tp)
    return assemble(pieces, places, (tp_parts * part_rows, per_tp * width))


def share_columns(features, outer, tp_parts):
    rows, cols = features.shape
    per_tp = outer // tp_parts
    tp_place = lax.axis_index("tp")
    blocks = features.reshape(rows, per_tp, tp_parts, cols // outer)
    held = []
    for step in range(tp_parts):
        piece = lax.dynamic_index_in_dim(blocks, (tp_place + step) % tp_parts, axis=2, keepdims=False)
        piece = jnp.swapaxes(piece, 0, 1)
        if step:
            piece = lax.ppermute(piece, "tp", [(i, (i + step) % tp_parts) for i in range(tp_parts)])
        held.append(piece)
    return jnp.concatenate(held)


def cross_outer(held, outer, inner_parts, tp_parts):
    per_tp = outer // tp_parts
    seq_parts = outer * inner_parts
    tp_place = lax.axis_index("tp")
    outer_place = lax.axis_index("seq") // inner_parts
    arrived = []
    for step in range(outer):
        target = (outer_place + step) % outer
        which = (tp_place - target // per_tp + tp_parts) % tp_parts * per_tp + target % per_tp
        piece = lax.dynamic_index_in_dim(held, which, axis=0, keepdims=False)
        if step:
            far = step * inner_parts
            piece = lax.ppermute(piece, "seq", [(i, (i + far) % seq_parts) for i in range(seq_parts)])
        arrived.append(piece)
    return jnp.stack(arrived)


def share_over_tp(part, tp_parts):
    pieces = [part]
    for step in range(1, tp_parts):
        pairs = [(i, (i + step) % tp_parts) for i in range(tp_parts)]
        pieces.append(lax.ppermute(part, "tp", pairs))
    return pieces


def project_kernel(place_ref, *refs):
    *share_refs, weight_ref, out_ref = refs
    tp_parts = len(share_refs)
    seq_parts, _, chans, count = out_ref.shape
    outer, rows, width = share_refs[0].shape
    sums = jnp.zeros((count, seq_parts * chans), jnp.float32)
    for step, share_ref in enumerate(share_refs):
        which = lax.rem(place_ref[0] - step + tp_parts, tp_parts)
        left = [share_ref[lax.rem(place_ref[1] - src + outer, outer)] for src in range(outer)]
        sums = sums + jnp.dot(
            jnp.concatenate(left), weight_ref[0, which], preferred_element_type=jnp.float32
        )
    turned = sums.T.astype(out_ref.dtype)
    for seq in range(seq_parts):
        out_ref[seq, 0] = turned[seq * chans : (seq + 1) * chans]


def project_in(pieces, weight, outer_place, seq_parts):
    tp_parts = len(pieces)
    outer, rows, width = pieces[0].shape
    streams, _, chan_tp = weight.shape
    weight = weight.reshape(streams, tp_parts, width, chan_tp)
    chans = chan_tp // seq_parts
    count = outer * rows
    place = jnp.stack([lax.axis_index("tp"), outer_place]).astype(jnp.int32)
    whole = pl.BlockSpec((outer, rows, width), lambda i, place: (0, 0, 0))
    return pl.pallas_call(
        project_kernel,
        grid_spec=pltpu.PrefetchScalarGridSpec(
            num_scalar_prefetch=1,
            grid=(streams,),
            in_specs=[whole] * tp_parts
            + [pl.BlockSpec((1, tp_parts, width, chan_tp), lambda i, place: (i, 0, 0, 0))],
            out_specs=pl.BlockSpec((seq_parts, 1, chans, count), lambda i, place: (0, i, 0, 0)),
        ),
        out_shape=jax.ShapeDtypeStruct((seq_parts, streams, chans, count), jnp.bfloat16),
        compiler_params=pltpu.CompilerParams(vmem_limit_bytes=56 * 2**20),
        cost_estimate=pl.CostEstimate(
            flops=2 * count * weight.size,
            bytes_accessed=2 * (weight.size + tp_parts * pieces[0].size)
            + 2 * streams * count * chan_tp,
            transcendentals=0,
        ),
    )(place, *pieces, weight)


def tables(block):
    place = np.arange(block)
    angle = 2.0 * math.pi * np.outer(place, place + 0.5) / (2 * block)
    forward = np.concatenate([np.cos(angle), -np.sin(angle)], 1)
    place = np.arange(2 * block)
    angle = 2.0 * math.pi * np.outer(np.arange(block) + 0.5, place) / (2 * block)
    backward = np.concatenate([np.cos(angle), -np.sin(angle)], 0) / block
    return forward.astype(np.float32), backward.astype(np.float32)


def each(count, body):
    if isinstance(count, int) and count <= UNROLL:
        for index in range(count):
            body(index)
    else:
        lax.fori_loop(0, count, lambda index, carry: (body(index), carry)[1], 0)


def total(count, term, zero):
    if isinstance(count, int) and count <= UNROLL:
        result = zero
        for index in range(count):
            result = jax.tree.map(jnp.add, result, term(index))
        return result
    return lax.fori_loop(
        0, count, lambda index, sums: jax.tree.map(jnp.add, sums, term(index)), zero
    )


def conv_kernel(
    outer, chunks, *refs
):
    part_refs, refs = refs[:chunks], refs[chunks:]
    filter_ref, taps_ref, skip_ref, fwd_ref, bwd_ref, out_ref, *refs = refs
    proj, query, inner, spec, filter_spec, product, back = refs
    blocks, streams, chans, _ = part_refs[0].shape
    rows = filter_ref.shape[2]
    inner_parts = blocks // outer
    taps_count = taps_ref.shape[1]
    lane = lax.broadcasted_iota(jnp.int32, (chans, rows), 1)

    chunk_rows = rows // chunks

    def add_up(inner_index, stream, group):
        column = slice(group * rows, (group + 1) * rows)
        sums = []
        for part_ref in part_refs:
            value = jnp.zeros((chans, rows), jnp.float32)
            for part in range(outer):
                value = value + part_ref[part * inner_parts + inner_index, stream, :, column].astype(jnp.float32)
            sums.append(value)
        for place in range(chunks):
            block = sums[0]
            for chunk, value in enumerate(sums):
                shift = (chunk - place) * chunk_rows % rows
                value = pltpu.roll(value, shift, 1) if shift else value
                block = jnp.where(lane // chunk_rows == chunk, value, block)
            proj[1 + (group * chunks + place) * inner_parts + inner_index, stream] = block

    for group in range(outer // chunks):
        for stream in range(streams):
            each(inner_parts, functools.partial(add_up, stream=stream, group=group))

    for stream in range(streams):
        proj[0, stream] = jnp.zeros((chans, rows), jnp.float32)

    def first(index):
        filtered = []
        for stream in range(streams):
            now, past = proj[index + 1, stream], proj[index, stream]
            value = taps_ref[stream, 0] * now
            for offset in range(1, taps_count):
                moved = jnp.where(
                    lane < offset, pltpu.roll(past, offset, 1), pltpu.roll(now, offset, 1)
                )
                value = value + taps_ref[stream, offset] * moved
            filtered.append(value)
        query[index] = filtered[0]
        inner[index] = filtered[1] * filtered[2]

    each(blocks, first)

    def apply(source, table_ref, target):
        if chans % 8 == 0:
            flat = source[...].reshape(blocks * chans, source.shape[2])
            done = jnp.dot(flat, table_ref[...], precision=HIGHEST, preferred_element_type=jnp.float32)
            target[...] = done.reshape(target.shape)
        else:

            def one(index):
                target[index] = jnp.dot(
                    source[index], table_ref[...], precision=HIGHEST, preferred_element_type=jnp.float32
                )

            each(blocks, one)

    apply(filter_ref, fwd_ref, filter_spec)
    apply(inner, fwd_ref, spec)

    def multiply(index):
        def term(step):
            left, right = spec[step], filter_spec[index - step]
            left_real, left_imag = left[:, :rows], left[:, rows:]
            right_real, right_imag = right[:, :rows], right[:, rows:]
            return (
                left_real * right_real - left_imag * right_imag,
                left_real * right_imag + left_imag * right_real,
            )

        zero = jnp.zeros((chans, rows), jnp.float32)
        real, imag = total(index + 1, term, (zero, zero))
        product[index, :, :rows] = real
        product[index, :, rows:] = imag

    each(blocks, multiply)
    apply(product, bwd_ref, back)

    def last(index, carried):
        long_mix = back[index, :, :rows] + carried
        query[index] = query[index] * (long_mix + skip_ref[...] * inner[index])

    last(0, jnp.zeros((chans, rows), jnp.float32))
    each(blocks - 1, lambda index: last(index + 1, back[index, :, rows:]))

    tp_parts = out_ref.shape[0]
    part_rows = rows // tp_parts

    def spread(inner_index):
        for part in range(tp_parts):
            for group in range(outer // tp_parts):
                packed = jnp.zeros((chans, rows), jnp.float32)
                for place in range(tp_parts):
                    block = query[(group * tp_parts + place) * inner_parts + inner_index]
                    shift = (place - part) * part_rows % rows
                    block = pltpu.roll(block, shift, 1) if shift else block
                    packed = jnp.where(lane // part_rows == place, block, packed)
                out_ref[part, inner_index, :, group * rows : (group + 1) * rows] = packed.astype(out_ref.dtype)

    each(inner_parts, spread)


def convolve(parts, filter_blocks, taps, skip, outer, tp_parts):
    blocks, streams, chans, _ = parts[0].shape
    rows = filter_blocks.shape[2]
    forward, backward = tables(rows)
    wide = (blocks, chans, 2 * rows)
    narrow = (blocks, chans, rows)
    vmem = pl.BlockSpec(memory_space=pltpu.VMEM)
    return pl.pallas_call(
        functools.partial(conv_kernel, outer, len(parts)),
        out_shape=jax.ShapeDtypeStruct(
            (tp_parts, blocks // outer, chans, outer // tp_parts * rows), jnp.bfloat16
        ),
        in_specs=[vmem] * (5 + len(parts)),
        out_specs=vmem,
        scratch_shapes=[
            pltpu.VMEM((blocks + 1, streams, chans, rows), jnp.float32),
            pltpu.VMEM(narrow, jnp.float32),
            pltpu.VMEM(narrow, jnp.float32),
            pltpu.VMEM(wide, jnp.float32),
            pltpu.VMEM(wide, jnp.float32),
            pltpu.VMEM(wide, jnp.float32),
            pltpu.VMEM(wide, jnp.float32),
        ],
        compiler_params=pltpu.CompilerParams(vmem_limit_bytes=40 * 2**20),
        cost_estimate=pl.CostEstimate(flops=10**9, bytes_accessed=4 * 2**20, transcendentals=0),
    )(*parts, filter_blocks, taps, skip, jnp.asarray(forward), jnp.asarray(backward))


def out_kernel(place_ref, gated_ref, weight_ref, out_ref):
    tp_parts = gated_ref.shape[0]
    sums = jnp.zeros(out_ref.shape, jnp.float32)
    for step in range(tp_parts):
        which = lax.rem(place_ref[0] - step + tp_parts, tp_parts)
        sums = sums + jnp.dot(gated_ref[which], weight_ref[0, step], preferred_element_type=jnp.float32)
    out_ref[...] = sums.astype(out_ref.dtype)


def project_out(gated, weight):
    tp_parts, rows, depth = gated.shape
    inner_parts, _, _, width = weight.shape
    columns = inner_parts * width
    place = lax.axis_index("tp").astype(jnp.int32)[None]
    return pl.pallas_call(
        out_kernel,
        grid_spec=pltpu.PrefetchScalarGridSpec(
            num_scalar_prefetch=1,
            grid=(inner_parts,),
            in_specs=[
                pl.BlockSpec((tp_parts, rows, depth), lambda b, place: (0, 0, 0)),
                pl.BlockSpec((1, tp_parts, depth, width), lambda b, place: (b, 0, 0, 0)),
            ],
            out_specs=pl.BlockSpec((rows, width), lambda b, place: (0, b)),
        ),
        out_shape=jax.ShapeDtypeStruct((rows, columns), jnp.bfloat16),
        compiler_params=pltpu.CompilerParams(vmem_limit_bytes=56 * 2**20),
        cost_estimate=pl.CostEstimate(
            flops=2 * gated.size * columns,
            bytes_accessed=2 * (weight.size + gated.size + rows * columns),
            transcendentals=0,
        ),
    )(place, gated, weight)


def per_device(features, in_proj, short_taps, long_filter, skip_gain, out_proj):
    rows = features.shape[0]
    seq_parts = lax.axis_size("seq")
    tp_parts = lax.axis_size("tp")
    outer = outer_factor(seq_parts, tp_parts)
    inner_parts = seq_parts // outer
    streams, _, chan_tp = in_proj.shape
    chans = chan_tp // seq_parts
    position = lax.axis_index("seq")
    inner_groups = [[a * inner_parts + b for b in range(inner_parts)] for a in range(outer)]
    outer_groups = [[a * inner_parts + b for a in range(outer)] for b in range(inner_parts)]

    weight = lax.all_gather(in_proj, "seq", axis=1, tiled=True, axis_index_groups=inner_groups)

    outer_place = position // inner_parts
    chunk_rows = rows // CHUNKS
    shared = [
        share_columns(features[index * chunk_rows : (index + 1) * chunk_rows], outer, tp_parts)
        for index in range(CHUNKS)
    ]
    crossed = [cross_outer(part, outer, inner_parts, tp_parts) for part in shared]

    _, out_proj = lax.optimization_barrier((shared, out_proj))
    out_block = jnp.stack(share_over_tp(out_proj, tp_parts))
    out_weight = lax.all_gather(out_block, "seq", axis_index_groups=inner_groups)

    filter_blocks = lax.all_to_all(
        long_filter.T.reshape(seq_parts, chans, rows), "seq", split_axis=0, concat_axis=0, tiled=True
    )
    taps = lax.dynamic_slice_in_dim(short_taps, position * chans, chans, axis=2)
    taps = jnp.broadcast_to(taps[..., None], taps.shape + (rows,))
    skip = lax.dynamic_slice_in_dim(skip_gain, position * chans, chans, axis=0)
    skip = jnp.broadcast_to(skip[:, None], (chans, rows))

    parts = []
    for index, part in enumerate(crossed):
        pieces = share_over_tp(part, tp_parts)
        if index + 1 == CHUNKS:
            pieces, filter_blocks, taps, skip = lax.optimization_barrier(
                (pieces, filter_blocks, taps, skip)
            )
        partial = project_in(pieces, weight, outer_place, seq_parts)
        parts.append(lax.all_to_all(partial, "seq", split_axis=0, concat_axis=0, tiled=True))

    gated = convolve(parts, filter_blocks, taps, skip, outer, tp_parts)
    gated = jnp.broadcast_to(gated[:, None], (tp_parts, outer) + gated.shape[1:])
    gated = lax.all_to_all(
        gated.reshape((-1,) + gated.shape[3:]), ("tp", "seq"), split_axis=0, concat_axis=0, tiled=True
    )
    gated = jnp.swapaxes(gated.reshape(tp_parts, chan_tp, -1), 1, 2)
    out = project_out(gated, out_weight)
    return return_output(out.reshape(outer, rows // tp_parts, -1), outer, inner_parts, tp_parts)


def solution(mesh):
    return jax.shard_map(
        per_device,
        mesh=mesh,
        in_specs=(
            P("seq", "tp"),
            P(None, "seq", "tp"),
            P(None, None, "tp"),
            P("seq", "tp"),
            P("tp"),
            P("tp", "seq"),
        ),
        out_specs=P("seq", "tp"),
        check_vma=False,
    )
```

```python
import functools
import math

import jax
import jax.numpy as jnp
import numpy as np
from jax import lax
from jax.experimental import pallas as pl
from jax.experimental.pallas import tpu as pltpu
from jax.sharding import PartitionSpec as P

HIGHEST = lax.Precision.HIGHEST
UNROLL = 16
CHUNKS = 2


def outer_factor(seq_parts, tp_parts):
    outer = tp_parts
    while 4 * outer * outer <= seq_parts and seq_parts % (2 * outer) == 0:
        outer *= 2
    return outer


def assemble_kernel(place_ref, *refs):
    *piece_refs, out_ref = refs
    for index, piece_ref in enumerate(piece_refs):

        @pl.when(pl.program_id(0) == index)
        def _():
            out_ref[...] = piece_ref[...]


def assemble(pieces, places, shape):
    return pl.pallas_call(
        assemble_kernel,
        grid_spec=pltpu.PrefetchScalarGridSpec(
            num_scalar_prefetch=1,
            grid=(len(pieces),),
            in_specs=[pl.BlockSpec(memory_space=pltpu.VMEM)] * len(pieces),
            out_specs=pl.BlockSpec(
                pieces[0].shape, lambda i, place: (place[2 * i], place[2 * i + 1])
            ),
        ),
        out_shape=jax.ShapeDtypeStruct(shape, pieces[0].dtype),
        cost_estimate=pl.CostEstimate(
            flops=0, bytes_accessed=4 * shape[0] * shape[1], transcendentals=0
        ),
    )(jnp.stack(places).astype(jnp.int32), *pieces)


def return_output(out, outer, inner_parts, tp_parts):
    _, part_rows, width = out.shape
    per_tp = outer // tp_parts
    tp_place = lax.axis_index("tp")
    outer_place = lax.axis_index("seq") // inner_parts
    pieces, places = [], []
    for far in range(tp_parts):
        for near in range(per_tp):

            def target(seq, tp):
                src = seq // inner_parts
                dst = (tp + far) % tp_parts * per_tp + (src % per_tp + near) % per_tp
                return (dst * inner_parts + seq % inner_parts) * tp_parts + src // per_tp

            pairs = [
                (seq * tp_parts + tp, target(seq, tp))
                for seq in range(outer * inner_parts)
                for tp in range(tp_parts)
            ]
            block = (tp_place + far) % tp_parts * per_tp + (outer_place % per_tp + near) % per_tp
            piece = lax.dynamic_index_in_dim(out, block, axis=0, keepdims=False)
            pieces.append(lax.ppermute(piece, ("seq", "tp"), pairs))
            places.append((outer_place // per_tp - far + tp_parts) % tp_parts)
            places.append((outer_place % per_tp - near + per_tp) % per_tp)
    return assemble(pieces, places, (tp_parts * part_rows, per_tp * width))


def share_columns(features, outer, tp_parts):
    rows, cols = features.shape
    per_tp = outer // tp_parts
    tp_place = lax.axis_index("tp")
    blocks = features.reshape(rows, per_tp, tp_parts, cols // outer)
    held = []
    for step in range(tp_parts):
        piece = lax.dynamic_index_in_dim(blocks, (tp_place + step) % tp_parts, axis=2, keepdims=False)
        piece = jnp.swapaxes(piece, 0, 1)
        if step:
            piece = lax.ppermute(piece, "tp", [(i, (i + step) % tp_parts) for i in range(tp_parts)])
        held.append(piece)
    return jnp.concatenate(held)


def cross_outer(held, outer, inner_parts, tp_parts):
    per_tp = outer // tp_parts
    seq_parts = outer * inner_parts
    tp_place = lax.axis_index("tp")
    outer_place = lax.axis_index("seq") // inner_parts
    arrived = []
    for step in range(outer):
        target = (outer_place + step) % outer
        which = (tp_place - target // per_tp + tp_parts) % tp_parts * per_tp + target % per_tp
        piece = lax.dynamic_index_in_dim(held, which, axis=0, keepdims=False)
        if step:
            far = step * inner_parts
            piece = lax.ppermute(piece, "seq", [(i, (i + far) % seq_parts) for i in range(seq_parts)])
        arrived.append(piece)
    return arrived


def share_over_tp(part, tp_parts):
    pieces = [part]
    for step in range(1, tp_parts):
        pairs = [(i, (i + step) % tp_parts) for i in range(tp_parts)]
        pieces.append(lax.ppermute(part, "tp", pairs))
    return pieces


def project_kernel(place_ref, *refs):
    *share_refs, weight_ref, out_ref = refs
    tp_parts = len(share_refs)
    seq_parts, _, chans, count = out_ref.shape
    width = share_refs[0].shape[2]
    sums = jnp.zeros((count, seq_parts * chans), jnp.float32)
    for step, share_ref in enumerate(share_refs):
        which = lax.rem(place_ref[0] - step + tp_parts, tp_parts)
        sums = sums + jnp.dot(
            share_ref[...].reshape(count, width),
            weight_ref[0, which],
            preferred_element_type=jnp.float32,
        )
    turned = sums.T.astype(out_ref.dtype)
    for seq in range(seq_parts):
        out_ref[seq, 0] = turned[seq * chans : (seq + 1) * chans]


def project_in(pieces, weight, seq_parts):
    tp_parts = len(pieces)
    outer, rows, width = pieces[0].shape
    streams, _, chan_tp = weight.shape
    weight = weight.reshape(streams, tp_parts, width, chan_tp)
    chans = chan_tp // seq_parts
    count = outer * rows
    place = lax.axis_index("tp").astype(jnp.int32)[None]
    whole = pl.BlockSpec((outer, rows, width), lambda i, place: (0, 0, 0))
    return pl.pallas_call(
        project_kernel,
        grid_spec=pltpu.PrefetchScalarGridSpec(
            num_scalar_prefetch=1,
            grid=(streams,),
            in_specs=[whole] * tp_parts
            + [pl.BlockSpec((1, tp_parts, width, chan_tp), lambda i, place: (i, 0, 0, 0))],
            out_specs=pl.BlockSpec((seq_parts, 1, chans, count), lambda i, place: (0, i, 0, 0)),
        ),
        out_shape=jax.ShapeDtypeStruct((seq_parts, streams, chans, count), jnp.bfloat16),
        compiler_params=pltpu.CompilerParams(vmem_limit_bytes=56 * 2**20),
        cost_estimate=pl.CostEstimate(
            flops=2 * count * weight.size,
            bytes_accessed=2 * (weight.size + tp_parts * pieces[0].size)
            + 2 * streams * count * chan_tp,
            transcendentals=0,
        ),
    )(place, *pieces, weight)


def tables(block):
    place = np.arange(block)
    angle = 2.0 * math.pi * np.outer(place, place + 0.5) / (2 * block)
    forward = np.concatenate([np.cos(angle), -np.sin(angle)], 1)
    place = np.arange(2 * block)
    angle = 2.0 * math.pi * np.outer(np.arange(block) + 0.5, place) / (2 * block)
    backward = np.concatenate([np.cos(angle), -np.sin(angle)], 0) / block
    return forward.astype(np.float32), backward.astype(np.float32)


def each(count, body):
    if isinstance(count, int) and count <= UNROLL:
        for index in range(count):
            body(index)
    else:
        lax.fori_loop(0, count, lambda index, carry: (body(index), carry)[1], 0)


def total(count, term, zero):
    if isinstance(count, int) and count <= UNROLL:
        result = zero
        for index in range(count):
            result = jax.tree.map(jnp.add, result, term(index))
        return result
    return lax.fori_loop(
        0, count, lambda index, sums: jax.tree.map(jnp.add, sums, term(index)), zero
    )


def conv_kernel(
    outer, chunks, *refs
):
    part_refs, refs = refs[:chunks], refs[chunks:]
    filter_ref, taps_ref, skip_ref, fwd_ref, bwd_ref, out_ref, *refs = refs
    proj, query, inner, spec, filter_spec, product, back = refs
    blocks, streams, chans, _ = part_refs[0].shape
    rows = filter_ref.shape[2]
    inner_parts = blocks // outer
    taps_count = taps_ref.shape[1]
    lane = lax.broadcasted_iota(jnp.int32, (chans, rows), 1)

    depth = outer // chunks

    def add_up(inner_index, stream, group):
        value = jnp.zeros((chans, rows), jnp.float32)
        for part in range(outer):
            slot = (part - group) % outer
            column = slice(slot % depth * rows, (slot % depth + 1) * rows)
            source = part_refs[slot // depth]
            value = value + source[part * inner_parts + inner_index, stream, :, column].astype(jnp.float32)
        proj[1 + group * inner_parts + inner_index, stream] = value

    for group in range(outer):
        for stream in range(streams):
            each(inner_parts, functools.partial(add_up, stream=stream, group=group))

    for stream in range(streams):
        proj[0, stream] = jnp.zeros((chans, rows), jnp.float32)

    def first(index):
        filtered = []
        for stream in range(streams):
            now, past = proj[index + 1, stream], proj[index, stream]
            value = taps_ref[stream, 0] * now
            for offset in range(1, taps_count):
                moved = jnp.where(
                    lane < offset, pltpu.roll(past, offset, 1), pltpu.roll(now, offset, 1)
                )
                value = value + taps_ref[stream, offset] * moved
            filtered.append(value)
        query[index] = filtered[0]
        inner[index] = filtered[1] * filtered[2]

    each(blocks, first)

    def apply(source, table_ref, target):
        if chans % 8 == 0:
            flat = source[...].reshape(blocks * chans, source.shape[2])
            done = jnp.dot(flat, table_ref[...], precision=HIGHEST, preferred_element_type=jnp.float32)
            target[...] = done.reshape(target.shape)
        else:

            def one(index):
                target[index] = jnp.dot(
                    source[index], table_ref[...], precision=HIGHEST, preferred_element_type=jnp.float32
                )

            each(blocks, one)

    apply(filter_ref, fwd_ref, filter_spec)
    apply(inner, fwd_ref, spec)

    def multiply(index):
        def term(step):
            left, right = spec[step], filter_spec[index - step]
            left_real, left_imag = left[:, :rows], left[:, rows:]
            right_real, right_imag = right[:, :rows], right[:, rows:]
            return (
                left_real * right_real - left_imag * right_imag,
                left_real * right_imag + left_imag * right_real,
            )

        zero = jnp.zeros((chans, rows), jnp.float32)
        real, imag = total(index + 1, term, (zero, zero))
        product[index, :, :rows] = real
        product[index, :, rows:] = imag

    each(blocks, multiply)
    apply(product, bwd_ref, back)

    def last(index, carried):
        long_mix = back[index, :, :rows] + carried
        query[index] = query[index] * (long_mix + skip_ref[...] * inner[index])

    last(0, jnp.zeros((chans, rows), jnp.float32))
    each(blocks - 1, lambda index: last(index + 1, back[index, :, rows:]))

    tp_parts = out_ref.shape[0]
    part_rows = rows // tp_parts

    def spread(inner_index):
        for part in range(tp_parts):
            for group in range(outer // tp_parts):
                packed = jnp.zeros((chans, rows), jnp.float32)
                for place in range(tp_parts):
                    block = query[(group * tp_parts + place) * inner_parts + inner_index]
                    shift = (place - part) * part_rows % rows
                    block = pltpu.roll(block, shift, 1) if shift else block
                    packed = jnp.where(lane // part_rows == place, block, packed)
                out_ref[part, inner_index, :, group * rows : (group + 1) * rows] = packed.astype(out_ref.dtype)

    each(inner_parts, spread)


def convolve(parts, filter_blocks, taps, skip, outer, tp_parts):
    blocks, streams, chans, _ = parts[0].shape
    rows = filter_blocks.shape[2]
    forward, backward = tables(rows)
    wide = (blocks, chans, 2 * rows)
    narrow = (blocks, chans, rows)
    vmem = pl.BlockSpec(memory_space=pltpu.VMEM)
    return pl.pallas_call(
        functools.partial(conv_kernel, outer, len(parts)),
        out_shape=jax.ShapeDtypeStruct(
            (tp_parts, blocks // outer, chans, outer // tp_parts * rows), jnp.bfloat16
        ),
        in_specs=[vmem] * (5 + len(parts)),
        out_specs=vmem,
        scratch_shapes=[
            pltpu.VMEM((blocks + 1, streams, chans, rows), jnp.float32),
            pltpu.VMEM(narrow, jnp.float32),
            pltpu.VMEM(narrow, jnp.float32),
            pltpu.VMEM(wide, jnp.float32),
            pltpu.VMEM(wide, jnp.float32),
            pltpu.VMEM(wide, jnp.float32),
            pltpu.VMEM(wide, jnp.float32),
        ],
        compiler_params=pltpu.CompilerParams(vmem_limit_bytes=40 * 2**20),
        cost_estimate=pl.CostEstimate(flops=10**9, bytes_accessed=4 * 2**20, transcendentals=0),
    )(*parts, filter_blocks, taps, skip, jnp.asarray(forward), jnp.asarray(backward))


def out_kernel(place_ref, gated_ref, weight_ref, out_ref):
    tp_parts = gated_ref.shape[0]
    sums = jnp.zeros(out_ref.shape, jnp.float32)
    for step in range(tp_parts):
        which = lax.rem(place_ref[0] - step + tp_parts, tp_parts)
        sums = sums + jnp.dot(gated_ref[which], weight_ref[0, step], preferred_element_type=jnp.float32)
    out_ref[...] = sums.astype(out_ref.dtype)


def project_out(gated, weight):
    tp_parts, rows, depth = gated.shape
    inner_parts, _, _, width = weight.shape
    columns = inner_parts * width
    place = lax.axis_index("tp").astype(jnp.int32)[None]
    return pl.pallas_call(
        out_kernel,
        grid_spec=pltpu.PrefetchScalarGridSpec(
            num_scalar_prefetch=1,
            grid=(inner_parts,),
            in_specs=[
                pl.BlockSpec((tp_parts, rows, depth), lambda b, place: (0, 0, 0)),
                pl.BlockSpec((1, tp_parts, depth, width), lambda b, place: (b, 0, 0, 0)),
            ],
            out_specs=pl.BlockSpec((rows, width), lambda b, place: (0, b)),
        ),
        out_shape=jax.ShapeDtypeStruct((rows, columns), jnp.bfloat16),
        compiler_params=pltpu.CompilerParams(vmem_limit_bytes=56 * 2**20),
        cost_estimate=pl.CostEstimate(
            flops=2 * gated.size * columns,
            bytes_accessed=2 * (weight.size + gated.size + rows * columns),
            transcendentals=0,
        ),
    )(place, gated, weight)


def per_device(features, in_proj, short_taps, long_filter, skip_gain, out_proj):
    rows = features.shape[0]
    seq_parts = lax.axis_size("seq")
    tp_parts = lax.axis_size("tp")
    outer = outer_factor(seq_parts, tp_parts)
    inner_parts = seq_parts // outer
    streams, _, chan_tp = in_proj.shape
    chans = chan_tp // seq_parts
    position = lax.axis_index("seq")
    inner_groups = [[a * inner_parts + b for b in range(inner_parts)] for a in range(outer)]
    outer_groups = [[a * inner_parts + b for a in range(outer)] for b in range(inner_parts)]

    weight = lax.all_gather(in_proj, "seq", axis=1, tiled=True, axis_index_groups=inner_groups)

    held = share_columns(features, outer, tp_parts)
    held, out_proj, long_filter = lax.optimization_barrier((held, out_proj, long_filter))
    arrived = cross_outer(held, outer, inner_parts, tp_parts)
    depth = outer // CHUNKS
    crossed = [jnp.stack(arrived[index * depth : (index + 1) * depth]) for index in range(CHUNKS)]

    out_block = jnp.stack(share_over_tp(out_proj, tp_parts))
    out_weight = lax.all_gather(out_block, "seq", axis_index_groups=inner_groups)

    filter_blocks = lax.all_to_all(
        long_filter.T.reshape(seq_parts, chans, rows), "seq", split_axis=0, concat_axis=0, tiled=True
    )
    taps = lax.dynamic_slice_in_dim(short_taps, position * chans, chans, axis=2)
    taps = jnp.broadcast_to(taps[..., None], taps.shape + (rows,))
    skip = lax.dynamic_slice_in_dim(skip_gain, position * chans, chans, axis=0)
    skip = jnp.broadcast_to(skip[:, None], (chans, rows))

    parts = []
    for index, part in enumerate(crossed):
        pieces = share_over_tp(part, tp_parts)
        if index + 1 == CHUNKS:
            pieces, filter_blocks, taps, skip = lax.optimization_barrier(
                (pieces, filter_blocks, taps, skip)
            )
        partial = project_in(pieces, weight, seq_parts)
        parts.append(lax.all_to_all(partial, "seq", split_axis=0, concat_axis=0, tiled=True))

    gated = convolve(parts, filter_blocks, taps, skip, outer, tp_parts)
    gated = jnp.broadcast_to(gated[:, None], (tp_parts, outer) + gated.shape[1:])
    gated = lax.all_to_all(
        gated.reshape((-1,) + gated.shape[3:]), ("tp", "seq"), split_axis=0, concat_axis=0, tiled=True
    )
    gated = jnp.swapaxes(gated.reshape(tp_parts, chan_tp, -1), 1, 2)
    out = project_out(gated, out_weight)
    return return_output(out.reshape(outer, rows // tp_parts, -1), outer, inner_parts, tp_parts)


def solution(mesh):
    return jax.shard_map(
        per_device,
        mesh=mesh,
        in_specs=(
            P("seq", "tp"),
            P(None, "seq", "tp"),
            P(None, None, "tp"),
            P("seq", "tp"),
            P("tp"),
            P("tp", "seq"),
        ),
        out_specs=P("seq", "tp"),
        check_vma=False,
    )
```

```python
import functools
import math

import jax
import jax.numpy as jnp
import numpy as np
from jax import lax
from jax.experimental import pallas as pl
from jax.experimental.pallas import tpu as pltpu
from jax.sharding import PartitionSpec as P

HIGHEST = lax.Precision.HIGHEST
UNROLL = 16
CHUNKS = 2
HEAVY = 30


def outer_factor(seq_parts, tp_parts):
    outer = tp_parts
    while 4 * outer * outer <= seq_parts and seq_parts % (2 * outer) == 0:
        outer *= 2
    return outer


def assemble_kernel(place_ref, *refs):
    *piece_refs, out_ref = refs
    for index, piece_ref in enumerate(piece_refs):

        @pl.when(pl.program_id(0) == index)
        def _():
            out_ref[...] = piece_ref[...]


def assemble(pieces, places, shape):
    return pl.pallas_call(
        assemble_kernel,
        grid_spec=pltpu.PrefetchScalarGridSpec(
            num_scalar_prefetch=1,
            grid=(len(pieces),),
            in_specs=[pl.BlockSpec(memory_space=pltpu.VMEM)] * len(pieces),
            out_specs=pl.BlockSpec(
                pieces[0].shape, lambda i, place: (place[2 * i], place[2 * i + 1])
            ),
        ),
        out_shape=jax.ShapeDtypeStruct(shape, pieces[0].dtype),
        compiler_params=pltpu.CompilerParams(vmem_limit_bytes=4 * 2**20),
        cost_estimate=pl.CostEstimate(
            flops=0, bytes_accessed=4 * shape[0] * shape[1], transcendentals=0
        ),
    )(jnp.stack(places).astype(jnp.int32), *pieces)


def return_output(out, outer, inner_parts, tp_parts):
    _, part_rows, width = out.shape
    per_tp = outer // tp_parts
    tp_place = lax.axis_index("tp")
    outer_place = lax.axis_index("seq") // inner_parts
    pieces, places = [], []
    for far in range(tp_parts):
        for near in range(per_tp):

            def target(seq, tp):
                src = seq // inner_parts
                dst = (tp + far) % tp_parts * per_tp + (src % per_tp + near) % per_tp
                return (dst * inner_parts + seq % inner_parts) * tp_parts + src // per_tp

            pairs = [
                (seq * tp_parts + tp, target(seq, tp))
                for seq in range(outer * inner_parts)
                for tp in range(tp_parts)
            ]
            block = (tp_place + far) % tp_parts * per_tp + (outer_place % per_tp + near) % per_tp
            piece = lax.dynamic_index_in_dim(out, block, axis=0, keepdims=False)
            pieces.append(lax.ppermute(piece, ("seq", "tp"), pairs))
            places.append((outer_place // per_tp - far + tp_parts) % tp_parts)
            places.append((outer_place % per_tp - near + per_tp) % per_tp)
    return assemble(pieces, places, (tp_parts * part_rows, per_tp * width))


def share_columns(features, outer, tp_parts):
    rows, cols = features.shape
    per_tp = outer // tp_parts
    tp_place = lax.axis_index("tp")
    width = cols // outer
    held = []
    for step in range(tp_parts):
        which = (tp_place + step) % tp_parts
        piece = jnp.stack(
            [
                lax.dynamic_slice_in_dim(features, (group * tp_parts + which) * width, width, axis=1)
                for group in range(per_tp)
            ]
        )
        if step:
            piece = lax.ppermute(piece, "tp", [(i, (i + step) % tp_parts) for i in range(tp_parts)])
        held.append(piece)
    return jnp.concatenate(held)


def cross_outer(held, outer, inner_parts, tp_parts):
    per_tp = outer // tp_parts
    seq_parts = outer * inner_parts
    tp_place = lax.axis_index("tp")
    outer_place = lax.axis_index("seq") // inner_parts
    arrived = []
    for step in range(outer):
        target = (outer_place + step) % outer
        which = (tp_place - target // per_tp + tp_parts) % tp_parts * per_tp + target % per_tp
        piece = lax.dynamic_index_in_dim(held, which, axis=0, keepdims=False)
        if step:
            far = step * inner_parts
            piece = lax.ppermute(piece, "seq", [(i, (i + far) % seq_parts) for i in range(seq_parts)])
        arrived.append(piece)
    return arrived


def share_over_tp(part, tp_parts):
    pieces = [part]
    for step in range(1, tp_parts):
        pairs = [(i, (i + step) % tp_parts) for i in range(tp_parts)]
        pieces.append(lax.ppermute(part, "tp", pairs))
    return pieces


def project_kernel(place_ref, *refs):
    *share_refs, weight_ref, out_ref = refs
    tp_parts = len(share_refs)
    seq_parts, _, chans, count = out_ref.shape
    width = share_refs[0].shape[2]
    sums = jnp.zeros((count, seq_parts * chans), jnp.float32)
    for step, share_ref in enumerate(share_refs):
        which = lax.rem(place_ref[0] - step + tp_parts, tp_parts)
        sums = sums + jnp.dot(
            share_ref[...].reshape(count, width),
            weight_ref[0, which],
            preferred_element_type=jnp.float32,
        )
    turned = sums.T.astype(out_ref.dtype)
    for seq in range(seq_parts):
        out_ref[seq, 0] = turned[seq * chans : (seq + 1) * chans]


def project_in(pieces, weight, seq_parts):
    tp_parts = len(pieces)
    outer, rows, width = pieces[0].shape
    streams, _, chan_tp = weight.shape
    weight = weight.reshape(streams, tp_parts, width, chan_tp)
    chans = chan_tp // seq_parts
    count = outer * rows
    place = lax.axis_index("tp").astype(jnp.int32)[None]
    whole = pl.BlockSpec((outer, rows, width), lambda i, place: (0, 0, 0))
    return pl.pallas_call(
        project_kernel,
        grid_spec=pltpu.PrefetchScalarGridSpec(
            num_scalar_prefetch=1,
            grid=(streams,),
            in_specs=[whole] * tp_parts
            + [pl.BlockSpec((1, tp_parts, width, chan_tp), lambda i, place: (i, 0, 0, 0))],
            out_specs=pl.BlockSpec((seq_parts, 1, chans, count), lambda i, place: (0, i, 0, 0)),
        ),
        out_shape=jax.ShapeDtypeStruct((seq_parts, streams, chans, count), jnp.bfloat16),
        compiler_params=pltpu.CompilerParams(vmem_limit_bytes=56 * 2**20),
        cost_estimate=pl.CostEstimate(
            flops=HEAVY * 2 * count * weight.size,
            bytes_accessed=2 * (weight.size + tp_parts * pieces[0].size)
            + 2 * streams * count * chan_tp,
            transcendentals=0,
        ),
    )(place, *pieces, weight)


def tables(block):
    place = np.arange(block)
    angle = 2.0 * math.pi * np.outer(place, place + 0.5) / (2 * block)
    forward = np.concatenate([np.cos(angle), -np.sin(angle)], 1)
    place = np.arange(2 * block)
    angle = 2.0 * math.pi * np.outer(np.arange(block) + 0.5, place) / (2 * block)
    backward = np.concatenate([np.cos(angle), -np.sin(angle)], 0) / block
    return forward.astype(np.float32), backward.astype(np.float32)


def each(count, body):
    if isinstance(count, int) and count <= UNROLL:
        for index in range(count):
            body(index)
    else:
        lax.fori_loop(0, count, lambda index, carry: (body(index), carry)[1], 0)


def total(count, term, zero):
    if isinstance(count, int) and count <= UNROLL:
        result = zero
        for index in range(count):
            result = jax.tree.map(jnp.add, result, term(index))
        return result
    return lax.fori_loop(
        0, count, lambda index, sums: jax.tree.map(jnp.add, sums, term(index)), zero
    )


def conv_kernel(
    outer, chunks, *refs
):
    part_refs, refs = refs[:chunks], refs[chunks:]
    filter_ref, taps_ref, skip_ref, fwd_ref, bwd_ref, out_ref, *refs = refs
    proj, query, inner, spec, filter_spec, product, back = refs
    blocks, streams, chans, _ = part_refs[0].shape
    rows = filter_ref.shape[2]
    inner_parts = blocks // outer
    taps_count = taps_ref.shape[1]
    lane = lax.broadcasted_iota(jnp.int32, (chans, rows), 1)

    depth = outer // chunks

    def add_up(inner_index, stream, group):
        value = jnp.zeros((chans, rows), jnp.float32)
        for part in range(outer):
            slot = (part - group) % outer
            column = slice(slot % depth * rows, (slot % depth + 1) * rows)
            source = part_refs[slot // depth]
            value = value + source[part * inner_parts + inner_index, stream, :, column].astype(jnp.float32)
        proj[1 + group * inner_parts + inner_index, stream] = value

    for group in range(outer):
        for stream in range(streams):
            each(inner_parts, functools.partial(add_up, stream=stream, group=group))

    for stream in range(streams):
        proj[0, stream] = jnp.zeros((chans, rows), jnp.float32)

    def first(index):
        filtered = []
        for stream in range(streams):
            now, past = proj[index + 1, stream], proj[index, stream]
            value = taps_ref[stream, 0] * now
            for offset in range(1, taps_count):
                moved = jnp.where(
                    lane < offset, pltpu.roll(past, offset, 1), pltpu.roll(now, offset, 1)
                )
                value = value + taps_ref[stream, offset] * moved
            filtered.append(value)
        query[index] = filtered[0]
        inner[index] = filtered[1] * filtered[2]

    each(blocks, first)

    def apply(source, table_ref, target):
        if chans % 8 == 0:
            flat = source[...].reshape(blocks * chans, source.shape[2])
            done = jnp.dot(flat, table_ref[...], precision=HIGHEST, preferred_element_type=jnp.float32)
            target[...] = done.reshape(target.shape)
        else:

            def one(index):
                target[index] = jnp.dot(
                    source[index], table_ref[...], precision=HIGHEST, preferred_element_type=jnp.float32
                )

            each(blocks, one)

    apply(filter_ref, fwd_ref, filter_spec)
    apply(inner, fwd_ref, spec)

    def multiply(index):
        def term(step):
            left, right = spec[step], filter_spec[index - step]
            left_real, left_imag = left[:, :rows], left[:, rows:]
            right_real, right_imag = right[:, :rows], right[:, rows:]
            return (
                left_real * right_real - left_imag * right_imag,
                left_real * right_imag + left_imag * right_real,
            )

        zero = jnp.zeros((chans, rows), jnp.float32)
        real, imag = total(index + 1, term, (zero, zero))
        product[index, :, :rows] = real
        product[index, :, rows:] = imag

    each(blocks, multiply)
    apply(product, bwd_ref, back)

    def last(index, carried):
        long_mix = back[index, :, :rows] + carried
        query[index] = query[index] * (long_mix + skip_ref[...] * inner[index])

    last(0, jnp.zeros((chans, rows), jnp.float32))
    each(blocks - 1, lambda index: last(index + 1, back[index, :, rows:]))

    tp_parts = out_ref.shape[0]
    part_rows = rows // tp_parts

    def spread(inner_index):
        for part in range(tp_parts):
            for group in range(outer // tp_parts):
                packed = jnp.zeros((chans, rows), jnp.float32)
                for place in range(tp_parts):
                    block = query[(group * tp_parts + place) * inner_parts + inner_index]
                    shift = (place - part) * part_rows % rows
                    block = pltpu.roll(block, shift, 1) if shift else block
                    packed = jnp.where(lane // part_rows == place, block, packed)
                out_ref[part, inner_index, :, group * rows : (group + 1) * rows] = packed.astype(out_ref.dtype)

    each(inner_parts, spread)


def convolve(parts, filter_blocks, taps, skip, outer, tp_parts):
    blocks, streams, chans, _ = parts[0].shape
    rows = filter_blocks.shape[2]
    forward, backward = tables(rows)
    wide = (blocks, chans, 2 * rows)
    narrow = (blocks, chans, rows)
    vmem = pl.BlockSpec(memory_space=pltpu.VMEM)
    return pl.pallas_call(
        functools.partial(conv_kernel, outer, len(parts)),
        out_shape=jax.ShapeDtypeStruct(
            (tp_parts, blocks // outer, chans, outer // tp_parts * rows), jnp.bfloat16
        ),
        in_specs=[vmem] * (5 + len(parts)),
        out_specs=vmem,
        scratch_shapes=[
            pltpu.VMEM((blocks + 1, streams, chans, rows), jnp.float32),
            pltpu.VMEM(narrow, jnp.float32),
            pltpu.VMEM(narrow, jnp.float32),
            pltpu.VMEM(wide, jnp.float32),
            pltpu.VMEM(wide, jnp.float32),
            pltpu.VMEM(wide, jnp.float32),
            pltpu.VMEM(wide, jnp.float32),
        ],
        compiler_params=pltpu.CompilerParams(vmem_limit_bytes=40 * 2**20),
        cost_estimate=pl.CostEstimate(flops=10**9, bytes_accessed=4 * 2**20, transcendentals=0),
    )(*parts, filter_blocks, taps, skip, jnp.asarray(forward), jnp.asarray(backward))


def out_kernel(place_ref, gated_ref, weight_ref, out_ref):
    tp_parts = gated_ref.shape[0]
    sums = jnp.zeros(out_ref.shape, jnp.float32)
    for step in range(tp_parts):
        which = lax.rem(place_ref[0] - step + tp_parts, tp_parts)
        sums = sums + jnp.dot(gated_ref[which], weight_ref[0, step], preferred_element_type=jnp.float32)
    out_ref[...] = sums.astype(out_ref.dtype)


def project_out(gated, weight):
    tp_parts, rows, depth = gated.shape
    inner_parts, _, _, width = weight.shape
    columns = inner_parts * width
    place = lax.axis_index("tp").astype(jnp.int32)[None]
    return pl.pallas_call(
        out_kernel,
        grid_spec=pltpu.PrefetchScalarGridSpec(
            num_scalar_prefetch=1,
            grid=(inner_parts,),
            in_specs=[
                pl.BlockSpec((tp_parts, rows, depth), lambda b, place: (0, 0, 0)),
                pl.BlockSpec((1, tp_parts, depth, width), lambda b, place: (b, 0, 0, 0)),
            ],
            out_specs=pl.BlockSpec((rows, width), lambda b, place: (0, b)),
        ),
        out_shape=jax.ShapeDtypeStruct((rows, columns), jnp.bfloat16),
        compiler_params=pltpu.CompilerParams(vmem_limit_bytes=56 * 2**20),
        cost_estimate=pl.CostEstimate(
            flops=2 * gated.size * columns,
            bytes_accessed=2 * (weight.size + gated.size + rows * columns),
            transcendentals=0,
        ),
    )(place, gated, weight)


def per_device(features, in_proj, short_taps, long_filter, skip_gain, out_proj):
    rows = features.shape[0]
    seq_parts = lax.axis_size("seq")
    tp_parts = lax.axis_size("tp")
    outer = outer_factor(seq_parts, tp_parts)
    inner_parts = seq_parts // outer
    streams, _, chan_tp = in_proj.shape
    chans = chan_tp // seq_parts
    position = lax.axis_index("seq")
    inner_groups = [[a * inner_parts + b for b in range(inner_parts)] for a in range(outer)]
    outer_groups = [[a * inner_parts + b for a in range(outer)] for b in range(inner_parts)]

    weight = lax.all_gather(in_proj, "seq", axis=1, tiled=True, axis_index_groups=inner_groups)

    held = share_columns(features, outer, tp_parts)
    held, long_filter = lax.optimization_barrier((held, long_filter))
    arrived = cross_outer(held, outer, inner_parts, tp_parts)
    depth = outer // CHUNKS
    crossed = [jnp.stack(arrived[index * depth : (index + 1) * depth]) for index in range(CHUNKS)]

    filter_blocks = lax.all_to_all(
        long_filter.T.reshape(seq_parts, chans, rows), "seq", split_axis=0, concat_axis=0, tiled=True
    )
    taps = lax.dynamic_slice_in_dim(short_taps, position * chans, chans, axis=2)
    taps = jnp.broadcast_to(taps[..., None], taps.shape + (rows,))
    skip = lax.dynamic_slice_in_dim(skip_gain, position * chans, chans, axis=0)
    skip = jnp.broadcast_to(skip[:, None], (chans, rows))

    parts = []
    for index, part in enumerate(crossed):
        pieces = share_over_tp(part, tp_parts)
        if index + 1 == CHUNKS:
            pieces, out_proj, filter_blocks, taps, skip = lax.optimization_barrier(
                (pieces, out_proj, filter_blocks, taps, skip)
            )
        partial = project_in(pieces, weight, seq_parts)
        parts.append(lax.all_to_all(partial, "seq", split_axis=0, concat_axis=0, tiled=True))

    out_block = jnp.stack(share_over_tp(out_proj, tp_parts))
    out_weight = lax.all_gather(out_block, "seq", axis_index_groups=inner_groups)

    gated = convolve(parts, filter_blocks, taps, skip, outer, tp_parts)
    gated = jnp.broadcast_to(gated[:, None], (tp_parts, outer) + gated.shape[1:])
    gated = lax.all_to_all(
        gated.reshape((-1,) + gated.shape[3:]), ("tp", "seq"), split_axis=0, concat_axis=0, tiled=True
    )
    gated = jnp.swapaxes(gated.reshape(tp_parts, chan_tp, -1), 1, 2)
    out = project_out(gated, out_weight)
    return return_output(out.reshape(outer, rows // tp_parts, -1), outer, inner_parts, tp_parts)


def solution(mesh):
    return jax.shard_map(
        per_device,
        mesh=mesh,
        in_specs=(
            P("seq", "tp"),
            P(None, "seq", "tp"),
            P(None, None, "tp"),
            P("seq", "tp"),
            P("tp"),
            P("tp", "seq"),
        ),
        out_specs=P("seq", "tp"),
        check_vma=False,
    )
```

```python
import functools
import math

import jax
import jax.numpy as jnp
import numpy as np
from jax import lax
from jax.experimental import pallas as pl
from jax.experimental.pallas import tpu as pltpu
from jax.sharding import PartitionSpec as P

HIGHEST = lax.Precision.HIGHEST
UNROLL = 16
CHUNKS = 2
HEAVY = 30


def outer_factor(seq_parts, tp_parts):
    outer = tp_parts
    while 4 * outer * outer <= seq_parts and seq_parts % (2 * outer) == 0:
        outer *= 2
    return outer


def assemble_kernel(place_ref, *refs):
    *piece_refs, out_ref = refs
    for index, piece_ref in enumerate(piece_refs):

        @pl.when(pl.program_id(0) == index)
        def _():
            out_ref[...] = piece_ref[...]


def assemble(pieces, places, shape):
    return pl.pallas_call(
        assemble_kernel,
        grid_spec=pltpu.PrefetchScalarGridSpec(
            num_scalar_prefetch=1,
            grid=(len(pieces),),
            in_specs=[pl.BlockSpec(memory_space=pltpu.VMEM)] * len(pieces),
            out_specs=pl.BlockSpec(
                pieces[0].shape, lambda i, place: (place[2 * i], place[2 * i + 1])
            ),
        ),
        out_shape=jax.ShapeDtypeStruct(shape, pieces[0].dtype),
        compiler_params=pltpu.CompilerParams(vmem_limit_bytes=4 * 2**20),
        cost_estimate=pl.CostEstimate(
            flops=0, bytes_accessed=4 * shape[0] * shape[1], transcendentals=0
        ),
    )(jnp.stack(places).astype(jnp.int32), *pieces)


def return_output(out, outer, inner_parts, tp_parts):
    _, part_rows, width = out.shape
    per_tp = outer // tp_parts
    tp_place = lax.axis_index("tp")
    outer_place = lax.axis_index("seq") // inner_parts
    pieces, places = [], []
    for far in range(tp_parts):
        for near in range(per_tp):

            def target(seq, tp):
                src = seq // inner_parts
                dst = (tp + far) % tp_parts * per_tp + (src % per_tp + near) % per_tp
                return (dst * inner_parts + seq % inner_parts) * tp_parts + src // per_tp

            pairs = [
                (seq * tp_parts + tp, target(seq, tp))
                for seq in range(outer * inner_parts)
                for tp in range(tp_parts)
            ]
            block = (tp_place + far) % tp_parts * per_tp + (outer_place % per_tp + near) % per_tp
            piece = lax.dynamic_index_in_dim(out, block, axis=0, keepdims=False)
            pieces.append(lax.ppermute(piece, ("seq", "tp"), pairs))
            places.append((outer_place // per_tp - far + tp_parts) % tp_parts)
            places.append((outer_place % per_tp - near + per_tp) % per_tp)
    return assemble(pieces, places, (tp_parts * part_rows, per_tp * width))


def share_columns(features, outer, tp_parts):
    rows, cols = features.shape
    per_tp = outer // tp_parts
    tp_place = lax.axis_index("tp")
    width = cols // outer
    held = []
    for step in range(tp_parts):
        which = (tp_place + step) % tp_parts
        piece = jnp.stack(
            [
                lax.dynamic_slice_in_dim(features, (group * tp_parts + which) * width, width, axis=1)
                for group in range(per_tp)
            ]
        )
        if step:
            piece = lax.ppermute(piece, "tp", [(i, (i + step) % tp_parts) for i in range(tp_parts)])
        held.append(piece)
    return jnp.concatenate(held)


def cross_outer(held, outer, inner_parts, tp_parts):
    per_tp = outer // tp_parts
    seq_parts = outer * inner_parts
    tp_place = lax.axis_index("tp")
    outer_place = lax.axis_index("seq") // inner_parts
    arrived = []
    for step in range(outer):
        target = (outer_place + step) % outer
        which = (tp_place - target // per_tp + tp_parts) % tp_parts * per_tp + target % per_tp
        piece = lax.dynamic_index_in_dim(held, which, axis=0, keepdims=False)
        if step:
            far = step * inner_parts
            piece = lax.ppermute(piece, "seq", [(i, (i + far) % seq_parts) for i in range(seq_parts)])
        arrived.append(piece)
    return arrived


def share_over_tp(part, tp_parts):
    pieces = [part]
    for step in range(1, tp_parts):
        pairs = [(i, (i + step) % tp_parts) for i in range(tp_parts)]
        pieces.append(lax.ppermute(part, "tp", pairs))
    return pieces


def project_kernel(tp_parts, place_ref, *refs):
    *share_refs, weight_ref, out_ref = refs
    seq_parts, _, chans, _ = out_ref.shape
    depth, rows, width = share_refs[0].shape
    count = depth * rows
    for chunk in range(len(share_refs) // tp_parts):
        sums = jnp.zeros((count, seq_parts * chans), jnp.float32)
        for step in range(tp_parts):
            which = lax.rem(place_ref[0] - step + tp_parts, tp_parts)
            sums = sums + jnp.dot(
                share_refs[chunk * tp_parts + step][...].reshape(count, width),
                weight_ref[0, which],
                preferred_element_type=jnp.float32,
            )
        turned = sums.T.astype(out_ref.dtype)
        for seq in range(seq_parts):
            out_ref[seq, 0, :, chunk * count : (chunk + 1) * count] = turned[
                seq * chans : (seq + 1) * chans
            ]


def project_in(chunks, weight, seq_parts):
    tp_parts = len(chunks[0])
    depth, rows, width = chunks[0][0].shape
    streams, _, chan_tp = weight.shape
    weight = weight.reshape(streams, tp_parts, width, chan_tp)
    chans = chan_tp // seq_parts
    count = len(chunks) * depth * rows
    pieces = [piece for chunk in chunks for piece in chunk]
    place = lax.axis_index("tp").astype(jnp.int32)[None]
    whole = pl.BlockSpec((depth, rows, width), lambda i, place: (0, 0, 0))
    return pl.pallas_call(
        functools.partial(project_kernel, tp_parts),
        grid_spec=pltpu.PrefetchScalarGridSpec(
            num_scalar_prefetch=1,
            grid=(streams,),
            in_specs=[whole] * len(pieces)
            + [pl.BlockSpec((1, tp_parts, width, chan_tp), lambda i, place: (i, 0, 0, 0))],
            out_specs=pl.BlockSpec((seq_parts, 1, chans, count), lambda i, place: (0, i, 0, 0)),
        ),
        out_shape=jax.ShapeDtypeStruct((seq_parts, streams, chans, count), jnp.bfloat16),
        compiler_params=pltpu.CompilerParams(vmem_limit_bytes=56 * 2**20),
        cost_estimate=pl.CostEstimate(
            flops=HEAVY * 2 * count * weight.size,
            bytes_accessed=2 * (weight.size + len(pieces) * pieces[0].size)
            + 2 * streams * count * chan_tp,
            transcendentals=0,
        ),
    )(place, *pieces, weight)


def tables(block):
    place = np.arange(block)
    angle = 2.0 * math.pi * np.outer(place, place + 0.5) / (2 * block)
    forward = np.concatenate([np.cos(angle), -np.sin(angle)], 1)
    place = np.arange(2 * block)
    angle = 2.0 * math.pi * np.outer(np.arange(block) + 0.5, place) / (2 * block)
    backward = np.concatenate([np.cos(angle), -np.sin(angle)], 0) / block
    return forward.astype(np.float32), backward.astype(np.float32)


def each(count, body):
    if isinstance(count, int) and count <= UNROLL:
        for index in range(count):
            body(index)
    else:
        lax.fori_loop(0, count, lambda index, carry: (body(index), carry)[1], 0)


def total(count, term, zero):
    if isinstance(count, int) and count <= UNROLL:
        result = zero
        for index in range(count):
            result = jax.tree.map(jnp.add, result, term(index))
        return result
    return lax.fori_loop(
        0, count, lambda index, sums: jax.tree.map(jnp.add, sums, term(index)), zero
    )


def conv_kernel(
    outer, chunks, *refs
):
    part_refs, refs = refs[:chunks], refs[chunks:]
    filter_ref, taps_ref, skip_ref, fwd_ref, bwd_ref, out_ref, *refs = refs
    proj, query, inner, spec, filter_spec, product, back = refs
    blocks, streams, chans, _ = part_refs[0].shape
    rows = filter_ref.shape[2]
    inner_parts = blocks // outer
    taps_count = taps_ref.shape[1]
    lane = lax.broadcasted_iota(jnp.int32, (chans, rows), 1)

    depth = outer // chunks

    def add_up(inner_index, stream, group):
        value = jnp.zeros((chans, rows), jnp.float32)
        for part in range(outer):
            slot = (part - group) % outer
            column = slice(slot % depth * rows, (slot % depth + 1) * rows)
            source = part_refs[slot // depth]
            value = value + source[part * inner_parts + inner_index, stream, :, column].astype(jnp.float32)
        proj[1 + group * inner_parts + inner_index, stream] = value

    for group in range(outer):
        for stream in range(streams):
            each(inner_parts, functools.partial(add_up, stream=stream, group=group))

    for stream in range(streams):
        proj[0, stream] = jnp.zeros((chans, rows), jnp.float32)

    def first(index):
        filtered = []
        for stream in range(streams):
            now, past = proj[index + 1, stream], proj[index, stream]
            value = taps_ref[stream, 0] * now
            for offset in range(1, taps_count):
                moved = jnp.where(
                    lane < offset, pltpu.roll(past, offset, 1), pltpu.roll(now, offset, 1)
                )
                value = value + taps_ref[stream, offset] * moved
            filtered.append(value)
        query[index] = filtered[0]
        inner[index] = filtered[1] * filtered[2]

    each(blocks, first)

    def apply(source, table_ref, target):
        if chans % 8 == 0:
            flat = source[...].reshape(blocks * chans, source.shape[2])
            done = jnp.dot(flat, table_ref[...], precision=HIGHEST, preferred_element_type=jnp.float32)
            target[...] = done.reshape(target.shape)
        else:

            def one(index):
                target[index] = jnp.dot(
                    source[index], table_ref[...], precision=HIGHEST, preferred_element_type=jnp.float32
                )

            each(blocks, one)

    apply(filter_ref, fwd_ref, filter_spec)
    apply(inner, fwd_ref, spec)

    def multiply(index):
        def term(step):
            left, right = spec[step], filter_spec[index - step]
            left_real, left_imag = left[:, :rows], left[:, rows:]
            right_real, right_imag = right[:, :rows], right[:, rows:]
            return (
                left_real * right_real - left_imag * right_imag,
                left_real * right_imag + left_imag * right_real,
            )

        zero = jnp.zeros((chans, rows), jnp.float32)
        real, imag = total(index + 1, term, (zero, zero))
        product[index, :, :rows] = real
        product[index, :, rows:] = imag

    each(blocks, multiply)
    apply(product, bwd_ref, back)

    def last(index, carried):
        long_mix = back[index, :, :rows] + carried
        query[index] = query[index] * (long_mix + skip_ref[...] * inner[index])

    last(0, jnp.zeros((chans, rows), jnp.float32))
    each(blocks - 1, lambda index: last(index + 1, back[index, :, rows:]))

    tp_parts = out_ref.shape[0]
    part_rows = rows // tp_parts

    def spread(inner_index):
        for part in range(tp_parts):
            for group in range(outer // tp_parts):
                packed = jnp.zeros((chans, rows), jnp.float32)
                for place in range(tp_parts):
                    block = query[(group * tp_parts + place) * inner_parts + inner_index]
                    shift = (place - part) * part_rows % rows
                    block = pltpu.roll(block, shift, 1) if shift else block
                    packed = jnp.where(lane // part_rows == place, block, packed)
                out_ref[part, inner_index, :, group * rows : (group + 1) * rows] = packed.astype(out_ref.dtype)

    each(inner_parts, spread)


def convolve(parts, filter_blocks, taps, skip, outer, tp_parts):
    blocks, streams, chans, _ = parts[0].shape
    rows = filter_blocks.shape[2]
    forward, backward = tables(rows)
    wide = (blocks, chans, 2 * rows)
    narrow = (blocks, chans, rows)
    vmem = pl.BlockSpec(memory_space=pltpu.VMEM)
    return pl.pallas_call(
        functools.partial(conv_kernel, outer, len(parts)),
        out_shape=jax.ShapeDtypeStruct(
            (tp_parts, blocks // outer, chans, outer // tp_parts * rows), jnp.bfloat16
        ),
        in_specs=[vmem] * (5 + len(parts)),
        out_specs=vmem,
        scratch_shapes=[
            pltpu.VMEM((blocks + 1, streams, chans, rows), jnp.float32),
            pltpu.VMEM(narrow, jnp.float32),
            pltpu.VMEM(narrow, jnp.float32),
            pltpu.VMEM(wide, jnp.float32),
            pltpu.VMEM(wide, jnp.float32),
            pltpu.VMEM(wide, jnp.float32),
            pltpu.VMEM(wide, jnp.float32),
        ],
        compiler_params=pltpu.CompilerParams(vmem_limit_bytes=40 * 2**20),
        cost_estimate=pl.CostEstimate(flops=10**9, bytes_accessed=4 * 2**20, transcendentals=0),
    )(*parts, filter_blocks, taps, skip, jnp.asarray(forward), jnp.asarray(backward))


def out_kernel(place_ref, gated_ref, weight_ref, out_ref):
    tp_parts = gated_ref.shape[0]
    sums = jnp.zeros(out_ref.shape, jnp.float32)
    for step in range(tp_parts):
        which = lax.rem(place_ref[0] - step + tp_parts, tp_parts)
        sums = sums + jnp.dot(gated_ref[which], weight_ref[0, step], preferred_element_type=jnp.float32)
    out_ref[...] = sums.astype(out_ref.dtype)


def project_out(gated, weight):
    tp_parts, rows, depth = gated.shape
    inner_parts, _, _, width = weight.shape
    columns = inner_parts * width
    place = lax.axis_index("tp").astype(jnp.int32)[None]
    return pl.pallas_call(
        out_kernel,
        grid_spec=pltpu.PrefetchScalarGridSpec(
            num_scalar_prefetch=1,
            grid=(inner_parts,),
            in_specs=[
                pl.BlockSpec((tp_parts, rows, depth), lambda b, place: (0, 0, 0)),
                pl.BlockSpec((1, tp_parts, depth, width), lambda b, place: (b, 0, 0, 0)),
            ],
            out_specs=pl.BlockSpec((rows, width), lambda b, place: (0, b)),
        ),
        out_shape=jax.ShapeDtypeStruct((rows, columns), jnp.bfloat16),
        compiler_params=pltpu.CompilerParams(vmem_limit_bytes=56 * 2**20),
        cost_estimate=pl.CostEstimate(
            flops=2 * gated.size * columns,
            bytes_accessed=2 * (weight.size + gated.size + rows * columns),
            transcendentals=0,
        ),
    )(place, gated, weight)


def per_device(features, in_proj, short_taps, long_filter, skip_gain, out_proj):
    rows = features.shape[0]
    seq_parts = lax.axis_size("seq")
    tp_parts = lax.axis_size("tp")
    outer = outer_factor(seq_parts, tp_parts)
    inner_parts = seq_parts // outer
    streams, _, chan_tp = in_proj.shape
    chans = chan_tp // seq_parts
    position = lax.axis_index("seq")
    inner_groups = [[a * inner_parts + b for b in range(inner_parts)] for a in range(outer)]
    outer_groups = [[a * inner_parts + b for a in range(outer)] for b in range(inner_parts)]

    weight = lax.all_gather(in_proj, "seq", axis=1, tiled=True, axis_index_groups=inner_groups)

    filter_blocks = lax.all_to_all(
        long_filter.T.reshape(seq_parts, chans, rows), "seq", split_axis=0, concat_axis=0, tiled=True
    )
    taps = lax.dynamic_slice_in_dim(short_taps, position * chans, chans, axis=2)
    taps = jnp.broadcast_to(taps[..., None], taps.shape + (rows,))
    skip = lax.dynamic_slice_in_dim(skip_gain, position * chans, chans, axis=0)
    skip = jnp.broadcast_to(skip[:, None], (chans, rows))

    held = share_columns(features, outer, tp_parts)
    held, filter_blocks, taps, skip = lax.optimization_barrier((held, filter_blocks, taps, skip))
    arrived = cross_outer(held, outer, inner_parts, tp_parts)
    depth = outer // CHUNKS
    chunks = [
        share_over_tp(jnp.stack(arrived[index * depth : (index + 1) * depth]), tp_parts)
        for index in range(CHUNKS)
    ]
    chunks, out_proj = lax.optimization_barrier((chunks, out_proj))

    partial = project_in(chunks, weight, seq_parts)
    parts = lax.all_to_all(partial, "seq", split_axis=0, concat_axis=0, tiled=True)
    out_block = jnp.stack(share_over_tp(out_proj, tp_parts))
    out_weight = lax.all_gather(out_block, "seq", axis_index_groups=inner_groups)

    gated = convolve([parts], filter_blocks, taps, skip, outer, tp_parts)
    gated = jnp.broadcast_to(gated[:, None], (tp_parts, outer) + gated.shape[1:])
    gated = lax.all_to_all(
        gated.reshape((-1,) + gated.shape[3:]), ("tp", "seq"), split_axis=0, concat_axis=0, tiled=True
    )
    gated = jnp.swapaxes(gated.reshape(tp_parts, chan_tp, -1), 1, 2)
    out = project_out(gated, out_weight)
    return return_output(out.reshape(outer, rows // tp_parts, -1), outer, inner_parts, tp_parts)


def solution(mesh):
    return jax.shard_map(
        per_device,
        mesh=mesh,
        in_specs=(
            P("seq", "tp"),
            P(None, "seq", "tp"),
            P(None, None, "tp"),
            P("seq", "tp"),
            P("tp"),
            P("tp", "seq"),
        ),
        out_specs=P("seq", "tp"),
        check_vma=False,
    )
```

```python
import functools
import math

import jax
import jax.numpy as jnp
import numpy as np
from jax import lax
from jax.experimental import pallas as pl
from jax.experimental.pallas import tpu as pltpu
from jax.sharding import PartitionSpec as P

HIGHEST = lax.Precision.HIGHEST
UNROLL = 16
HEAVY = 30


def outer_factor(seq_parts, tp_parts):
    outer = tp_parts
    while 4 * outer * outer <= seq_parts and seq_parts % (2 * outer) == 0:
        outer *= 2
    return outer


def assemble_kernel(place_ref, *refs):
    *piece_refs, out_ref = refs
    for index, piece_ref in enumerate(piece_refs):

        @pl.when(pl.program_id(0) == index)
        def _():
            out_ref[...] = piece_ref[...]


def assemble(pieces, places, shape):
    return pl.pallas_call(
        assemble_kernel,
        grid_spec=pltpu.PrefetchScalarGridSpec(
            num_scalar_prefetch=1,
            grid=(len(pieces),),
            in_specs=[pl.BlockSpec(memory_space=pltpu.VMEM)] * len(pieces),
            out_specs=pl.BlockSpec(
                pieces[0].shape, lambda i, place: (place[2 * i], place[2 * i + 1])
            ),
        ),
        out_shape=jax.ShapeDtypeStruct(shape, pieces[0].dtype),
        compiler_params=pltpu.CompilerParams(vmem_limit_bytes=4 * 2**20),
        cost_estimate=pl.CostEstimate(
            flops=0, bytes_accessed=4 * shape[0] * shape[1], transcendentals=0
        ),
    )(jnp.stack(places).astype(jnp.int32), *pieces)


def return_places(outer, inner_parts, tp_parts):
    per_tp = outer // tp_parts
    tp_place = lax.axis_index("tp")
    outer_place = lax.axis_index("seq") // inner_parts
    blocks, places = [], []
    for far in range(tp_parts):
        for near in range(per_tp):
            blocks.append((tp_place + far) % tp_parts * per_tp + (outer_place % per_tp + near) % per_tp)
            places.append((outer_place // per_tp - far + tp_parts) % tp_parts)
            places.append((outer_place % per_tp - near + per_tp) % per_tp)
    return blocks, places


def return_output(pieces, places, inner_parts, tp_parts):
    outer = len(pieces)
    part_rows, width = pieces[0].shape
    per_tp = outer // tp_parts
    arrived = []
    for index, piece in enumerate(pieces):
        far, near = divmod(index, per_tp)

        def target(seq, tp):
            src = seq // inner_parts
            dst = (tp + far) % tp_parts * per_tp + (src % per_tp + near) % per_tp
            return (dst * inner_parts + seq % inner_parts) * tp_parts + src // per_tp

        pairs = [
            (seq * tp_parts + tp, target(seq, tp))
            for seq in range(outer * inner_parts)
            for tp in range(tp_parts)
        ]
        arrived.append(lax.ppermute(piece, ("seq", "tp"), pairs))
    return assemble(arrived, places, (tp_parts * part_rows, per_tp * width))


def share_columns(features, outer, tp_parts):
    rows, cols = features.shape
    per_tp = outer // tp_parts
    tp_place = lax.axis_index("tp")
    width = cols // outer
    held = []
    for step in range(tp_parts):
        which = (tp_place + step) % tp_parts
        piece = jnp.stack(
            [
                lax.dynamic_slice_in_dim(features, (group * tp_parts + which) * width, width, axis=1)
                for group in range(per_tp)
            ]
        )
        if step:
            piece = lax.ppermute(piece, "tp", [(i, (i + step) % tp_parts) for i in range(tp_parts)])
        held.append(piece)
    return jnp.concatenate(held)


def cross_outer(held, outer, inner_parts, tp_parts):
    per_tp = outer // tp_parts
    seq_parts = outer * inner_parts
    tp_place = lax.axis_index("tp")
    outer_place = lax.axis_index("seq") // inner_parts
    arrived = []
    for step in range(outer):
        target = (outer_place + step) % outer
        which = (tp_place - target // per_tp + tp_parts) % tp_parts * per_tp + target % per_tp
        piece = lax.dynamic_index_in_dim(held, which, axis=0, keepdims=False)
        if step:
            far = step * inner_parts
            piece = lax.ppermute(piece, "seq", [(i, (i + far) % seq_parts) for i in range(seq_parts)])
        arrived.append(piece)
    return arrived


def share_over_tp(part, tp_parts):
    pieces = [part]
    for step in range(1, tp_parts):
        pairs = [(i, (i + step) % tp_parts) for i in range(tp_parts)]
        pieces.append(lax.ppermute(part, "tp", pairs))
    return pieces


def project_kernel(tp_parts, place_ref, *refs):
    *share_refs, weight_ref, out_ref = refs
    seq_parts, _, chans, count = out_ref.shape
    inner_parts, _, chan_tp, width = weight_ref.shape
    blocks = inner_parts // tp_parts
    sums = jnp.zeros((chan_tp, count), jnp.float32)
    for step in range(tp_parts):
        which = lax.rem(place_ref[0] - step + tp_parts, tp_parts)
        right = jnp.concatenate([share_ref[...] for share_ref in share_refs[step::tp_parts]])
        for block in range(blocks):
            sums = sums + lax.dot_general(
                weight_ref[which * blocks + block, 0],
                right[:, block * width : (block + 1) * width],
                (((1,), (1,)), ((), ())),
                preferred_element_type=jnp.float32,
            )
    done = sums.astype(out_ref.dtype)
    for seq in range(seq_parts):
        out_ref[seq, 0] = done[seq * chans : (seq + 1) * chans]


def project_in(chunks, weight, seq_parts):
    tp_parts = len(chunks[0])
    inner_parts, streams, chan_tp, width = weight.shape
    chans = chan_tp // seq_parts
    pieces = [piece for chunk in chunks for piece in chunk]
    count = len(chunks) * pieces[0].shape[0]
    place = lax.axis_index("tp").astype(jnp.int32)[None]
    return pl.pallas_call(
        functools.partial(project_kernel, tp_parts),
        grid_spec=pltpu.PrefetchScalarGridSpec(
            num_scalar_prefetch=1,
            grid=(streams,),
            in_specs=[pl.BlockSpec(pieces[0].shape, lambda i, place: (0, 0))] * len(pieces)
            + [pl.BlockSpec((inner_parts, 1, chan_tp, width), lambda i, place: (0, i, 0, 0))],
            out_specs=pl.BlockSpec((seq_parts, 1, chans, count), lambda i, place: (0, i, 0, 0)),
        ),
        out_shape=jax.ShapeDtypeStruct((seq_parts, streams, chans, count), jnp.bfloat16),
        compiler_params=pltpu.CompilerParams(vmem_limit_bytes=56 * 2**20),
        cost_estimate=pl.CostEstimate(
            flops=HEAVY * 2 * count * weight.size,
            bytes_accessed=2 * (weight.size + len(pieces) * pieces[0].size)
            + 2 * streams * count * chan_tp,
            transcendentals=0,
        ),
    )(place, *pieces, weight)


def tables(block):
    place = np.arange(block)
    angle = 2.0 * math.pi * np.outer(place, place + 0.5) / (2 * block)
    forward = np.concatenate([np.cos(angle), -np.sin(angle)], 1)
    place = np.arange(2 * block)
    angle = 2.0 * math.pi * np.outer(np.arange(block) + 0.5, place) / (2 * block)
    backward = np.concatenate([np.cos(angle), -np.sin(angle)], 0) / block
    return forward.astype(np.float32), backward.astype(np.float32)


def each(count, body):
    if isinstance(count, int) and count <= UNROLL:
        for index in range(count):
            body(index)
    else:
        lax.fori_loop(0, count, lambda index, carry: (body(index), carry)[1], 0)


def total(count, term, zero):
    if isinstance(count, int) and count <= UNROLL:
        result = zero
        for index in range(count):
            result = jax.tree.map(jnp.add, result, term(index))
        return result
    return lax.fori_loop(
        0, count, lambda index, sums: jax.tree.map(jnp.add, sums, term(index)), zero
    )


def conv_kernel(
    outer, chunks, *refs
):
    part_refs, refs = refs[:chunks], refs[chunks:]
    filter_ref, taps_ref, skip_ref, fwd_ref, bwd_ref, out_ref, *refs = refs
    proj, query, inner, spec, filter_spec, product, back = refs
    blocks, streams, chans, _ = part_refs[0].shape
    rows = filter_ref.shape[2]
    inner_parts = blocks // outer
    taps_count = taps_ref.shape[1]
    lane = lax.broadcasted_iota(jnp.int32, (chans, rows), 1)

    depth = outer // chunks

    def add_up(inner_index, stream, group):
        value = jnp.zeros((chans, rows), jnp.float32)
        for part in range(outer):
            slot = (part - group) % outer
            column = slice(slot % depth * rows, (slot % depth + 1) * rows)
            source = part_refs[slot // depth]
            value = value + source[part * inner_parts + inner_index, stream, :, column].astype(jnp.float32)
        proj[1 + group * inner_parts + inner_index, stream] = value

    for group in range(outer):
        for stream in range(streams):
            each(inner_parts, functools.partial(add_up, stream=stream, group=group))

    for stream in range(streams):
        proj[0, stream] = jnp.zeros((chans, rows), jnp.float32)

    def first(index):
        filtered = []
        for stream in range(streams):
            now, past = proj[index + 1, stream], proj[index, stream]
            value = taps_ref[stream, 0] * now
            for offset in range(1, taps_count):
                moved = jnp.where(
                    lane < offset, pltpu.roll(past, offset, 1), pltpu.roll(now, offset, 1)
                )
                value = value + taps_ref[stream, offset] * moved
            filtered.append(value)
        query[index] = filtered[0]
        inner[index] = filtered[1] * filtered[2]

    each(blocks, first)

    def apply(source, table_ref, target):
        if chans % 8 == 0:
            flat = source[...].reshape(blocks * chans, source.shape[2])
            done = jnp.dot(flat, table_ref[...], precision=HIGHEST, preferred_element_type=jnp.float32)
            target[...] = done.reshape(target.shape)
        else:

            def one(index):
                target[index] = jnp.dot(
                    source[index], table_ref[...], precision=HIGHEST, preferred_element_type=jnp.float32
                )

            each(blocks, one)

    apply(filter_ref, fwd_ref, filter_spec)
    apply(inner, fwd_ref, spec)

    def multiply(index):
        def term(step):
            left, right = spec[step], filter_spec[index - step]
            left_real, left_imag = left[:, :rows], left[:, rows:]
            right_real, right_imag = right[:, :rows], right[:, rows:]
            return (
                left_real * right_real - left_imag * right_imag,
                left_real * right_imag + left_imag * right_real,
            )

        zero = jnp.zeros((chans, rows), jnp.float32)
        real, imag = total(index + 1, term, (zero, zero))
        product[index, :, :rows] = real
        product[index, :, rows:] = imag

    each(blocks, multiply)
    apply(product, bwd_ref, back)

    def last(index, carried):
        long_mix = back[index, :, :rows] + carried
        query[index] = query[index] * (long_mix + skip_ref[...] * inner[index])

    last(0, jnp.zeros((chans, rows), jnp.float32))
    each(blocks - 1, lambda index: last(index + 1, back[index, :, rows:]))

    tp_parts = out_ref.shape[0]
    part_rows = rows // tp_parts
    copies = out_ref.shape[1]

    def spread(inner_index):
        for part in range(tp_parts):
            for group in range(outer // tp_parts):
                packed = jnp.zeros((chans, rows), jnp.float32)
                for place in range(tp_parts):
                    block = query[(group * tp_parts + place) * inner_parts + inner_index]
                    shift = (place - part) * part_rows % rows
                    block = pltpu.roll(block, shift, 1) if shift else block
                    packed = jnp.where(lane // part_rows == place, block, packed)
                packed = packed.astype(out_ref.dtype)
                for copy in range(copies):
                    out_ref[part, copy, inner_index, :, group * rows : (group + 1) * rows] = packed

    each(inner_parts, spread)


def convolve(parts, filter_blocks, taps, skip, outer, tp_parts):
    blocks, streams, chans, _ = parts[0].shape
    rows = filter_blocks.shape[2]
    forward, backward = tables(rows)
    wide = (blocks, chans, 2 * rows)
    narrow = (blocks, chans, rows)
    vmem = pl.BlockSpec(memory_space=pltpu.VMEM)
    return pl.pallas_call(
        functools.partial(conv_kernel, outer, len(parts)),
        out_shape=jax.ShapeDtypeStruct(
            (tp_parts, outer, blocks // outer, chans, outer // tp_parts * rows), jnp.bfloat16
        ),
        in_specs=[vmem] * (5 + len(parts)),
        out_specs=vmem,
        scratch_shapes=[
            pltpu.VMEM((blocks + 1, streams, chans, rows), jnp.float32),
            pltpu.VMEM(narrow, jnp.float32),
            pltpu.VMEM(narrow, jnp.float32),
            pltpu.VMEM(wide, jnp.float32),
            pltpu.VMEM(wide, jnp.float32),
            pltpu.VMEM(wide, jnp.float32),
            pltpu.VMEM(wide, jnp.float32),
        ],
        compiler_params=pltpu.CompilerParams(vmem_limit_bytes=40 * 2**20),
        cost_estimate=pl.CostEstimate(flops=10**9, bytes_accessed=4 * 2**20, transcendentals=0),
    )(*parts, filter_blocks, taps, skip, jnp.asarray(forward), jnp.asarray(backward))


def out_kernel(block_ref, gated_ref, weight_ref, *refs):
    *out_refs, turned, left = refs
    tp_parts = gated_ref.shape[0]
    part_rows = out_refs[0].shape[0]

    @pl.when(pl.program_id(0) == 0)
    def _():
        for part in range(tp_parts):
            turned[...] = gated_ref[part].T
            for index in range(len(out_refs)):
                begin = pl.multiple_of(block_ref[index] * part_rows, part_rows)
                left[part, index * part_rows : (index + 1) * part_rows] = turned[pl.ds(begin, part_rows)]

    sums = jnp.zeros((left.shape[1], weight_ref.shape[3]), jnp.float32)
    for part in range(tp_parts):
        sums = sums + jnp.dot(left[part], weight_ref[0, part], preferred_element_type=jnp.float32)
    for index, out_ref in enumerate(out_refs):
        out_ref[...] = sums[index * part_rows : (index + 1) * part_rows].astype(out_ref.dtype)


def project_out(gated, weight, blocks):
    tp_parts, depth, rows = gated.shape
    inner_parts, _, _, width = weight.shape
    columns = inner_parts * width
    part_rows = rows // len(blocks)
    return pl.pallas_call(
        out_kernel,
        grid_spec=pltpu.PrefetchScalarGridSpec(
            num_scalar_prefetch=1,
            grid=(inner_parts,),
            in_specs=[
                pl.BlockSpec((tp_parts, depth, rows), lambda b, place: (0, 0, 0)),
                pl.BlockSpec((1, tp_parts, depth, width), lambda b, place: (b, 0, 0, 0)),
            ],
            out_specs=[pl.BlockSpec((part_rows, width), lambda b, place: (0, b))] * len(blocks),
            scratch_shapes=[
                pltpu.VMEM((rows, depth), jnp.bfloat16),
                pltpu.VMEM((tp_parts, rows, depth), jnp.bfloat16),
            ],
        ),
        out_shape=[jax.ShapeDtypeStruct((part_rows, columns), jnp.bfloat16)] * len(blocks),
        compiler_params=pltpu.CompilerParams(vmem_limit_bytes=56 * 2**20),
        cost_estimate=pl.CostEstimate(
            flops=2 * gated.size * columns,
            bytes_accessed=2 * (weight.size + gated.size + rows * columns),
            transcendentals=0,
        ),
    )(jnp.stack(blocks).astype(jnp.int32), gated, weight)


def per_device(features, in_proj, short_taps, long_filter, skip_gain, out_proj):
    rows = features.shape[0]
    seq_parts = lax.axis_size("seq")
    tp_parts = lax.axis_size("tp")
    outer = outer_factor(seq_parts, tp_parts)
    inner_parts = seq_parts // outer
    streams, _, chan_tp = in_proj.shape
    chans = chan_tp // seq_parts
    position = lax.axis_index("seq")
    inner_groups = [[a * inner_parts + b for b in range(inner_parts)] for a in range(outer)]
    tp_groups = [
        [index * tp_parts + tp for index in group for tp in range(tp_parts)] for group in inner_groups
    ]

    weight = lax.all_gather(jnp.swapaxes(in_proj, 1, 2), "seq", axis_index_groups=inner_groups)

    filter_blocks = lax.all_to_all(
        long_filter.T.reshape(seq_parts, chans, rows), "seq", split_axis=0, concat_axis=0, tiled=True
    )
    taps = lax.dynamic_slice_in_dim(short_taps, position * chans, chans, axis=2)
    taps = jnp.broadcast_to(taps[..., None], taps.shape + (rows,))
    skip = lax.dynamic_slice_in_dim(skip_gain, position * chans, chans, axis=0)
    skip = jnp.broadcast_to(skip[:, None], (chans, rows))

    held = share_columns(features, outer, tp_parts)
    held, filter_blocks, taps, skip = lax.optimization_barrier((held, filter_blocks, taps, skip))
    arrived = cross_outer(held, outer, inner_parts, tp_parts)
    chunks = [share_over_tp(piece, tp_parts) for piece in arrived]
    chunks, out_proj = lax.optimization_barrier((chunks, out_proj))
    out_weight = lax.all_gather(out_proj, ("seq", "tp"), axis_index_groups=tp_groups)
    out_weight = out_weight.reshape((inner_parts, tp_parts) + out_proj.shape)

    partial = project_in(chunks, weight, seq_parts)
    parts = lax.all_to_all(partial, "seq", split_axis=0, concat_axis=0, tiled=True)

    gated = convolve([parts], filter_blocks, taps, skip, outer, tp_parts)
    gated = lax.all_to_all(
        gated.reshape((-1,) + gated.shape[3:]), ("tp", "seq"), split_axis=0, concat_axis=0, tiled=True
    )
    blocks, places = return_places(outer, inner_parts, tp_parts)
    pieces = project_out(gated.reshape(tp_parts, chan_tp, -1), out_weight, blocks)
    return return_output(pieces, places, inner_parts, tp_parts)


def solution(mesh):
    return jax.shard_map(
        per_device,
        mesh=mesh,
        in_specs=(
            P("seq", "tp"),
            P(None, "seq", "tp"),
            P(None, None, "tp"),
            P("seq", "tp"),
            P("tp"),
            P("tp", "seq"),
        ),
        out_specs=P("seq", "tp"),
        check_vma=False,
    )
```

```python
import functools
import math

import jax
import jax.numpy as jnp
import numpy as np
from jax import lax
from jax.experimental import pallas as pl
from jax.experimental.pallas import tpu as pltpu
from jax.sharding import PartitionSpec as P

HIGHEST = lax.Precision.HIGHEST
UNROLL = 16
HEAVY = 30


def outer_factor(seq_parts, tp_parts):
    outer = tp_parts
    while 4 * outer * outer <= seq_parts and seq_parts % (2 * outer) == 0:
        outer *= 2
    return outer


def assemble_kernel(place_ref, *refs):
    *piece_refs, out_ref = refs
    for index, piece_ref in enumerate(piece_refs):

        @pl.when(pl.program_id(0) == index)
        def _():
            out_ref[...] = piece_ref[...]


def assemble(pieces, places, shape):
    return pl.pallas_call(
        assemble_kernel,
        grid_spec=pltpu.PrefetchScalarGridSpec(
            num_scalar_prefetch=1,
            grid=(len(pieces),),
            in_specs=[pl.BlockSpec(memory_space=pltpu.VMEM)] * len(pieces),
            out_specs=pl.BlockSpec(
                pieces[0].shape, lambda i, place: (place[2 * i], place[2 * i + 1])
            ),
        ),
        out_shape=jax.ShapeDtypeStruct(shape, pieces[0].dtype),
        compiler_params=pltpu.CompilerParams(vmem_limit_bytes=4 * 2**20),
        cost_estimate=pl.CostEstimate(
            flops=0, bytes_accessed=4 * shape[0] * shape[1], transcendentals=0
        ),
    )(jnp.stack(places).astype(jnp.int32), *pieces)


def return_places(outer, inner_parts, tp_parts):
    per_tp = outer // tp_parts
    tp_place = lax.axis_index("tp")
    outer_place = lax.axis_index("seq") // inner_parts
    blocks, places = [], []
    for far in range(tp_parts):
        for near in range(per_tp):
            low = outer_place % per_tp
            blocks.append((tp_place + low + far) % tp_parts * per_tp + (low + near) % per_tp)
            low = (low - near + per_tp) % per_tp
            places.append((outer_place // per_tp - far - low + tp_parts + per_tp * tp_parts) % tp_parts)
            places.append(low)
    return blocks, places


def return_output(pieces, places, inner_parts, tp_parts):
    outer = len(pieces)
    part_rows, width = pieces[0].shape
    per_tp = outer // tp_parts
    arrived = []
    for index, piece in enumerate(pieces):
        far, near = divmod(index, per_tp)

        def target(seq, tp):
            src = seq // inner_parts
            low = src % per_tp
            dst = (tp + low + far) % tp_parts * per_tp + (low + near) % per_tp
            return (dst * inner_parts + seq % inner_parts) * tp_parts + src // per_tp

        pairs = [
            (seq * tp_parts + tp, target(seq, tp))
            for seq in range(outer * inner_parts)
            for tp in range(tp_parts)
        ]
        arrived.append(lax.ppermute(piece, ("seq", "tp"), pairs))
    return assemble(arrived, places, (tp_parts * part_rows, per_tp * width))


def share_columns(features, outer, tp_parts):
    rows, cols = features.shape
    per_tp = outer // tp_parts
    tp_place = lax.axis_index("tp")
    width = cols // outer
    held = []
    for step in range(tp_parts):
        which = (tp_place + step) % tp_parts
        piece = jnp.stack(
            [
                lax.dynamic_slice_in_dim(features, (group * tp_parts + which) * width, width, axis=1)
                for group in range(per_tp)
            ]
        )
        if step:
            piece = lax.ppermute(piece, "tp", [(i, (i + step) % tp_parts) for i in range(tp_parts)])
        held.append(piece)
    return jnp.concatenate(held)


def cross_outer(held, outer, inner_parts, tp_parts):
    per_tp = outer // tp_parts
    seq_parts = outer * inner_parts
    tp_place = lax.axis_index("tp")
    outer_place = lax.axis_index("seq") // inner_parts
    arrived = []
    for step in range(outer):
        target = (outer_place + step) % outer
        which = (tp_place - target // per_tp + tp_parts) % tp_parts * per_tp + target % per_tp
        piece = lax.dynamic_index_in_dim(held, which, axis=0, keepdims=False)
        if step:
            far = step * inner_parts
            piece = lax.ppermute(piece, "seq", [(i, (i + far) % seq_parts) for i in range(seq_parts)])
        arrived.append(piece)
    return arrived


def share_over_tp(part, tp_parts):
    pieces = [part]
    for step in range(1, tp_parts):
        pairs = [(i, (i + step) % tp_parts) for i in range(tp_parts)]
        pieces.append(lax.ppermute(part, "tp", pairs))
    return pieces


def project_kernel(tp_parts, place_ref, *refs):
    *share_refs, weight_ref, out_ref = refs
    seq_parts, _, chans, count = out_ref.shape
    sums = jnp.zeros((count, seq_parts * chans), jnp.float32)
    for step in range(tp_parts):
        which = lax.rem(place_ref[0] - step + tp_parts, tp_parts)
        left = jnp.concatenate([share_ref[...] for share_ref in share_refs[step::tp_parts]])
        sums = sums + jnp.dot(left, weight_ref[0, which], preferred_element_type=jnp.float32)
    turned = sums.astype(out_ref.dtype).T
    for seq in range(seq_parts):
        out_ref[seq, 0] = turned[seq * chans : (seq + 1) * chans]


def project_in(chunks, weight, seq_parts):
    tp_parts = len(chunks[0])
    rows, width = chunks[0][0].shape
    streams, _, chan_tp = weight.shape
    weight = weight.reshape(streams, tp_parts, width, chan_tp)
    chans = chan_tp // seq_parts
    pieces = [piece for chunk in chunks for piece in chunk]
    count = len(chunks) * rows
    place = lax.axis_index("tp").astype(jnp.int32)[None]
    return pl.pallas_call(
        functools.partial(project_kernel, tp_parts),
        grid_spec=pltpu.PrefetchScalarGridSpec(
            num_scalar_prefetch=1,
            grid=(streams,),
            in_specs=[pl.BlockSpec((rows, width), lambda i, place: (0, 0))] * len(pieces)
            + [pl.BlockSpec((1, tp_parts, width, chan_tp), lambda i, place: (i, 0, 0, 0))],
            out_specs=pl.BlockSpec((seq_parts, 1, chans, count), lambda i, place: (0, i, 0, 0)),
        ),
        out_shape=jax.ShapeDtypeStruct((seq_parts, streams, chans, count), jnp.bfloat16),
        compiler_params=pltpu.CompilerParams(vmem_limit_bytes=56 * 2**20),
        cost_estimate=pl.CostEstimate(
            flops=HEAVY * 2 * count * weight.size,
            bytes_accessed=2 * (weight.size + len(pieces) * pieces[0].size)
            + 2 * streams * count * chan_tp,
            transcendentals=0,
        ),
    )(place, *pieces, weight)


def tables(block):
    place = np.arange(block)
    angle = 2.0 * math.pi * np.outer(place, place + 0.5) / (2 * block)
    forward = np.concatenate([np.cos(angle), -np.sin(angle)], 1)
    place = np.arange(2 * block)
    angle = 2.0 * math.pi * np.outer(np.arange(block) + 0.5, place) / (2 * block)
    backward = np.concatenate([np.cos(angle), -np.sin(angle)], 0) / block
    return forward.astype(np.float32), backward.astype(np.float32)


def each(count, body):
    if isinstance(count, int) and count <= UNROLL:
        for index in range(count):
            body(index)
    else:
        lax.fori_loop(0, count, lambda index, carry: (body(index), carry)[1], 0)


def total(count, term, zero):
    if isinstance(count, int) and count <= UNROLL:
        result = zero
        for index in range(count):
            result = jax.tree.map(jnp.add, result, term(index))
        return result
    return lax.fori_loop(
        0, count, lambda index, sums: jax.tree.map(jnp.add, sums, term(index)), zero
    )


def conv_kernel(
    outer, chunks, *refs
):
    part_refs, refs = refs[:chunks], refs[chunks:]
    filter_ref, taps_ref, skip_ref, fwd_ref, bwd_ref, out_ref, *refs = refs
    proj, query, inner, spec, filter_spec, product, back = refs
    blocks, streams, chans, _ = part_refs[0].shape
    rows = filter_ref.shape[2]
    inner_parts = blocks // outer
    taps_count = taps_ref.shape[1]
    lane = lax.broadcasted_iota(jnp.int32, (chans, rows), 1)

    depth = outer // chunks

    def add_up(inner_index, stream, group):
        value = jnp.zeros((chans, rows), jnp.float32)
        for part in range(outer):
            slot = (part - group) % outer
            column = slice(slot % depth * rows, (slot % depth + 1) * rows)
            source = part_refs[slot // depth]
            value = value + source[part * inner_parts + inner_index, stream, :, column].astype(jnp.float32)
        proj[1 + group * inner_parts + inner_index, stream] = value

    for group in range(outer):
        for stream in range(streams):
            each(inner_parts, functools.partial(add_up, stream=stream, group=group))

    for stream in range(streams):
        proj[0, stream] = jnp.zeros((chans, rows), jnp.float32)

    def first(index):
        filtered = []
        for stream in range(streams):
            now, past = proj[index + 1, stream], proj[index, stream]
            value = taps_ref[stream, 0] * now
            for offset in range(1, taps_count):
                moved = jnp.where(
                    lane < offset, pltpu.roll(past, offset, 1), pltpu.roll(now, offset, 1)
                )
                value = value + taps_ref[stream, offset] * moved
            filtered.append(value)
        query[index] = filtered[0]
        inner[index] = filtered[1] * filtered[2]

    each(blocks, first)

    def apply(source, table_ref, target):
        if chans % 8 == 0:
            flat = source[...].reshape(blocks * chans, source.shape[2])
            done = jnp.dot(flat, table_ref[...], precision=HIGHEST, preferred_element_type=jnp.float32)
            target[...] = done.reshape(target.shape)
        else:

            def one(index):
                target[index] = jnp.dot(
                    source[index], table_ref[...], precision=HIGHEST, preferred_element_type=jnp.float32
                )

            each(blocks, one)

    apply(filter_ref, fwd_ref, filter_spec)
    apply(inner, fwd_ref, spec)

    def multiply(index):
        def term(step):
            left, right = spec[step], filter_spec[index - step]
            left_real, left_imag = left[:, :rows], left[:, rows:]
            right_real, right_imag = right[:, :rows], right[:, rows:]
            return (
                left_real * right_real - left_imag * right_imag,
                left_real * right_imag + left_imag * right_real,
            )

        zero = jnp.zeros((chans, rows), jnp.float32)
        real, imag = total(index + 1, term, (zero, zero))
        product[index, :, :rows] = real
        product[index, :, rows:] = imag

    each(blocks, multiply)
    apply(product, bwd_ref, back)

    def last(index, carried):
        long_mix = back[index, :, :rows] + carried
        query[index] = query[index] * (long_mix + skip_ref[...] * inner[index])

    last(0, jnp.zeros((chans, rows), jnp.float32))
    each(blocks - 1, lambda index: last(index + 1, back[index, :, rows:]))

    tp_parts = out_ref.shape[0]
    part_rows = rows // tp_parts
    copies = out_ref.shape[1]

    def spread(inner_index):
        for part in range(tp_parts):
            for group in range(outer // tp_parts):
                packed = jnp.zeros((chans, rows), jnp.float32)
                for place in range(tp_parts):
                    block = query[(group * tp_parts + place) * inner_parts + inner_index]
                    shift = (place - part) * part_rows % rows
                    block = pltpu.roll(block, shift, 1) if shift else block
                    packed = jnp.where(lane // part_rows == place, block, packed)
                packed = packed.astype(out_ref.dtype)
                for copy in range(copies):
                    out_ref[part, copy, inner_index, :, group * rows : (group + 1) * rows] = packed

    each(inner_parts, spread)


def convolve(parts, filter_blocks, taps, skip, outer, tp_parts):
    blocks, streams, chans, _ = parts[0].shape
    rows = filter_blocks.shape[2]
    forward, backward = tables(rows)
    wide = (blocks, chans, 2 * rows)
    narrow = (blocks, chans, rows)
    vmem = pl.BlockSpec(memory_space=pltpu.VMEM)
    return pl.pallas_call(
        functools.partial(conv_kernel, outer, len(parts)),
        out_shape=jax.ShapeDtypeStruct(
            (tp_parts, outer, blocks // outer, chans, outer // tp_parts * rows), jnp.bfloat16
        ),
        in_specs=[vmem] * (5 + len(parts)),
        out_specs=vmem,
        scratch_shapes=[
            pltpu.VMEM((blocks + 1, streams, chans, rows), jnp.float32),
            pltpu.VMEM(narrow, jnp.float32),
            pltpu.VMEM(narrow, jnp.float32),
            pltpu.VMEM(wide, jnp.float32),
            pltpu.VMEM(wide, jnp.float32),
            pltpu.VMEM(wide, jnp.float32),
            pltpu.VMEM(wide, jnp.float32),
        ],
        compiler_params=pltpu.CompilerParams(vmem_limit_bytes=40 * 2**20),
        cost_estimate=pl.CostEstimate(flops=10**9, bytes_accessed=4 * 2**20, transcendentals=0),
    )(*parts, filter_blocks, taps, skip, jnp.asarray(forward), jnp.asarray(backward))


def out_kernel(block_ref, gated_ref, weight_ref, *refs):
    *out_refs, turned, left = refs
    tp_parts = gated_ref.shape[0]
    part_rows = out_refs[0].shape[0]

    @pl.when(pl.program_id(0) == 0)
    def _():
        for part in range(tp_parts):
            turned[...] = gated_ref[part].T
            for index in range(len(out_refs)):
                begin = pl.multiple_of(block_ref[index] * part_rows, part_rows)
                left[part, index * part_rows : (index + 1) * part_rows] = turned[pl.ds(begin, part_rows)]

    sums = jnp.zeros((left.shape[1], weight_ref.shape[3]), jnp.float32)
    for part in range(tp_parts):
        sums = sums + jnp.dot(left[part], weight_ref[0, part], preferred_element_type=jnp.float32)
    for index, out_ref in enumerate(out_refs):
        out_ref[...] = sums[index * part_rows : (index + 1) * part_rows].astype(out_ref.dtype)


def project_out(gated, weight, blocks):
    tp_parts, depth, rows = gated.shape
    inner_parts, _, _, width = weight.shape
    columns = inner_parts * width
    part_rows = rows // len(blocks)
    return pl.pallas_call(
        out_kernel,
        grid_spec=pltpu.PrefetchScalarGridSpec(
            num_scalar_prefetch=1,
            grid=(inner_parts,),
            in_specs=[
                pl.BlockSpec((tp_parts, depth, rows), lambda b, place: (0, 0, 0)),
                pl.BlockSpec((1, tp_parts, depth, width), lambda b, place: (b, 0, 0, 0)),
            ],
            out_specs=[pl.BlockSpec((part_rows, width), lambda b, place: (0, b))] * len(blocks),
            scratch_shapes=[
                pltpu.VMEM((rows, depth), jnp.bfloat16),
                pltpu.VMEM((tp_parts, rows, depth), jnp.bfloat16),
            ],
        ),
        out_shape=[jax.ShapeDtypeStruct((part_rows, columns), jnp.bfloat16)] * len(blocks),
        compiler_params=pltpu.CompilerParams(vmem_limit_bytes=16 * 2**20),
        cost_estimate=pl.CostEstimate(
            flops=2 * gated.size * columns,
            bytes_accessed=2 * (weight.size + gated.size + rows * columns),
            transcendentals=0,
        ),
    )(jnp.stack(blocks).astype(jnp.int32), gated, weight)


def per_device(features, in_proj, short_taps, long_filter, skip_gain, out_proj):
    rows = features.shape[0]
    seq_parts = lax.axis_size("seq")
    tp_parts = lax.axis_size("tp")
    outer = outer_factor(seq_parts, tp_parts)
    inner_parts = seq_parts // outer
    streams, _, chan_tp = in_proj.shape
    chans = chan_tp // seq_parts
    position = lax.axis_index("seq")
    inner_groups = [[a * inner_parts + b for b in range(inner_parts)] for a in range(outer)]
    tp_groups = [
        [index * tp_parts + tp for index in group for tp in range(tp_parts)] for group in inner_groups
    ]

    weight = lax.all_gather(in_proj, "seq", axis=1, tiled=True, axis_index_groups=inner_groups)

    taps = lax.dynamic_slice_in_dim(short_taps, position * chans, chans, axis=2)
    taps = jnp.broadcast_to(taps[..., None], taps.shape + (rows,))
    skip = lax.dynamic_slice_in_dim(skip_gain, position * chans, chans, axis=0)
    skip = jnp.broadcast_to(skip[:, None], (chans, rows))
    filter_blocks = long_filter.T.reshape(seq_parts, chans, rows)

    held = share_columns(features, outer, tp_parts)
    held, taps, skip, filter_blocks = lax.optimization_barrier((held, taps, skip, filter_blocks))
    arrived = cross_outer(held, outer, inner_parts, tp_parts)
    arrived[-1], filter_blocks = lax.optimization_barrier((arrived[-1], filter_blocks))
    filter_blocks = lax.all_to_all(filter_blocks, "seq", split_axis=0, concat_axis=0, tiled=True)
    chunks = [share_over_tp(piece, tp_parts) for piece in arrived]
    chunks, out_proj = lax.optimization_barrier((chunks, out_proj))
    out_weight = lax.all_gather(out_proj, ("seq", "tp"), axis_index_groups=tp_groups)
    out_weight = out_weight.reshape((inner_parts, tp_parts) + out_proj.shape)

    partial = project_in(chunks, weight, seq_parts)
    parts = lax.all_to_all(partial, "seq", split_axis=0, concat_axis=0, tiled=True)

    parts, out_weight = lax.optimization_barrier((parts, out_weight))

    gated = convolve([parts], filter_blocks, taps, skip, outer, tp_parts)
    gated = lax.all_to_all(
        gated.reshape((-1,) + gated.shape[3:]), ("tp", "seq"), split_axis=0, concat_axis=0, tiled=True
    )
    blocks, places = return_places(outer, inner_parts, tp_parts)
    pieces = project_out(gated.reshape(tp_parts, chan_tp, -1), out_weight, blocks)
    return return_output(pieces, places, inner_parts, tp_parts)


def solution(mesh):
    return jax.shard_map(
        per_device,
        mesh=mesh,
        in_specs=(
            P("seq", "tp"),
            P(None, "seq", "tp"),
            P(None, None, "tp"),
            P("seq", "tp"),
            P("tp"),
            P("tp", "seq"),
        ),
        out_specs=P("seq", "tp"),
        check_vma=False,
    )
```

```python
import functools
import math

import jax
import jax.numpy as jnp
import numpy as np
from jax import lax
from jax.experimental import pallas as pl
from jax.experimental.pallas import tpu as pltpu
from jax.sharding import PartitionSpec as P

HIGHEST = lax.Precision.HIGHEST
UNROLL = 16
HEAVY = 30


def outer_factor(seq_parts, tp_parts):
    outer = tp_parts
    while 4 * outer * outer <= seq_parts and seq_parts % (2 * outer) == 0:
        outer *= 2
    return outer


def assemble_kernel(place_ref, *refs):
    *piece_refs, out_ref = refs
    for index, piece_ref in enumerate(piece_refs):

        @pl.when(pl.program_id(0) == index)
        def _():
            out_ref[...] = piece_ref[...]


def assemble(pieces, places, shape):
    return pl.pallas_call(
        assemble_kernel,
        grid_spec=pltpu.PrefetchScalarGridSpec(
            num_scalar_prefetch=1,
            grid=(len(pieces),),
            in_specs=[pl.BlockSpec(memory_space=pltpu.VMEM)] * len(pieces),
            out_specs=pl.BlockSpec(
                pieces[0].shape, lambda i, place: (place[2 * i], place[2 * i + 1])
            ),
        ),
        out_shape=jax.ShapeDtypeStruct(shape, pieces[0].dtype),
        compiler_params=pltpu.CompilerParams(vmem_limit_bytes=4 * 2**20),
        cost_estimate=pl.CostEstimate(
            flops=0, bytes_accessed=4 * shape[0] * shape[1], transcendentals=0
        ),
    )(jnp.stack(places).astype(jnp.int32), *pieces)


def return_places(outer, inner_parts, tp_parts):
    per_tp = outer // tp_parts
    tp_place = lax.axis_index("tp")
    outer_place = lax.axis_index("seq") // inner_parts
    blocks, places = [], []
    for far in range(tp_parts):
        for near in range(per_tp):
            low = outer_place % per_tp
            blocks.append((tp_place + low + far) % tp_parts * per_tp + (low + near) % per_tp)
            low = (low - near + per_tp) % per_tp
            places.append((outer_place // per_tp - far - low + tp_parts + per_tp * tp_parts) % tp_parts)
            places.append(low)
    return blocks, places


def return_output(pieces, places, inner_parts, tp_parts):
    outer = len(pieces)
    part_rows, width = pieces[0].shape
    per_tp = outer // tp_parts
    arrived = []
    for index, piece in enumerate(pieces):
        far, near = divmod(index, per_tp)

        def target(seq, tp):
            src = seq // inner_parts
            low = src % per_tp
            dst = (tp + low + far) % tp_parts * per_tp + (low + near) % per_tp
            return (dst * inner_parts + seq % inner_parts) * tp_parts + src // per_tp

        pairs = [
            (seq * tp_parts + tp, target(seq, tp))
            for seq in range(outer * inner_parts)
            for tp in range(tp_parts)
        ]
        arrived.append(lax.ppermute(piece, ("seq", "tp"), pairs))
    return assemble(arrived, places, (tp_parts * part_rows, per_tp * width))


def share_columns(features, outer, tp_parts):
    rows, cols = features.shape
    per_tp = outer // tp_parts
    tp_place = lax.axis_index("tp")
    width = cols // outer
    held = []
    for step in range(tp_parts):
        which = (tp_place + step) % tp_parts
        piece = jnp.stack(
            [
                lax.dynamic_slice_in_dim(features, (group * tp_parts + which) * width, width, axis=1)
                for group in range(per_tp)
            ]
        )
        if step:
            piece = lax.ppermute(piece, "tp", [(i, (i + step) % tp_parts) for i in range(tp_parts)])
        held.append(piece)
    return jnp.concatenate(held)


def cross_outer(held, outer, inner_parts, tp_parts):
    per_tp = outer // tp_parts
    seq_parts = outer * inner_parts
    tp_place = lax.axis_index("tp")
    outer_place = lax.axis_index("seq") // inner_parts
    arrived = []
    for step in range(outer):
        target = (outer_place + step) % outer
        which = (tp_place - target // per_tp + tp_parts) % tp_parts * per_tp + target % per_tp
        piece = lax.dynamic_index_in_dim(held, which, axis=0, keepdims=False)
        if step:
            far = step * inner_parts
            piece = lax.ppermute(piece, "seq", [(i, (i + far) % seq_parts) for i in range(seq_parts)])
        arrived.append(piece)
    return arrived


def share_over_tp(part, tp_parts):
    pieces = [part]
    for step in range(1, tp_parts):
        pairs = [(i, (i + step) % tp_parts) for i in range(tp_parts)]
        pieces.append(lax.ppermute(part, "tp", pairs))
    return pieces


def fetch_kernel(source_ref, out_ref, sems):
    copies = [
        pltpu.make_async_copy(source_ref.at[index], out_ref.at[index], sems.at[index])
        for index in range(source_ref.shape[0])
    ]
    for copy in copies:
        copy.start()
    for copy in copies:
        copy.wait()


def fetch(source):
    return pl.pallas_call(
        fetch_kernel,
        out_shape=jax.ShapeDtypeStruct(source.shape, source.dtype),
        in_specs=[pl.BlockSpec(memory_space=pl.ANY)],
        out_specs=pl.BlockSpec(memory_space=pltpu.VMEM),
        scratch_shapes=[pltpu.SemaphoreType.DMA((source.shape[0],))],
        compiler_params=pltpu.CompilerParams(vmem_limit_bytes=60 * 2**20 - 2 * source.size),
        cost_estimate=pl.CostEstimate(
            flops=0, bytes_accessed=4 * source.size, transcendentals=0
        ),
    )(source)


def project_kernel(tp_parts, place_ref, *refs):
    *share_refs, weight_ref, out_ref = refs
    seq_parts, streams, chans, count = out_ref.shape
    left = [
        jnp.concatenate([share_ref[...] for share_ref in share_refs[step::tp_parts]])
        for step in range(tp_parts)
    ]
    for stream in range(streams):
        sums = jnp.zeros((count, seq_parts * chans), jnp.float32)
        for step in range(tp_parts):
            which = lax.rem(place_ref[0] - step + tp_parts, tp_parts)
            sums = sums + jnp.dot(
                left[step],
                weight_ref[stream * tp_parts + which],
                preferred_element_type=jnp.float32,
            )
        turned = sums.astype(out_ref.dtype).T
        for seq in range(seq_parts):
            out_ref[seq, stream] = turned[seq * chans : (seq + 1) * chans]


def project_in(chunks, weight, seq_parts):
    tp_parts = len(chunks[0])
    rows, width = chunks[0][0].shape
    streams = weight.shape[0] // tp_parts
    chans = weight.shape[2] // seq_parts
    pieces = [piece for chunk in chunks for piece in chunk]
    count = len(chunks) * rows
    place = lax.axis_index("tp").astype(jnp.int32)[None]
    vmem = pl.BlockSpec(memory_space=pltpu.VMEM)
    return pl.pallas_call(
        functools.partial(project_kernel, tp_parts),
        in_specs=[pl.BlockSpec(memory_space=pltpu.SMEM)] + [vmem] * (len(pieces) + 1),
        out_specs=vmem,
        out_shape=jax.ShapeDtypeStruct((seq_parts, streams, chans, count), jnp.bfloat16),
        compiler_params=pltpu.CompilerParams(vmem_limit_bytes=32 * 2**20),
        cost_estimate=pl.CostEstimate(
            flops=HEAVY * 2 * count * weight.size,
            bytes_accessed=2 * (weight.size + len(pieces) * pieces[0].size)
            + 2 * streams * count * seq_parts * chans,
            transcendentals=0,
        ),
    )(place, *pieces, weight)


def tables(block):
    place = np.arange(block)
    angle = 2.0 * math.pi * np.outer(place, place + 0.5) / (2 * block)
    forward = np.concatenate([np.cos(angle), -np.sin(angle)], 1)
    place = np.arange(2 * block)
    angle = 2.0 * math.pi * np.outer(np.arange(block) + 0.5, place) / (2 * block)
    backward = np.concatenate([np.cos(angle), -np.sin(angle)], 0) / block
    return forward.astype(np.float32), backward.astype(np.float32)


def each(count, body):
    if isinstance(count, int) and count <= UNROLL:
        for index in range(count):
            body(index)
    else:
        lax.fori_loop(0, count, lambda index, carry: (body(index), carry)[1], 0)


def total(count, term, zero):
    if isinstance(count, int) and count <= UNROLL:
        result = zero
        for index in range(count):
            result = jax.tree.map(jnp.add, result, term(index))
        return result
    return lax.fori_loop(
        0, count, lambda index, sums: jax.tree.map(jnp.add, sums, term(index)), zero
    )


def conv_kernel(
    outer, chunks, *refs
):
    part_refs, refs = refs[:chunks], refs[chunks:]
    filter_ref, taps_ref, skip_ref, fwd_ref, bwd_ref, out_ref, *refs = refs
    proj, query, inner, spec, filter_spec, product, back = refs
    blocks, streams, chans, _ = part_refs[0].shape
    rows = filter_ref.shape[2]
    inner_parts = blocks // outer
    taps_count = taps_ref.shape[1]
    lane = lax.broadcasted_iota(jnp.int32, (chans, rows), 1)

    depth = outer // chunks

    def add_up(inner_index, stream, group):
        value = jnp.zeros((chans, rows), jnp.float32)
        for part in range(outer):
            slot = (part - group) % outer
            column = slice(slot % depth * rows, (slot % depth + 1) * rows)
            source = part_refs[slot // depth]
            value = value + source[part * inner_parts + inner_index, stream, :, column].astype(jnp.float32)
        proj[1 + group * inner_parts + inner_index, stream] = value

    for group in range(outer):
        for stream in range(streams):
            each(inner_parts, functools.partial(add_up, stream=stream, group=group))

    for stream in range(streams):
        proj[0, stream] = jnp.zeros((chans, rows), jnp.float32)

    def first(index):
        filtered = []
        for stream in range(streams):
            now, past = proj[index + 1, stream], proj[index, stream]
            value = taps_ref[stream, 0] * now
            for offset in range(1, taps_count):
                moved = jnp.where(
                    lane < offset, pltpu.roll(past, offset, 1), pltpu.roll(now, offset, 1)
                )
                value = value + taps_ref[stream, offset] * moved
            filtered.append(value)
        query[index] = filtered[0]
        inner[index] = filtered[1] * filtered[2]

    each(blocks, first)

    def apply(source, table_ref, target):
        if chans % 8 == 0:
            flat = source[...].reshape(blocks * chans, source.shape[2])
            done = jnp.dot(flat, table_ref[...], precision=HIGHEST, preferred_element_type=jnp.float32)
            target[...] = done.reshape(target.shape)
        else:

            def one(index):
                target[index] = jnp.dot(
                    source[index], table_ref[...], precision=HIGHEST, preferred_element_type=jnp.float32
                )

            each(blocks, one)

    apply(filter_ref, fwd_ref, filter_spec)
    apply(inner, fwd_ref, spec)

    def multiply(index):
        def term(step):
            left, right = spec[step], filter_spec[index - step]
            left_real, left_imag = left[:, :rows], left[:, rows:]
            right_real, right_imag = right[:, :rows], right[:, rows:]
            return (
                left_real * right_real - left_imag * right_imag,
                left_real * right_imag + left_imag * right_real,
            )

        zero = jnp.zeros((chans, rows), jnp.float32)
        real, imag = total(index + 1, term, (zero, zero))
        product[index, :, :rows] = real
        product[index, :, rows:] = imag

    each(blocks, multiply)
    apply(product, bwd_ref, back)

    def last(index, carried):
        long_mix = back[index, :, :rows] + carried
        query[index] = query[index] * (long_mix + skip_ref[...] * inner[index])

    last(0, jnp.zeros((chans, rows), jnp.float32))
    each(blocks - 1, lambda index: last(index + 1, back[index, :, rows:]))

    tp_parts = out_ref.shape[0]
    part_rows = rows // tp_parts
    copies = out_ref.shape[1]

    def spread(inner_index):
        for part in range(tp_parts):
            for group in range(outer // tp_parts):
                packed = jnp.zeros((chans, rows), jnp.float32)
                for place in range(tp_parts):
                    block = query[(group * tp_parts + place) * inner_parts + inner_index]
                    shift = (place - part) * part_rows % rows
                    block = pltpu.roll(block, shift, 1) if shift else block
                    packed = jnp.where(lane // part_rows == place, block, packed)
                packed = packed.astype(out_ref.dtype)
                for copy in range(copies):
                    out_ref[part, copy, inner_index, :, group * rows : (group + 1) * rows] = packed

    each(inner_parts, spread)


def convolve(parts, filter_blocks, taps, skip, outer, tp_parts):
    blocks, streams, chans, _ = parts[0].shape
    rows = filter_blocks.shape[2]
    forward, backward = tables(rows)
    wide = (blocks, chans, 2 * rows)
    narrow = (blocks, chans, rows)
    vmem = pl.BlockSpec(memory_space=pltpu.VMEM)
    return pl.pallas_call(
        functools.partial(conv_kernel, outer, len(parts)),
        out_shape=jax.ShapeDtypeStruct(
            (tp_parts, outer, blocks // outer, chans, outer // tp_parts * rows), jnp.bfloat16
        ),
        in_specs=[vmem] * (5 + len(parts)),
        out_specs=vmem,
        scratch_shapes=[
            pltpu.VMEM((blocks + 1, streams, chans, rows), jnp.float32),
            pltpu.VMEM(narrow, jnp.float32),
            pltpu.VMEM(narrow, jnp.float32),
            pltpu.VMEM(wide, jnp.float32),
            pltpu.VMEM(wide, jnp.float32),
            pltpu.VMEM(wide, jnp.float32),
            pltpu.VMEM(wide, jnp.float32),
        ],
        compiler_params=pltpu.CompilerParams(vmem_limit_bytes=40 * 2**20),
        cost_estimate=pl.CostEstimate(flops=10**9, bytes_accessed=4 * 2**20, transcendentals=0),
    )(*parts, filter_blocks, taps, skip, jnp.asarray(forward), jnp.asarray(backward))


def out_kernel(block_ref, gated_ref, weight_ref, *refs):
    *out_refs, turned, left = refs
    tp_parts = gated_ref.shape[0]
    part_rows = out_refs[0].shape[0]

    @pl.when(pl.program_id(0) == 0)
    def _():
        for part in range(tp_parts):
            turned[...] = gated_ref[part].T
            for index in range(len(out_refs)):
                begin = pl.multiple_of(block_ref[index] * part_rows, part_rows)
                left[part, index * part_rows : (index + 1) * part_rows] = turned[pl.ds(begin, part_rows)]

    sums = jnp.zeros((left.shape[1], weight_ref.shape[3]), jnp.float32)
    for part in range(tp_parts):
        sums = sums + jnp.dot(left[part], weight_ref[0, part], preferred_element_type=jnp.float32)
    for index, out_ref in enumerate(out_refs):
        out_ref[...] = sums[index * part_rows : (index + 1) * part_rows].astype(out_ref.dtype)


def project_out(gated, weight, blocks):
    tp_parts, depth, rows = gated.shape
    inner_parts, _, _, width = weight.shape
    columns = inner_parts * width
    part_rows = rows // len(blocks)
    return pl.pallas_call(
        out_kernel,
        grid_spec=pltpu.PrefetchScalarGridSpec(
            num_scalar_prefetch=1,
            grid=(inner_parts,),
            in_specs=[
                pl.BlockSpec((tp_parts, depth, rows), lambda b, place: (0, 0, 0)),
                pl.BlockSpec((1, tp_parts, depth, width), lambda b, place: (b, 0, 0, 0)),
            ],
            out_specs=[pl.BlockSpec((part_rows, width), lambda b, place: (0, b))] * len(blocks),
            scratch_shapes=[
                pltpu.VMEM((rows, depth), jnp.bfloat16),
                pltpu.VMEM((tp_parts, rows, depth), jnp.bfloat16),
            ],
        ),
        out_shape=[jax.ShapeDtypeStruct((part_rows, columns), jnp.bfloat16)] * len(blocks),
        compiler_params=pltpu.CompilerParams(vmem_limit_bytes=16 * 2**20),
        cost_estimate=pl.CostEstimate(
            flops=2 * gated.size * columns,
            bytes_accessed=2 * (weight.size + gated.size + rows * columns),
            transcendentals=0,
        ),
    )(jnp.stack(blocks).astype(jnp.int32), gated, weight)


def per_device(features, in_proj, short_taps, long_filter, skip_gain, out_proj):
    rows = features.shape[0]
    seq_parts = lax.axis_size("seq")
    tp_parts = lax.axis_size("tp")
    outer = outer_factor(seq_parts, tp_parts)
    inner_parts = seq_parts // outer
    streams, _, chan_tp = in_proj.shape
    chans = chan_tp // seq_parts
    position = lax.axis_index("seq")
    inner_groups = [[a * inner_parts + b for b in range(inner_parts)] for a in range(outer)]
    tp_groups = [
        [index * tp_parts + tp for index in group for tp in range(tp_parts)] for group in inner_groups
    ]

    weight = lax.all_gather(in_proj, "seq", axis=1, tiled=True, axis_index_groups=inner_groups)

    taps = lax.dynamic_slice_in_dim(short_taps, position * chans, chans, axis=2)
    taps = jnp.broadcast_to(taps[..., None], taps.shape + (rows,))
    skip = lax.dynamic_slice_in_dim(skip_gain, position * chans, chans, axis=0)
    skip = jnp.broadcast_to(skip[:, None], (chans, rows))
    filter_blocks = long_filter.T.reshape(seq_parts, chans, rows)

    held = share_columns(features, outer, tp_parts)
    held, taps, skip = lax.optimization_barrier((held, taps, skip))
    arrived = cross_outer(held, outer, inner_parts, tp_parts)
    filter_blocks = lax.all_to_all(filter_blocks, "seq", split_axis=0, concat_axis=0, tiled=True)
    arrived[1], filter_blocks = lax.optimization_barrier((arrived[1], filter_blocks))
    chunks = [share_over_tp(piece, tp_parts) for piece in arrived]
    chunks, out_proj = lax.optimization_barrier((chunks, out_proj))
    out_weight = lax.all_gather(out_proj, ("seq", "tp"), axis_index_groups=tp_groups)
    out_weight = out_weight.reshape((inner_parts, tp_parts) + out_proj.shape)

    weight = fetch(weight.reshape(streams * tp_parts, -1, chan_tp))
    partial = project_in(chunks, weight, seq_parts)
    parts = lax.all_to_all(partial, "seq", split_axis=0, concat_axis=0, tiled=True)

    parts, out_weight = lax.optimization_barrier((parts, out_weight))
    out_weight = fetch(out_weight)

    gated = convolve([parts], filter_blocks, taps, skip, outer, tp_parts)
    gated = lax.all_to_all(
        gated.reshape((-1,) + gated.shape[3:]), ("tp", "seq"), split_axis=0, concat_axis=0, tiled=True
    )
    blocks, places = return_places(outer, inner_parts, tp_parts)
    pieces = project_out(gated.reshape(tp_parts, chan_tp, -1), out_weight, blocks)
    return return_output(pieces, places, inner_parts, tp_parts)


def solution(mesh):
    return jax.shard_map(
        per_device,
        mesh=mesh,
        in_specs=(
            P("seq", "tp"),
            P(None, "seq", "tp"),
            P(None, None, "tp"),
            P("seq", "tp"),
            P("tp"),
            P("tp", "seq"),
        ),
        out_specs=P("seq", "tp"),
        check_vma=False,
    )
```

```python
import functools
import math

import jax
import jax.numpy as jnp
import numpy as np
from jax import lax
from jax.experimental import pallas as pl
from jax.experimental.pallas import tpu as pltpu
from jax.sharding import PartitionSpec as P

HIGHEST = lax.Precision.HIGHEST
UNROLL = 16
HEAVY = 30
HALVES = 2


def outer_factor(seq_parts, tp_parts):
    outer = tp_parts
    while 4 * outer * outer <= seq_parts and seq_parts % (2 * outer) == 0:
        outer *= 2
    return outer


def assemble_kernel(place_ref, *refs):
    *piece_refs, out_ref = refs
    for index, piece_ref in enumerate(piece_refs):

        @pl.when(pl.program_id(0) == index)
        def _():
            out_ref[...] = piece_ref[...]


def assemble(pieces, places, shape):
    return pl.pallas_call(
        assemble_kernel,
        grid_spec=pltpu.PrefetchScalarGridSpec(
            num_scalar_prefetch=1,
            grid=(len(pieces),),
            in_specs=[pl.BlockSpec(memory_space=pltpu.VMEM)] * len(pieces),
            out_specs=pl.BlockSpec(
                pieces[0].shape, lambda i, place: (place[2 * i], place[2 * i + 1])
            ),
        ),
        out_shape=jax.ShapeDtypeStruct(shape, pieces[0].dtype),
        compiler_params=pltpu.CompilerParams(vmem_limit_bytes=4 * 2**20),
        cost_estimate=pl.CostEstimate(
            flops=0, bytes_accessed=4 * shape[0] * shape[1], transcendentals=0
        ),
    )(jnp.stack(places).astype(jnp.int32), *pieces)


def return_places(outer, inner_parts, tp_parts):
    per_tp = outer // tp_parts
    tp_place = lax.axis_index("tp")
    outer_place = lax.axis_index("seq") // inner_parts
    blocks, places = [], []
    for far in range(tp_parts):
        for near in range(per_tp):
            low = outer_place % per_tp
            blocks.append((tp_place + low + far) % tp_parts * per_tp + (low + near) % per_tp)
            low = (low - near + per_tp) % per_tp
            places.append((outer_place // per_tp - far - low + tp_parts + per_tp * tp_parts) % tp_parts)
            places.append(low)
    return blocks, places


def return_output(pieces, places, inner_parts, tp_parts):
    outer = len(pieces)
    part_rows, width = pieces[0].shape
    per_tp = outer // tp_parts
    arrived = []
    for index, piece in enumerate(pieces):
        far, near = divmod(index, per_tp)

        def target(seq, tp):
            src = seq // inner_parts
            low = src % per_tp
            dst = (tp + low + far) % tp_parts * per_tp + (low + near) % per_tp
            return (dst * inner_parts + seq % inner_parts) * tp_parts + src // per_tp

        pairs = [
            (seq * tp_parts + tp, target(seq, tp))
            for seq in range(outer * inner_parts)
            for tp in range(tp_parts)
        ]
        arrived.append(lax.ppermute(piece, ("seq", "tp"), pairs))
    return assemble(arrived, places, (tp_parts * part_rows, per_tp * width))


def share_columns(features, outer, tp_parts):
    rows, cols = features.shape
    per_tp = outer // tp_parts
    tp_place = lax.axis_index("tp")
    width = cols // outer
    held = []
    for step in range(tp_parts):
        which = (tp_place + step) % tp_parts
        piece = jnp.stack(
            [
                lax.dynamic_slice_in_dim(features, (group * tp_parts + which) * width, width, axis=1)
                for group in range(per_tp)
            ]
        )
        if step:
            piece = lax.ppermute(piece, "tp", [(i, (i + step) % tp_parts) for i in range(tp_parts)])
        held.append(piece)
    return jnp.concatenate(held)


def cross_outer(held, outer, inner_parts, tp_parts):
    per_tp = outer // tp_parts
    seq_parts = outer * inner_parts
    tp_place = lax.axis_index("tp")
    outer_place = lax.axis_index("seq") // inner_parts
    arrived = []
    for step in range(outer):
        target = (outer_place + step) % outer
        which = (tp_place - target // per_tp + tp_parts) % tp_parts * per_tp + target % per_tp
        piece = lax.dynamic_index_in_dim(held, which, axis=0, keepdims=False)
        if step:
            far = step * inner_parts
            piece = lax.ppermute(piece, "seq", [(i, (i + far) % seq_parts) for i in range(seq_parts)])
        arrived.append(piece)
    return arrived


def share_over_tp(part, tp_parts):
    pieces = [part]
    for step in range(1, tp_parts):
        pairs = [(i, (i + step) % tp_parts) for i in range(tp_parts)]
        pieces.append(lax.ppermute(part, "tp", pairs))
    return pieces


def fetch_kernel(source_ref, out_ref, sems):
    copies = [
        pltpu.make_async_copy(source_ref.at[index], out_ref.at[index], sems.at[index])
        for index in range(source_ref.shape[0])
    ]
    for copy in copies:
        copy.start()
    for copy in copies:
        copy.wait()


def fetch(source):
    return pl.pallas_call(
        fetch_kernel,
        out_shape=jax.ShapeDtypeStruct(source.shape, source.dtype),
        in_specs=[pl.BlockSpec(memory_space=pl.ANY)],
        out_specs=pl.BlockSpec(memory_space=pltpu.VMEM),
        scratch_shapes=[pltpu.SemaphoreType.DMA((source.shape[0],))],
        compiler_params=pltpu.CompilerParams(vmem_limit_bytes=16 * 2**20),
        cost_estimate=pl.CostEstimate(
            flops=0, bytes_accessed=4 * source.size, transcendentals=0
        ),
    )(source)


def project_kernel(tp_parts, place_ref, *refs):
    *share_refs, weight_ref, out_ref, held, sems = refs
    seq_parts, streams, chans, count = out_ref.shape
    copies = [
        pltpu.make_async_copy(weight_ref.at[stream], held.at[stream], sems.at[stream])
        for stream in range(streams)
    ]
    for copy in copies:
        copy.start()
    left = [
        jnp.concatenate([share_ref[...] for share_ref in share_refs[step::tp_parts]])
        for step in range(tp_parts)
    ]
    for stream in range(streams):
        copies[stream].wait()
        sums = jnp.zeros((count, seq_parts * chans), jnp.float32)
        for step in range(tp_parts):
            which = lax.rem(place_ref[0] - step + tp_parts, tp_parts)
            sums = sums + jnp.dot(
                left[step], held[stream, which], preferred_element_type=jnp.float32
            )
        turned = sums.astype(out_ref.dtype).T
        for seq in range(seq_parts):
            out_ref[seq, stream] = turned[seq * chans : (seq + 1) * chans]


def project_in(chunks, weight, seq_parts):
    tp_parts = len(chunks[0])
    rows, width = chunks[0][0].shape
    streams, _, chan_tp = weight.shape
    weight = weight.reshape(streams, tp_parts, width, chan_tp)
    chans = chan_tp // seq_parts
    pieces = [piece for chunk in chunks for piece in chunk]
    count = len(chunks) * rows
    place = lax.axis_index("tp").astype(jnp.int32)[None]
    vmem = pl.BlockSpec(memory_space=pltpu.VMEM)
    return pl.pallas_call(
        functools.partial(project_kernel, tp_parts),
        in_specs=[pl.BlockSpec(memory_space=pltpu.SMEM)]
        + [vmem] * len(pieces)
        + [pl.BlockSpec(memory_space=pl.ANY)],
        out_specs=vmem,
        out_shape=jax.ShapeDtypeStruct((seq_parts, streams, chans, count), jnp.bfloat16),
        scratch_shapes=[
            pltpu.VMEM(weight.shape, weight.dtype),
            pltpu.SemaphoreType.DMA((streams,)),
        ],
        compiler_params=pltpu.CompilerParams(vmem_limit_bytes=56 * 2**20),
        cost_estimate=pl.CostEstimate(
            flops=HEAVY * 2 * count * weight.size,
            bytes_accessed=2 * (weight.size + len(pieces) * pieces[0].size)
            + 2 * streams * count * seq_parts * chans,
            transcendentals=0,
        ),
    )(place, *pieces, weight)


def tables(block):
    place = np.arange(block)
    angle = 2.0 * math.pi * np.outer(place, place + 0.5) / (2 * block)
    forward = np.concatenate([np.cos(angle), -np.sin(angle)], 1)
    place = np.arange(2 * block)
    angle = 2.0 * math.pi * np.outer(np.arange(block) + 0.5, place) / (2 * block)
    backward = np.concatenate([np.cos(angle), -np.sin(angle)], 0) / block
    return forward.astype(np.float32), backward.astype(np.float32)


def each(count, body):
    if isinstance(count, int) and count <= UNROLL:
        for index in range(count):
            body(index)
    else:
        lax.fori_loop(0, count, lambda index, carry: (body(index), carry)[1], 0)


def total(count, term, zero):
    if isinstance(count, int) and count <= UNROLL:
        result = zero
        for index in range(count):
            result = jax.tree.map(jnp.add, result, term(index))
        return result
    return lax.fori_loop(
        0, count, lambda index, sums: jax.tree.map(jnp.add, sums, term(index)), zero
    )


def conv_kernel(
    outer, chunks, *refs
):
    part_refs, refs = refs[:chunks], refs[chunks:]
    filter_ref, taps_ref, skip_ref, fwd_ref, bwd_ref, out_ref, *refs = refs
    proj, query, inner, spec, filter_spec, product, back = refs
    blocks, streams, chans, _ = part_refs[0].shape
    rows = filter_ref.shape[2]
    inner_parts = blocks // outer
    taps_count = taps_ref.shape[1]
    lane = lax.broadcasted_iota(jnp.int32, (chans, rows), 1)

    depth = outer // chunks

    def add_up(inner_index, stream, group):
        value = jnp.zeros((chans, rows), jnp.float32)
        for part in range(outer):
            slot = (part - group) % outer
            column = slice(slot % depth * rows, (slot % depth + 1) * rows)
            source = part_refs[slot // depth]
            value = value + source[part * inner_parts + inner_index, stream, :, column].astype(jnp.float32)
        proj[1 + group * inner_parts + inner_index, stream] = value

    for group in range(outer):
        for stream in range(streams):
            each(inner_parts, functools.partial(add_up, stream=stream, group=group))

    for stream in range(streams):
        proj[0, stream] = jnp.zeros((chans, rows), jnp.float32)

    def first(index):
        filtered = []
        for stream in range(streams):
            now, past = proj[index + 1, stream], proj[index, stream]
            value = taps_ref[stream, 0] * now
            for offset in range(1, taps_count):
                moved = jnp.where(
                    lane < offset, pltpu.roll(past, offset, 1), pltpu.roll(now, offset, 1)
                )
                value = value + taps_ref[stream, offset] * moved
            filtered.append(value)
        query[index] = filtered[0]
        inner[index] = filtered[1] * filtered[2]

    each(blocks, first)

    def apply(source, table_ref, target):
        if chans % 8 == 0:
            flat = source[...].reshape(blocks * chans, source.shape[2])
            done = jnp.dot(flat, table_ref[...], precision=HIGHEST, preferred_element_type=jnp.float32)
            target[...] = done.reshape(target.shape)
        else:

            def one(index):
                target[index] = jnp.dot(
                    source[index], table_ref[...], precision=HIGHEST, preferred_element_type=jnp.float32
                )

            each(blocks, one)

    apply(filter_ref, fwd_ref, filter_spec)
    apply(inner, fwd_ref, spec)

    def multiply(index):
        def term(step):
            left, right = spec[step], filter_spec[index - step]
            left_real, left_imag = left[:, :rows], left[:, rows:]
            right_real, right_imag = right[:, :rows], right[:, rows:]
            return (
                left_real * right_real - left_imag * right_imag,
                left_real * right_imag + left_imag * right_real,
            )

        zero = jnp.zeros((chans, rows), jnp.float32)
        real, imag = total(index + 1, term, (zero, zero))
        product[index, :, :rows] = real
        product[index, :, rows:] = imag

    each(blocks, multiply)
    apply(product, bwd_ref, back)

    def last(index, carried):
        long_mix = back[index, :, :rows] + carried
        query[index] = query[index] * (long_mix + skip_ref[...] * inner[index])

    last(0, jnp.zeros((chans, rows), jnp.float32))
    each(blocks - 1, lambda index: last(index + 1, back[index, :, rows:]))

    tp_parts = out_ref.shape[0]
    part_rows = rows // tp_parts
    copies = out_ref.shape[1]

    def spread(inner_index):
        for part in range(tp_parts):
            for group in range(outer // tp_parts):
                packed = jnp.zeros((chans, rows), jnp.float32)
                for place in range(tp_parts):
                    block = query[(group * tp_parts + place) * inner_parts + inner_index]
                    shift = (place - part) * part_rows % rows
                    block = pltpu.roll(block, shift, 1) if shift else block
                    packed = jnp.where(lane // part_rows == place, block, packed)
                packed = packed.astype(out_ref.dtype)
                for copy in range(copies):
                    out_ref[part, copy, inner_index, :, group * rows : (group + 1) * rows] = packed

    each(inner_parts, spread)


def convolve(parts, filter_blocks, taps, skip, outer, tp_parts):
    blocks, streams, chans, _ = parts[0].shape
    rows = filter_blocks.shape[2]
    forward, backward = tables(rows)
    wide = (blocks, chans, 2 * rows)
    narrow = (blocks, chans, rows)
    vmem = pl.BlockSpec(memory_space=pltpu.VMEM)
    return pl.pallas_call(
        functools.partial(conv_kernel, outer, len(parts)),
        out_shape=jax.ShapeDtypeStruct(
            (tp_parts, outer, blocks // outer, chans, outer // tp_parts * rows), jnp.bfloat16
        ),
        in_specs=[vmem] * (5 + len(parts)),
        out_specs=vmem,
        scratch_shapes=[
            pltpu.VMEM((blocks + 1, streams, chans, rows), jnp.float32),
            pltpu.VMEM(narrow, jnp.float32),
            pltpu.VMEM(narrow, jnp.float32),
            pltpu.VMEM(wide, jnp.float32),
            pltpu.VMEM(wide, jnp.float32),
            pltpu.VMEM(wide, jnp.float32),
            pltpu.VMEM(wide, jnp.float32),
        ],
        compiler_params=pltpu.CompilerParams(vmem_limit_bytes=40 * 2**20),
        cost_estimate=pl.CostEstimate(flops=10**9, bytes_accessed=4 * 2**20, transcendentals=0),
    )(*parts, filter_blocks, taps, skip, jnp.asarray(forward), jnp.asarray(backward))


def out_kernel(block_ref, gated_ref, weight_ref, *refs):
    *out_refs, turned, left = refs
    tp_parts = gated_ref.shape[0]
    part_rows = out_refs[0].shape[0]

    @pl.when(pl.program_id(0) == 0)
    def _():
        for part in range(tp_parts):
            turned[...] = gated_ref[part].T
            for index in range(len(out_refs)):
                begin = pl.multiple_of(block_ref[index] * part_rows, part_rows)
                left[part, index * part_rows : (index + 1) * part_rows] = turned[pl.ds(begin, part_rows)]

    sums = jnp.zeros((left.shape[1], weight_ref.shape[3]), jnp.float32)
    for part in range(tp_parts):
        sums = sums + jnp.dot(left[part], weight_ref[0, part], preferred_element_type=jnp.float32)
    for index, out_ref in enumerate(out_refs):
        out_ref[...] = sums[index * part_rows : (index + 1) * part_rows].astype(out_ref.dtype)


def project_out(gated, weight, blocks):
    tp_parts, depth, rows = gated.shape
    inner_parts, _, _, width = weight.shape
    columns = inner_parts * width
    part_rows = rows // len(blocks)
    return pl.pallas_call(
        out_kernel,
        grid_spec=pltpu.PrefetchScalarGridSpec(
            num_scalar_prefetch=1,
            grid=(inner_parts,),
            in_specs=[
                pl.BlockSpec((tp_parts, depth, rows), lambda b, place: (0, 0, 0)),
                pl.BlockSpec((1, tp_parts, depth, width), lambda b, place: (b, 0, 0, 0)),
            ],
            out_specs=[pl.BlockSpec((part_rows, width), lambda b, place: (0, b))] * len(blocks),
            scratch_shapes=[
                pltpu.VMEM((rows, depth), jnp.bfloat16),
                pltpu.VMEM((tp_parts, rows, depth), jnp.bfloat16),
            ],
        ),
        out_shape=[jax.ShapeDtypeStruct((part_rows, columns), jnp.bfloat16)] * len(blocks),
        compiler_params=pltpu.CompilerParams(vmem_limit_bytes=16 * 2**20),
        cost_estimate=pl.CostEstimate(
            flops=2 * gated.size * columns,
            bytes_accessed=2 * (weight.size + gated.size + rows * columns),
            transcendentals=0,
        ),
    )(jnp.stack(blocks).astype(jnp.int32), gated, weight)


def per_device(features, in_proj, short_taps, long_filter, skip_gain, out_proj):
    rows = features.shape[0]
    seq_parts = lax.axis_size("seq")
    tp_parts = lax.axis_size("tp")
    outer = outer_factor(seq_parts, tp_parts)
    inner_parts = seq_parts // outer
    streams, _, chan_tp = in_proj.shape
    chans = chan_tp // seq_parts
    position = lax.axis_index("seq")
    inner_groups = [[a * inner_parts + b for b in range(inner_parts)] for a in range(outer)]
    tp_groups = [
        [index * tp_parts + tp for index in group for tp in range(tp_parts)] for group in inner_groups
    ]

    weight = lax.all_gather(in_proj, "seq", axis=1, tiled=True, axis_index_groups=inner_groups)

    taps = lax.dynamic_slice_in_dim(short_taps, position * chans, chans, axis=2)
    taps = jnp.broadcast_to(taps[..., None], taps.shape + (rows,))
    skip = lax.dynamic_slice_in_dim(skip_gain, position * chans, chans, axis=0)
    skip = jnp.broadcast_to(skip[:, None], (chans, rows))
    filter_blocks = long_filter.T.reshape(seq_parts, chans, rows)

    half = rows // HALVES
    held = [
        share_columns(features[index * half : (index + 1) * half], outer, tp_parts)
        for index in range(HALVES)
    ]
    held[-1], taps, skip = lax.optimization_barrier((held[-1], taps, skip))
    arrived = [cross_outer(part, outer, inner_parts, tp_parts) for part in held]
    arrived = [jnp.concatenate(parts) for parts in zip(*arrived)]
    filter_blocks = lax.all_to_all(filter_blocks, "seq", split_axis=0, concat_axis=0, tiled=True)
    arrived[1], filter_blocks = lax.optimization_barrier((arrived[1], filter_blocks))
    chunks = [share_over_tp(piece, tp_parts) for piece in arrived]
    chunks, out_proj = lax.optimization_barrier((chunks, out_proj))
    out_weight = lax.all_gather(out_proj, ("seq", "tp"), axis_index_groups=tp_groups)
    out_weight = out_weight.reshape((inner_parts, tp_parts) + out_proj.shape)

    partial = project_in(chunks, weight, seq_parts)
    parts = lax.all_to_all(partial, "seq", split_axis=0, concat_axis=0, tiled=True)

    parts, out_weight = lax.optimization_barrier((parts, out_weight))
    out_weight = fetch(out_weight)

    gated = convolve([parts], filter_blocks, taps, skip, outer, tp_parts)
    gated = lax.all_to_all(
        gated.reshape((-1,) + gated.shape[3:]), ("tp", "seq"), split_axis=0, concat_axis=0, tiled=True
    )
    blocks, places = return_places(outer, inner_parts, tp_parts)
    pieces = project_out(gated.reshape(tp_parts, chan_tp, -1), out_weight, blocks)
    return return_output(pieces, places, inner_parts, tp_parts)


def solution(mesh):
    return jax.shard_map(
        per_device,
        mesh=mesh,
        in_specs=(
            P("seq", "tp"),
            P(None, "seq", "tp"),
            P(None, None, "tp"),
            P("seq", "tp"),
            P("tp"),
            P("tp", "seq"),
        ),
        out_specs=P("seq", "tp"),
        check_vma=False,
    )
```

```python
import functools
import math

import jax
import jax.numpy as jnp
import numpy as np
from jax import lax
from jax.experimental import pallas as pl
from jax.experimental.pallas import tpu as pltpu
from jax.sharding import PartitionSpec as P

HIGHEST = lax.Precision.HIGHEST
UNROLL = 16
HEAVY = 30


def outer_factor(seq_parts, tp_parts):
    outer = tp_parts
    while 4 * outer * outer <= seq_parts and seq_parts % (2 * outer) == 0:
        outer *= 2
    return outer


def assemble_kernel(place_ref, *refs):
    *piece_refs, out_ref = refs
    for index, piece_ref in enumerate(piece_refs):

        @pl.when(pl.program_id(0) == index)
        def _():
            out_ref[...] = piece_ref[...]


def assemble(pieces, places, shape):
    return pl.pallas_call(
        assemble_kernel,
        grid_spec=pltpu.PrefetchScalarGridSpec(
            num_scalar_prefetch=1,
            grid=(len(pieces),),
            in_specs=[pl.BlockSpec(memory_space=pltpu.VMEM)] * len(pieces),
            out_specs=pl.BlockSpec(
                pieces[0].shape, lambda i, place: (place[2 * i], place[2 * i + 1])
            ),
        ),
        out_shape=jax.ShapeDtypeStruct(shape, pieces[0].dtype),
        compiler_params=pltpu.CompilerParams(vmem_limit_bytes=4 * 2**20),
        cost_estimate=pl.CostEstimate(
            flops=0, bytes_accessed=4 * shape[0] * shape[1], transcendentals=0
        ),
    )(jnp.stack(places).astype(jnp.int32), *pieces)


def return_places(outer, inner_parts, tp_parts):
    per_tp = outer // tp_parts
    tp_place = lax.axis_index("tp")
    outer_place = lax.axis_index("seq") // inner_parts
    blocks, places = [], []
    for far in range(tp_parts):
        for near in range(per_tp):
            low = outer_place % per_tp
            blocks.append((tp_place + low + far) % tp_parts * per_tp + (low + near) % per_tp)
            low = (low - near + per_tp) % per_tp
            places.append((outer_place // per_tp - far - low + tp_parts + per_tp * tp_parts) % tp_parts)
            places.append(low)
    return blocks, places


def return_output(pieces, places, inner_parts, tp_parts):
    outer = len(pieces)
    part_rows, width = pieces[0].shape
    per_tp = outer // tp_parts
    arrived = []
    for index, piece in enumerate(pieces):
        far, near = divmod(index, per_tp)

        def target(seq, tp):
            src = seq // inner_parts
            low = src % per_tp
            dst = (tp + low + far) % tp_parts * per_tp + (low + near) % per_tp
            return (dst * inner_parts + seq % inner_parts) * tp_parts + src // per_tp

        pairs = [
            (seq * tp_parts + tp, target(seq, tp))
            for seq in range(outer * inner_parts)
            for tp in range(tp_parts)
        ]
        arrived.append(lax.ppermute(piece, ("seq", "tp"), pairs))
    return assemble(arrived, places, (tp_parts * part_rows, per_tp * width))


def share_columns(features, outer, tp_parts):
    rows, cols = features.shape
    per_tp = outer // tp_parts
    tp_place = lax.axis_index("tp")
    width = cols // outer
    held = []
    for step in range(tp_parts):
        which = (tp_place + step) % tp_parts
        piece = jnp.stack(
            [
                lax.dynamic_slice_in_dim(features, (group * tp_parts + which) * width, width, axis=1)
                for group in range(per_tp)
            ]
        )
        if step:
            piece = lax.ppermute(piece, "tp", [(i, (i + step) % tp_parts) for i in range(tp_parts)])
        held.append(piece)
    return jnp.concatenate(held)


def cross_outer(held, outer, inner_parts, tp_parts):
    per_tp = outer // tp_parts
    seq_parts = outer * inner_parts
    tp_place = lax.axis_index("tp")
    outer_place = lax.axis_index("seq") // inner_parts
    arrived = {}
    for step in sorted(range(outer), key=lambda step: min(step, outer - step)):
        if step not in (0, 1, outer - 1):
            arrived[1], held = lax.optimization_barrier((arrived[1], held))
        target = (outer_place + step) % outer
        which = (tp_place - target // per_tp + tp_parts) % tp_parts * per_tp + target % per_tp
        piece = lax.dynamic_index_in_dim(held, which, axis=0, keepdims=False)
        if step:
            far = step * inner_parts
            piece = lax.ppermute(piece, "seq", [(i, (i + far) % seq_parts) for i in range(seq_parts)])
        arrived[step] = piece
    return [arrived[step] for step in range(outer)]


def share_over_tp(part, tp_parts):
    pieces = [part]
    for step in range(1, tp_parts):
        pairs = [(i, (i + step) % tp_parts) for i in range(tp_parts)]
        pieces.append(lax.ppermute(part, "tp", pairs))
    return pieces


def project_kernel(tp_parts, place_ref, *refs):
    *share_refs, weight_ref, out_ref, held, sems = refs
    seq_parts, streams, chans, count = out_ref.shape
    copies = [
        pltpu.make_async_copy(weight_ref.at[stream], held.at[stream], sems.at[stream])
        for stream in range(streams)
    ]
    for copy in copies:
        copy.start()
    left = [
        jnp.concatenate([share_ref[...] for share_ref in share_refs[step::tp_parts]])
        for step in range(tp_parts)
    ]
    for stream in range(streams):
        copies[stream].wait()
        sums = jnp.zeros((count, seq_parts * chans), jnp.float32)
        for step in range(tp_parts):
            which = lax.rem(place_ref[0] - step + tp_parts, tp_parts)
            sums = sums + jnp.dot(
                left[step], held[stream, which], preferred_element_type=jnp.float32
            )
        turned = sums.astype(out_ref.dtype).T
        for seq in range(seq_parts):
            out_ref[seq, stream] = turned[seq * chans : (seq + 1) * chans]


def project_in(chunks, weight, seq_parts):
    tp_parts = len(chunks[0])
    rows, width = chunks[0][0].shape
    streams, _, chan_tp = weight.shape
    weight = weight.reshape(streams, tp_parts, width, chan_tp)
    chans = chan_tp // seq_parts
    pieces = [piece for chunk in chunks for piece in chunk]
    count = len(chunks) * rows
    place = lax.axis_index("tp").astype(jnp.int32)[None]
    vmem = pl.BlockSpec(memory_space=pltpu.VMEM)
    return pl.pallas_call(
        functools.partial(project_kernel, tp_parts),
        in_specs=[pl.BlockSpec(memory_space=pltpu.SMEM)]
        + [vmem] * len(pieces)
        + [pl.BlockSpec(memory_space=pltpu.HBM)],
        out_specs=vmem,
        out_shape=jax.ShapeDtypeStruct((seq_parts, streams, chans, count), jnp.bfloat16),
        scratch_shapes=[
            pltpu.VMEM(weight.shape, weight.dtype),
            pltpu.SemaphoreType.DMA((streams,)),
        ],
        compiler_params=pltpu.CompilerParams(vmem_limit_bytes=32 * 2**20),
        cost_estimate=pl.CostEstimate(
            flops=HEAVY * 2 * count * weight.size,
            bytes_accessed=2 * (weight.size + len(pieces) * pieces[0].size)
            + 2 * streams * count * seq_parts * chans,
            transcendentals=0,
        ),
    )(place, *pieces, weight)


def tables(block):
    place = np.arange(block)
    angle = 2.0 * math.pi * np.outer(place, place + 0.5) / (2 * block)
    forward = np.concatenate([np.cos(angle), -np.sin(angle)], 1)
    place = np.arange(2 * block)
    angle = 2.0 * math.pi * np.outer(np.arange(block) + 0.5, place) / (2 * block)
    backward = np.concatenate([np.cos(angle), -np.sin(angle)], 0) / block
    return forward.astype(np.float32), backward.astype(np.float32)


def each(count, body):
    if isinstance(count, int) and count <= UNROLL:
        for index in range(count):
            body(index)
    else:
        lax.fori_loop(0, count, lambda index, carry: (body(index), carry)[1], 0)


def total(count, term, zero):
    if isinstance(count, int) and count <= UNROLL:
        result = zero
        for index in range(count):
            result = jax.tree.map(jnp.add, result, term(index))
        return result
    return lax.fori_loop(
        0, count, lambda index, sums: jax.tree.map(jnp.add, sums, term(index)), zero
    )


def conv_kernel(
    outer, chunks, *refs
):
    part_refs, refs = refs[:chunks], refs[chunks:]
    filter_ref, taps_ref, skip_ref, fwd_ref, bwd_ref, out_ref, *refs = refs
    proj, query, inner, spec, filter_spec, product, back = refs
    blocks, streams, chans, _ = part_refs[0].shape
    rows = filter_ref.shape[2]
    inner_parts = blocks // outer
    taps_count = taps_ref.shape[1]
    lane = lax.broadcasted_iota(jnp.int32, (chans, rows), 1)

    depth = outer // chunks

    def add_up(inner_index, stream, group):
        value = jnp.zeros((chans, rows), jnp.float32)
        for part in range(outer):
            slot = (part - group) % outer
            column = slice(slot % depth * rows, (slot % depth + 1) * rows)
            source = part_refs[slot // depth]
            value = value + source[part * inner_parts + inner_index, stream, :, column].astype(jnp.float32)
        proj[1 + group * inner_parts + inner_index, stream] = value

    for group in range(outer):
        for stream in range(streams):
            each(inner_parts, functools.partial(add_up, stream=stream, group=group))

    for stream in range(streams):
        proj[0, stream] = jnp.zeros((chans, rows), jnp.float32)

    def first(index):
        filtered = []
        for stream in range(streams):
            now, past = proj[index + 1, stream], proj[index, stream]
            value = taps_ref[stream, 0] * now
            for offset in range(1, taps_count):
                moved = jnp.where(
                    lane < offset, pltpu.roll(past, offset, 1), pltpu.roll(now, offset, 1)
                )
                value = value + taps_ref[stream, offset] * moved
            filtered.append(value)
        query[index] = filtered[0]
        inner[index] = filtered[1] * filtered[2]

    each(blocks, first)

    def apply(source, table_ref, target):
        if chans % 8 == 0:
            flat = source[...].reshape(blocks * chans, source.shape[2])
            done = jnp.dot(flat, table_ref[...], precision=HIGHEST, preferred_element_type=jnp.float32)
            target[...] = done.reshape(target.shape)
        else:

            def one(index):
                target[index] = jnp.dot(
                    source[index], table_ref[...], precision=HIGHEST, preferred_element_type=jnp.float32
                )

            each(blocks, one)

    apply(filter_ref, fwd_ref, filter_spec)
    apply(inner, fwd_ref, spec)

    def multiply(index):
        def term(step):
            left, right = spec[step], filter_spec[index - step]
            left_real, left_imag = left[:, :rows], left[:, rows:]
            right_real, right_imag = right[:, :rows], right[:, rows:]
            return (
                left_real * right_real - left_imag * right_imag,
                left_real * right_imag + left_imag * right_real,
            )

        zero = jnp.zeros((chans, rows), jnp.float32)
        real, imag = total(index + 1, term, (zero, zero))
        product[index, :, :rows] = real
        product[index, :, rows:] = imag

    each(blocks, multiply)
    apply(product, bwd_ref, back)

    def last(index, carried):
        long_mix = back[index, :, :rows] + carried
        query[index] = query[index] * (long_mix + skip_ref[...] * inner[index])

    last(0, jnp.zeros((chans, rows), jnp.float32))
    each(blocks - 1, lambda index: last(index + 1, back[index, :, rows:]))

    tp_parts = out_ref.shape[0]
    part_rows = rows // tp_parts
    copies = out_ref.shape[1]

    def spread(inner_index):
        for part in range(tp_parts):
            for group in range(outer // tp_parts):
                packed = jnp.zeros((chans, rows), jnp.float32)
                for place in range(tp_parts):
                    block = query[(group * tp_parts + place) * inner_parts + inner_index]
                    shift = (place - part) * part_rows % rows
                    block = pltpu.roll(block, shift, 1) if shift else block
                    packed = jnp.where(lane // part_rows == place, block, packed)
                packed = packed.astype(out_ref.dtype)
                for copy in range(copies):
                    out_ref[part, copy, inner_index, :, group * rows : (group + 1) * rows] = packed

    each(inner_parts, spread)


def convolve(parts, filter_blocks, taps, skip, outer, tp_parts):
    blocks, streams, chans, _ = parts[0].shape
    rows = filter_blocks.shape[2]
    forward, backward = tables(rows)
    wide = (blocks, chans, 2 * rows)
    narrow = (blocks, chans, rows)
    vmem = pl.BlockSpec(memory_space=pltpu.VMEM)
    return pl.pallas_call(
        functools.partial(conv_kernel, outer, len(parts)),
        out_shape=jax.ShapeDtypeStruct(
            (tp_parts, outer, blocks // outer, chans, outer // tp_parts * rows), jnp.bfloat16
        ),
        in_specs=[vmem] * (5 + len(parts)),
        out_specs=vmem,
        scratch_shapes=[
            pltpu.VMEM((blocks + 1, streams, chans, rows), jnp.float32),
            pltpu.VMEM(narrow, jnp.float32),
            pltpu.VMEM(narrow, jnp.float32),
            pltpu.VMEM(wide, jnp.float32),
            pltpu.VMEM(wide, jnp.float32),
            pltpu.VMEM(wide, jnp.float32),
            pltpu.VMEM(wide, jnp.float32),
        ],
        compiler_params=pltpu.CompilerParams(vmem_limit_bytes=40 * 2**20),
        cost_estimate=pl.CostEstimate(flops=10**9, bytes_accessed=4 * 2**20, transcendentals=0),
    )(*parts, filter_blocks, taps, skip, jnp.asarray(forward), jnp.asarray(backward))


def out_kernel(block_ref, gated_ref, weight_ref, *refs):
    *out_refs, turned, left, held, sems = refs
    tp_parts = gated_ref.shape[0]
    part_rows = out_refs[0].shape[0]
    inner_parts, _, _, width = held.shape
    copies = [
        pltpu.make_async_copy(weight_ref.at[inner], held.at[inner], sems.at[inner])
        for inner in range(inner_parts)
    ]
    for copy in copies:
        copy.start()
    for part in range(tp_parts):
        turned[...] = gated_ref[part].T
        for index in range(len(out_refs)):
            begin = pl.multiple_of(block_ref[index] * part_rows, part_rows)
            left[part, index * part_rows : (index + 1) * part_rows] = turned[pl.ds(begin, part_rows)]
    for inner in range(inner_parts):
        copies[inner].wait()
        sums = jnp.zeros((left.shape[1], width), jnp.float32)
        for part in range(tp_parts):
            sums = sums + jnp.dot(left[part], held[inner, part], preferred_element_type=jnp.float32)
        for index, out_ref in enumerate(out_refs):
            out_ref[:, inner * width : (inner + 1) * width] = sums[
                index * part_rows : (index + 1) * part_rows
            ].astype(out_ref.dtype)


def project_out(gated, weight, blocks):
    tp_parts, depth, rows = gated.shape
    inner_parts, _, _, width = weight.shape
    columns = inner_parts * width
    part_rows = rows // len(blocks)
    vmem = pl.BlockSpec(memory_space=pltpu.VMEM)
    return pl.pallas_call(
        out_kernel,
        in_specs=[
            pl.BlockSpec(memory_space=pltpu.SMEM),
            vmem,
            pl.BlockSpec(memory_space=pltpu.HBM),
        ],
        out_specs=[vmem] * len(blocks),
        scratch_shapes=[
            pltpu.VMEM((rows, depth), jnp.bfloat16),
            pltpu.VMEM((tp_parts, rows, depth), jnp.bfloat16),
            pltpu.VMEM(weight.shape, weight.dtype),
            pltpu.SemaphoreType.DMA((inner_parts,)),
        ],
        out_shape=[jax.ShapeDtypeStruct((part_rows, columns), jnp.bfloat16)] * len(blocks),
        compiler_params=pltpu.CompilerParams(vmem_limit_bytes=24 * 2**20),
        cost_estimate=pl.CostEstimate(
            flops=2 * gated.size * columns,
            bytes_accessed=2 * (weight.size + gated.size + rows * columns),
            transcendentals=0,
        ),
    )(jnp.stack(blocks).astype(jnp.int32), gated, weight)


def per_device(features, in_proj, short_taps, long_filter, skip_gain, out_proj):
    rows = features.shape[0]
    seq_parts = lax.axis_size("seq")
    tp_parts = lax.axis_size("tp")
    outer = outer_factor(seq_parts, tp_parts)
    inner_parts = seq_parts // outer
    streams, _, chan_tp = in_proj.shape
    chans = chan_tp // seq_parts
    position = lax.axis_index("seq")
    inner_groups = [[a * inner_parts + b for b in range(inner_parts)] for a in range(outer)]
    tp_groups = [
        [index * tp_parts + tp for index in group for tp in range(tp_parts)] for group in inner_groups
    ]

    weight = lax.all_gather(in_proj, "seq", axis=1, tiled=True, axis_index_groups=inner_groups)

    taps = lax.dynamic_slice_in_dim(short_taps, position * chans, chans, axis=2)
    taps = jnp.broadcast_to(taps[..., None], taps.shape + (rows,))
    skip = lax.dynamic_slice_in_dim(skip_gain, position * chans, chans, axis=0)
    skip = jnp.broadcast_to(skip[:, None], (chans, rows))
    filter_blocks = long_filter.T.reshape(seq_parts, chans, rows)

    held = share_columns(features, outer, tp_parts)
    held, taps, skip = lax.optimization_barrier((held, taps, skip))
    arrived = cross_outer(held, outer, inner_parts, tp_parts)
    filter_blocks = lax.all_to_all(filter_blocks, "seq", split_axis=0, concat_axis=0, tiled=True)
    arrived[1], filter_blocks = lax.optimization_barrier((arrived[1], filter_blocks))
    chunks = [share_over_tp(piece, tp_parts) for piece in arrived]
    chunks, out_proj = lax.optimization_barrier((chunks, out_proj))
    out_weight = lax.all_gather(out_proj, ("seq", "tp"), axis_index_groups=tp_groups)
    out_weight = out_weight.reshape((inner_parts, tp_parts) + out_proj.shape)

    partial = project_in(chunks, weight, seq_parts)
    parts = lax.all_to_all(partial, "seq", split_axis=0, concat_axis=0, tiled=True)

    parts, out_weight = lax.optimization_barrier((parts, out_weight))

    gated = convolve([parts], filter_blocks, taps, skip, outer, tp_parts)
    gated = lax.all_to_all(
        gated.reshape((-1,) + gated.shape[3:]), ("tp", "seq"), split_axis=0, concat_axis=0, tiled=True
    )
    blocks, places = return_places(outer, inner_parts, tp_parts)
    pieces = project_out(gated.reshape(tp_parts, chan_tp, -1), out_weight, blocks)
    return return_output(pieces, places, inner_parts, tp_parts)


def solution(mesh):
    return jax.shard_map(
        per_device,
        mesh=mesh,
        in_specs=(
            P("seq", "tp"),
            P(None, "seq", "tp"),
            P(None, None, "tp"),
            P("seq", "tp"),
            P("tp"),
            P("tp", "seq"),
        ),
        out_specs=P("seq", "tp"),
        check_vma=False,
    )
```

```python
import functools
import math

import jax
import jax.numpy as jnp
import numpy as np
from jax import lax
from jax.experimental import pallas as pl
from jax.experimental.pallas import tpu as pltpu
from jax.sharding import PartitionSpec as P

HIGHEST = lax.Precision.HIGHEST
UNROLL = 16
HEAVY = 30


def outer_factor(seq_parts, tp_parts):
    outer = tp_parts
    while 4 * outer * outer <= seq_parts and seq_parts % (2 * outer) == 0:
        outer *= 2
    return outer


def assemble_kernel(place_ref, *refs):
    *piece_refs, out_ref, sems = refs
    part_rows, width = piece_refs[0].shape
    copies = []
    for index, piece_ref in enumerate(piece_refs):
        row = pl.multiple_of(place_ref[2 * index] * part_rows, part_rows)
        column = pl.multiple_of(place_ref[2 * index + 1] * width, width)
        target = out_ref.at[pl.ds(row, part_rows), pl.ds(column, width)]
        copies.append(pltpu.make_async_copy(piece_ref, target, sems.at[index]))
    for copy in copies:
        copy.start()
    for copy in copies:
        copy.wait()


def assemble(pieces, places, shape):
    return pl.pallas_call(
        assemble_kernel,
        in_specs=[pl.BlockSpec(memory_space=pltpu.SMEM)]
        + [pl.BlockSpec(memory_space=pltpu.VMEM)] * len(pieces),
        out_specs=pl.BlockSpec(memory_space=pl.ANY),
        out_shape=jax.ShapeDtypeStruct(shape, pieces[0].dtype),
        scratch_shapes=[pltpu.SemaphoreType.DMA((len(pieces),))],
        compiler_params=pltpu.CompilerParams(vmem_limit_bytes=4 * 2**20),
        cost_estimate=pl.CostEstimate(
            flops=0, bytes_accessed=4 * shape[0] * shape[1], transcendentals=0
        ),
    )(jnp.stack(places).astype(jnp.int32), *pieces)


def return_places(outer, inner_parts, tp_parts):
    per_tp = outer // tp_parts
    tp_place = lax.axis_index("tp")
    outer_place = lax.axis_index("seq") // inner_parts
    blocks, places = [], []
    for far in range(tp_parts):
        for near in range(per_tp):
            low = outer_place % per_tp
            blocks.append((tp_place + low + far) % tp_parts * per_tp + (low + near) % per_tp)
            low = (low - near + per_tp) % per_tp
            places.append((outer_place // per_tp - far - low + tp_parts + per_tp * tp_parts) % tp_parts)
            places.append(low)
    return blocks, places


def return_output(pieces, places, inner_parts, tp_parts):
    outer = len(pieces)
    part_rows, width = pieces[0].shape
    per_tp = outer // tp_parts
    arrived = []
    for index, piece in enumerate(pieces):
        far, near = divmod(index, per_tp)

        def target(seq, tp):
            src = seq // inner_parts
            low = src % per_tp
            dst = (tp + low + far) % tp_parts * per_tp + (low + near) % per_tp
            return (dst * inner_parts + seq % inner_parts) * tp_parts + src // per_tp

        pairs = [
            (seq * tp_parts + tp, target(seq, tp))
            for seq in range(outer * inner_parts)
            for tp in range(tp_parts)
        ]
        arrived.append(lax.ppermute(piece, ("seq", "tp"), pairs))
    return assemble(arrived, places, (tp_parts * part_rows, per_tp * width))


def share_columns(features, outer, tp_parts):
    rows, cols = features.shape
    per_tp = outer // tp_parts
    tp_place = lax.axis_index("tp")
    width = cols // outer
    held = []
    for step in range(tp_parts):
        which = (tp_place + step) % tp_parts
        piece = jnp.stack(
            [
                lax.dynamic_slice_in_dim(features, (group * tp_parts + which) * width, width, axis=1)
                for group in range(per_tp)
            ]
        )
        if step:
            piece = lax.ppermute(piece, "tp", [(i, (i + step) % tp_parts) for i in range(tp_parts)])
        held.append(piece)
    return jnp.concatenate(held)


def cross_outer(held, outer, inner_parts, tp_parts):
    per_tp = outer // tp_parts
    seq_parts = outer * inner_parts
    tp_place = lax.axis_index("tp")
    outer_place = lax.axis_index("seq") // inner_parts
    arrived = []
    for step in range(outer):
        target = (outer_place + step) % outer
        which = (tp_place - target // per_tp + tp_parts) % tp_parts * per_tp + target % per_tp
        piece = lax.dynamic_index_in_dim(held, which, axis=0, keepdims=False)
        if step:
            far = step * inner_parts
            piece = lax.ppermute(piece, "seq", [(i, (i + far) % seq_parts) for i in range(seq_parts)])
        arrived.append(piece)
    return arrived


def share_over_tp(part, tp_parts):
    pieces = [part]
    for step in range(1, tp_parts):
        pairs = [(i, (i + step) % tp_parts) for i in range(tp_parts)]
        pieces.append(lax.ppermute(part, "tp", pairs))
    return pieces


def gather_inner(block, inner_parts, settle):
    held, masks = [block], [0]
    bit = inner_parts // 2
    while bit:
        pairs = [(i, i ^ bit) for i in range(lax.axis_size("seq"))]
        held += [lax.ppermute(piece, "seq", pairs) for piece in held]
        masks += [mask ^ bit for mask in masks]
        if bit == inner_parts // 2:
            held = settle(held)
        bit //= 2
    return held, masks


def project_kernel(tp_parts, masks, place_ref, *refs):
    *refs, out_ref, left = refs
    share_refs, weight_refs = refs[: -len(masks)], refs[-len(masks) :]
    seq_parts, streams, chans, count = out_ref.shape
    blocks, rows, width = len(masks) // tp_parts, share_refs[0].shape[0], left.shape[2]
    for index, share_ref in enumerate(share_refs):
        chunk, step = divmod(index, tp_parts)
        for block in range(blocks):
            left[step * blocks + block, chunk * rows : (chunk + 1) * rows] = share_ref[
                :, block * width : (block + 1) * width
            ]
    slots = []
    for mask in masks:
        inner = jnp.bitwise_xor(place_ref[1], mask)
        step = lax.rem(place_ref[0] - inner // blocks + tp_parts, tp_parts)
        slots.append(step * blocks + lax.rem(inner, blocks))
    for stream in range(streams):
        sums = jnp.zeros((count, seq_parts * chans), jnp.float32)
        for slot, weight_ref in zip(slots, weight_refs):
            sums = sums + jnp.dot(left[slot], weight_ref[stream], preferred_element_type=jnp.float32)
        turned = sums.astype(out_ref.dtype).T
        for seq in range(seq_parts):
            out_ref[seq, stream] = turned[seq * chans : (seq + 1) * chans]


def project_in(chunks, weights, masks, inner_parts, seq_parts):
    tp_parts = len(chunks[0])
    rows, _ = chunks[0][0].shape
    streams, width, chan_tp = weights[0].shape
    chans = chan_tp // seq_parts
    pieces = [piece for chunk in chunks for piece in chunk]
    count = len(chunks) * rows
    place = jnp.stack([lax.axis_index("tp"), lax.axis_index("seq") % inner_parts]).astype(jnp.int32)
    vmem = pl.BlockSpec(memory_space=pltpu.VMEM)
    size = len(weights) * weights[0].size
    return pl.pallas_call(
        functools.partial(project_kernel, tp_parts, masks),
        in_specs=[pl.BlockSpec(memory_space=pltpu.SMEM)] + [vmem] * (len(pieces) + len(weights)),
        out_specs=vmem,
        out_shape=jax.ShapeDtypeStruct((seq_parts, streams, chans, count), jnp.bfloat16),
        scratch_shapes=[pltpu.VMEM((len(masks), count, width), jnp.bfloat16)],
        compiler_params=pltpu.CompilerParams(vmem_limit_bytes=32 * 2**20),
        cost_estimate=pl.CostEstimate(
            flops=HEAVY * 2 * count * size,
            bytes_accessed=2 * (size + len(pieces) * pieces[0].size)
            + 2 * streams * count * seq_parts * chans,
            transcendentals=0,
        ),
    )(place, *pieces, *weights)


def tables(block):
    place = np.arange(block)
    angle = 2.0 * math.pi * np.outer(place, place + 0.5) / (2 * block)
    forward = np.concatenate([np.cos(angle), -np.sin(angle)], 1)
    place = np.arange(2 * block)
    angle = 2.0 * math.pi * np.outer(np.arange(block) + 0.5, place) / (2 * block)
    backward = np.concatenate([np.cos(angle), -np.sin(angle)], 0) / block
    return forward.astype(np.float32), backward.astype(np.float32)


def each(count, body):
    if isinstance(count, int) and count <= UNROLL:
        for index in range(count):
            body(index)
    else:
        lax.fori_loop(0, count, lambda index, carry: (body(index), carry)[1], 0)


def total(count, term, zero):
    if isinstance(count, int) and count <= UNROLL:
        result = zero
        for index in range(count):
            result = jax.tree.map(jnp.add, result, term(index))
        return result
    return lax.fori_loop(
        0, count, lambda index, sums: jax.tree.map(jnp.add, sums, term(index)), zero
    )


def conv_kernel(
    outer, chunks, *refs
):
    part_refs, refs = refs[:chunks], refs[chunks:]
    filter_ref, taps_ref, skip_ref, fwd_ref, bwd_ref, out_ref, *refs = refs
    proj, query, inner, spec, filter_spec, product, back = refs
    blocks, streams, chans, _ = part_refs[0].shape
    rows = filter_ref.shape[2]
    inner_parts = blocks // outer
    taps_count = taps_ref.shape[1]
    lane = lax.broadcasted_iota(jnp.int32, (chans, rows), 1)

    depth = outer // chunks

    def add_up(inner_index, stream, group):
        value = jnp.zeros((chans, rows), jnp.float32)
        for part in range(outer):
            slot = (part - group) % outer
            column = slice(slot % depth * rows, (slot % depth + 1) * rows)
            source = part_refs[slot // depth]
            value = value + source[part * inner_parts + inner_index, stream, :, column].astype(jnp.float32)
        proj[1 + group * inner_parts + inner_index, stream] = value

    for group in range(outer):
        for stream in range(streams):
            each(inner_parts, functools.partial(add_up, stream=stream, group=group))

    for stream in range(streams):
        proj[0, stream] = jnp.zeros((chans, rows), jnp.float32)

    def first(index):
        filtered = []
        for stream in range(streams):
            now, past = proj[index + 1, stream], proj[index, stream]
            value = taps_ref[stream, 0] * now
            for offset in range(1, taps_count):
                moved = jnp.where(
                    lane < offset, pltpu.roll(past, offset, 1), pltpu.roll(now, offset, 1)
                )
                value = value + taps_ref[stream, offset] * moved
            filtered.append(value)
        query[index] = filtered[0]
        inner[index] = filtered[1] * filtered[2]

    each(blocks, first)

    def apply(source, table_ref, target):
        if chans % 8 == 0:
            flat = source[...].reshape(blocks * chans, source.shape[2])
            done = jnp.dot(flat, table_ref[...], precision=HIGHEST, preferred_element_type=jnp.float32)
            target[...] = done.reshape(target.shape)
        else:

            def one(index):
                target[index] = jnp.dot(
                    source[index], table_ref[...], precision=HIGHEST, preferred_element_type=jnp.float32
                )

            each(blocks, one)

    apply(filter_ref, fwd_ref, filter_spec)
    apply(inner, fwd_ref, spec)

    def multiply(index):
        def term(step):
            left, right = spec[step], filter_spec[index - step]
            left_real, left_imag = left[:, :rows], left[:, rows:]
            right_real, right_imag = right[:, :rows], right[:, rows:]
            return (
                left_real * right_real - left_imag * right_imag,
                left_real * right_imag + left_imag * right_real,
            )

        zero = jnp.zeros((chans, rows), jnp.float32)
        real, imag = total(index + 1, term, (zero, zero))
        product[index, :, :rows] = real
        product[index, :, rows:] = imag

    each(blocks, multiply)
    apply(product, bwd_ref, back)

    def last(index, carried):
        long_mix = back[index, :, :rows] + carried
        query[index] = query[index] * (long_mix + skip_ref[...] * inner[index])

    last(0, jnp.zeros((chans, rows), jnp.float32))
    each(blocks - 1, lambda index: last(index + 1, back[index, :, rows:]))

    tp_parts = out_ref.shape[0]
    part_rows = rows // tp_parts
    copies = out_ref.shape[1]

    def spread(inner_index):
        for part in range(tp_parts):
            for group in range(outer // tp_parts):
                packed = jnp.zeros((chans, rows), jnp.float32)
                for place in range(tp_parts):
                    block = query[(group * tp_parts + place) * inner_parts + inner_index]
                    shift = (place - part) * part_rows % rows
                    block = pltpu.roll(block, shift, 1) if shift else block
                    packed = jnp.where(lane // part_rows == place, block, packed)
                packed = packed.astype(out_ref.dtype)
                for copy in range(copies):
                    out_ref[part, copy, inner_index, :, group * rows : (group + 1) * rows] = packed

    each(inner_parts, spread)


def convolve(parts, filter_blocks, taps, skip, outer, tp_parts):
    blocks, streams, chans, _ = parts[0].shape
    rows = filter_blocks.shape[2]
    forward, backward = tables(rows)
    wide = (blocks, chans, 2 * rows)
    narrow = (blocks, chans, rows)
    vmem = pl.BlockSpec(memory_space=pltpu.VMEM)
    return pl.pallas_call(
        functools.partial(conv_kernel, outer, len(parts)),
        out_shape=jax.ShapeDtypeStruct(
            (tp_parts, outer, blocks // outer, chans, outer // tp_parts * rows), jnp.bfloat16
        ),
        in_specs=[vmem] * (5 + len(parts)),
        out_specs=vmem,
        scratch_shapes=[
            pltpu.VMEM((blocks + 1, streams, chans, rows), jnp.float32),
            pltpu.VMEM(narrow, jnp.float32),
            pltpu.VMEM(narrow, jnp.float32),
            pltpu.VMEM(wide, jnp.float32),
            pltpu.VMEM(wide, jnp.float32),
            pltpu.VMEM(wide, jnp.float32),
            pltpu.VMEM(wide, jnp.float32),
        ],
        compiler_params=pltpu.CompilerParams(vmem_limit_bytes=40 * 2**20),
        cost_estimate=pl.CostEstimate(flops=10**9, bytes_accessed=4 * 2**20, transcendentals=0),
    )(*parts, filter_blocks, taps, skip, jnp.asarray(forward), jnp.asarray(backward))


def out_kernel(block_ref, gated_ref, weight_ref, *refs):
    *out_refs, turned, left = refs
    tp_parts = gated_ref.shape[0]
    part_rows = out_refs[0].shape[0]

    @pl.when(pl.program_id(0) == 0)
    def _():
        for part in range(tp_parts):
            turned[...] = gated_ref[part].T
            for index in range(len(out_refs)):
                begin = pl.multiple_of(block_ref[index] * part_rows, part_rows)
                left[part, index * part_rows : (index + 1) * part_rows] = turned[pl.ds(begin, part_rows)]

    sums = jnp.zeros((left.shape[1], weight_ref.shape[3]), jnp.float32)
    for part in range(tp_parts):
        sums = sums + jnp.dot(left[part], weight_ref[0, part], preferred_element_type=jnp.float32)
    for index, out_ref in enumerate(out_refs):
        out_ref[...] = sums[index * part_rows : (index + 1) * part_rows].astype(out_ref.dtype)


def project_out(gated, weight, blocks):
    tp_parts, depth, rows = gated.shape
    inner_parts, _, _, width = weight.shape
    columns = inner_parts * width
    part_rows = rows // len(blocks)
    return pl.pallas_call(
        out_kernel,
        grid_spec=pltpu.PrefetchScalarGridSpec(
            num_scalar_prefetch=1,
            grid=(inner_parts,),
            in_specs=[
                pl.BlockSpec((tp_parts, depth, rows), lambda b, place: (0, 0, 0)),
                pl.BlockSpec((1, tp_parts, depth, width), lambda b, place: (b, 0, 0, 0)),
            ],
            out_specs=[pl.BlockSpec((part_rows, width), lambda b, place: (0, b))] * len(blocks),
            scratch_shapes=[
                pltpu.VMEM((rows, depth), jnp.bfloat16),
                pltpu.VMEM((tp_parts, rows, depth), jnp.bfloat16),
            ],
        ),
        out_shape=[jax.ShapeDtypeStruct((part_rows, columns), jnp.bfloat16)] * len(blocks),
        compiler_params=pltpu.CompilerParams(vmem_limit_bytes=16 * 2**20),
        cost_estimate=pl.CostEstimate(
            flops=2 * gated.size * columns,
            bytes_accessed=2 * (weight.size + gated.size + rows * columns),
            transcendentals=0,
        ),
    )(jnp.stack(blocks).astype(jnp.int32), gated, weight)


def per_device(features, in_proj, short_taps, long_filter, skip_gain, out_proj):
    rows = features.shape[0]
    seq_parts = lax.axis_size("seq")
    tp_parts = lax.axis_size("tp")
    outer = outer_factor(seq_parts, tp_parts)
    inner_parts = seq_parts // outer
    streams, _, chan_tp = in_proj.shape
    chans = chan_tp // seq_parts
    position = lax.axis_index("seq")
    inner_groups = [[a * inner_parts + b for b in range(inner_parts)] for a in range(outer)]
    tp_groups = [
        [index * tp_parts + tp for index in group for tp in range(tp_parts)] for group in inner_groups
    ]

    taps = lax.dynamic_slice_in_dim(short_taps, position * chans, chans, axis=2)
    taps = jnp.broadcast_to(taps[..., None], taps.shape + (rows,))
    skip = lax.dynamic_slice_in_dim(skip_gain, position * chans, chans, axis=0)
    skip = jnp.broadcast_to(skip[:, None], (chans, rows))
    filter_blocks = long_filter.T.reshape(seq_parts, chans, rows)

    held = share_columns(features, outer, tp_parts)
    held, taps, skip = lax.optimization_barrier((held, taps, skip))
    arrived = cross_outer(held, outer, inner_parts, tp_parts)
    filter_blocks = lax.all_to_all(filter_blocks, "seq", split_axis=0, concat_axis=0, tiled=True)
    arrived[1], filter_blocks = lax.optimization_barrier((arrived[1], filter_blocks))

    def settle(held):
        arrived[2], *held = lax.optimization_barrier((arrived[2], *held))
        return held

    weights, masks = gather_inner(in_proj, inner_parts, settle)
    chunks = [share_over_tp(piece, tp_parts) for piece in arrived]
    chunks, out_proj = lax.optimization_barrier((chunks, out_proj))
    out_weight = lax.all_gather(out_proj, ("seq", "tp"), axis_index_groups=tp_groups)
    out_weight = out_weight.reshape((inner_parts, tp_parts) + out_proj.shape)

    partial = project_in(chunks, weights, masks, inner_parts, seq_parts)
    parts = lax.all_to_all(partial, "seq", split_axis=0, concat_axis=0, tiled=True)

    parts, out_weight = lax.optimization_barrier((parts, out_weight))

    gated = convolve([parts], filter_blocks, taps, skip, outer, tp_parts)
    gated = lax.all_to_all(
        gated.reshape((-1,) + gated.shape[3:]), ("tp", "seq"), split_axis=0, concat_axis=0, tiled=True
    )
    blocks, places = return_places(outer, inner_parts, tp_parts)
    pieces = project_out(gated.reshape(tp_parts, chan_tp, -1), out_weight, blocks)
    return return_output(pieces, places, inner_parts, tp_parts)


def solution(mesh):
    return jax.shard_map(
        per_device,
        mesh=mesh,
        in_specs=(
            P("seq", "tp"),
            P(None, "seq", "tp"),
            P(None, None, "tp"),
            P("seq", "tp"),
            P("tp"),
            P("tp", "seq"),
        ),
        out_specs=P("seq", "tp"),
        check_vma=False,
    )
```

```python
import functools
import math

import jax
import jax.numpy as jnp
import numpy as np
from jax import lax
from jax.experimental import pallas as pl
from jax.experimental.pallas import tpu as pltpu
from jax.sharding import PartitionSpec as P

HIGHEST = lax.Precision.HIGHEST
UNROLL = 16
HEAVY = 30


def outer_factor(seq_parts, tp_parts):
    outer = tp_parts
    while 4 * outer * outer <= seq_parts and seq_parts % (2 * outer) == 0:
        outer *= 2
    return outer


def assemble_kernel(place_ref, *refs):
    *piece_refs, out_ref, sems = refs
    part_rows, width = piece_refs[0].shape
    copies = []
    for index, piece_ref in enumerate(piece_refs):
        row = pl.multiple_of(place_ref[2 * index] * part_rows, part_rows)
        column = pl.multiple_of(place_ref[2 * index + 1] * width, width)
        target = out_ref.at[pl.ds(row, part_rows), pl.ds(column, width)]
        copies.append(pltpu.make_async_copy(piece_ref, target, sems.at[index]))
    for copy in copies:
        copy.start()
    for copy in copies:
        copy.wait()


def assemble(pieces, places, shape):
    return pl.pallas_call(
        assemble_kernel,
        in_specs=[pl.BlockSpec(memory_space=pltpu.SMEM)]
        + [pl.BlockSpec(memory_space=pltpu.VMEM)] * len(pieces),
        out_specs=pl.BlockSpec(memory_space=pl.ANY),
        out_shape=jax.ShapeDtypeStruct(shape, pieces[0].dtype),
        scratch_shapes=[pltpu.SemaphoreType.DMA((len(pieces),))],
        compiler_params=pltpu.CompilerParams(vmem_limit_bytes=4 * 2**20),
        cost_estimate=pl.CostEstimate(
            flops=0, bytes_accessed=4 * shape[0] * shape[1], transcendentals=0
        ),
    )(jnp.stack(places).astype(jnp.int32), *pieces)


def return_places(outer, inner_parts, tp_parts):
    per_tp = outer // tp_parts
    tp_place = lax.axis_index("tp")
    outer_place = lax.axis_index("seq") // inner_parts
    blocks, places = [], []
    for far in range(tp_parts):
        for near in range(per_tp):
            low = outer_place % per_tp
            blocks.append((tp_place + low + far) % tp_parts * per_tp + (low + near) % per_tp)
            low = (low - near + per_tp) % per_tp
            places.append((outer_place // per_tp - far - low + tp_parts + per_tp * tp_parts) % tp_parts)
            places.append(low)
    return blocks, places


def return_output(pieces, places, inner_parts, tp_parts):
    outer = len(pieces)
    part_rows, width = pieces[0].shape
    per_tp = outer // tp_parts
    arrived = []
    for index, piece in enumerate(pieces):
        far, near = divmod(index, per_tp)

        def target(seq, tp):
            src = seq // inner_parts
            low = src % per_tp
            dst = (tp + low + far) % tp_parts * per_tp + (low + near) % per_tp
            return (dst * inner_parts + seq % inner_parts) * tp_parts + src // per_tp

        pairs = [
            (seq * tp_parts + tp, target(seq, tp))
            for seq in range(outer * inner_parts)
            for tp in range(tp_parts)
        ]
        arrived.append(lax.ppermute(piece, ("seq", "tp"), pairs))
    return assemble(arrived, places, (tp_parts * part_rows, per_tp * width))


def share_columns(features, outer, tp_parts):
    rows, cols = features.shape
    per_tp = outer // tp_parts
    tp_place = lax.axis_index("tp")
    width = cols // outer
    held = []
    for step in range(tp_parts):
        which = (tp_place + step) % tp_parts
        piece = jnp.stack(
            [
                lax.dynamic_slice_in_dim(features, (group * tp_parts + which) * width, width, axis=1)
                for group in range(per_tp)
            ]
        )
        if step:
            piece = lax.ppermute(piece, "tp", [(i, (i + step) % tp_parts) for i in range(tp_parts)])
        held.append(piece)
    return jnp.concatenate(held)


def cross_outer(held, outer, inner_parts, tp_parts):
    per_tp = outer // tp_parts
    seq_parts = outer * inner_parts
    tp_place = lax.axis_index("tp")
    outer_place = lax.axis_index("seq") // inner_parts
    arrived = []
    for step in range(outer):
        target = (outer_place + step) % outer
        which = (tp_place - target // per_tp + tp_parts) % tp_parts * per_tp + target % per_tp
        piece = lax.dynamic_index_in_dim(held, which, axis=0, keepdims=False)
        if step:
            far = step * inner_parts
            piece = lax.ppermute(piece, "seq", [(i, (i + far) % seq_parts) for i in range(seq_parts)])
        arrived.append(piece)
    return arrived


def share_over_tp(part, tp_parts):
    pieces = [part]
    for step in range(1, tp_parts):
        pairs = [(i, (i + step) % tp_parts) for i in range(tp_parts)]
        pieces.append(lax.ppermute(part, "tp", pairs))
    return pieces


def gather_inner(block, inner_parts):
    held, masks = [block], [0]
    bit = inner_parts // 2
    while bit:
        pairs = [(i, i ^ bit) for i in range(lax.axis_size("seq"))]
        held += [lax.ppermute(piece, "seq", pairs) for piece in held]
        masks += [mask ^ bit for mask in masks]
        bit //= 2
    return held, masks


def project_kernel(tp_parts, masks, place_ref, *refs):
    *refs, out_ref, left = refs
    share_refs, weight_refs = refs[: -len(masks)], refs[-len(masks) :]
    seq_parts, streams, chans, count = out_ref.shape
    blocks, rows, width = len(masks) // tp_parts, share_refs[0].shape[0], left.shape[2]
    for index, share_ref in enumerate(share_refs):
        chunk, step = divmod(index, tp_parts)
        for block in range(blocks):
            left[step * blocks + block, chunk * rows : (chunk + 1) * rows] = share_ref[
                :, block * width : (block + 1) * width
            ]
    slots = []
    for mask in masks:
        inner = jnp.bitwise_xor(place_ref[1], mask)
        step = lax.rem(place_ref[0] - inner // blocks + tp_parts, tp_parts)
        slots.append(step * blocks + lax.rem(inner, blocks))
    for stream in range(streams):
        sums = jnp.zeros((count, seq_parts * chans), jnp.float32)
        for slot, weight_ref in zip(slots, weight_refs):
            sums = sums + jnp.dot(left[slot], weight_ref[stream], preferred_element_type=jnp.float32)
        turned = sums.astype(out_ref.dtype).T
        for seq in range(seq_parts):
            out_ref[seq, stream] = turned[seq * chans : (seq + 1) * chans]


def project_in(chunks, weights, masks, inner_parts, seq_parts):
    tp_parts = len(chunks[0])
    rows, _ = chunks[0][0].shape
    streams, width, chan_tp = weights[0].shape
    chans = chan_tp // seq_parts
    pieces = [piece for chunk in chunks for piece in chunk]
    count = len(chunks) * rows
    place = jnp.stack([lax.axis_index("tp"), lax.axis_index("seq") % inner_parts]).astype(jnp.int32)
    vmem = pl.BlockSpec(memory_space=pltpu.VMEM)
    size = len(weights) * weights[0].size
    return pl.pallas_call(
        functools.partial(project_kernel, tp_parts, masks),
        in_specs=[pl.BlockSpec(memory_space=pltpu.SMEM)] + [vmem] * (len(pieces) + len(weights)),
        out_specs=vmem,
        out_shape=jax.ShapeDtypeStruct((seq_parts, streams, chans, count), jnp.bfloat16),
        scratch_shapes=[pltpu.VMEM((len(masks), count, width), jnp.bfloat16)],
        compiler_params=pltpu.CompilerParams(vmem_limit_bytes=32 * 2**20),
        cost_estimate=pl.CostEstimate(
            flops=HEAVY * 2 * count * size,
            bytes_accessed=2 * (size + len(pieces) * pieces[0].size)
            + 2 * streams * count * seq_parts * chans,
            transcendentals=0,
        ),
    )(place, *pieces, *weights)


def tables(block):
    place = np.arange(block)
    angle = 2.0 * math.pi * np.outer(place, place + 0.5) / (2 * block)
    forward = np.concatenate([np.cos(angle), -np.sin(angle)], 1)
    place = np.arange(2 * block)
    angle = 2.0 * math.pi * np.outer(np.arange(block) + 0.5, place) / (2 * block)
    backward = np.concatenate([np.cos(angle), -np.sin(angle)], 0) / block
    return forward.astype(np.float32), backward.astype(np.float32)


def each(count, body):
    if isinstance(count, int) and count <= UNROLL:
        for index in range(count):
            body(index)
    else:
        lax.fori_loop(0, count, lambda index, carry: (body(index), carry)[1], 0)


def total(count, term, zero):
    if isinstance(count, int) and count <= UNROLL:
        result = zero
        for index in range(count):
            result = jax.tree.map(jnp.add, result, term(index))
        return result
    return lax.fori_loop(
        0, count, lambda index, sums: jax.tree.map(jnp.add, sums, term(index)), zero
    )


def conv_kernel(
    outer, chunks, *refs
):
    part_refs, refs = refs[:chunks], refs[chunks:]
    filter_ref, taps_ref, skip_ref, fwd_ref, bwd_ref, out_ref, *refs = refs
    proj, query, inner, spec, filter_spec, product, back = refs
    blocks, streams, chans, _ = part_refs[0].shape
    rows = filter_ref.shape[2]
    inner_parts = blocks // outer
    taps_count = taps_ref.shape[1]
    lane = lax.broadcasted_iota(jnp.int32, (chans, rows), 1)

    depth = outer // chunks

    def add_up(inner_index, stream, group):
        value = jnp.zeros((chans, rows), jnp.float32)
        for part in range(outer):
            slot = (part - group) % outer
            column = slice(slot % depth * rows, (slot % depth + 1) * rows)
            source = part_refs[slot // depth]
            value = value + source[part * inner_parts + inner_index, stream, :, column].astype(jnp.float32)
        proj[1 + group * inner_parts + inner_index, stream] = value

    for group in range(outer):
        for stream in range(streams):
            each(inner_parts, functools.partial(add_up, stream=stream, group=group))

    for stream in range(streams):
        proj[0, stream] = jnp.zeros((chans, rows), jnp.float32)

    def first(index):
        filtered = []
        for stream in range(streams):
            now, past = proj[index + 1, stream], proj[index, stream]
            value = taps_ref[stream, 0] * now
            for offset in range(1, taps_count):
                moved = jnp.where(
                    lane < offset, pltpu.roll(past, offset, 1), pltpu.roll(now, offset, 1)
                )
                value = value + taps_ref[stream, offset] * moved
            filtered.append(value)
        query[index] = filtered[0]
        inner[index] = filtered[1] * filtered[2]

    each(blocks, first)

    def apply(source, table_ref, target):
        if chans % 8 == 0:
            flat = source[...].reshape(blocks * chans, source.shape[2])
            done = jnp.dot(flat, table_ref[...], precision=HIGHEST, preferred_element_type=jnp.float32)
            target[...] = done.reshape(target.shape)
        else:

            def one(index):
                target[index] = jnp.dot(
                    source[index], table_ref[...], precision=HIGHEST, preferred_element_type=jnp.float32
                )

            each(blocks, one)

    apply(filter_ref, fwd_ref, filter_spec)
    apply(inner, fwd_ref, spec)

    def multiply(index):
        def term(step):
            left, right = spec[step], filter_spec[index - step]
            left_real, left_imag = left[:, :rows], left[:, rows:]
            right_real, right_imag = right[:, :rows], right[:, rows:]
            return (
                left_real * right_real - left_imag * right_imag,
                left_real * right_imag + left_imag * right_real,
            )

        zero = jnp.zeros((chans, rows), jnp.float32)
        real, imag = total(index + 1, term, (zero, zero))
        product[index, :, :rows] = real
        product[index, :, rows:] = imag

    each(blocks, multiply)
    apply(product, bwd_ref, back)

    def last(index, carried):
        long_mix = back[index, :, :rows] + carried
        query[index] = query[index] * (long_mix + skip_ref[...] * inner[index])

    last(0, jnp.zeros((chans, rows), jnp.float32))
    each(blocks - 1, lambda index: last(index + 1, back[index, :, rows:]))

    tp_parts = out_ref.shape[0]
    part_rows = rows // tp_parts
    copies = out_ref.shape[1]

    def spread(inner_index):
        for part in range(tp_parts):
            for group in range(outer // tp_parts):
                packed = jnp.zeros((chans, rows), jnp.float32)
                for place in range(tp_parts):
                    block = query[(group * tp_parts + place) * inner_parts + inner_index]
                    shift = (place - part) * part_rows % rows
                    block = pltpu.roll(block, shift, 1) if shift else block
                    packed = jnp.where(lane // part_rows == place, block, packed)
                packed = packed.astype(out_ref.dtype)
                for copy in range(copies):
                    out_ref[part, copy, inner_index, :, group * rows : (group + 1) * rows] = packed

    each(inner_parts, spread)


def convolve(parts, filter_blocks, taps, skip, outer, tp_parts):
    blocks, streams, chans, _ = parts[0].shape
    rows = filter_blocks.shape[2]
    forward, backward = tables(rows)
    wide = (blocks, chans, 2 * rows)
    narrow = (blocks, chans, rows)
    vmem = pl.BlockSpec(memory_space=pltpu.VMEM)
    return pl.pallas_call(
        functools.partial(conv_kernel, outer, len(parts)),
        out_shape=jax.ShapeDtypeStruct(
            (tp_parts, outer, blocks // outer, chans, outer // tp_parts * rows), jnp.bfloat16
        ),
        in_specs=[vmem] * (5 + len(parts)),
        out_specs=vmem,
        scratch_shapes=[
            pltpu.VMEM((blocks + 1, streams, chans, rows), jnp.float32),
            pltpu.VMEM(narrow, jnp.float32),
            pltpu.VMEM(narrow, jnp.float32),
            pltpu.VMEM(wide, jnp.float32),
            pltpu.VMEM(wide, jnp.float32),
            pltpu.VMEM(wide, jnp.float32),
            pltpu.VMEM(wide, jnp.float32),
        ],
        compiler_params=pltpu.CompilerParams(vmem_limit_bytes=40 * 2**20),
        cost_estimate=pl.CostEstimate(flops=10**9, bytes_accessed=4 * 2**20, transcendentals=0),
    )(*parts, filter_blocks, taps, skip, jnp.asarray(forward), jnp.asarray(backward))


def out_kernel(block_ref, gated_ref, weight_ref, *refs):
    *out_refs, turned, left = refs
    tp_parts = gated_ref.shape[0]
    part_rows = out_refs[0].shape[0]

    @pl.when(pl.program_id(0) == 0)
    def _():
        for part in range(tp_parts):
            turned[...] = gated_ref[part].T
            for index in range(len(out_refs)):
                begin = pl.multiple_of(block_ref[index] * part_rows, part_rows)
                left[part, index * part_rows : (index + 1) * part_rows] = turned[pl.ds(begin, part_rows)]

    sums = jnp.zeros((left.shape[1], weight_ref.shape[3]), jnp.float32)
    for part in range(tp_parts):
        sums = sums + jnp.dot(left[part], weight_ref[0, part], preferred_element_type=jnp.float32)
    for index, out_ref in enumerate(out_refs):
        out_ref[...] = sums[index * part_rows : (index + 1) * part_rows].astype(out_ref.dtype)


def project_out(gated, weight, blocks):
    tp_parts, depth, rows = gated.shape
    inner_parts, _, _, width = weight.shape
    columns = inner_parts * width
    part_rows = rows // len(blocks)
    return pl.pallas_call(
        out_kernel,
        grid_spec=pltpu.PrefetchScalarGridSpec(
            num_scalar_prefetch=1,
            grid=(inner_parts,),
            in_specs=[
                pl.BlockSpec((tp_parts, depth, rows), lambda b, place: (0, 0, 0)),
                pl.BlockSpec((1, tp_parts, depth, width), lambda b, place: (b, 0, 0, 0)),
            ],
            out_specs=[pl.BlockSpec((part_rows, width), lambda b, place: (0, b))] * len(blocks),
            scratch_shapes=[
                pltpu.VMEM((rows, depth), jnp.bfloat16),
                pltpu.VMEM((tp_parts, rows, depth), jnp.bfloat16),
            ],
        ),
        out_shape=[jax.ShapeDtypeStruct((part_rows, columns), jnp.bfloat16)] * len(blocks),
        compiler_params=pltpu.CompilerParams(vmem_limit_bytes=16 * 2**20),
        cost_estimate=pl.CostEstimate(
            flops=2 * gated.size * columns,
            bytes_accessed=2 * (weight.size + gated.size + rows * columns),
            transcendentals=0,
        ),
    )(jnp.stack(blocks).astype(jnp.int32), gated, weight)


def per_device(features, in_proj, short_taps, long_filter, skip_gain, out_proj):
    rows = features.shape[0]
    seq_parts = lax.axis_size("seq")
    tp_parts = lax.axis_size("tp")
    outer = outer_factor(seq_parts, tp_parts)
    inner_parts = seq_parts // outer
    streams, _, chan_tp = in_proj.shape
    chans = chan_tp // seq_parts
    position = lax.axis_index("seq")
    inner_groups = [[a * inner_parts + b for b in range(inner_parts)] for a in range(outer)]
    tp_groups = [
        [index * tp_parts + tp for index in group for tp in range(tp_parts)] for group in inner_groups
    ]

    taps = lax.dynamic_slice_in_dim(short_taps, position * chans, chans, axis=2)
    taps = jnp.broadcast_to(taps[..., None], taps.shape + (rows,))
    skip = lax.dynamic_slice_in_dim(skip_gain, position * chans, chans, axis=0)
    skip = jnp.broadcast_to(skip[:, None], (chans, rows))
    filter_blocks = long_filter.T.reshape(seq_parts, chans, rows)

    held = share_columns(features, outer, tp_parts)
    held, taps, skip = lax.optimization_barrier((held, taps, skip))
    arrived = cross_outer(held, outer, inner_parts, tp_parts)
    filter_blocks = lax.all_to_all(filter_blocks, "seq", split_axis=0, concat_axis=0, tiled=True)
    arrived[1], filter_blocks = lax.optimization_barrier((arrived[1], filter_blocks))

    weights, masks = gather_inner(in_proj, inner_parts)
    chunks = [share_over_tp(piece, tp_parts) for piece in arrived]
    chunks, out_proj = lax.optimization_barrier((chunks, out_proj))
    out_weight = lax.all_gather(out_proj, ("seq", "tp"), axis_index_groups=tp_groups)
    out_weight = out_weight.reshape((inner_parts, tp_parts) + out_proj.shape)

    partial = project_in(chunks, weights, masks, inner_parts, seq_parts)
    parts = lax.all_to_all(partial, "seq", split_axis=0, concat_axis=0, tiled=True)

    parts, out_weight = lax.optimization_barrier((parts, out_weight))

    gated = convolve([parts], filter_blocks, taps, skip, outer, tp_parts)
    gated = lax.all_to_all(
        gated.reshape((-1,) + gated.shape[3:]), ("tp", "seq"), split_axis=0, concat_axis=0, tiled=True
    )
    blocks, places = return_places(outer, inner_parts, tp_parts)
    pieces = project_out(gated.reshape(tp_parts, chan_tp, -1), out_weight, blocks)
    return return_output(pieces, places, inner_parts, tp_parts)


def solution(mesh):
    return jax.shard_map(
        per_device,
        mesh=mesh,
        in_specs=(
            P("seq", "tp"),
            P(None, "seq", "tp"),
            P(None, None, "tp"),
            P("seq", "tp"),
            P("tp"),
            P("tp", "seq"),
        ),
        out_specs=P("seq", "tp"),
        check_vma=False,
    )
```

```python
import functools
import math

import jax
import jax.numpy as jnp
import numpy as np
from jax import lax
from jax.experimental import pallas as pl
from jax.experimental.pallas import tpu as pltpu
from jax.sharding import PartitionSpec as P

HIGHEST = lax.Precision.HIGHEST
UNROLL = 16
HEAVY = 30


def outer_factor(seq_parts, tp_parts):
    outer = tp_parts
    while 4 * outer * outer <= seq_parts and seq_parts % (2 * outer) == 0:
        outer *= 2
    return outer


def assemble_kernel(place_ref, *refs):
    *piece_refs, out_ref, sems = refs
    part_rows, width = piece_refs[0].shape
    copies = []
    for index, piece_ref in enumerate(piece_refs):
        row = pl.multiple_of(place_ref[2 * index] * part_rows, part_rows)
        column = pl.multiple_of(place_ref[2 * index + 1] * width, width)
        target = out_ref.at[pl.ds(row, part_rows), pl.ds(column, width)]
        copies.append(pltpu.make_async_copy(piece_ref, target, sems.at[index]))
    for copy in copies:
        copy.start()
    for copy in copies:
        copy.wait()


def assemble(pieces, places, shape):
    return pl.pallas_call(
        assemble_kernel,
        in_specs=[pl.BlockSpec(memory_space=pltpu.SMEM)]
        + [pl.BlockSpec(memory_space=pltpu.VMEM)] * len(pieces),
        out_specs=pl.BlockSpec(memory_space=pl.ANY),
        out_shape=jax.ShapeDtypeStruct(shape, pieces[0].dtype),
        scratch_shapes=[pltpu.SemaphoreType.DMA((len(pieces),))],
        compiler_params=pltpu.CompilerParams(vmem_limit_bytes=4 * 2**20),
        cost_estimate=pl.CostEstimate(
            flops=0, bytes_accessed=4 * shape[0] * shape[1], transcendentals=0
        ),
    )(jnp.stack(places).astype(jnp.int32), *pieces)


def return_places(outer, inner_parts, tp_parts):
    per_tp = outer // tp_parts
    tp_place = lax.axis_index("tp")
    outer_place = lax.axis_index("seq") // inner_parts
    blocks, places = [], []
    for far in range(tp_parts):
        for near in range(per_tp):
            low = outer_place % per_tp
            blocks.append((tp_place + low + far) % tp_parts * per_tp + (low + near) % per_tp)
            low = (low - near + per_tp) % per_tp
            places.append((outer_place // per_tp - far - low + tp_parts + per_tp * tp_parts) % tp_parts)
            places.append(low)
    return blocks, places


def return_output(pieces, places, inner_parts, tp_parts):
    outer = len(pieces)
    part_rows, width = pieces[0].shape
    per_tp = outer // tp_parts
    arrived = []
    for index, piece in enumerate(pieces):
        far, near = divmod(index, per_tp)

        def target(seq, tp):
            src = seq // inner_parts
            low = src % per_tp
            dst = (tp + low + far) % tp_parts * per_tp + (low + near) % per_tp
            return (dst * inner_parts + seq % inner_parts) * tp_parts + src // per_tp

        pairs = [
            (seq * tp_parts + tp, target(seq, tp))
            for seq in range(outer * inner_parts)
            for tp in range(tp_parts)
        ]
        arrived.append(lax.ppermute(piece, ("seq", "tp"), pairs))
    return assemble(arrived, places, (tp_parts * part_rows, per_tp * width))


def share_columns(features, outer, tp_parts):
    rows, cols = features.shape
    per_tp = outer // tp_parts
    tp_place = lax.axis_index("tp")
    width = cols // outer
    held = []
    for step in range(tp_parts):
        which = (tp_place + step) % tp_parts
        piece = jnp.stack(
            [
                lax.dynamic_slice_in_dim(features, (group * tp_parts + which) * width, width, axis=1)
                for group in range(per_tp)
            ]
        )
        if step:
            piece = lax.ppermute(piece, "tp", [(i, (i + step) % tp_parts) for i in range(tp_parts)])
        held.append(piece)
    return jnp.concatenate(held)


def cross_outer(held, outer, inner_parts, tp_parts):
    per_tp = outer // tp_parts
    seq_parts = outer * inner_parts
    tp_place = lax.axis_index("tp")
    outer_place = lax.axis_index("seq") // inner_parts
    arrived = {}
    for step in sorted(range(outer), key=lambda step: min(step, outer - step)):
        if step not in (0, 1, outer - 1):
            arrived[1], held = lax.optimization_barrier((arrived[1], held))
        target = (outer_place + step) % outer
        which = (tp_place - target // per_tp + tp_parts) % tp_parts * per_tp + target % per_tp
        piece = lax.dynamic_index_in_dim(held, which, axis=0, keepdims=False)
        if step:
            far = step * inner_parts
            piece = lax.ppermute(piece, "seq", [(i, (i + far) % seq_parts) for i in range(seq_parts)])
        arrived[step] = piece
    return [arrived[step] for step in range(outer)]


def share_over_tp(part, tp_parts):
    pieces = [part]
    for step in range(1, tp_parts):
        pairs = [(i, (i + step) % tp_parts) for i in range(tp_parts)]
        pieces.append(lax.ppermute(part, "tp", pairs))
    return pieces


def project_kernel(tp_parts, place_ref, *refs):
    *share_refs, weight_ref, out_ref = refs
    seq_parts, _, chans, count = out_ref.shape
    sums = jnp.zeros((count, seq_parts * chans), jnp.float32)
    for step in range(tp_parts):
        which = lax.rem(place_ref[0] - step + tp_parts, tp_parts)
        left = jnp.concatenate([share_ref[...] for share_ref in share_refs[step::tp_parts]])
        sums = sums + jnp.dot(left, weight_ref[0, which], preferred_element_type=jnp.float32)
    turned = sums.astype(out_ref.dtype).T
    for seq in range(seq_parts):
        out_ref[seq, 0] = turned[seq * chans : (seq + 1) * chans]


def project_in(chunks, weight, seq_parts):
    tp_parts = len(chunks[0])
    rows, width = chunks[0][0].shape
    streams, _, chan_tp = weight.shape
    weight = weight.reshape(streams, tp_parts, width, chan_tp)
    chans = chan_tp // seq_parts
    pieces = [piece for chunk in chunks for piece in chunk]
    count = len(chunks) * rows
    place = lax.axis_index("tp").astype(jnp.int32)[None]
    return pl.pallas_call(
        functools.partial(project_kernel, tp_parts),
        grid_spec=pltpu.PrefetchScalarGridSpec(
            num_scalar_prefetch=1,
            grid=(streams,),
            in_specs=[pl.BlockSpec((rows, width), lambda i, place: (0, 0))] * len(pieces)
            + [pl.BlockSpec((1, tp_parts, width, chan_tp), lambda i, place: (i, 0, 0, 0))],
            out_specs=pl.BlockSpec((seq_parts, 1, chans, count), lambda i, place: (0, i, 0, 0)),
        ),
        out_shape=jax.ShapeDtypeStruct((seq_parts, streams, chans, count), jnp.bfloat16),
        compiler_params=pltpu.CompilerParams(vmem_limit_bytes=56 * 2**20),
        cost_estimate=pl.CostEstimate(
            flops=HEAVY * 2 * count * weight.size,
            bytes_accessed=2 * (weight.size + len(pieces) * pieces[0].size)
            + 2 * streams * count * chan_tp,
            transcendentals=0,
        ),
    )(place, *pieces, weight)


def tables(block):
    place = np.arange(block)
    angle = 2.0 * math.pi * np.outer(place, place + 0.5) / (2 * block)
    forward = np.concatenate([np.cos(angle), -np.sin(angle)], 1)
    place = np.arange(2 * block)
    angle = 2.0 * math.pi * np.outer(np.arange(block) + 0.5, place) / (2 * block)
    backward = np.concatenate([np.cos(angle), -np.sin(angle)], 0) / block
    return forward.astype(np.float32), backward.astype(np.float32)


def each(count, body):
    if isinstance(count, int) and count <= UNROLL:
        for index in range(count):
            body(index)
    else:
        lax.fori_loop(0, count, lambda index, carry: (body(index), carry)[1], 0)


def total(count, term, zero):
    if isinstance(count, int) and count <= UNROLL:
        result = zero
        for index in range(count):
            result = jax.tree.map(jnp.add, result, term(index))
        return result
    return lax.fori_loop(
        0, count, lambda index, sums: jax.tree.map(jnp.add, sums, term(index)), zero
    )


def conv_kernel(
    outer, chunks, *refs
):
    part_refs, refs = refs[:chunks], refs[chunks:]
    filter_ref, taps_ref, skip_ref, fwd_ref, bwd_ref, out_ref, *refs = refs
    proj, query, inner, spec, filter_spec, product, back = refs
    blocks, streams, chans, _ = part_refs[0].shape
    rows = filter_ref.shape[2]
    inner_parts = blocks // outer
    taps_count = taps_ref.shape[1]
    lane = lax.broadcasted_iota(jnp.int32, (chans, rows), 1)

    depth = outer // chunks

    def add_up(inner_index, stream, group):
        value = jnp.zeros((chans, rows), jnp.float32)
        for part in range(outer):
            slot = (part - group) % outer
            column = slice(slot % depth * rows, (slot % depth + 1) * rows)
            source = part_refs[slot // depth]
            value = value + source[part * inner_parts + inner_index, stream, :, column].astype(jnp.float32)
        proj[1 + group * inner_parts + inner_index, stream] = value

    for group in range(outer):
        for stream in range(streams):
            each(inner_parts, functools.partial(add_up, stream=stream, group=group))

    for stream in range(streams):
        proj[0, stream] = jnp.zeros((chans, rows), jnp.float32)

    def first(index):
        filtered = []
        for stream in range(streams):
            now, past = proj[index + 1, stream], proj[index, stream]
            value = taps_ref[stream, 0] * now
            for offset in range(1, taps_count):
                moved = jnp.where(
                    lane < offset, pltpu.roll(past, offset, 1), pltpu.roll(now, offset, 1)
                )
                value = value + taps_ref[stream, offset] * moved
            filtered.append(value)
        query[index] = filtered[0]
        inner[index] = filtered[1] * filtered[2]

    each(blocks, first)

    def apply(source, table_ref, target):
        if chans % 8 == 0:
            flat = source[...].reshape(blocks * chans, source.shape[2])
            done = jnp.dot(flat, table_ref[...], precision=HIGHEST, preferred_element_type=jnp.float32)
            target[...] = done.reshape(target.shape)
        else:

            def one(index):
                target[index] = jnp.dot(
                    source[index], table_ref[...], precision=HIGHEST, preferred_element_type=jnp.float32
                )

            each(blocks, one)

    apply(filter_ref, fwd_ref, filter_spec)
    apply(inner, fwd_ref, spec)

    def multiply(index):
        def term(step):
            left, right = spec[step], filter_spec[index - step]
            left_real, left_imag = left[:, :rows], left[:, rows:]
            right_real, right_imag = right[:, :rows], right[:, rows:]
            return (
                left_real * right_real - left_imag * right_imag,
                left_real * right_imag + left_imag * right_real,
            )

        zero = jnp.zeros((chans, rows), jnp.float32)
        real, imag = total(index + 1, term, (zero, zero))
        product[index, :, :rows] = real
        product[index, :, rows:] = imag

    each(blocks, multiply)
    apply(product, bwd_ref, back)

    def last(index, carried):
        long_mix = back[index, :, :rows] + carried
        query[index] = query[index] * (long_mix + skip_ref[...] * inner[index])

    last(0, jnp.zeros((chans, rows), jnp.float32))
    each(blocks - 1, lambda index: last(index + 1, back[index, :, rows:]))

    tp_parts = out_ref.shape[0]
    part_rows = rows // tp_parts
    copies = out_ref.shape[1]

    def spread(inner_index):
        for part in range(tp_parts):
            for group in range(outer // tp_parts):
                packed = jnp.zeros((chans, rows), jnp.float32)
                for place in range(tp_parts):
                    block = query[(group * tp_parts + place) * inner_parts + inner_index]
                    shift = (place - part) * part_rows % rows
                    block = pltpu.roll(block, shift, 1) if shift else block
                    packed = jnp.where(lane // part_rows == place, block, packed)
                packed = packed.astype(out_ref.dtype)
                for copy in range(copies):
                    out_ref[part, copy, inner_index, :, group * rows : (group + 1) * rows] = packed

    each(inner_parts, spread)


def convolve(parts, filter_blocks, taps, skip, outer, tp_parts):
    blocks, streams, chans, _ = parts[0].shape
    rows = filter_blocks.shape[2]
    forward, backward = tables(rows)
    wide = (blocks, chans, 2 * rows)
    narrow = (blocks, chans, rows)
    vmem = pl.BlockSpec(memory_space=pltpu.VMEM)
    return pl.pallas_call(
        functools.partial(conv_kernel, outer, len(parts)),
        out_shape=jax.ShapeDtypeStruct(
            (tp_parts, outer, blocks // outer, chans, outer // tp_parts * rows), jnp.bfloat16
        ),
        in_specs=[vmem] * (5 + len(parts)),
        out_specs=vmem,
        scratch_shapes=[
            pltpu.VMEM((blocks + 1, streams, chans, rows), jnp.float32),
            pltpu.VMEM(narrow, jnp.float32),
            pltpu.VMEM(narrow, jnp.float32),
            pltpu.VMEM(wide, jnp.float32),
            pltpu.VMEM(wide, jnp.float32),
            pltpu.VMEM(wide, jnp.float32),
            pltpu.VMEM(wide, jnp.float32),
        ],
        compiler_params=pltpu.CompilerParams(vmem_limit_bytes=40 * 2**20),
        cost_estimate=pl.CostEstimate(flops=10**9, bytes_accessed=4 * 2**20, transcendentals=0),
    )(*parts, filter_blocks, taps, skip, jnp.asarray(forward), jnp.asarray(backward))


def out_kernel(block_ref, gated_ref, weight_ref, *refs):
    *out_refs, turned, left = refs
    tp_parts = gated_ref.shape[0]
    part_rows = out_refs[0].shape[0]

    @pl.when(pl.program_id(0) == 0)
    def _():
        for part in range(tp_parts):
            turned[...] = gated_ref[part].T
            for index in range(len(out_refs)):
                begin = pl.multiple_of(block_ref[index] * part_rows, part_rows)
                left[part, index * part_rows : (index + 1) * part_rows] = turned[pl.ds(begin, part_rows)]

    sums = jnp.zeros((left.shape[1], weight_ref.shape[3]), jnp.float32)
    for part in range(tp_parts):
        sums = sums + jnp.dot(left[part], weight_ref[0, part], preferred_element_type=jnp.float32)
    for index, out_ref in enumerate(out_refs):
        out_ref[...] = sums[index * part_rows : (index + 1) * part_rows].astype(out_ref.dtype)


def project_out(gated, weight, blocks):
    tp_parts, depth, rows = gated.shape
    inner_parts, _, _, width = weight.shape
    columns = inner_parts * width
    part_rows = rows // len(blocks)
    return pl.pallas_call(
        out_kernel,
        grid_spec=pltpu.PrefetchScalarGridSpec(
            num_scalar_prefetch=1,
            grid=(inner_parts,),
            in_specs=[
                pl.BlockSpec((tp_parts, depth, rows), lambda b, place: (0, 0, 0)),
                pl.BlockSpec((1, tp_parts, depth, width), lambda b, place: (b, 0, 0, 0)),
            ],
            out_specs=[pl.BlockSpec((part_rows, width), lambda b, place: (0, b))] * len(blocks),
            scratch_shapes=[
                pltpu.VMEM((rows, depth), jnp.bfloat16),
                pltpu.VMEM((tp_parts, rows, depth), jnp.bfloat16),
            ],
        ),
        out_shape=[jax.ShapeDtypeStruct((part_rows, columns), jnp.bfloat16)] * len(blocks),
        compiler_params=pltpu.CompilerParams(vmem_limit_bytes=16 * 2**20),
        cost_estimate=pl.CostEstimate(
            flops=2 * gated.size * columns,
            bytes_accessed=2 * (weight.size + gated.size + rows * columns),
            transcendentals=0,
        ),
    )(jnp.stack(blocks).astype(jnp.int32), gated, weight)


def per_device(features, in_proj, short_taps, long_filter, skip_gain, out_proj):
    rows = features.shape[0]
    seq_parts = lax.axis_size("seq")
    tp_parts = lax.axis_size("tp")
    outer = outer_factor(seq_parts, tp_parts)
    inner_parts = seq_parts // outer
    streams, _, chan_tp = in_proj.shape
    chans = chan_tp // seq_parts
    position = lax.axis_index("seq")
    inner_groups = [[a * inner_parts + b for b in range(inner_parts)] for a in range(outer)]
    tp_groups = [
        [index * tp_parts + tp for index in group for tp in range(tp_parts)] for group in inner_groups
    ]

    weight = lax.all_gather(in_proj, "seq", axis=1, tiled=True, axis_index_groups=inner_groups)

    taps = lax.dynamic_slice_in_dim(short_taps, position * chans, chans, axis=2)
    taps = jnp.broadcast_to(taps[..., None], taps.shape + (rows,))
    skip = lax.dynamic_slice_in_dim(skip_gain, position * chans, chans, axis=0)
    skip = jnp.broadcast_to(skip[:, None], (chans, rows))
    filter_blocks = lax.all_to_all(
        long_filter.T.reshape(seq_parts, chans, rows), "seq", split_axis=0, concat_axis=0, tiled=True
    )

    held = share_columns(features, outer, tp_parts)
    held, taps, skip, filter_blocks = lax.optimization_barrier((held, taps, skip, filter_blocks))
    arrived = cross_outer(held, outer, inner_parts, tp_parts)
    chunks = [share_over_tp(piece, tp_parts) for piece in arrived]
    chunks, out_proj = lax.optimization_barrier((chunks, out_proj))
    out_weight = lax.all_gather(out_proj, ("seq", "tp"), axis_index_groups=tp_groups)
    out_weight = out_weight.reshape((inner_parts, tp_parts) + out_proj.shape)

    partial = project_in(chunks, weight, seq_parts)
    parts = lax.all_to_all(partial, "seq", split_axis=0, concat_axis=0, tiled=True)

    parts, out_weight = lax.optimization_barrier((parts, out_weight))

    gated = convolve([parts], filter_blocks, taps, skip, outer, tp_parts)
    gated = lax.all_to_all(
        gated.reshape((-1,) + gated.shape[3:]), ("tp", "seq"), split_axis=0, concat_axis=0, tiled=True
    )
    blocks, places = return_places(outer, inner_parts, tp_parts)
    pieces = project_out(gated.reshape(tp_parts, chan_tp, -1), out_weight, blocks)
    return return_output(pieces, places, inner_parts, tp_parts)


def solution(mesh):
    return jax.shard_map(
        per_device,
        mesh=mesh,
        in_specs=(
            P("seq", "tp"),
            P(None, "seq", "tp"),
            P(None, None, "tp"),
            P("seq", "tp"),
            P("tp"),
            P("tp", "seq"),
        ),
        out_specs=P("seq", "tp"),
        check_vma=False,
    )
```

```python
import functools
import math

import jax
import jax.numpy as jnp
import numpy as np
from jax import lax
from jax.experimental import pallas as pl
from jax.experimental.pallas import tpu as pltpu
from jax.sharding import PartitionSpec as P

HIGHEST = lax.Precision.HIGHEST
UNROLL = 16
HEAVY = 30


def outer_factor(seq_parts, tp_parts):
    outer = tp_parts
    while 4 * outer * outer <= seq_parts and seq_parts % (2 * outer) == 0:
        outer *= 2
    return outer


def assemble_kernel(place_ref, *refs):
    *piece_refs, out_ref, sems = refs
    part_rows, width = piece_refs[0].shape
    copies = []
    for index, piece_ref in enumerate(piece_refs):
        row = pl.multiple_of(place_ref[2 * index] * part_rows, part_rows)
        column = pl.multiple_of(place_ref[2 * index + 1] * width, width)
        target = out_ref.at[pl.ds(row, part_rows), pl.ds(column, width)]
        copies.append(pltpu.make_async_copy(piece_ref, target, sems.at[index]))
    for copy in copies:
        copy.start()
    for copy in copies:
        copy.wait()


def assemble(pieces, places, shape):
    return pl.pallas_call(
        assemble_kernel,
        in_specs=[pl.BlockSpec(memory_space=pltpu.SMEM)]
        + [pl.BlockSpec(memory_space=pltpu.VMEM)] * len(pieces),
        out_specs=pl.BlockSpec(memory_space=pl.ANY),
        out_shape=jax.ShapeDtypeStruct(shape, pieces[0].dtype),
        scratch_shapes=[pltpu.SemaphoreType.DMA((len(pieces),))],
        compiler_params=pltpu.CompilerParams(vmem_limit_bytes=4 * 2**20),
        cost_estimate=pl.CostEstimate(
            flops=0, bytes_accessed=4 * shape[0] * shape[1], transcendentals=0
        ),
    )(jnp.stack(places).astype(jnp.int32), *pieces)


def return_places(outer, inner_parts, tp_parts):
    per_tp = outer // tp_parts
    tp_place = lax.axis_index("tp")
    outer_place = lax.axis_index("seq") // inner_parts
    blocks, places = [], []
    for far in range(tp_parts):
        for near in range(per_tp):
            low = outer_place % per_tp
            blocks.append((tp_place + low + far) % tp_parts * per_tp + (low + near) % per_tp)
            low = (low - near + per_tp) % per_tp
            places.append((outer_place // per_tp - far - low + tp_parts + per_tp * tp_parts) % tp_parts)
            places.append(low)
    return blocks, places


def return_output(pieces, places, inner_parts, tp_parts):
    outer = len(pieces)
    part_rows, width = pieces[0].shape
    per_tp = outer // tp_parts
    arrived = []
    for index, piece in enumerate(pieces):
        far, near = divmod(index, per_tp)

        def target(seq, tp):
            src = seq // inner_parts
            low = src % per_tp
            dst = (tp + low + far) % tp_parts * per_tp + (low + near) % per_tp
            return (dst * inner_parts + seq % inner_parts) * tp_parts + src // per_tp

        pairs = [
            (seq * tp_parts + tp, target(seq, tp))
            for seq in range(outer * inner_parts)
            for tp in range(tp_parts)
        ]
        arrived.append(lax.ppermute(piece, ("seq", "tp"), pairs))
    return assemble(arrived, places, (tp_parts * part_rows, per_tp * width))


def share_columns(features, outer, tp_parts):
    rows, cols = features.shape
    per_tp = outer // tp_parts
    tp_place = lax.axis_index("tp")
    width = cols // outer
    held = []
    for step in range(tp_parts):
        which = (tp_place + step) % tp_parts
        piece = jnp.stack(
            [
                lax.dynamic_slice_in_dim(features, (group * tp_parts + which) * width, width, axis=1)
                for group in range(per_tp)
            ]
        )
        if step:
            piece = lax.ppermute(piece, "tp", [(i, (i + step) % tp_parts) for i in range(tp_parts)])
        held.append(piece)
    return jnp.concatenate(held)


def cross_outer(held, steps, outer, inner_parts, tp_parts):
    per_tp = outer // tp_parts
    seq_parts = outer * inner_parts
    tp_place = lax.axis_index("tp")
    outer_place = lax.axis_index("seq") // inner_parts
    arrived = {}
    for step in steps:
        target = (outer_place + step) % outer
        which = (tp_place - target // per_tp + tp_parts) % tp_parts * per_tp + target % per_tp
        piece = lax.dynamic_index_in_dim(held, which, axis=0, keepdims=False)
        if step:
            far = step * inner_parts
            piece = lax.ppermute(piece, "seq", [(i, (i + far) % seq_parts) for i in range(seq_parts)])
        arrived[step] = piece
    return arrived


def share_over_tp(part, tp_parts):
    pieces = [part]
    for step in range(1, tp_parts):
        pairs = [(i, (i + step) % tp_parts) for i in range(tp_parts)]
        pieces.append(lax.ppermute(part, "tp", pairs))
    return pieces


def project_kernel(tp_parts, place_ref, *refs):
    *share_refs, weight_ref, out_ref = refs
    seq_parts, _, chans, count = out_ref.shape
    sums = jnp.zeros((count, seq_parts * chans), jnp.float32)
    for step in range(tp_parts):
        which = lax.rem(place_ref[0] - step + tp_parts, tp_parts)
        left = jnp.concatenate([share_ref[...] for share_ref in share_refs[step::tp_parts]])
        sums = sums + jnp.dot(left, weight_ref[0, which], preferred_element_type=jnp.float32)
    turned = sums.astype(out_ref.dtype).T
    for seq in range(seq_parts):
        out_ref[seq, 0] = turned[seq * chans : (seq + 1) * chans]


def project_in(chunks, weight, seq_parts):
    tp_parts = len(chunks[0])
    rows, width = chunks[0][0].shape
    streams, _, chan_tp = weight.shape
    weight = weight.reshape(streams, tp_parts, width, chan_tp)
    chans = chan_tp // seq_parts
    pieces = [piece for chunk in chunks for piece in chunk]
    count = len(chunks) * rows
    place = lax.axis_index("tp").astype(jnp.int32)[None]
    return pl.pallas_call(
        functools.partial(project_kernel, tp_parts),
        grid_spec=pltpu.PrefetchScalarGridSpec(
            num_scalar_prefetch=1,
            grid=(streams,),
            in_specs=[pl.BlockSpec((rows, width), lambda i, place: (0, 0))] * len(pieces)
            + [pl.BlockSpec((1, tp_parts, width, chan_tp), lambda i, place: (i, 0, 0, 0))],
            out_specs=pl.BlockSpec((seq_parts, 1, chans, count), lambda i, place: (0, i, 0, 0)),
        ),
        out_shape=jax.ShapeDtypeStruct((seq_parts, streams, chans, count), jnp.bfloat16),
        compiler_params=pltpu.CompilerParams(vmem_limit_bytes=56 * 2**20),
        cost_estimate=pl.CostEstimate(
            flops=HEAVY * 2 * count * weight.size,
            bytes_accessed=2 * (weight.size + len(pieces) * pieces[0].size)
            + 2 * streams * count * chan_tp,
            transcendentals=0,
        ),
    )(place, *pieces, weight)


def tables(block):
    place = np.arange(block)
    angle = 2.0 * math.pi * np.outer(place, place + 0.5) / (2 * block)
    forward = np.concatenate([np.cos(angle), -np.sin(angle)], 1)
    place = np.arange(2 * block)
    angle = 2.0 * math.pi * np.outer(np.arange(block) + 0.5, place) / (2 * block)
    backward = np.concatenate([np.cos(angle), -np.sin(angle)], 0) / block
    return forward.astype(np.float32), backward.astype(np.float32)


def each(count, body):
    if isinstance(count, int) and count <= UNROLL:
        for index in range(count):
            body(index)
    else:
        lax.fori_loop(0, count, lambda index, carry: (body(index), carry)[1], 0)


def total(count, term, zero):
    if isinstance(count, int) and count <= UNROLL:
        result = zero
        for index in range(count):
            result = jax.tree.map(jnp.add, result, term(index))
        return result
    return lax.fori_loop(
        0, count, lambda index, sums: jax.tree.map(jnp.add, sums, term(index)), zero
    )


def conv_kernel(
    outer, chunks, *refs
):
    part_refs, refs = refs[:chunks], refs[chunks:]
    filter_ref, taps_ref, skip_ref, fwd_ref, bwd_ref, out_ref, *refs = refs
    proj, query, inner, spec, filter_spec, product, back = refs
    blocks, streams, chans, _ = part_refs[0].shape
    rows = filter_ref.shape[2]
    inner_parts = blocks // outer
    taps_count = taps_ref.shape[1]
    lane = lax.broadcasted_iota(jnp.int32, (chans, rows), 1)

    depth = outer // chunks

    def add_up(inner_index, stream, group):
        value = jnp.zeros((chans, rows), jnp.float32)
        for part in range(outer):
            slot = (part - group) % outer
            column = slice(slot % depth * rows, (slot % depth + 1) * rows)
            source = part_refs[slot // depth]
            value = value + source[part * inner_parts + inner_index, stream, :, column].astype(jnp.float32)
        proj[1 + group * inner_parts + inner_index, stream] = value

    for group in range(outer):
        for stream in range(streams):
            each(inner_parts, functools.partial(add_up, stream=stream, group=group))

    for stream in range(streams):
        proj[0, stream] = jnp.zeros((chans, rows), jnp.float32)

    def first(index):
        filtered = []
        for stream in range(streams):
            now, past = proj[index + 1, stream], proj[index, stream]
            value = taps_ref[stream, 0] * now
            for offset in range(1, taps_count):
                moved = jnp.where(
                    lane < offset, pltpu.roll(past, offset, 1), pltpu.roll(now, offset, 1)
                )
                value = value + taps_ref[stream, offset] * moved
            filtered.append(value)
        query[index] = filtered[0]
        inner[index] = filtered[1] * filtered[2]

    each(blocks, first)

    def apply(source, table_ref, target):
        if chans % 8 == 0:
            flat = source[...].reshape(blocks * chans, source.shape[2])
            done = jnp.dot(flat, table_ref[...], precision=HIGHEST, preferred_element_type=jnp.float32)
            target[...] = done.reshape(target.shape)
        else:

            def one(index):
                target[index] = jnp.dot(
                    source[index], table_ref[...], precision=HIGHEST, preferred_element_type=jnp.float32
                )

            each(blocks, one)

    apply(filter_ref, fwd_ref, filter_spec)
    apply(inner, fwd_ref, spec)

    def multiply(index):
        def term(step):
            left, right = spec[step], filter_spec[index - step]
            left_real, left_imag = left[:, :rows], left[:, rows:]
            right_real, right_imag = right[:, :rows], right[:, rows:]
            return (
                left_real * right_real - left_imag * right_imag,
                left_real * right_imag + left_imag * right_real,
            )

        zero = jnp.zeros((chans, rows), jnp.float32)
        real, imag = total(index + 1, term, (zero, zero))
        product[index, :, :rows] = real
        product[index, :, rows:] = imag

    each(blocks, multiply)
    apply(product, bwd_ref, back)

    def last(index, carried):
        long_mix = back[index, :, :rows] + carried
        query[index] = query[index] * (long_mix + skip_ref[...] * inner[index])

    last(0, jnp.zeros((chans, rows), jnp.float32))
    each(blocks - 1, lambda index: last(index + 1, back[index, :, rows:]))

    tp_parts = out_ref.shape[0]
    part_rows = rows // tp_parts
    copies = out_ref.shape[1]

    def spread(inner_index):
        for part in range(tp_parts):
            for group in range(outer // tp_parts):
                packed = jnp.zeros((chans, rows), jnp.float32)
                for place in range(tp_parts):
                    block = query[(group * tp_parts + place) * inner_parts + inner_index]
                    shift = (place - part) * part_rows % rows
                    block = pltpu.roll(block, shift, 1) if shift else block
                    packed = jnp.where(lane // part_rows == place, block, packed)
                packed = packed.astype(out_ref.dtype)
                for copy in range(copies):
                    out_ref[part, copy, inner_index, :, group * rows : (group + 1) * rows] = packed

    each(inner_parts, spread)


def convolve(parts, filter_blocks, taps, skip, outer, tp_parts):
    blocks, streams, chans, _ = parts[0].shape
    rows = filter_blocks.shape[2]
    forward, backward = tables(rows)
    wide = (blocks, chans, 2 * rows)
    narrow = (blocks, chans, rows)
    vmem = pl.BlockSpec(memory_space=pltpu.VMEM)
    return pl.pallas_call(
        functools.partial(conv_kernel, outer, len(parts)),
        out_shape=jax.ShapeDtypeStruct(
            (tp_parts, outer, blocks // outer, chans, outer // tp_parts * rows), jnp.bfloat16
        ),
        in_specs=[vmem] * (5 + len(parts)),
        out_specs=vmem,
        scratch_shapes=[
            pltpu.VMEM((blocks + 1, streams, chans, rows), jnp.float32),
            pltpu.VMEM(narrow, jnp.float32),
            pltpu.VMEM(narrow, jnp.float32),
            pltpu.VMEM(wide, jnp.float32),
            pltpu.VMEM(wide, jnp.float32),
            pltpu.VMEM(wide, jnp.float32),
            pltpu.VMEM(wide, jnp.float32),
        ],
        compiler_params=pltpu.CompilerParams(vmem_limit_bytes=40 * 2**20),
        cost_estimate=pl.CostEstimate(flops=10**9, bytes_accessed=4 * 2**20, transcendentals=0),
    )(*parts, filter_blocks, taps, skip, jnp.asarray(forward), jnp.asarray(backward))


def out_kernel(block_ref, gated_ref, weight_ref, *refs):
    *out_refs, turned, left = refs
    tp_parts = gated_ref.shape[0]
    part_rows = out_refs[0].shape[0]

    @pl.when(pl.program_id(0) == 0)
    def _():
        for part in range(tp_parts):
            turned[...] = gated_ref[part].T
            for index in range(len(out_refs)):
                begin = pl.multiple_of(block_ref[index] * part_rows, part_rows)
                left[part, index * part_rows : (index + 1) * part_rows] = turned[pl.ds(begin, part_rows)]

    sums = jnp.zeros((left.shape[1], weight_ref.shape[3]), jnp.float32)
    for part in range(tp_parts):
        sums = sums + jnp.dot(left[part], weight_ref[0, part], preferred_element_type=jnp.float32)
    for index, out_ref in enumerate(out_refs):
        out_ref[...] = sums[index * part_rows : (index + 1) * part_rows].astype(out_ref.dtype)


def project_out(gated, weight, blocks):
    tp_parts, depth, rows = gated.shape
    inner_parts, _, _, width = weight.shape
    columns = inner_parts * width
    part_rows = rows // len(blocks)
    return pl.pallas_call(
        out_kernel,
        grid_spec=pltpu.PrefetchScalarGridSpec(
            num_scalar_prefetch=1,
            grid=(inner_parts,),
            in_specs=[
                pl.BlockSpec((tp_parts, depth, rows), lambda b, place: (0, 0, 0)),
                pl.BlockSpec((1, tp_parts, depth, width), lambda b, place: (b, 0, 0, 0)),
            ],
            out_specs=[pl.BlockSpec((part_rows, width), lambda b, place: (0, b))] * len(blocks),
            scratch_shapes=[
                pltpu.VMEM((rows, depth), jnp.bfloat16),
                pltpu.VMEM((tp_parts, rows, depth), jnp.bfloat16),
            ],
        ),
        out_shape=[jax.ShapeDtypeStruct((part_rows, columns), jnp.bfloat16)] * len(blocks),
        compiler_params=pltpu.CompilerParams(vmem_limit_bytes=16 * 2**20),
        cost_estimate=pl.CostEstimate(
            flops=2 * gated.size * columns,
            bytes_accessed=2 * (weight.size + gated.size + rows * columns),
            transcendentals=0,
        ),
    )(jnp.stack(blocks).astype(jnp.int32), gated, weight)


def per_device(features, in_proj, short_taps, long_filter, skip_gain, out_proj):
    rows = features.shape[0]
    seq_parts = lax.axis_size("seq")
    tp_parts = lax.axis_size("tp")
    outer = outer_factor(seq_parts, tp_parts)
    inner_parts = seq_parts // outer
    streams, _, chan_tp = in_proj.shape
    chans = chan_tp // seq_parts
    position = lax.axis_index("seq")
    inner_groups = [[a * inner_parts + b for b in range(inner_parts)] for a in range(outer)]
    tp_groups = [
        [index * tp_parts + tp for index in group for tp in range(tp_parts)] for group in inner_groups
    ]

    weight = lax.all_gather(in_proj, "seq", axis=1, tiled=True, axis_index_groups=inner_groups)

    taps = lax.dynamic_slice_in_dim(short_taps, position * chans, chans, axis=2)
    taps = jnp.broadcast_to(taps[..., None], taps.shape + (rows,))
    skip = lax.dynamic_slice_in_dim(skip_gain, position * chans, chans, axis=0)
    skip = jnp.broadcast_to(skip[:, None], (chans, rows))
    filter_blocks = lax.all_to_all(
        long_filter.T.reshape(seq_parts, chans, rows), "seq", split_axis=0, concat_axis=0, tiled=True
    )

    held = share_columns(features, outer, tp_parts)
    held, taps, skip, filter_blocks = lax.optimization_barrier((held, taps, skip, filter_blocks))
    arrived = cross_outer(held, sorted({0, 1, outer - 1}), outer, inner_parts, tp_parts)
    own = share_over_tp(arrived[0], tp_parts)
    held, arrived[1], own = lax.optimization_barrier((held, arrived[1], own))
    arrived |= cross_outer(held, range(2, outer - 1), outer, inner_parts, tp_parts)
    chunks = [own] + [share_over_tp(arrived[step], tp_parts) for step in range(1, outer)]
    chunks, out_proj = lax.optimization_barrier((chunks, out_proj))
    out_weight = lax.all_gather(out_proj, ("seq", "tp"), axis_index_groups=tp_groups)
    out_weight = out_weight.reshape((inner_parts, tp_parts) + out_proj.shape)

    partial = project_in(chunks, weight, seq_parts)
    parts = lax.all_to_all(partial, "seq", split_axis=0, concat_axis=0, tiled=True)

    parts, out_weight = lax.optimization_barrier((parts, out_weight))

    gated = convolve([parts], filter_blocks, taps, skip, outer, tp_parts)
    gated = lax.all_to_all(
        gated.reshape((-1,) + gated.shape[3:]), ("tp", "seq"), split_axis=0, concat_axis=0, tiled=True
    )
    blocks, places = return_places(outer, inner_parts, tp_parts)
    pieces = project_out(gated.reshape(tp_parts, chan_tp, -1), out_weight, blocks)
    return return_output(pieces, places, inner_parts, tp_parts)


def solution(mesh):
    return jax.shard_map(
        per_device,
        mesh=mesh,
        in_specs=(
            P("seq", "tp"),
            P(None, "seq", "tp"),
            P(None, None, "tp"),
            P("seq", "tp"),
            P("tp"),
            P("tp", "seq"),
        ),
        out_specs=P("seq", "tp"),
        check_vma=False,
    )
```

```python
import functools
import math

import jax
import jax.numpy as jnp
import numpy as np
from jax import lax
from jax.experimental import pallas as pl
from jax.experimental.pallas import tpu as pltpu
from jax.sharding import PartitionSpec as P

HIGHEST = lax.Precision.HIGHEST
UNROLL = 16
HEAVY = 30


def outer_factor(seq_parts, tp_parts):
    outer = tp_parts
    while 4 * outer * outer <= seq_parts and seq_parts % (2 * outer) == 0:
        outer *= 2
    return outer


def assemble_kernel(place_ref, *refs):
    *piece_refs, out_ref, sems = refs
    part_rows, width = piece_refs[0].shape
    copies = []
    for index, piece_ref in enumerate(piece_refs):
        row = pl.multiple_of(place_ref[2 * index] * part_rows, part_rows)
        column = pl.multiple_of(place_ref[2 * index + 1] * width, width)
        target = out_ref.at[pl.ds(row, part_rows), pl.ds(column, width)]
        copies.append(pltpu.make_async_copy(piece_ref, target, sems.at[index]))
    for copy in copies:
        copy.start()
    for copy in copies:
        copy.wait()


def assemble(pieces, places, shape):
    return pl.pallas_call(
        assemble_kernel,
        in_specs=[pl.BlockSpec(memory_space=pltpu.SMEM)]
        + [pl.BlockSpec(memory_space=pltpu.VMEM)] * len(pieces),
        out_specs=pl.BlockSpec(memory_space=pl.ANY),
        out_shape=jax.ShapeDtypeStruct(shape, pieces[0].dtype),
        scratch_shapes=[pltpu.SemaphoreType.DMA((len(pieces),))],
        compiler_params=pltpu.CompilerParams(vmem_limit_bytes=4 * 2**20),
        cost_estimate=pl.CostEstimate(
            flops=0, bytes_accessed=4 * shape[0] * shape[1], transcendentals=0
        ),
    )(jnp.stack(places).astype(jnp.int32), *pieces)


def return_places(outer, inner_parts, tp_parts):
    per_tp = outer // tp_parts
    tp_place = lax.axis_index("tp")
    outer_place = lax.axis_index("seq") // inner_parts
    blocks, places = [], []
    for far in range(tp_parts):
        for near in range(per_tp):
            low = outer_place % per_tp
            blocks.append((tp_place + low + far) % tp_parts * per_tp + (low + near) % per_tp)
            low = (low - near + per_tp) % per_tp
            places.append((outer_place // per_tp - far - low + tp_parts + per_tp * tp_parts) % tp_parts)
            places.append(low)
    return blocks, places


def return_output(pieces, places, inner_parts, tp_parts):
    outer = len(pieces)
    part_rows, width = pieces[0].shape
    per_tp = outer // tp_parts
    arrived = []
    for index, piece in enumerate(pieces):
        far, near = divmod(index, per_tp)

        def target(seq, tp):
            src = seq // inner_parts
            low = src % per_tp
            dst = (tp + low + far) % tp_parts * per_tp + (low + near) % per_tp
            return (dst * inner_parts + seq % inner_parts) * tp_parts + src // per_tp

        pairs = [
            (seq * tp_parts + tp, target(seq, tp))
            for seq in range(outer * inner_parts)
            for tp in range(tp_parts)
        ]
        arrived.append(lax.ppermute(piece, ("seq", "tp"), pairs))
    return assemble(arrived, places, (tp_parts * part_rows, per_tp * width))


def share_columns(features, outer, tp_parts):
    rows, cols = features.shape
    per_tp = outer // tp_parts
    tp_place = lax.axis_index("tp")
    width = cols // outer
    held = []
    for step in range(tp_parts):
        which = (tp_place + step) % tp_parts
        piece = jnp.stack(
            [
                lax.dynamic_slice_in_dim(features, (group * tp_parts + which) * width, width, axis=1)
                for group in range(per_tp)
            ]
        )
        if step:
            piece = lax.ppermute(piece, "tp", [(i, (i + step) % tp_parts) for i in range(tp_parts)])
        held.append(piece)
    return jnp.concatenate(held)


def cross_outer(held, steps, outer, inner_parts, tp_parts):
    per_tp = outer // tp_parts
    seq_parts = outer * inner_parts
    tp_place = lax.axis_index("tp")
    outer_place = lax.axis_index("seq") // inner_parts
    arrived = {}
    for step in steps:
        target = (outer_place + step) % outer
        which = (tp_place - target // per_tp + tp_parts) % tp_parts * per_tp + target % per_tp
        piece = lax.dynamic_index_in_dim(held, which, axis=0, keepdims=False)
        if step:
            far = step * inner_parts
            piece = lax.ppermute(piece, "seq", [(i, (i + far) % seq_parts) for i in range(seq_parts)])
        arrived[step] = piece
    return arrived


def share_over_tp(part, tp_parts):
    pieces = [part]
    for step in range(1, tp_parts):
        pairs = [(i, (i + step) % tp_parts) for i in range(tp_parts)]
        pieces.append(lax.ppermute(part, "tp", pairs))
    return pieces


def project_kernel(tp_parts, place_ref, *refs):
    *share_refs, weight_ref, out_ref, held, sems = refs
    seq_parts, streams, chans, count = out_ref.shape
    copies = []
    for stream in range(streams):
        for step in range(tp_parts):
            which = lax.rem(place_ref[0] - step + tp_parts, tp_parts)
            copies.append(
                pltpu.make_async_copy(
                    weight_ref.at[stream, which], held.at[stream, step], sems.at[len(copies)]
                )
            )
            copies[-1].start()
    left = [
        jnp.concatenate([share_ref[...] for share_ref in share_refs[step::tp_parts]])
        for step in range(tp_parts)
    ]
    for stream in range(streams):
        sums = jnp.zeros((count, seq_parts * chans), jnp.float32)
        for step in range(tp_parts):
            copies[stream * tp_parts + step].wait()
            sums = sums + jnp.dot(
                left[step], held[stream, step], preferred_element_type=jnp.float32
            )
        turned = sums.astype(out_ref.dtype).T
        for seq in range(seq_parts):
            out_ref[seq, stream] = turned[seq * chans : (seq + 1) * chans]


def project_in(chunks, weight, seq_parts):
    tp_parts = len(chunks[0])
    rows, width = chunks[0][0].shape
    streams, _, chan_tp = weight.shape
    weight = weight.reshape(streams, tp_parts, width, chan_tp)
    chans = chan_tp // seq_parts
    pieces = [piece for chunk in chunks for piece in chunk]
    count = len(chunks) * rows
    place = lax.axis_index("tp").astype(jnp.int32)[None]
    vmem = pl.BlockSpec(memory_space=pltpu.VMEM)
    return pl.pallas_call(
        functools.partial(project_kernel, tp_parts),
        in_specs=[pl.BlockSpec(memory_space=pltpu.SMEM)]
        + [vmem] * len(pieces)
        + [pl.BlockSpec(memory_space=pl.ANY)],
        out_specs=vmem,
        out_shape=jax.ShapeDtypeStruct((seq_parts, streams, chans, count), jnp.bfloat16),
        scratch_shapes=[
            pltpu.VMEM(weight.shape, weight.dtype),
            pltpu.SemaphoreType.DMA((streams * tp_parts,)),
        ],
        compiler_params=pltpu.CompilerParams(vmem_limit_bytes=48 * 2**20),
        cost_estimate=pl.CostEstimate(
            flops=HEAVY * 2 * count * weight.size,
            bytes_accessed=2 * (weight.size + len(pieces) * pieces[0].size)
            + 2 * streams * count * seq_parts * chans,
            transcendentals=0,
        ),
    )(place, *pieces, weight)


def tables(block):
    place = np.arange(block)
    angle = 2.0 * math.pi * np.outer(place, place + 0.5) / (2 * block)
    forward = np.concatenate([np.cos(angle), -np.sin(angle)], 1)
    place = np.arange(2 * block)
    angle = 2.0 * math.pi * np.outer(np.arange(block) + 0.5, place) / (2 * block)
    backward = np.concatenate([np.cos(angle), -np.sin(angle)], 0) / block
    return forward.astype(np.float32), backward.astype(np.float32)


def each(count, body):
    if isinstance(count, int) and count <= UNROLL:
        for index in range(count):
            body(index)
    else:
        lax.fori_loop(0, count, lambda index, carry: (body(index), carry)[1], 0)


def total(count, term, zero):
    if isinstance(count, int) and count <= UNROLL:
        result = zero
        for index in range(count):
            result = jax.tree.map(jnp.add, result, term(index))
        return result
    return lax.fori_loop(
        0, count, lambda index, sums: jax.tree.map(jnp.add, sums, term(index)), zero
    )


def conv_kernel(
    outer, chunks, *refs
):
    part_refs, refs = refs[:chunks], refs[chunks:]
    filter_ref, taps_ref, skip_ref, fwd_ref, bwd_ref, out_ref, *refs = refs
    proj, query, inner, spec, filter_spec, product, back = refs
    blocks, streams, chans, _ = part_refs[0].shape
    rows = filter_ref.shape[2]
    inner_parts = blocks // outer
    taps_count = taps_ref.shape[1]
    lane = lax.broadcasted_iota(jnp.int32, (chans, rows), 1)

    depth = outer // chunks

    def add_up(inner_index, stream, group):
        value = jnp.zeros((chans, rows), jnp.float32)
        for part in range(outer):
            slot = (part - group) % outer
            column = slice(slot % depth * rows, (slot % depth + 1) * rows)
            source = part_refs[slot // depth]
            value = value + source[part * inner_parts + inner_index, stream, :, column].astype(jnp.float32)
        proj[1 + group * inner_parts + inner_index, stream] = value

    for group in range(outer):
        for stream in range(streams):
            each(inner_parts, functools.partial(add_up, stream=stream, group=group))

    for stream in range(streams):
        proj[0, stream] = jnp.zeros((chans, rows), jnp.float32)

    def first(index):
        filtered = []
        for stream in range(streams):
            now, past = proj[index + 1, stream], proj[index, stream]
            value = taps_ref[stream, 0] * now
            for offset in range(1, taps_count):
                moved = jnp.where(
                    lane < offset, pltpu.roll(past, offset, 1), pltpu.roll(now, offset, 1)
                )
                value = value + taps_ref[stream, offset] * moved
            filtered.append(value)
        query[index] = filtered[0]
        inner[index] = filtered[1] * filtered[2]

    each(blocks, first)

    def apply(source, table_ref, target):
        if chans % 8 == 0:
            flat = source[...].reshape(blocks * chans, source.shape[2])
            done = jnp.dot(flat, table_ref[...], precision=HIGHEST, preferred_element_type=jnp.float32)
            target[...] = done.reshape(target.shape)
        else:

            def one(index):
                target[index] = jnp.dot(
                    source[index], table_ref[...], precision=HIGHEST, preferred_element_type=jnp.float32
                )

            each(blocks, one)

    apply(filter_ref, fwd_ref, filter_spec)
    apply(inner, fwd_ref, spec)

    def multiply(index):
        def term(step):
            left, right = spec[step], filter_spec[index - step]
            left_real, left_imag = left[:, :rows], left[:, rows:]
            right_real, right_imag = right[:, :rows], right[:, rows:]
            return (
                left_real * right_real - left_imag * right_imag,
                left_real * right_imag + left_imag * right_real,
            )

        zero = jnp.zeros((chans, rows), jnp.float32)
        real, imag = total(index + 1, term, (zero, zero))
        product[index, :, :rows] = real
        product[index, :, rows:] = imag

    each(blocks, multiply)
    apply(product, bwd_ref, back)

    def last(index, carried):
        long_mix = back[index, :, :rows] + carried
        query[index] = query[index] * (long_mix + skip_ref[...] * inner[index])

    last(0, jnp.zeros((chans, rows), jnp.float32))
    each(blocks - 1, lambda index: last(index + 1, back[index, :, rows:]))

    tp_parts = out_ref.shape[0]
    part_rows = rows // tp_parts
    copies = out_ref.shape[1]

    def spread(inner_index):
        for part in range(tp_parts):
            for group in range(outer // tp_parts):
                packed = jnp.zeros((chans, rows), jnp.float32)
                for place in range(tp_parts):
                    block = query[(group * tp_parts + place) * inner_parts + inner_index]
                    shift = (place - part) * part_rows % rows
                    block = pltpu.roll(block, shift, 1) if shift else block
                    packed = jnp.where(lane // part_rows == place, block, packed)
                packed = packed.astype(out_ref.dtype)
                for copy in range(copies):
                    out_ref[part, copy, inner_index, :, group * rows : (group + 1) * rows] = packed

    each(inner_parts, spread)


def convolve(parts, filter_blocks, taps, skip, outer, tp_parts):
    blocks, streams, chans, _ = parts[0].shape
    rows = filter_blocks.shape[2]
    forward, backward = tables(rows)
    wide = (blocks, chans, 2 * rows)
    narrow = (blocks, chans, rows)
    vmem = pl.BlockSpec(memory_space=pltpu.VMEM)
    return pl.pallas_call(
        functools.partial(conv_kernel, outer, len(parts)),
        out_shape=jax.ShapeDtypeStruct(
            (tp_parts, outer, blocks // outer, chans, outer // tp_parts * rows), jnp.bfloat16
        ),
        in_specs=[vmem] * (5 + len(parts)),
        out_specs=vmem,
        scratch_shapes=[
            pltpu.VMEM((blocks + 1, streams, chans, rows), jnp.float32),
            pltpu.VMEM(narrow, jnp.float32),
            pltpu.VMEM(narrow, jnp.float32),
            pltpu.VMEM(wide, jnp.float32),
            pltpu.VMEM(wide, jnp.float32),
            pltpu.VMEM(wide, jnp.float32),
            pltpu.VMEM(wide, jnp.float32),
        ],
        compiler_params=pltpu.CompilerParams(vmem_limit_bytes=40 * 2**20),
        cost_estimate=pl.CostEstimate(flops=10**9, bytes_accessed=4 * 2**20, transcendentals=0),
    )(*parts, filter_blocks, taps, skip, jnp.asarray(forward), jnp.asarray(backward))


def out_kernel(block_ref, gated_ref, weight_ref, *refs):
    *out_refs, turned, left, held, sems = refs
    tp_parts = gated_ref.shape[0]
    part_rows = out_refs[0].shape[0]
    inner_parts, _, _, width = held.shape
    copies = [
        pltpu.make_async_copy(weight_ref.at[inner], held.at[inner], sems.at[inner])
        for inner in range(inner_parts)
    ]
    for copy in copies:
        copy.start()
    for part in range(tp_parts):
        turned[...] = gated_ref[part].T
        for index in range(len(out_refs)):
            begin = pl.multiple_of(block_ref[index] * part_rows, part_rows)
            left[part, index * part_rows : (index + 1) * part_rows] = turned[pl.ds(begin, part_rows)]
    for inner in range(inner_parts):
        copies[inner].wait()
        sums = jnp.zeros((left.shape[1], width), jnp.float32)
        for part in range(tp_parts):
            sums = sums + jnp.dot(left[part], held[inner, part], preferred_element_type=jnp.float32)
        for index, out_ref in enumerate(out_refs):
            out_ref[:, inner * width : (inner + 1) * width] = sums[
                index * part_rows : (index + 1) * part_rows
            ].astype(out_ref.dtype)


def project_out(gated, weight, blocks):
    tp_parts, depth, rows = gated.shape
    inner_parts, _, _, width = weight.shape
    columns = inner_parts * width
    part_rows = rows // len(blocks)
    vmem = pl.BlockSpec(memory_space=pltpu.VMEM)
    return pl.pallas_call(
        out_kernel,
        in_specs=[
            pl.BlockSpec(memory_space=pltpu.SMEM),
            vmem,
            pl.BlockSpec(memory_space=pl.ANY),
        ],
        out_specs=[vmem] * len(blocks),
        scratch_shapes=[
            pltpu.VMEM((rows, depth), jnp.bfloat16),
            pltpu.VMEM((tp_parts, rows, depth), jnp.bfloat16),
            pltpu.VMEM(weight.shape, weight.dtype),
            pltpu.SemaphoreType.DMA((inner_parts,)),
        ],
        out_shape=[jax.ShapeDtypeStruct((part_rows, columns), jnp.bfloat16)] * len(blocks),
        compiler_params=pltpu.CompilerParams(vmem_limit_bytes=52 * 2**20),
        cost_estimate=pl.CostEstimate(
            flops=2 * gated.size * columns,
            bytes_accessed=2 * (weight.size + gated.size + rows * columns),
            transcendentals=0,
        ),
    )(jnp.stack(blocks).astype(jnp.int32), gated, weight)


def per_device(features, in_proj, short_taps, long_filter, skip_gain, out_proj):
    rows = features.shape[0]
    seq_parts = lax.axis_size("seq")
    tp_parts = lax.axis_size("tp")
    outer = outer_factor(seq_parts, tp_parts)
    inner_parts = seq_parts // outer
    streams, _, chan_tp = in_proj.shape
    chans = chan_tp // seq_parts
    position = lax.axis_index("seq")
    inner_groups = [[a * inner_parts + b for b in range(inner_parts)] for a in range(outer)]
    tp_groups = [
        [index * tp_parts + tp for index in group for tp in range(tp_parts)] for group in inner_groups
    ]

    weight = lax.all_gather(in_proj, "seq", axis=1, tiled=True, axis_index_groups=inner_groups)

    taps = lax.dynamic_slice_in_dim(short_taps, position * chans, chans, axis=2)
    taps = jnp.broadcast_to(taps[..., None], taps.shape + (rows,))
    skip = lax.dynamic_slice_in_dim(skip_gain, position * chans, chans, axis=0)
    skip = jnp.broadcast_to(skip[:, None], (chans, rows))
    filter_blocks = lax.all_to_all(
        long_filter.T.reshape(seq_parts, chans, rows), "seq", split_axis=0, concat_axis=0, tiled=True
    )

    held = share_columns(features, outer, tp_parts)
    arrived = cross_outer(held, (0, 1), outer, inner_parts, tp_parts)
    held, taps, skip, filter_blocks = lax.optimization_barrier((held, taps, skip, filter_blocks))
    if outer > 2:
        arrived |= cross_outer(held, (outer - 1,), outer, inner_parts, tp_parts)
    own = share_over_tp(arrived[0], tp_parts)
    held, arrived[1], own = lax.optimization_barrier((held, arrived[1], own))
    arrived |= cross_outer(held, range(2, outer - 1), outer, inner_parts, tp_parts)
    chunks = [own] + [share_over_tp(arrived[step], tp_parts) for step in range(1, outer)]
    chunks, out_proj = lax.optimization_barrier((chunks, out_proj))
    out_weight = lax.all_gather(out_proj, ("seq", "tp"), axis_index_groups=tp_groups)
    out_weight = out_weight.reshape((inner_parts, tp_parts) + out_proj.shape)

    partial = project_in(chunks, weight, seq_parts)
    parts = lax.all_to_all(partial, "seq", split_axis=0, concat_axis=0, tiled=True)

    parts, out_weight = lax.optimization_barrier((parts, out_weight))

    gated = convolve([parts], filter_blocks, taps, skip, outer, tp_parts)
    gated = lax.all_to_all(
        gated.reshape((-1,) + gated.shape[3:]), ("tp", "seq"), split_axis=0, concat_axis=0, tiled=True
    )
    blocks, places = return_places(outer, inner_parts, tp_parts)
    pieces = project_out(gated.reshape(tp_parts, chan_tp, -1), out_weight, blocks)
    return return_output(pieces, places, inner_parts, tp_parts)


def solution(mesh):
    return jax.shard_map(
        per_device,
        mesh=mesh,
        in_specs=(
            P("seq", "tp"),
            P(None, "seq", "tp"),
            P(None, None, "tp"),
            P("seq", "tp"),
            P("tp"),
            P("tp", "seq"),
        ),
        out_specs=P("seq", "tp"),
        check_vma=False,
    )
```

```python
import functools
import math

import jax
import jax.numpy as jnp
import numpy as np
from jax import lax
from jax.experimental import pallas as pl
from jax.experimental.pallas import tpu as pltpu
from jax.sharding import PartitionSpec as P

HIGHEST = lax.Precision.HIGHEST
UNROLL = 16
HEAVY = 30


def outer_factor(seq_parts, tp_parts):
    outer = tp_parts
    while 4 * outer * outer <= seq_parts and seq_parts % (2 * outer) == 0:
        outer *= 2
    return outer


def assemble_kernel(place_ref, *refs):
    *piece_refs, out_ref, sems = refs
    part_rows, width = piece_refs[0].shape
    copies = []
    for index, piece_ref in enumerate(piece_refs):
        row = pl.multiple_of(place_ref[2 * index] * part_rows, part_rows)
        column = pl.multiple_of(place_ref[2 * index + 1] * width, width)
        target = out_ref.at[pl.ds(row, part_rows), pl.ds(column, width)]
        copies.append(pltpu.make_async_copy(piece_ref, target, sems.at[index]))
    for copy in copies:
        copy.start()
    for copy in copies:
        copy.wait()


def assemble(pieces, places, shape):
    return pl.pallas_call(
        assemble_kernel,
        in_specs=[pl.BlockSpec(memory_space=pltpu.SMEM)]
        + [pl.BlockSpec(memory_space=pltpu.VMEM)] * len(pieces),
        out_specs=pl.BlockSpec(memory_space=pl.ANY),
        out_shape=jax.ShapeDtypeStruct(shape, pieces[0].dtype),
        scratch_shapes=[pltpu.SemaphoreType.DMA((len(pieces),))],
        compiler_params=pltpu.CompilerParams(vmem_limit_bytes=4 * 2**20),
        cost_estimate=pl.CostEstimate(
            flops=0, bytes_accessed=4 * shape[0] * shape[1], transcendentals=0
        ),
    )(jnp.stack(places).astype(jnp.int32), *pieces)


def return_places(outer, inner_parts, tp_parts):
    per_tp = outer // tp_parts
    tp_place = lax.axis_index("tp")
    outer_place = lax.axis_index("seq") // inner_parts
    blocks, places = [], []
    for far in range(tp_parts):
        for near in range(per_tp):
            low = outer_place % per_tp
            blocks.append((tp_place + low + far) % tp_parts * per_tp + (low + near) % per_tp)
            low = (low - near + per_tp) % per_tp
            places.append((outer_place // per_tp - far - low + tp_parts + per_tp * tp_parts) % tp_parts)
            places.append(low)
    return blocks, places


def return_output(pieces, places, inner_parts, tp_parts):
    outer = len(pieces)
    part_rows, width = pieces[0].shape
    per_tp = outer // tp_parts
    arrived = []
    for index, piece in enumerate(pieces):
        far, near = divmod(index, per_tp)

        def target(seq, tp):
            src = seq // inner_parts
            low = src % per_tp
            dst = (tp + low + far) % tp_parts * per_tp + (low + near) % per_tp
            return (dst * inner_parts + seq % inner_parts) * tp_parts + src // per_tp

        pairs = [
            (seq * tp_parts + tp, target(seq, tp))
            for seq in range(outer * inner_parts)
            for tp in range(tp_parts)
        ]
        arrived.append(lax.ppermute(piece, ("seq", "tp"), pairs))
    return assemble(arrived, places, (tp_parts * part_rows, per_tp * width))


def share_columns(features, outer, tp_parts):
    rows, cols = features.shape
    per_tp = outer // tp_parts
    tp_place = lax.axis_index("tp")
    width = cols // outer
    held = []
    for step in range(tp_parts):
        which = (tp_place + step) % tp_parts
        piece = jnp.stack(
            [
                lax.dynamic_slice_in_dim(features, (group * tp_parts + which) * width, width, axis=1)
                for group in range(per_tp)
            ]
        )
        if step:
            piece = lax.ppermute(piece, "tp", [(i, (i + step) % tp_parts) for i in range(tp_parts)])
        held.append(piece)
    return jnp.concatenate(held)


def cross_outer(held, steps, outer, inner_parts, tp_parts):
    per_tp = outer // tp_parts
    seq_parts = outer * inner_parts
    tp_place = lax.axis_index("tp")
    outer_place = lax.axis_index("seq") // inner_parts
    arrived = {}
    for step in steps:
        target = (outer_place + step) % outer
        which = (tp_place - target // per_tp + tp_parts) % tp_parts * per_tp + target % per_tp
        piece = lax.dynamic_index_in_dim(held, which, axis=0, keepdims=False)
        if step:
            far = step * inner_parts
            piece = lax.ppermute(piece, "seq", [(i, (i + far) % seq_parts) for i in range(seq_parts)])
        arrived[step] = piece
    return arrived


def share_over_tp(part, tp_parts):
    pieces = [part]
    for step in range(1, tp_parts):
        pairs = [(i, (i + step) % tp_parts) for i in range(tp_parts)]
        pieces.append(lax.ppermute(part, "tp", pairs))
    return pieces


def project_kernel(tp_parts, place_ref, *refs):
    *share_refs, weight_ref, out_ref, held, sems = refs
    seq_parts, streams, chans, count = out_ref.shape
    copies = []
    for stream in range(streams):
        for step in range(tp_parts):
            which = lax.rem(place_ref[0] - step + tp_parts, tp_parts)
            copies.append(
                pltpu.make_async_copy(
                    weight_ref.at[stream, which], held.at[stream, step], sems.at[len(copies)]
                )
            )
            copies[-1].start()
    left = [
        jnp.concatenate([share_ref[...] for share_ref in share_refs[step::tp_parts]])
        for step in range(tp_parts)
    ]
    for stream in range(streams):
        sums = jnp.zeros((count, seq_parts * chans), jnp.float32)
        for step in range(tp_parts):
            copies[stream * tp_parts + step].wait()
            sums = sums + jnp.dot(
                left[step], held[stream, step], preferred_element_type=jnp.float32
            )
        turned = sums.astype(out_ref.dtype).T
        for seq in range(seq_parts):
            out_ref[seq, stream] = turned[seq * chans : (seq + 1) * chans]


def project_in(chunks, weight, seq_parts):
    tp_parts = len(chunks[0])
    rows, width = chunks[0][0].shape
    streams, _, chan_tp = weight.shape
    weight = weight.reshape(streams, tp_parts, width, chan_tp)
    chans = chan_tp // seq_parts
    pieces = [piece for chunk in chunks for piece in chunk]
    count = len(chunks) * rows
    place = lax.axis_index("tp").astype(jnp.int32)[None]
    vmem = pl.BlockSpec(memory_space=pltpu.VMEM)
    return pl.pallas_call(
        functools.partial(project_kernel, tp_parts),
        in_specs=[pl.BlockSpec(memory_space=pltpu.SMEM)]
        + [vmem] * len(pieces)
        + [pl.BlockSpec(memory_space=pl.ANY)],
        out_specs=vmem,
        out_shape=jax.ShapeDtypeStruct((seq_parts, streams, chans, count), jnp.bfloat16),
        scratch_shapes=[
            pltpu.VMEM(weight.shape, weight.dtype),
            pltpu.SemaphoreType.DMA((streams * tp_parts,)),
        ],
        compiler_params=pltpu.CompilerParams(vmem_limit_bytes=48 * 2**20),
        cost_estimate=pl.CostEstimate(
            flops=HEAVY * 2 * count * weight.size,
            bytes_accessed=2 * (weight.size + len(pieces) * pieces[0].size)
            + 2 * streams * count * seq_parts * chans,
            transcendentals=0,
        ),
    )(place, *pieces, weight)


def tables(block):
    place = np.arange(block)
    angle = 2.0 * math.pi * np.outer(place, place + 0.5) / (2 * block)
    forward = np.concatenate([np.cos(angle), -np.sin(angle)], 1)
    place = np.arange(2 * block)
    angle = 2.0 * math.pi * np.outer(np.arange(block) + 0.5, place) / (2 * block)
    backward = np.concatenate([np.cos(angle), -np.sin(angle)], 0) / block
    return forward.astype(np.float32), backward.astype(np.float32)


def each(count, body):
    if isinstance(count, int) and count <= UNROLL:
        for index in range(count):
            body(index)
    else:
        lax.fori_loop(0, count, lambda index, carry: (body(index), carry)[1], 0)


def total(count, term, zero):
    if isinstance(count, int) and count <= UNROLL:
        result = zero
        for index in range(count):
            result = jax.tree.map(jnp.add, result, term(index))
        return result
    return lax.fori_loop(
        0, count, lambda index, sums: jax.tree.map(jnp.add, sums, term(index)), zero
    )


def conv_kernel(
    outer, chunks, *refs
):
    part_refs, refs = refs[:chunks], refs[chunks:]
    filter_ref, taps_ref, skip_ref, fwd_ref, bwd_ref, out_ref, *refs = refs
    proj, query, inner, spec, filter_spec, product, back = refs
    blocks, streams, chans, _ = part_refs[0].shape
    rows = filter_ref.shape[2]
    inner_parts = blocks // outer
    taps_count = taps_ref.shape[1]
    lane = lax.broadcasted_iota(jnp.int32, (chans, rows), 1)

    depth = outer // chunks

    def add_up(inner_index, stream, group):
        value = jnp.zeros((chans, rows), jnp.float32)
        for part in range(outer):
            slot = (part - group) % outer
            column = slice(slot % depth * rows, (slot % depth + 1) * rows)
            source = part_refs[slot // depth]
            value = value + source[part * inner_parts + inner_index, stream, :, column].astype(jnp.float32)
        proj[1 + group * inner_parts + inner_index, stream] = value

    for group in range(outer):
        for stream in range(streams):
            each(inner_parts, functools.partial(add_up, stream=stream, group=group))

    for stream in range(streams):
        proj[0, stream] = jnp.zeros((chans, rows), jnp.float32)

    def first(index):
        filtered = []
        for stream in range(streams):
            now, past = proj[index + 1, stream], proj[index, stream]
            value = taps_ref[stream, 0] * now
            for offset in range(1, taps_count):
                moved = jnp.where(
                    lane < offset, pltpu.roll(past, offset, 1), pltpu.roll(now, offset, 1)
                )
                value = value + taps_ref[stream, offset] * moved
            filtered.append(value)
        query[index] = filtered[0]
        inner[index] = filtered[1] * filtered[2]

    each(blocks, first)

    def apply(source, table_ref, target):
        if chans % 8 == 0:
            flat = source[...].reshape(blocks * chans, source.shape[2])
            done = jnp.dot(flat, table_ref[...], precision=HIGHEST, preferred_element_type=jnp.float32)
            target[...] = done.reshape(target.shape)
        else:

            def one(index):
                target[index] = jnp.dot(
                    source[index], table_ref[...], precision=HIGHEST, preferred_element_type=jnp.float32
                )

            each(blocks, one)

    apply(filter_ref, fwd_ref, filter_spec)
    apply(inner, fwd_ref, spec)

    def multiply(index):
        def term(step):
            left, right = spec[step], filter_spec[index - step]
            left_real, left_imag = left[:, :rows], left[:, rows:]
            right_real, right_imag = right[:, :rows], right[:, rows:]
            return (
                left_real * right_real - left_imag * right_imag,
                left_real * right_imag + left_imag * right_real,
            )

        zero = jnp.zeros((chans, rows), jnp.float32)
        real, imag = total(index + 1, term, (zero, zero))
        product[index, :, :rows] = real
        product[index, :, rows:] = imag

    each(blocks, multiply)
    apply(product, bwd_ref, back)

    def last(index, carried):
        long_mix = back[index, :, :rows] + carried
        query[index] = query[index] * (long_mix + skip_ref[...] * inner[index])

    last(0, jnp.zeros((chans, rows), jnp.float32))
    each(blocks - 1, lambda index: last(index + 1, back[index, :, rows:]))

    tp_parts = out_ref.shape[0]
    part_rows = rows // tp_parts
    copies = out_ref.shape[1]

    def spread(inner_index):
        for part in range(tp_parts):
            for group in range(outer // tp_parts):
                packed = jnp.zeros((chans, rows), jnp.float32)
                for place in range(tp_parts):
                    block = query[(group * tp_parts + place) * inner_parts + inner_index]
                    shift = (place - part) * part_rows % rows
                    block = pltpu.roll(block, shift, 1) if shift else block
                    packed = jnp.where(lane // part_rows == place, block, packed)
                packed = packed.astype(out_ref.dtype)
                for copy in range(copies):
                    out_ref[part, copy, inner_index, :, group * rows : (group + 1) * rows] = packed

    each(inner_parts, spread)


def convolve(parts, filter_blocks, taps, skip, outer, tp_parts):
    blocks, streams, chans, _ = parts[0].shape
    rows = filter_blocks.shape[2]
    forward, backward = tables(rows)
    wide = (blocks, chans, 2 * rows)
    narrow = (blocks, chans, rows)
    vmem = pl.BlockSpec(memory_space=pltpu.VMEM)
    return pl.pallas_call(
        functools.partial(conv_kernel, outer, len(parts)),
        out_shape=jax.ShapeDtypeStruct(
            (tp_parts, outer, blocks // outer, chans, outer // tp_parts * rows), jnp.bfloat16
        ),
        in_specs=[vmem] * (5 + len(parts)),
        out_specs=vmem,
        scratch_shapes=[
            pltpu.VMEM((blocks + 1, streams, chans, rows), jnp.float32),
            pltpu.VMEM(narrow, jnp.float32),
            pltpu.VMEM(narrow, jnp.float32),
            pltpu.VMEM(wide, jnp.float32),
            pltpu.VMEM(wide, jnp.float32),
            pltpu.VMEM(wide, jnp.float32),
            pltpu.VMEM(wide, jnp.float32),
        ],
        compiler_params=pltpu.CompilerParams(vmem_limit_bytes=40 * 2**20),
        cost_estimate=pl.CostEstimate(flops=10**9, bytes_accessed=4 * 2**20, transcendentals=0),
    )(*parts, filter_blocks, taps, skip, jnp.asarray(forward), jnp.asarray(backward))


def out_kernel(block_ref, gated_ref, weight_ref, *refs):
    *out_refs, turned, left, held, sems = refs
    tp_parts = gated_ref.shape[0]
    part_rows = out_refs[0].shape[0]
    inner_parts, _, _, width = held.shape
    copies = [
        pltpu.make_async_copy(weight_ref.at[inner], held.at[inner], sems.at[inner])
        for inner in range(inner_parts)
    ]
    for copy in copies:
        copy.start()
    for part in range(tp_parts):
        turned[...] = gated_ref[part].T
        for index in range(len(out_refs)):
            begin = pl.multiple_of(block_ref[index] * part_rows, part_rows)
            left[part, index * part_rows : (index + 1) * part_rows] = turned[pl.ds(begin, part_rows)]
    for inner in range(inner_parts):
        copies[inner].wait()
        sums = jnp.zeros((left.shape[1], width), jnp.float32)
        for part in range(tp_parts):
            sums = sums + jnp.dot(left[part], held[inner, part], preferred_element_type=jnp.float32)
        for index, out_ref in enumerate(out_refs):
            out_ref[:, inner * width : (inner + 1) * width] = sums[
                index * part_rows : (index + 1) * part_rows
            ].astype(out_ref.dtype)


def project_out(gated, weight, blocks):
    tp_parts, depth, rows = gated.shape
    inner_parts, _, _, width = weight.shape
    columns = inner_parts * width
    part_rows = rows // len(blocks)
    vmem = pl.BlockSpec(memory_space=pltpu.VMEM)
    return pl.pallas_call(
        out_kernel,
        in_specs=[
            pl.BlockSpec(memory_space=pltpu.SMEM),
            vmem,
            pl.BlockSpec(memory_space=pl.ANY),
        ],
        out_specs=[vmem] * len(blocks),
        scratch_shapes=[
            pltpu.VMEM((rows, depth), jnp.bfloat16),
            pltpu.VMEM((tp_parts, rows, depth), jnp.bfloat16),
            pltpu.VMEM(weight.shape, weight.dtype),
            pltpu.SemaphoreType.DMA((inner_parts,)),
        ],
        out_shape=[jax.ShapeDtypeStruct((part_rows, columns), jnp.bfloat16)] * len(blocks),
        compiler_params=pltpu.CompilerParams(vmem_limit_bytes=52 * 2**20),
        cost_estimate=pl.CostEstimate(
            flops=2 * gated.size * columns,
            bytes_accessed=2 * (weight.size + gated.size + rows * columns),
            transcendentals=0,
        ),
    )(jnp.stack(blocks).astype(jnp.int32), gated, weight)


def per_device(features, in_proj, short_taps, long_filter, skip_gain, out_proj):
    rows = features.shape[0]
    seq_parts = lax.axis_size("seq")
    tp_parts = lax.axis_size("tp")
    outer = outer_factor(seq_parts, tp_parts)
    inner_parts = seq_parts // outer
    streams, _, chan_tp = in_proj.shape
    chans = chan_tp // seq_parts
    position = lax.axis_index("seq")
    inner_groups = [[a * inner_parts + b for b in range(inner_parts)] for a in range(outer)]
    tp_groups = [
        [index * tp_parts + tp for index in group for tp in range(tp_parts)] for group in inner_groups
    ]

    weight = lax.all_gather(in_proj, "seq", axis=1, tiled=True, axis_index_groups=inner_groups)

    taps = lax.dynamic_slice_in_dim(short_taps, position * chans, chans, axis=2)
    taps = jnp.broadcast_to(taps[..., None], taps.shape + (rows,))
    skip = lax.dynamic_slice_in_dim(skip_gain, position * chans, chans, axis=0)
    skip = jnp.broadcast_to(skip[:, None], (chans, rows))
    filter_blocks = lax.all_to_all(
        long_filter.T.reshape(seq_parts, chans, rows), "seq", split_axis=0, concat_axis=0, tiled=True
    )

    held = share_columns(features, outer, tp_parts)
    arrived = cross_outer(held, (0, 1), outer, inner_parts, tp_parts)
    held, taps, skip, filter_blocks = lax.optimization_barrier((held, taps, skip, filter_blocks))
    if outer > 2:
        arrived |= cross_outer(held, (outer - 1,), outer, inner_parts, tp_parts)
    own = share_over_tp(arrived[0], tp_parts)
    held, arrived[1], own = lax.optimization_barrier((held, arrived[1], own))
    arrived |= cross_outer(held, range(2, outer - 1), outer, inner_parts, tp_parts)
    chunks = [own] + [share_over_tp(arrived[step], tp_parts) for step in range(1, outer)]
    chunks, out_proj = lax.optimization_barrier((chunks, out_proj))
    out_weight = lax.all_gather(out_proj, ("seq", "tp"), axis_index_groups=tp_groups)
    out_weight = out_weight.reshape((inner_parts, tp_parts) + out_proj.shape)

    partial = project_in(chunks, weight, seq_parts)
    parts = lax.all_to_all(partial, "seq", split_axis=0, concat_axis=0, tiled=True)

    gated = convolve([parts], filter_blocks, taps, skip, outer, tp_parts)
    gated = lax.all_to_all(
        gated.reshape((-1,) + gated.shape[3:]), ("tp", "seq"), split_axis=0, concat_axis=0, tiled=True
    )
    blocks, places = return_places(outer, inner_parts, tp_parts)
    pieces = project_out(gated.reshape(tp_parts, chan_tp, -1), out_weight, blocks)
    return return_output(pieces, places, inner_parts, tp_parts)


def solution(mesh):
    return jax.shard_map(
        per_device,
        mesh=mesh,
        in_specs=(
            P("seq", "tp"),
            P(None, "seq", "tp"),
            P(None, None, "tp"),
            P("seq", "tp"),
            P("tp"),
            P("tp", "seq"),
        ),
        out_specs=P("seq", "tp"),
        check_vma=False,
    )
```

```python
import functools
import math

import jax
import jax.numpy as jnp
import numpy as np
from jax import lax
from jax.experimental import pallas as pl
from jax.experimental.pallas import tpu as pltpu
from jax.sharding import PartitionSpec as P

HIGHEST = lax.Precision.HIGHEST
UNROLL = 16
HEAVY = 30


def outer_factor(seq_parts, tp_parts):
    outer = tp_parts
    while 4 * outer * outer <= seq_parts and seq_parts % (2 * outer) == 0:
        outer *= 2
    return outer


def assemble_kernel(place_ref, *refs):
    *piece_refs, out_ref, sems = refs
    part_rows, width = piece_refs[0].shape
    copies = []
    for index, piece_ref in enumerate(piece_refs):
        row = pl.multiple_of(place_ref[2 * index] * part_rows, part_rows)
        column = pl.multiple_of(place_ref[2 * index + 1] * width, width)
        target = out_ref.at[pl.ds(row, part_rows), pl.ds(column, width)]
        copies.append(pltpu.make_async_copy(piece_ref, target, sems.at[index]))
    for copy in copies:
        copy.start()
    for copy in copies:
        copy.wait()


def assemble(pieces, places, shape):
    return pl.pallas_call(
        assemble_kernel,
        in_specs=[pl.BlockSpec(memory_space=pltpu.SMEM)]
        + [pl.BlockSpec(memory_space=pltpu.VMEM)] * len(pieces),
        out_specs=pl.BlockSpec(memory_space=pl.ANY),
        out_shape=jax.ShapeDtypeStruct(shape, pieces[0].dtype),
        scratch_shapes=[pltpu.SemaphoreType.DMA((len(pieces),))],
        compiler_params=pltpu.CompilerParams(vmem_limit_bytes=4 * 2**20),
        cost_estimate=pl.CostEstimate(
            flops=0, bytes_accessed=4 * shape[0] * shape[1], transcendentals=0
        ),
    )(jnp.stack(places).astype(jnp.int32), *pieces)


def return_places(outer, inner_parts, tp_parts):
    per_tp = outer // tp_parts
    tp_place = lax.axis_index("tp")
    outer_place = lax.axis_index("seq") // inner_parts
    blocks, places = [], []
    for far in range(tp_parts):
        for near in range(per_tp):
            low = outer_place % per_tp
            blocks.append((tp_place + low + far) % tp_parts * per_tp + (low + near) % per_tp)
            low = (low - near + per_tp) % per_tp
            places.append((outer_place // per_tp - far - low + tp_parts + per_tp * tp_parts) % tp_parts)
            places.append(low)
    return blocks, places


def return_output(pieces, places, inner_parts, tp_parts):
    outer = len(pieces)
    part_rows, width = pieces[0].shape
    per_tp = outer // tp_parts
    arrived = []
    for index, piece in enumerate(pieces):
        far, near = divmod(index, per_tp)

        def target(seq, tp):
            src = seq // inner_parts
            low = src % per_tp
            dst = (tp + low + far) % tp_parts * per_tp + (low + near) % per_tp
            return (dst * inner_parts + seq % inner_parts) * tp_parts + src // per_tp

        pairs = [
            (seq * tp_parts + tp, target(seq, tp))
            for seq in range(outer * inner_parts)
            for tp in range(tp_parts)
        ]
        arrived.append(lax.ppermute(piece, ("seq", "tp"), pairs))
    return assemble(arrived, places, (tp_parts * part_rows, per_tp * width))


def share_columns(features, outer, inner_parts, tp_parts):
    _, cols = features.shape
    per_tp = outer // tp_parts
    width = cols // outer
    tp_place = lax.axis_index("tp")
    outer_place = lax.axis_index("seq") // inner_parts
    held = []
    for after in range(per_tp):
        group = (outer_place + 1 + after) % per_tp
        pieces = []
        for step in range(tp_parts):
            column = (group * tp_parts + (tp_place + step) % tp_parts) * width
            piece = lax.dynamic_slice_in_dim(features, column, width, axis=1)
            if step:
                pairs = [(i, (i + step) % tp_parts) for i in range(tp_parts)]
                piece = lax.ppermute(piece, "tp", pairs)
            pieces.append(piece)
        held.append(jnp.stack(pieces))
    return held


def cross_outer(held, steps, outer, inner_parts, tp_parts):
    per_tp = outer // tp_parts
    seq_parts = outer * inner_parts
    tp_place = lax.axis_index("tp")
    outer_place = lax.axis_index("seq") // inner_parts
    arrived = {}
    for step in steps:
        target = (outer_place + step) % outer
        which = (tp_place - target // per_tp + tp_parts) % tp_parts
        piece = lax.dynamic_index_in_dim(held[(step - 1) % per_tp], which, axis=0, keepdims=False)
        if step:
            far = step * inner_parts
            piece = lax.ppermute(piece, "seq", [(i, (i + far) % seq_parts) for i in range(seq_parts)])
        arrived[step] = piece
    return arrived


def share_over_tp(part, tp_parts):
    pieces = [part]
    for step in range(1, tp_parts):
        pairs = [(i, (i + step) % tp_parts) for i in range(tp_parts)]
        pieces.append(lax.ppermute(part, "tp", pairs))
    return pieces


def gather_inner(block, inner_parts, settle):
    held, masks = [block], [0]
    bit = inner_parts // 2
    while bit:
        pairs = [(i, i ^ bit) for i in range(lax.axis_size("seq"))]
        held += [lax.ppermute(piece, "seq", pairs) for piece in held]
        masks += [mask ^ bit for mask in masks]
        if bit == inner_parts // 2:
            held = settle(held)
        bit //= 2
    return held, masks


def project_kernel(tp_parts, masks, place_ref, *refs):
    *refs, out_ref, left = refs
    share_refs, weight_refs = refs[: -len(masks)], refs[-len(masks) :]
    seq_parts, streams, chans, count = out_ref.shape
    blocks, rows, width = len(masks) // tp_parts, share_refs[0].shape[0], left.shape[2]
    for index, share_ref in enumerate(share_refs):
        chunk, step = divmod(index, tp_parts)
        for block in range(blocks):
            left[step * blocks + block, chunk * rows : (chunk + 1) * rows] = share_ref[
                :, block * width : (block + 1) * width
            ]
    slots = []
    for mask in masks:
        inner = jnp.bitwise_xor(place_ref[1], mask)
        step = lax.rem(place_ref[0] - inner // blocks + tp_parts, tp_parts)
        slots.append(step * blocks + lax.rem(inner, blocks))
    for stream in range(streams):
        sums = jnp.zeros((count, seq_parts * chans), jnp.float32)
        for slot, weight_ref in zip(slots, weight_refs):
            sums = sums + jnp.dot(left[slot], weight_ref[stream], preferred_element_type=jnp.float32)
        turned = sums.astype(out_ref.dtype).T
        for seq in range(seq_parts):
            out_ref[seq, stream] = turned[seq * chans : (seq + 1) * chans]


def project_in(chunks, weights, masks, inner_parts, seq_parts):
    tp_parts = len(chunks[0])
    rows, _ = chunks[0][0].shape
    streams, width, chan_tp = weights[0].shape
    chans = chan_tp // seq_parts
    pieces = [piece for chunk in chunks for piece in chunk]
    count = len(chunks) * rows
    place = jnp.stack([lax.axis_index("tp"), lax.axis_index("seq") % inner_parts]).astype(jnp.int32)
    vmem = pl.BlockSpec(memory_space=pltpu.VMEM)
    size = len(weights) * weights[0].size
    return pl.pallas_call(
        functools.partial(project_kernel, tp_parts, masks),
        in_specs=[pl.BlockSpec(memory_space=pltpu.SMEM)] + [vmem] * (len(pieces) + len(weights)),
        out_specs=vmem,
        out_shape=jax.ShapeDtypeStruct((seq_parts, streams, chans, count), jnp.bfloat16),
        scratch_shapes=[pltpu.VMEM((len(masks), count, width), jnp.bfloat16)],
        compiler_params=pltpu.CompilerParams(vmem_limit_bytes=32 * 2**20),
        cost_estimate=pl.CostEstimate(
            flops=HEAVY * 2 * count * size,
            bytes_accessed=2 * (size + len(pieces) * pieces[0].size)
            + 2 * streams * count * seq_parts * chans,
            transcendentals=0,
        ),
    )(place, *pieces, *weights)


def tables(block):
    place = np.arange(block)
    angle = 2.0 * math.pi * np.outer(place, place + 0.5) / (2 * block)
    forward = np.concatenate([np.cos(angle), -np.sin(angle)], 1)
    place = np.arange(2 * block)
    angle = 2.0 * math.pi * np.outer(np.arange(block) + 0.5, place) / (2 * block)
    backward = np.concatenate([np.cos(angle), -np.sin(angle)], 0) / block
    return forward.astype(np.float32), backward.astype(np.float32)


def each(count, body):
    if isinstance(count, int) and count <= UNROLL:
        for index in range(count):
            body(index)
    else:
        lax.fori_loop(0, count, lambda index, carry: (body(index), carry)[1], 0)


def total(count, term, zero):
    if isinstance(count, int) and count <= UNROLL:
        result = zero
        for index in range(count):
            result = jax.tree.map(jnp.add, result, term(index))
        return result
    return lax.fori_loop(
        0, count, lambda index, sums: jax.tree.map(jnp.add, sums, term(index)), zero
    )


def conv_kernel(
    outer, chunks, *refs
):
    part_refs, refs = refs[:chunks], refs[chunks:]
    filter_ref, taps_ref, skip_ref, fwd_ref, bwd_ref, out_ref, *refs = refs
    proj, query, inner, spec, filter_spec, product, back = refs
    blocks, streams, chans, _ = part_refs[0].shape
    rows = filter_ref.shape[2]
    inner_parts = blocks // outer
    taps_count = taps_ref.shape[1]
    lane = lax.broadcasted_iota(jnp.int32, (chans, rows), 1)

    depth = outer // chunks

    def add_up(inner_index, stream, group):
        value = jnp.zeros((chans, rows), jnp.float32)
        for part in range(outer):
            slot = (part - group) % outer
            column = slice(slot % depth * rows, (slot % depth + 1) * rows)
            source = part_refs[slot // depth]
            value = value + source[part * inner_parts + inner_index, stream, :, column].astype(jnp.float32)
        proj[1 + group * inner_parts + inner_index, stream] = value

    for group in range(outer):
        for stream in range(streams):
            each(inner_parts, functools.partial(add_up, stream=stream, group=group))

    for stream in range(streams):
        proj[0, stream] = jnp.zeros((chans, rows), jnp.float32)

    def first(index):
        filtered = []
        for stream in range(streams):
            now, past = proj[index + 1, stream], proj[index, stream]
            value = taps_ref[stream, 0] * now
            for offset in range(1, taps_count):
                moved = jnp.where(
                    lane < offset, pltpu.roll(past, offset, 1), pltpu.roll(now, offset, 1)
                )
                value = value + taps_ref[stream, offset] * moved
            filtered.append(value)
        query[index] = filtered[0]
        inner[index] = filtered[1] * filtered[2]

    each(blocks, first)

    def apply(source, table_ref, target):
        if chans % 8 == 0:
            flat = source[...].reshape(blocks * chans, source.shape[2])
            done = jnp.dot(flat, table_ref[...], precision=HIGHEST, preferred_element_type=jnp.float32)
            target[...] = done.reshape(target.shape)
        else:

            def one(index):
                target[index] = jnp.dot(
                    source[index], table_ref[...], precision=HIGHEST, preferred_element_type=jnp.float32
                )

            each(blocks, one)

    apply(filter_ref, fwd_ref, filter_spec)
    apply(inner, fwd_ref, spec)

    def multiply(index):
        def term(step):
            left, right = spec[step], filter_spec[index - step]
            left_real, left_imag = left[:, :rows], left[:, rows:]
            right_real, right_imag = right[:, :rows], right[:, rows:]
            return (
                left_real * right_real - left_imag * right_imag,
                left_real * right_imag + left_imag * right_real,
            )

        zero = jnp.zeros((chans, rows), jnp.float32)
        real, imag = total(index + 1, term, (zero, zero))
        product[index, :, :rows] = real
        product[index, :, rows:] = imag

    each(blocks, multiply)
    apply(product, bwd_ref, back)

    def last(index, carried):
        long_mix = back[index, :, :rows] + carried
        query[index] = query[index] * (long_mix + skip_ref[...] * inner[index])

    last(0, jnp.zeros((chans, rows), jnp.float32))
    each(blocks - 1, lambda index: last(index + 1, back[index, :, rows:]))

    tp_parts = out_ref.shape[0]
    part_rows = rows // tp_parts
    copies = out_ref.shape[1]

    def spread(inner_index):
        for part in range(tp_parts):
            for group in range(outer // tp_parts):
                packed = jnp.zeros((chans, rows), jnp.float32)
                for place in range(tp_parts):
                    block = query[(group * tp_parts + place) * inner_parts + inner_index]
                    shift = (place - part) * part_rows % rows
                    block = pltpu.roll(block, shift, 1) if shift else block
                    packed = jnp.where(lane // part_rows == place, block, packed)
                packed = packed.astype(out_ref.dtype)
                for copy in range(copies):
                    out_ref[part, copy, inner_index, :, group * rows : (group + 1) * rows] = packed

    each(inner_parts, spread)


def convolve(parts, filter_blocks, taps, skip, outer, tp_parts):
    blocks, streams, chans, _ = parts[0].shape
    rows = filter_blocks.shape[2]
    forward, backward = tables(rows)
    wide = (blocks, chans, 2 * rows)
    narrow = (blocks, chans, rows)
    vmem = pl.BlockSpec(memory_space=pltpu.VMEM)
    return pl.pallas_call(
        functools.partial(conv_kernel, outer, len(parts)),
        out_shape=jax.ShapeDtypeStruct(
            (tp_parts, outer, blocks // outer, chans, outer // tp_parts * rows), jnp.bfloat16
        ),
        in_specs=[vmem] * (5 + len(parts)),
        out_specs=vmem,
        scratch_shapes=[
            pltpu.VMEM((blocks + 1, streams, chans, rows), jnp.float32),
            pltpu.VMEM(narrow, jnp.float32),
            pltpu.VMEM(narrow, jnp.float32),
            pltpu.VMEM(wide, jnp.float32),
            pltpu.VMEM(wide, jnp.float32),
            pltpu.VMEM(wide, jnp.float32),
            pltpu.VMEM(wide, jnp.float32),
        ],
        compiler_params=pltpu.CompilerParams(vmem_limit_bytes=40 * 2**20),
        cost_estimate=pl.CostEstimate(flops=10**9, bytes_accessed=4 * 2**20, transcendentals=0),
    )(*parts, filter_blocks, taps, skip, jnp.asarray(forward), jnp.asarray(backward))


def out_kernel(block_ref, gated_ref, weight_ref, *refs):
    *out_refs, turned, left, held, sems = refs
    tp_parts = gated_ref.shape[0]
    part_rows = out_refs[0].shape[0]
    inner_parts, _, _, width = held.shape
    copies = [
        pltpu.make_async_copy(weight_ref.at[inner], held.at[inner], sems.at[inner])
        for inner in range(inner_parts)
    ]
    for copy in copies:
        copy.start()
    for part in range(tp_parts):
        turned[...] = gated_ref[part].T
        for index in range(len(out_refs)):
            begin = pl.multiple_of(block_ref[index] * part_rows, part_rows)
            left[part, index * part_rows : (index + 1) * part_rows] = turned[pl.ds(begin, part_rows)]
    for inner in range(inner_parts):
        copies[inner].wait()
        sums = jnp.zeros((left.shape[1], width), jnp.float32)
        for part in range(tp_parts):
            sums = sums + jnp.dot(left[part], held[inner, part], preferred_element_type=jnp.float32)
        for index, out_ref in enumerate(out_refs):
            out_ref[:, inner * width : (inner + 1) * width] = sums[
                index * part_rows : (index + 1) * part_rows
            ].astype(out_ref.dtype)


def project_out(gated, weight, blocks):
    tp_parts, depth, rows = gated.shape
    inner_parts, _, _, width = weight.shape
    columns = inner_parts * width
    part_rows = rows // len(blocks)
    vmem = pl.BlockSpec(memory_space=pltpu.VMEM)
    return pl.pallas_call(
        out_kernel,
        in_specs=[
            pl.BlockSpec(memory_space=pltpu.SMEM),
            vmem,
            pl.BlockSpec(memory_space=pl.ANY),
        ],
        out_specs=[vmem] * len(blocks),
        scratch_shapes=[
            pltpu.VMEM((rows, depth), jnp.bfloat16),
            pltpu.VMEM((tp_parts, rows, depth), jnp.bfloat16),
            pltpu.VMEM(weight.shape, weight.dtype),
            pltpu.SemaphoreType.DMA((inner_parts,)),
        ],
        out_shape=[jax.ShapeDtypeStruct((part_rows, columns), jnp.bfloat16)] * len(blocks),
        compiler_params=pltpu.CompilerParams(vmem_limit_bytes=52 * 2**20),
        cost_estimate=pl.CostEstimate(
            flops=2 * gated.size * columns,
            bytes_accessed=2 * (weight.size + gated.size + rows * columns),
            transcendentals=0,
        ),
    )(jnp.stack(blocks).astype(jnp.int32), gated, weight)


def per_device(features, in_proj, short_taps, long_filter, skip_gain, out_proj):
    rows = features.shape[0]
    seq_parts = lax.axis_size("seq")
    tp_parts = lax.axis_size("tp")
    outer = outer_factor(seq_parts, tp_parts)
    inner_parts = seq_parts // outer
    streams, _, chan_tp = in_proj.shape
    chans = chan_tp // seq_parts
    position = lax.axis_index("seq")
    inner_groups = [[a * inner_parts + b for b in range(inner_parts)] for a in range(outer)]
    tp_groups = [
        [index * tp_parts + tp for index in group for tp in range(tp_parts)] for group in inner_groups
    ]

    taps = lax.dynamic_slice_in_dim(short_taps, position * chans, chans, axis=2)
    taps = jnp.broadcast_to(taps[..., None], taps.shape + (rows,))
    skip = lax.dynamic_slice_in_dim(skip_gain, position * chans, chans, axis=0)
    skip = jnp.broadcast_to(skip[:, None], (chans, rows))
    filter_blocks = lax.all_to_all(
        long_filter.T.reshape(seq_parts, chans, rows), "seq", split_axis=0, concat_axis=0, tiled=True
    )

    held = share_columns(features, outer, inner_parts, tp_parts)
    arrived = cross_outer(held, (0, 1), outer, inner_parts, tp_parts)
    held[0], taps, skip, filter_blocks = lax.optimization_barrier((held[0], taps, skip, filter_blocks))
    if outer > 2:
        arrived |= cross_outer(held, (outer - 1,), outer, inner_parts, tp_parts)
    own = share_over_tp(arrived[0], tp_parts)
    held, arrived[1], own = lax.optimization_barrier((held, arrived[1], own))
    arrived |= cross_outer(held, range(2, outer - 1), outer, inner_parts, tp_parts)
    chunks = [own] + [share_over_tp(arrived[step], tp_parts) for step in range(1, outer)]

    def settle(shards):
        chunks[outer // 2][0], *shards = lax.optimization_barrier((chunks[outer // 2][0], *shards))
        return shards

    weights, masks = gather_inner(in_proj, inner_parts, settle)
    chunks, out_proj = lax.optimization_barrier((chunks, out_proj))
    out_weight = lax.all_gather(out_proj, ("seq", "tp"), axis_index_groups=tp_groups)
    out_weight = out_weight.reshape((inner_parts, tp_parts) + out_proj.shape)

    partial = project_in(chunks, weights, masks, inner_parts, seq_parts)
    parts = lax.all_to_all(partial, "seq", split_axis=0, concat_axis=0, tiled=True)

    gated = convolve([parts], filter_blocks, taps, skip, outer, tp_parts)
    gated = lax.all_to_all(
        gated.reshape((-1,) + gated.shape[3:]), ("tp", "seq"), split_axis=0, concat_axis=0, tiled=True
    )
    blocks, places = return_places(outer, inner_parts, tp_parts)
    pieces = project_out(gated.reshape(tp_parts, chan_tp, -1), out_weight, blocks)
    return return_output(pieces, places, inner_parts, tp_parts)


def solution(mesh):
    return jax.shard_map(
        per_device,
        mesh=mesh,
        in_specs=(
            P("seq", "tp"),
            P(None, "seq", "tp"),
            P(None, None, "tp"),
            P("seq", "tp"),
            P("tp"),
            P("tp", "seq"),
        ),
        out_specs=P("seq", "tp"),
        check_vma=False,
    )
```

```python
import functools
import math

import jax
import jax.numpy as jnp
import numpy as np
from jax import lax
from jax.experimental import pallas as pl
from jax.experimental.pallas import tpu as pltpu
from jax.sharding import PartitionSpec as P

HIGHEST = lax.Precision.HIGHEST
UNROLL = 16
HEAVY = 30


def outer_factor(seq_parts, tp_parts):
    outer = tp_parts
    while 4 * outer * outer <= seq_parts and seq_parts % (2 * outer) == 0:
        outer *= 2
    return outer


def assemble_kernel(place_ref, *refs):
    *piece_refs, out_ref, sems = refs
    part_rows, width = piece_refs[0].shape
    copies = []
    for index, piece_ref in enumerate(piece_refs):
        row = pl.multiple_of(place_ref[2 * index] * part_rows, part_rows)
        column = pl.multiple_of(place_ref[2 * index + 1] * width, width)
        target = out_ref.at[pl.ds(row, part_rows), pl.ds(column, width)]
        copies.append(pltpu.make_async_copy(piece_ref, target, sems.at[index]))
    for copy in copies:
        copy.start()
    for copy in copies:
        copy.wait()


def assemble(pieces, places, shape):
    return pl.pallas_call(
        assemble_kernel,
        in_specs=[pl.BlockSpec(memory_space=pltpu.SMEM)]
        + [pl.BlockSpec(memory_space=pltpu.VMEM)] * len(pieces),
        out_specs=pl.BlockSpec(memory_space=pl.ANY),
        out_shape=jax.ShapeDtypeStruct(shape, pieces[0].dtype),
        scratch_shapes=[pltpu.SemaphoreType.DMA((len(pieces),))],
        compiler_params=pltpu.CompilerParams(vmem_limit_bytes=4 * 2**20),
        cost_estimate=pl.CostEstimate(
            flops=0, bytes_accessed=4 * shape[0] * shape[1], transcendentals=0
        ),
    )(jnp.stack(places).astype(jnp.int32), *pieces)


def return_places(outer, inner_parts, tp_parts):
    per_tp = outer // tp_parts
    tp_place = lax.axis_index("tp")
    outer_place = lax.axis_index("seq") // inner_parts
    blocks, places = [], []
    for far in range(tp_parts):
        for near in range(per_tp):
            low = outer_place % per_tp
            blocks.append((tp_place + low + far) % tp_parts * per_tp + (low + near) % per_tp)
            low = (low - near + per_tp) % per_tp
            places.append((outer_place // per_tp - far - low + tp_parts + per_tp * tp_parts) % tp_parts)
            places.append(low)
    return blocks, places


def return_output(pieces, places, inner_parts, tp_parts):
    outer = len(pieces)
    part_rows, width = pieces[0].shape
    per_tp = outer // tp_parts
    arrived = []
    for index, piece in enumerate(pieces):
        far, near = divmod(index, per_tp)

        def target(seq, tp):
            src = seq // inner_parts
            low = src % per_tp
            dst = (tp + low + far) % tp_parts * per_tp + (low + near) % per_tp
            return (dst * inner_parts + seq % inner_parts) * tp_parts + src // per_tp

        pairs = [
            (seq * tp_parts + tp, target(seq, tp))
            for seq in range(outer * inner_parts)
            for tp in range(tp_parts)
        ]
        arrived.append(lax.ppermute(piece, ("seq", "tp"), pairs))
    return assemble(arrived, places, (tp_parts * part_rows, per_tp * width))


def share_columns(features, outer, inner_parts, tp_parts):
    _, cols = features.shape
    per_tp = outer // tp_parts
    width = cols // outer
    tp_place = lax.axis_index("tp")
    outer_place = lax.axis_index("seq") // inner_parts
    held = []
    for after in range(per_tp):
        group = (outer_place + 1 + after) % per_tp
        pieces = []
        for step in range(tp_parts):
            column = (group * tp_parts + (tp_place + step) % tp_parts) * width
            piece = lax.dynamic_slice_in_dim(features, column, width, axis=1)
            if step:
                pairs = [(i, (i + step) % tp_parts) for i in range(tp_parts)]
                piece = lax.ppermute(piece, "tp", pairs)
            pieces.append(piece)
        held.append(jnp.stack(pieces))
    return held


def cross_outer(held, steps, outer, inner_parts, tp_parts):
    per_tp = outer // tp_parts
    seq_parts = outer * inner_parts
    tp_place = lax.axis_index("tp")
    outer_place = lax.axis_index("seq") // inner_parts
    arrived = {}
    for step in steps:
        target = (outer_place + step) % outer
        which = (tp_place - target // per_tp + tp_parts) % tp_parts
        piece = lax.dynamic_index_in_dim(held[(step - 1) % per_tp], which, axis=0, keepdims=False)
        if step:
            far = step * inner_parts
            piece = lax.ppermute(piece, "seq", [(i, (i + far) % seq_parts) for i in range(seq_parts)])
        arrived[step] = piece
    return arrived


def share_over_tp(part, tp_parts):
    pieces = [part]
    for step in range(1, tp_parts):
        pairs = [(i, (i + step) % tp_parts) for i in range(tp_parts)]
        pieces.append(lax.ppermute(part, "tp", pairs))
    return pieces


def gather_inner(block, inner_parts, settle):
    held, masks = [block], [0]
    bit = inner_parts // 2
    while bit:
        pairs = [(i, i ^ bit) for i in range(lax.axis_size("seq"))]
        held += [lax.ppermute(piece, "seq", pairs) for piece in held]
        masks += [mask ^ bit for mask in masks]
        if bit == inner_parts // 2:
            held = settle(held)
        bit //= 2
    return held, masks


def project_kernel(tp_parts, masks, place_ref, *refs):
    *refs, out_ref, left = refs
    share_refs, weight_refs = refs[: -len(masks)], refs[-len(masks) :]
    seq_parts, streams, chans, count = out_ref.shape
    blocks, rows, width = len(masks) // tp_parts, share_refs[0].shape[0], left.shape[2]
    for index, share_ref in enumerate(share_refs):
        chunk, step = divmod(index, tp_parts)
        for block in range(blocks):
            left[step * blocks + block, chunk * rows : (chunk + 1) * rows] = share_ref[
                :, block * width : (block + 1) * width
            ]
    slots = []
    for mask in masks:
        inner = jnp.bitwise_xor(place_ref[1], mask)
        step = lax.rem(place_ref[0] - inner // blocks + tp_parts, tp_parts)
        slots.append(step * blocks + lax.rem(inner, blocks))
    for stream in range(streams):
        sums = jnp.zeros((count, seq_parts * chans), jnp.float32)
        for slot, weight_ref in zip(slots, weight_refs):
            sums = sums + jnp.dot(left[slot], weight_ref[stream], preferred_element_type=jnp.float32)
        turned = sums.astype(out_ref.dtype).T
        for seq in range(seq_parts):
            out_ref[seq, stream] = turned[seq * chans : (seq + 1) * chans]


def project_in(chunks, weights, masks, inner_parts, seq_parts):
    tp_parts = len(chunks[0])
    rows, _ = chunks[0][0].shape
    streams, width, chan_tp = weights[0].shape
    chans = chan_tp // seq_parts
    pieces = [piece for chunk in chunks for piece in chunk]
    count = len(chunks) * rows
    place = jnp.stack([lax.axis_index("tp"), lax.axis_index("seq") % inner_parts]).astype(jnp.int32)
    vmem = pl.BlockSpec(memory_space=pltpu.VMEM)
    size = len(weights) * weights[0].size
    return pl.pallas_call(
        functools.partial(project_kernel, tp_parts, masks),
        in_specs=[pl.BlockSpec(memory_space=pltpu.SMEM)] + [vmem] * (len(pieces) + len(weights)),
        out_specs=vmem,
        out_shape=jax.ShapeDtypeStruct((seq_parts, streams, chans, count), jnp.bfloat16),
        scratch_shapes=[pltpu.VMEM((len(masks), count, width), jnp.bfloat16)],
        compiler_params=pltpu.CompilerParams(vmem_limit_bytes=32 * 2**20),
        cost_estimate=pl.CostEstimate(
            flops=HEAVY * 2 * count * size,
            bytes_accessed=2 * (size + len(pieces) * pieces[0].size)
            + 2 * streams * count * seq_parts * chans,
            transcendentals=0,
        ),
    )(place, *pieces, *weights)


def tables(block):
    place = np.arange(block)
    angle = 2.0 * math.pi * np.outer(place, place + 0.5) / (2 * block)
    forward = np.concatenate([np.cos(angle), -np.sin(angle)], 1)
    place = np.arange(2 * block)
    angle = 2.0 * math.pi * np.outer(np.arange(block) + 0.5, place) / (2 * block)
    backward = np.concatenate([np.cos(angle), -np.sin(angle)], 0) / block
    return forward.astype(np.float32), backward.astype(np.float32)


def each(count, body):
    if isinstance(count, int) and count <= UNROLL:
        for index in range(count):
            body(index)
    else:
        lax.fori_loop(0, count, lambda index, carry: (body(index), carry)[1], 0)


def total(count, term, zero):
    if isinstance(count, int) and count <= UNROLL:
        result = zero
        for index in range(count):
            result = jax.tree.map(jnp.add, result, term(index))
        return result
    return lax.fori_loop(
        0, count, lambda index, sums: jax.tree.map(jnp.add, sums, term(index)), zero
    )


def conv_kernel(
    outer, chunks, *refs
):
    part_refs, refs = refs[:chunks], refs[chunks:]
    filter_ref, taps_ref, skip_ref, fwd_ref, bwd_ref, out_ref, *refs = refs
    proj, query, inner, spec, filter_spec, product, back = refs
    blocks, streams, chans, _ = part_refs[0].shape
    rows = filter_ref.shape[2]
    inner_parts = blocks // outer
    taps_count = taps_ref.shape[1]
    lane = lax.broadcasted_iota(jnp.int32, (chans, rows), 1)

    depth = outer // chunks

    def add_up(inner_index, stream, group):
        value = jnp.zeros((chans, rows), jnp.float32)
        for part in range(outer):
            slot = (part - group) % outer
            column = slice(slot % depth * rows, (slot % depth + 1) * rows)
            source = part_refs[slot // depth]
            value = value + source[part * inner_parts + inner_index, stream, :, column].astype(jnp.float32)
        proj[1 + group * inner_parts + inner_index, stream] = value

    for group in range(outer):
        for stream in range(streams):
            each(inner_parts, functools.partial(add_up, stream=stream, group=group))

    for stream in range(streams):
        proj[0, stream] = jnp.zeros((chans, rows), jnp.float32)

    def first(index):
        filtered = []
        for stream in range(streams):
            now, past = proj[index + 1, stream], proj[index, stream]
            value = taps_ref[stream, 0] * now
            for offset in range(1, taps_count):
                moved = jnp.where(
                    lane < offset, pltpu.roll(past, offset, 1), pltpu.roll(now, offset, 1)
                )
                value = value + taps_ref[stream, offset] * moved
            filtered.append(value)
        query[index] = filtered[0]
        inner[index] = filtered[1] * filtered[2]

    each(blocks, first)

    def apply(source, table_ref, target):
        if chans % 8 == 0:
            flat = source[...].reshape(blocks * chans, source.shape[2])
            done = jnp.dot(flat, table_ref[...], precision=HIGHEST, preferred_element_type=jnp.float32)
            target[...] = done.reshape(target.shape)
        else:

            def one(index):
                target[index] = jnp.dot(
                    source[index], table_ref[...], precision=HIGHEST, preferred_element_type=jnp.float32
                )

            each(blocks, one)

    apply(filter_ref, fwd_ref, filter_spec)
    apply(inner, fwd_ref, spec)

    def multiply(index):
        def term(step):
            left, right = spec[step], filter_spec[index - step]
            left_real, left_imag = left[:, :rows], left[:, rows:]
            right_real, right_imag = right[:, :rows], right[:, rows:]
            return (
                left_real * right_real - left_imag * right_imag,
                left_real * right_imag + left_imag * right_real,
            )

        zero = jnp.zeros((chans, rows), jnp.float32)
        real, imag = total(index + 1, term, (zero, zero))
        product[index, :, :rows] = real
        product[index, :, rows:] = imag

    each(blocks, multiply)
    apply(product, bwd_ref, back)

    def last(index, carried):
        long_mix = back[index, :, :rows] + carried
        query[index] = query[index] * (long_mix + skip_ref[...] * inner[index])

    last(0, jnp.zeros((chans, rows), jnp.float32))
    each(blocks - 1, lambda index: last(index + 1, back[index, :, rows:]))

    tp_parts = out_ref.shape[0]
    part_rows = rows // tp_parts
    copies = out_ref.shape[1]

    def spread(inner_index):
        for part in range(tp_parts):
            for group in range(outer // tp_parts):
                packed = jnp.zeros((chans, rows), jnp.float32)
                for place in range(tp_parts):
                    block = query[(group * tp_parts + place) * inner_parts + inner_index]
                    shift = (place - part) * part_rows % rows
                    block = pltpu.roll(block, shift, 1) if shift else block
                    packed = jnp.where(lane // part_rows == place, block, packed)
                packed = packed.astype(out_ref.dtype)
                for copy in range(copies):
                    out_ref[part, copy, inner_index, :, group * rows : (group + 1) * rows] = packed

    each(inner_parts, spread)


def convolve(parts, filter_blocks, taps, skip, outer, tp_parts):
    blocks, streams, chans, _ = parts[0].shape
    rows = filter_blocks.shape[2]
    forward, backward = tables(rows)
    wide = (blocks, chans, 2 * rows)
    narrow = (blocks, chans, rows)
    vmem = pl.BlockSpec(memory_space=pltpu.VMEM)
    return pl.pallas_call(
        functools.partial(conv_kernel, outer, len(parts)),
        out_shape=jax.ShapeDtypeStruct(
            (tp_parts, outer, blocks // outer, chans, outer // tp_parts * rows), jnp.bfloat16
        ),
        in_specs=[vmem] * (5 + len(parts)),
        out_specs=vmem,
        scratch_shapes=[
            pltpu.VMEM((blocks + 1, streams, chans, rows), jnp.float32),
            pltpu.VMEM(narrow, jnp.float32),
            pltpu.VMEM(narrow, jnp.float32),
            pltpu.VMEM(wide, jnp.float32),
            pltpu.VMEM(wide, jnp.float32),
            pltpu.VMEM(wide, jnp.float32),
            pltpu.VMEM(wide, jnp.float32),
        ],
        compiler_params=pltpu.CompilerParams(vmem_limit_bytes=40 * 2**20),
        cost_estimate=pl.CostEstimate(flops=10**9, bytes_accessed=4 * 2**20, transcendentals=0),
    )(*parts, filter_blocks, taps, skip, jnp.asarray(forward), jnp.asarray(backward))


def out_kernel(block_ref, gated_ref, weight_ref, *refs):
    *out_refs, turned, left, held, sems = refs
    tp_parts = gated_ref.shape[0]
    part_rows = out_refs[0].shape[0]
    inner_parts, _, _, width = held.shape
    copies = [
        pltpu.make_async_copy(weight_ref.at[inner], held.at[inner], sems.at[inner])
        for inner in range(inner_parts)
    ]
    for copy in copies:
        copy.start()
    for part in range(tp_parts):
        turned[...] = gated_ref[part].T
        for index in range(len(out_refs)):
            begin = pl.multiple_of(block_ref[index] * part_rows, part_rows)
            left[part, index * part_rows : (index + 1) * part_rows] = turned[pl.ds(begin, part_rows)]
    for inner in range(inner_parts):
        copies[inner].wait()
        sums = jnp.zeros((left.shape[1], width), jnp.float32)
        for part in range(tp_parts):
            sums = sums + jnp.dot(left[part], held[inner, part], preferred_element_type=jnp.float32)
        for index, out_ref in enumerate(out_refs):
            out_ref[:, inner * width : (inner + 1) * width] = sums[
                index * part_rows : (index + 1) * part_rows
            ].astype(out_ref.dtype)


def project_out(gated, weight, blocks):
    tp_parts, depth, rows = gated.shape
    inner_parts, _, _, width = weight.shape
    columns = inner_parts * width
    part_rows = rows // len(blocks)
    vmem = pl.BlockSpec(memory_space=pltpu.VMEM)
    return pl.pallas_call(
        out_kernel,
        in_specs=[
            pl.BlockSpec(memory_space=pltpu.SMEM),
            vmem,
            pl.BlockSpec(memory_space=pl.ANY),
        ],
        out_specs=[vmem] * len(blocks),
        scratch_shapes=[
            pltpu.VMEM((rows, depth), jnp.bfloat16),
            pltpu.VMEM((tp_parts, rows, depth), jnp.bfloat16),
            pltpu.VMEM(weight.shape, weight.dtype),
            pltpu.SemaphoreType.DMA((inner_parts,)),
        ],
        out_shape=[jax.ShapeDtypeStruct((part_rows, columns), jnp.bfloat16)] * len(blocks),
        compiler_params=pltpu.CompilerParams(vmem_limit_bytes=52 * 2**20),
        cost_estimate=pl.CostEstimate(
            flops=2 * gated.size * columns,
            bytes_accessed=2 * (weight.size + gated.size + rows * columns),
            transcendentals=0,
        ),
    )(jnp.stack(blocks).astype(jnp.int32), gated, weight)


def per_device(features, in_proj, short_taps, long_filter, skip_gain, out_proj):
    rows = features.shape[0]
    seq_parts = lax.axis_size("seq")
    tp_parts = lax.axis_size("tp")
    outer = outer_factor(seq_parts, tp_parts)
    inner_parts = seq_parts // outer
    streams, _, chan_tp = in_proj.shape
    chans = chan_tp // seq_parts
    position = lax.axis_index("seq")
    inner_groups = [[a * inner_parts + b for b in range(inner_parts)] for a in range(outer)]
    tp_groups = [
        [index * tp_parts + tp for index in group for tp in range(tp_parts)] for group in inner_groups
    ]

    taps = lax.dynamic_slice_in_dim(short_taps, position * chans, chans, axis=2)
    taps = jnp.broadcast_to(taps[..., None], taps.shape + (rows,))
    skip = lax.dynamic_slice_in_dim(skip_gain, position * chans, chans, axis=0)
    skip = jnp.broadcast_to(skip[:, None], (chans, rows))
    filter_blocks = lax.all_to_all(
        long_filter.T.reshape(seq_parts, chans, rows), "seq", split_axis=0, concat_axis=0, tiled=True
    )

    held = share_columns(features, outer, inner_parts, tp_parts)
    arrived = cross_outer(held, (0, 1), outer, inner_parts, tp_parts)
    held[0], taps, skip = lax.optimization_barrier((held[0], taps, skip))
    if outer > 2:
        arrived |= cross_outer(held, (outer - 1,), outer, inner_parts, tp_parts)
    own = share_over_tp(arrived[0], tp_parts)
    held, arrived[1], own = lax.optimization_barrier((held, arrived[1], own))
    arrived |= cross_outer(held, range(2, outer - 1), outer, inner_parts, tp_parts)
    chunks = [own] + [share_over_tp(arrived[step], tp_parts) for step in range(1, outer)]

    def settle(shards):
        chunks[outer // 2][0], *shards = lax.optimization_barrier((chunks[outer // 2][0], *shards))
        return shards

    weights, masks = gather_inner(in_proj, inner_parts, settle)
    chunks, out_proj, filter_blocks = lax.optimization_barrier((chunks, out_proj, filter_blocks))
    out_weight = lax.all_gather(out_proj, ("seq", "tp"), axis_index_groups=tp_groups)
    out_weight = out_weight.reshape((inner_parts, tp_parts) + out_proj.shape)

    partial = project_in(chunks, weights, masks, inner_parts, seq_parts)
    parts = lax.all_to_all(partial, "seq", split_axis=0, concat_axis=0, tiled=True)

    gated = convolve([parts], filter_blocks, taps, skip, outer, tp_parts)
    gated = lax.all_to_all(
        gated.reshape((-1,) + gated.shape[3:]), ("tp", "seq"), split_axis=0, concat_axis=0, tiled=True
    )
    blocks, places = return_places(outer, inner_parts, tp_parts)
    pieces = project_out(gated.reshape(tp_parts, chan_tp, -1), out_weight, blocks)
    return return_output(pieces, places, inner_parts, tp_parts)


def solution(mesh):
    return jax.shard_map(
        per_device,
        mesh=mesh,
        in_specs=(
            P("seq", "tp"),
            P(None, "seq", "tp"),
            P(None, None, "tp"),
            P("seq", "tp"),
            P("tp"),
            P("tp", "seq"),
        ),
        out_specs=P("seq", "tp"),
        check_vma=False,
    )
```

```python
import functools
import math

import jax
import jax.numpy as jnp
import ml_dtypes
import numpy as np
from jax import lax
from jax.experimental import pallas as pl
from jax.experimental.pallas import tpu as pltpu
from jax.sharding import PartitionSpec as P

UNROLL = 16
HEAVY = 30


def outer_factor(seq_parts, tp_parts):
    outer = tp_parts
    while 4 * outer * outer <= seq_parts and seq_parts % (2 * outer) == 0:
        outer *= 2
    return outer


def assemble_kernel(place_ref, *refs):
    *piece_refs, out_ref, sems = refs
    part_rows, width = piece_refs[0].shape
    copies = []
    for index, piece_ref in enumerate(piece_refs):
        row = pl.multiple_of(place_ref[2 * index] * part_rows, part_rows)
        column = pl.multiple_of(place_ref[2 * index + 1] * width, width)
        target = out_ref.at[pl.ds(row, part_rows), pl.ds(column, width)]
        copies.append(pltpu.make_async_copy(piece_ref, target, sems.at[index]))
    for copy in copies:
        copy.start()
    for copy in copies:
        copy.wait()


def assemble(pieces, places, shape):
    return pl.pallas_call(
        assemble_kernel,
        in_specs=[pl.BlockSpec(memory_space=pltpu.SMEM)]
        + [pl.BlockSpec(memory_space=pltpu.VMEM)] * len(pieces),
        out_specs=pl.BlockSpec(memory_space=pl.ANY),
        out_shape=jax.ShapeDtypeStruct(shape, pieces[0].dtype),
        scratch_shapes=[pltpu.SemaphoreType.DMA((len(pieces),))],
        compiler_params=pltpu.CompilerParams(vmem_limit_bytes=4 * 2**20),
        cost_estimate=pl.CostEstimate(
            flops=0, bytes_accessed=4 * shape[0] * shape[1], transcendentals=0
        ),
    )(jnp.stack(places).astype(jnp.int32), *pieces)


def return_places(outer, inner_parts, tp_parts):
    per_tp = outer // tp_parts
    tp_place = lax.axis_index("tp")
    outer_place = lax.axis_index("seq") // inner_parts
    blocks, places = [], []
    for far in range(tp_parts):
        for near in range(per_tp):
            low = outer_place % per_tp
            blocks.append((tp_place + low + far) % tp_parts * per_tp + (low + near) % per_tp)
            low = (low - near + per_tp) % per_tp
            places.append((outer_place // per_tp - far - low + tp_parts + per_tp * tp_parts) % tp_parts)
            places.append(low)
    return blocks, places


def return_output(pieces, places, inner_parts, tp_parts):
    outer = len(pieces)
    part_rows, width = pieces[0].shape
    per_tp = outer // tp_parts
    arrived = []
    for index, piece in enumerate(pieces):
        far, near = divmod(index, per_tp)

        def target(seq, tp):
            src = seq // inner_parts
            low = src % per_tp
            dst = (tp + low + far) % tp_parts * per_tp + (low + near) % per_tp
            return (dst * inner_parts + seq % inner_parts) * tp_parts + src // per_tp

        pairs = [
            (seq * tp_parts + tp, target(seq, tp))
            for seq in range(outer * inner_parts)
            for tp in range(tp_parts)
        ]
        arrived.append(lax.ppermute(piece, ("seq", "tp"), pairs))
    return assemble(arrived, places, (tp_parts * part_rows, per_tp * width))


def share_columns(features, outer, tp_parts):
    rows, cols = features.shape
    per_tp = outer // tp_parts
    tp_place = lax.axis_index("tp")
    width = cols // outer
    held = []
    for step in range(tp_parts):
        which = (tp_place + step) % tp_parts
        piece = jnp.stack(
            [
                lax.dynamic_slice_in_dim(features, (group * tp_parts + which) * width, width, axis=1)
                for group in range(per_tp)
            ]
        )
        if step:
            piece = lax.ppermute(piece, "tp", [(i, (i + step) % tp_parts) for i in range(tp_parts)])
        held.append(piece)
    return jnp.concatenate(held)


def cross_outer(held, steps, outer, inner_parts, tp_parts):
    per_tp = outer // tp_parts
    seq_parts = outer * inner_parts
    tp_place = lax.axis_index("tp")
    outer_place = lax.axis_index("seq") // inner_parts
    arrived = {}
    for step in steps:
        target = (outer_place + step) % outer
        which = (tp_place - target // per_tp + tp_parts) % tp_parts * per_tp + target % per_tp
        piece = lax.dynamic_index_in_dim(held, which, axis=0, keepdims=False)
        if step:
            far = step * inner_parts
            piece = lax.ppermute(piece, "seq", [(i, (i + far) % seq_parts) for i in range(seq_parts)])
        arrived[step] = piece
    return arrived


def share_over_tp(part, tp_parts):
    pieces = [part]
    for step in range(1, tp_parts):
        pairs = [(i, (i + step) % tp_parts) for i in range(tp_parts)]
        pieces.append(lax.ppermute(part, "tp", pairs))
    return pieces


def project_kernel(tp_parts, place_ref, *refs):
    *share_refs, weight_ref, out_ref, held, sems = refs
    seq_parts, streams, chans, count = out_ref.shape
    copies = []
    for stream in range(streams):
        for step in range(tp_parts):
            which = lax.rem(place_ref[0] - step + tp_parts, tp_parts)
            copies.append(
                pltpu.make_async_copy(
                    weight_ref.at[stream, which], held.at[stream, step], sems.at[len(copies)]
                )
            )
            copies[-1].start()
    left = [
        jnp.concatenate([share_ref[...] for share_ref in share_refs[step::tp_parts]])
        for step in range(tp_parts)
    ]
    for stream in range(streams):
        sums = jnp.zeros((count, seq_parts * chans), jnp.float32)
        for step in range(tp_parts):
            copies[stream * tp_parts + step].wait()
            sums = sums + jnp.dot(
                left[step], held[stream, step], preferred_element_type=jnp.float32
            )
        turned = sums.astype(out_ref.dtype).T
        for seq in range(seq_parts):
            out_ref[seq, stream] = turned[seq * chans : (seq + 1) * chans]


def project_in(chunks, weight, seq_parts):
    tp_parts = len(chunks[0])
    rows, width = chunks[0][0].shape
    streams, _, chan_tp = weight.shape
    weight = weight.reshape(streams, tp_parts, width, chan_tp)
    chans = chan_tp // seq_parts
    pieces = [piece for chunk in chunks for piece in chunk]
    count = len(chunks) * rows
    place = lax.axis_index("tp").astype(jnp.int32)[None]
    vmem = pl.BlockSpec(memory_space=pltpu.VMEM)
    return pl.pallas_call(
        functools.partial(project_kernel, tp_parts),
        in_specs=[pl.BlockSpec(memory_space=pltpu.SMEM)]
        + [vmem] * len(pieces)
        + [pl.BlockSpec(memory_space=pl.ANY)],
        out_specs=vmem,
        out_shape=jax.ShapeDtypeStruct((seq_parts, streams, chans, count), jnp.bfloat16),
        scratch_shapes=[
            pltpu.VMEM(weight.shape, weight.dtype),
            pltpu.SemaphoreType.DMA((streams * tp_parts,)),
        ],
        compiler_params=pltpu.CompilerParams(vmem_limit_bytes=48 * 2**20),
        cost_estimate=pl.CostEstimate(
            flops=HEAVY * 2 * count * weight.size,
            bytes_accessed=2 * (weight.size + len(pieces) * pieces[0].size)
            + 2 * streams * count * seq_parts * chans,
            transcendentals=0,
        ),
    )(place, *pieces, weight)


def tables(block):
    place = np.arange(block)
    angle = 2.0 * math.pi * np.outer(place, place + 0.5) / (2 * block)
    forward = np.concatenate([np.cos(angle), -np.sin(angle)], 1)
    place = np.arange(2 * block)
    angle = 2.0 * math.pi * np.outer(np.arange(block) + 0.5, place) / (2 * block)
    backward = np.concatenate([np.cos(angle), -np.sin(angle)], 0) / block
    return halves(forward), halves(backward)


def halves(table):
    high = table.astype(ml_dtypes.bfloat16)
    low = (table - high.astype(np.float64)).astype(ml_dtypes.bfloat16)
    return np.stack([high, low])


def each(count, body):
    if isinstance(count, int) and count <= UNROLL:
        for index in range(count):
            body(index)
    else:
        lax.fori_loop(0, count, lambda index, carry: (body(index), carry)[1], 0)


def total(count, term, zero):
    if isinstance(count, int) and count <= UNROLL:
        result = zero
        for index in range(count):
            result = jax.tree.map(jnp.add, result, term(index))
        return result
    return lax.fori_loop(
        0, count, lambda index, sums: jax.tree.map(jnp.add, sums, term(index)), zero
    )


def conv_kernel(
    outer, chunks, *refs
):
    part_refs, refs = refs[:chunks], refs[chunks:]
    filter_ref, taps_ref, skip_ref, fwd_ref, bwd_ref, out_ref, *refs = refs
    proj, query, inner, spec, filter_spec, product, back = refs
    blocks, streams, chans, _ = part_refs[0].shape
    rows = filter_ref.shape[2]
    inner_parts = blocks // outer
    taps_count = taps_ref.shape[1]
    lane = lax.broadcasted_iota(jnp.int32, (chans, rows), 1)

    depth = outer // chunks

    def add_up(inner_index, stream, group):
        value = jnp.zeros((chans, rows), jnp.float32)
        for part in range(outer):
            slot = (part - group) % outer
            column = slice(slot % depth * rows, (slot % depth + 1) * rows)
            source = part_refs[slot // depth]
            value = value + source[part * inner_parts + inner_index, stream, :, column].astype(jnp.float32)
        proj[1 + group * inner_parts + inner_index, stream] = value

    for group in range(outer):
        for stream in range(streams):
            each(inner_parts, functools.partial(add_up, stream=stream, group=group))

    for stream in range(streams):
        proj[0, stream] = jnp.zeros((chans, rows), jnp.float32)

    def first(index):
        filtered = []
        for stream in range(streams):
            now, past = proj[index + 1, stream], proj[index, stream]
            value = taps_ref[stream, 0] * now
            for offset in range(1, taps_count):
                moved = pltpu.roll(jnp.where(lane < rows - offset, now, past), offset, 1)
                value = value + taps_ref[stream, offset] * moved
            filtered.append(value)
        query[index] = filtered[0]
        inner[index] = filtered[1] * filtered[2]

    each(blocks, first)

    def product_of(value, table_ref):
        high = value.astype(jnp.bfloat16)
        low = (value - high.astype(jnp.float32)).astype(jnp.bfloat16)
        return (
            jnp.dot(high, table_ref[0], preferred_element_type=jnp.float32)
            + jnp.dot(low, table_ref[0], preferred_element_type=jnp.float32)
            + jnp.dot(high, table_ref[1], preferred_element_type=jnp.float32)
        )

    def apply(source, table_ref, target):
        if chans % 8 == 0:
            flat = source[...].reshape(blocks * chans, source.shape[2])
            target[...] = product_of(flat, table_ref).reshape(target.shape)
        else:

            def one(index):
                target[index] = product_of(source[index], table_ref)

            each(blocks, one)

    apply(filter_ref, fwd_ref, filter_spec)
    apply(inner, fwd_ref, spec)

    def multiply(index):
        def term(step):
            left, right = spec[step], filter_spec[index - step]
            left_real, left_imag = left[:, :rows], left[:, rows:]
            right_real, right_imag = right[:, :rows], right[:, rows:]
            return (
                left_real * right_real - left_imag * right_imag,
                left_real * right_imag + left_imag * right_real,
            )

        zero = jnp.zeros((chans, rows), jnp.float32)
        real, imag = total(index + 1, term, (zero, zero))
        product[index, :, :rows] = real
        product[index, :, rows:] = imag

    each(blocks, multiply)
    apply(product, bwd_ref, back)

    def last(index, carried):
        long_mix = back[index, :, :rows] + carried
        query[index] = query[index] * (long_mix + skip_ref[...] * inner[index])

    last(0, jnp.zeros((chans, rows), jnp.float32))
    each(blocks - 1, lambda index: last(index + 1, back[index, :, rows:]))

    tp_parts = out_ref.shape[0]
    part_rows = rows // tp_parts
    copies = out_ref.shape[1]

    def spread(inner_index):
        for part in range(tp_parts):
            for group in range(outer // tp_parts):
                packed = jnp.zeros((chans, rows), jnp.float32)
                for place in range(tp_parts):
                    block = query[(group * tp_parts + place) * inner_parts + inner_index]
                    shift = (place - part) * part_rows % rows
                    block = pltpu.roll(block, shift, 1) if shift else block
                    packed = jnp.where(lane // part_rows == place, block, packed)
                packed = packed.astype(out_ref.dtype)
                for copy in range(copies):
                    out_ref[part, copy, inner_index, :, group * rows : (group + 1) * rows] = packed

    each(inner_parts, spread)


def convolve(parts, filter_blocks, taps, skip, outer, tp_parts):
    blocks, streams, chans, _ = parts[0].shape
    rows = filter_blocks.shape[2]
    forward, backward = tables(rows)
    wide = (blocks, chans, 2 * rows)
    narrow = (blocks, chans, rows)
    vmem = pl.BlockSpec(memory_space=pltpu.VMEM)
    return pl.pallas_call(
        functools.partial(conv_kernel, outer, len(parts)),
        out_shape=jax.ShapeDtypeStruct(
            (tp_parts, outer, blocks // outer, chans, outer // tp_parts * rows), jnp.bfloat16
        ),
        in_specs=[vmem] * (5 + len(parts)),
        out_specs=vmem,
        scratch_shapes=[
            pltpu.VMEM((blocks + 1, streams, chans, rows), jnp.float32),
            pltpu.VMEM(narrow, jnp.float32),
            pltpu.VMEM(narrow, jnp.float32),
            pltpu.VMEM(wide, jnp.float32),
            pltpu.VMEM(wide, jnp.float32),
            pltpu.VMEM(wide, jnp.float32),
            pltpu.VMEM(wide, jnp.float32),
        ],
        compiler_params=pltpu.CompilerParams(vmem_limit_bytes=40 * 2**20),
        cost_estimate=pl.CostEstimate(flops=10**9, bytes_accessed=4 * 2**20, transcendentals=0),
    )(*parts, filter_blocks, taps, skip, jnp.asarray(forward), jnp.asarray(backward))


def out_kernel(block_ref, gated_ref, weight_ref, *refs):
    *out_refs, turned, left, held, sems = refs
    tp_parts = gated_ref.shape[0]
    part_rows = out_refs[0].shape[0]
    inner_parts, _, _, width = held.shape
    copies = [
        pltpu.make_async_copy(weight_ref.at[inner], held.at[inner], sems.at[inner])
        for inner in range(inner_parts)
    ]
    for copy in copies:
        copy.start()
    for part in range(tp_parts):
        turned[...] = gated_ref[part].T
        for index in range(len(out_refs)):
            begin = pl.multiple_of(block_ref[index] * part_rows, part_rows)
            left[part, index * part_rows : (index + 1) * part_rows] = turned[pl.ds(begin, part_rows)]
    for inner in range(inner_parts):
        copies[inner].wait()
        sums = jnp.zeros((left.shape[1], width), jnp.float32)
        for part in range(tp_parts):
            sums = sums + jnp.dot(left[part], held[inner, part], preferred_element_type=jnp.float32)
        for index, out_ref in enumerate(out_refs):
            out_ref[:, inner * width : (inner + 1) * width] = sums[
                index * part_rows : (index + 1) * part_rows
            ].astype(out_ref.dtype)


def project_out(gated, weight, blocks):
    tp_parts, depth, rows = gated.shape
    inner_parts, _, _, width = weight.shape
    columns = inner_parts * width
    part_rows = rows // len(blocks)
    vmem = pl.BlockSpec(memory_space=pltpu.VMEM)
    return pl.pallas_call(
        out_kernel,
        in_specs=[
            pl.BlockSpec(memory_space=pltpu.SMEM),
            vmem,
            pl.BlockSpec(memory_space=pl.ANY),
        ],
        out_specs=[vmem] * len(blocks),
        scratch_shapes=[
            pltpu.VMEM((rows, depth), jnp.bfloat16),
            pltpu.VMEM((tp_parts, rows, depth), jnp.bfloat16),
            pltpu.VMEM(weight.shape, weight.dtype),
            pltpu.SemaphoreType.DMA((inner_parts,)),
        ],
        out_shape=[jax.ShapeDtypeStruct((part_rows, columns), jnp.bfloat16)] * len(blocks),
        compiler_params=pltpu.CompilerParams(vmem_limit_bytes=52 * 2**20),
        cost_estimate=pl.CostEstimate(
            flops=2 * gated.size * columns,
            bytes_accessed=2 * (weight.size + gated.size + rows * columns),
            transcendentals=0,
        ),
    )(jnp.stack(blocks).astype(jnp.int32), gated, weight)


def per_device(features, in_proj, short_taps, long_filter, skip_gain, out_proj):
    rows = features.shape[0]
    seq_parts = lax.axis_size("seq")
    tp_parts = lax.axis_size("tp")
    outer = outer_factor(seq_parts, tp_parts)
    inner_parts = seq_parts // outer
    streams, _, chan_tp = in_proj.shape
    chans = chan_tp // seq_parts
    position = lax.axis_index("seq")
    inner_groups = [[a * inner_parts + b for b in range(inner_parts)] for a in range(outer)]
    tp_groups = [
        [index * tp_parts + tp for index in group for tp in range(tp_parts)] for group in inner_groups
    ]

    weight = lax.all_gather(in_proj, "seq", axis=1, tiled=True, axis_index_groups=inner_groups)

    taps = lax.dynamic_slice_in_dim(short_taps, position * chans, chans, axis=2)
    taps = jnp.broadcast_to(taps[..., None], taps.shape + (rows,))
    skip = lax.dynamic_slice_in_dim(skip_gain, position * chans, chans, axis=0)
    skip = jnp.broadcast_to(skip[:, None], (chans, rows))
    filter_blocks = lax.all_to_all(
        long_filter.T.reshape(seq_parts, chans, rows), "seq", split_axis=0, concat_axis=0, tiled=True
    )

    held = share_columns(features, outer, tp_parts)
    arrived = cross_outer(held, (0, 1), outer, inner_parts, tp_parts)
    held, taps, skip, filter_blocks = lax.optimization_barrier((held, taps, skip, filter_blocks))
    if outer > 2:
        arrived |= cross_outer(held, (outer - 1,), outer, inner_parts, tp_parts)
    own = share_over_tp(arrived[0], tp_parts)
    held, arrived[1], own = lax.optimization_barrier((held, arrived[1], own))
    arrived |= cross_outer(held, range(2, outer - 1), outer, inner_parts, tp_parts)
    chunks = [own] + [share_over_tp(arrived[step], tp_parts) for step in range(1, outer)]
    chunks, out_proj = lax.optimization_barrier((chunks, out_proj))
    out_weight = lax.all_gather(out_proj, ("seq", "tp"), axis_index_groups=tp_groups)
    out_weight = out_weight.reshape((inner_parts, tp_parts) + out_proj.shape)

    partial = project_in(chunks, weight, seq_parts)
    parts = lax.all_to_all(partial, "seq", split_axis=0, concat_axis=0, tiled=True)

    gated = convolve([parts], filter_blocks, taps, skip, outer, tp_parts)
    gated = lax.all_to_all(
        gated.reshape((-1,) + gated.shape[3:]), ("tp", "seq"), split_axis=0, concat_axis=0, tiled=True
    )
    blocks, places = return_places(outer, inner_parts, tp_parts)
    pieces = project_out(gated.reshape(tp_parts, chan_tp, -1), out_weight, blocks)
    return return_output(pieces, places, inner_parts, tp_parts)


def solution(mesh):
    return jax.shard_map(
        per_device,
        mesh=mesh,
        in_specs=(
            P("seq", "tp"),
            P(None, "seq", "tp"),
            P(None, None, "tp"),
            P("seq", "tp"),
            P("tp"),
            P("tp", "seq"),
        ),
        out_specs=P("seq", "tp"),
        check_vma=False,
    )
```

```python
import functools
import math

import jax
import jax.numpy as jnp
import ml_dtypes
import numpy as np
from jax import lax
from jax.experimental import pallas as pl
from jax.experimental.pallas import tpu as pltpu
from jax.sharding import PartitionSpec as P

UNROLL = 16
HEAVY = 30


def outer_factor(seq_parts, tp_parts):
    outer = tp_parts
    while 4 * outer * outer <= seq_parts and seq_parts % (2 * outer) == 0:
        outer *= 2
    return outer


def assemble_kernel(place_ref, *refs):
    *piece_refs, out_ref, sems = refs
    part_rows, width = piece_refs[0].shape
    copies = []
    for index, piece_ref in enumerate(piece_refs):
        row = pl.multiple_of(place_ref[2 * index] * part_rows, part_rows)
        column = pl.multiple_of(place_ref[2 * index + 1] * width, width)
        target = out_ref.at[pl.ds(row, part_rows), pl.ds(column, width)]
        copies.append(pltpu.make_async_copy(piece_ref, target, sems.at[index]))
    for copy in copies:
        copy.start()
    for copy in copies:
        copy.wait()


def assemble(pieces, places, shape):
    return pl.pallas_call(
        assemble_kernel,
        in_specs=[pl.BlockSpec(memory_space=pltpu.SMEM)]
        + [pl.BlockSpec(memory_space=pltpu.VMEM)] * len(pieces),
        out_specs=pl.BlockSpec(memory_space=pl.ANY),
        out_shape=jax.ShapeDtypeStruct(shape, pieces[0].dtype),
        scratch_shapes=[pltpu.SemaphoreType.DMA((len(pieces),))],
        compiler_params=pltpu.CompilerParams(vmem_limit_bytes=4 * 2**20),
        cost_estimate=pl.CostEstimate(
            flops=0, bytes_accessed=4 * shape[0] * shape[1], transcendentals=0
        ),
    )(jnp.stack(places).astype(jnp.int32), *pieces)


def return_places(outer, inner_parts, tp_parts):
    per_tp = outer // tp_parts
    tp_place = lax.axis_index("tp")
    outer_place = lax.axis_index("seq") // inner_parts
    blocks, places = [], []
    for far in range(tp_parts):
        for near in range(per_tp):
            low = outer_place % per_tp
            blocks.append((tp_place + low + far) % tp_parts * per_tp + (low + near) % per_tp)
            low = (low - near + per_tp) % per_tp
            places.append((outer_place // per_tp - far - low + tp_parts + per_tp * tp_parts) % tp_parts)
            places.append(low)
    return blocks, places


def return_output(pieces, places, inner_parts, tp_parts):
    outer = len(pieces)
    part_rows, width = pieces[0].shape
    per_tp = outer // tp_parts
    arrived = []
    for index, piece in enumerate(pieces):
        far, near = divmod(index, per_tp)

        def target(seq, tp):
            src = seq // inner_parts
            low = src % per_tp
            dst = (tp + low + far) % tp_parts * per_tp + (low + near) % per_tp
            return (dst * inner_parts + seq % inner_parts) * tp_parts + src // per_tp

        pairs = [
            (seq * tp_parts + tp, target(seq, tp))
            for seq in range(outer * inner_parts)
            for tp in range(tp_parts)
        ]
        arrived.append(lax.ppermute(piece, ("seq", "tp"), pairs))
    return assemble(arrived, places, (tp_parts * part_rows, per_tp * width))


def share_columns(features, outer, inner_parts, tp_parts):
    _, cols = features.shape
    per_tp = outer // tp_parts
    width = cols // outer
    tp_place = lax.axis_index("tp")
    outer_place = lax.axis_index("seq") // inner_parts
    held = []
    for after in range(per_tp):
        group = (outer_place + 1 + after) % per_tp
        pieces = []
        for step in range(tp_parts):
            column = (group * tp_parts + (tp_place + step) % tp_parts) * width
            piece = lax.dynamic_slice_in_dim(features, column, width, axis=1)
            if step:
                pairs = [(i, (i + step) % tp_parts) for i in range(tp_parts)]
                piece = lax.ppermute(piece, "tp", pairs)
            pieces.append(piece)
        held.append(jnp.stack(pieces))
    return held


def cross_outer(held, steps, outer, inner_parts, tp_parts):
    per_tp = outer // tp_parts
    seq_parts = outer * inner_parts
    tp_place = lax.axis_index("tp")
    outer_place = lax.axis_index("seq") // inner_parts
    arrived = {}
    for step in steps:
        target = (outer_place + step) % outer
        which = (tp_place - target // per_tp + tp_parts) % tp_parts
        piece = lax.dynamic_index_in_dim(held[(step - 1) % per_tp], which, axis=0, keepdims=False)
        if step:
            far = step * inner_parts
            piece = lax.ppermute(piece, "seq", [(i, (i + far) % seq_parts) for i in range(seq_parts)])
        arrived[step] = piece
    return arrived


def share_over_tp(part, tp_parts):
    pieces = [part]
    for step in range(1, tp_parts):
        pairs = [(i, (i + step) % tp_parts) for i in range(tp_parts)]
        pieces.append(lax.ppermute(part, "tp", pairs))
    return pieces


def project_kernel(tp_parts, place_ref, *refs):
    *share_refs, weight_ref, out_ref, held, sems = refs
    seq_parts, streams, chans, count = out_ref.shape
    near_parts, far_parts = weight_ref.shape[:2]
    blocks = near_parts * far_parts // tp_parts
    copies = []
    for stream in range(streams):
        for step in range(tp_parts):
            which = lax.rem(place_ref[0] - step + tp_parts, tp_parts)
            for block in range(blocks):
                inner = which * blocks + block
                source = weight_ref.at[lax.rem(inner, near_parts), inner // near_parts, stream]
                slot = len(copies)
                copies.append(
                    pltpu.make_async_copy(source, held.at[stream, step, block], sems.at[slot])
                )
                copies[-1].start()
    left = [
        jnp.concatenate([share_ref[...] for share_ref in share_refs[step::tp_parts]])
        for step in range(tp_parts)
    ]
    for stream in range(streams):
        sums = jnp.zeros((count, seq_parts * chans), jnp.float32)
        for step in range(tp_parts):
            first = (stream * tp_parts + step) * blocks
            for copy in copies[first : first + blocks]:
                copy.wait()
            sums = sums + jnp.dot(
                left[step],
                held[stream, step].reshape(left[step].shape[1], -1),
                preferred_element_type=jnp.float32,
            )
        turned = sums.astype(out_ref.dtype).T
        for seq in range(seq_parts):
            out_ref[seq, stream] = turned[seq * chans : (seq + 1) * chans]


def project_in(chunks, weight, seq_parts):
    tp_parts = len(chunks[0])
    rows, width = chunks[0][0].shape
    near_parts, far_parts, streams, depth, chan_tp = weight.shape
    blocks = near_parts * far_parts // tp_parts
    chans = chan_tp // seq_parts
    pieces = [piece for chunk in chunks for piece in chunk]
    count = len(chunks) * rows
    place = lax.axis_index("tp").astype(jnp.int32)[None]
    vmem = pl.BlockSpec(memory_space=pltpu.VMEM)
    return pl.pallas_call(
        functools.partial(project_kernel, tp_parts),
        in_specs=[pl.BlockSpec(memory_space=pltpu.SMEM)]
        + [vmem] * len(pieces)
        + [pl.BlockSpec(memory_space=pl.ANY)],
        out_specs=vmem,
        out_shape=jax.ShapeDtypeStruct((seq_parts, streams, chans, count), jnp.bfloat16),
        scratch_shapes=[
            pltpu.VMEM((streams, tp_parts, blocks, depth, chan_tp), weight.dtype),
            pltpu.SemaphoreType.DMA((streams * tp_parts * blocks,)),
        ],
        compiler_params=pltpu.CompilerParams(vmem_limit_bytes=48 * 2**20),
        cost_estimate=pl.CostEstimate(
            flops=HEAVY * 2 * count * weight.size,
            bytes_accessed=2 * (weight.size + len(pieces) * pieces[0].size)
            + 2 * streams * count * seq_parts * chans,
            transcendentals=0,
        ),
    )(place, *pieces, weight)


def tables(block):
    place = np.arange(block)
    angle = 2.0 * math.pi * np.outer(place, place + 0.5) / (2 * block)
    forward = np.concatenate([np.cos(angle), -np.sin(angle)], 1)
    place = np.arange(2 * block)
    angle = 2.0 * math.pi * np.outer(np.arange(block) + 0.5, place) / (2 * block)
    backward = np.concatenate([np.cos(angle), -np.sin(angle)], 0) / block
    return halves(forward), halves(backward)


def halves(table):
    high = table.astype(ml_dtypes.bfloat16)
    low = (table - high.astype(np.float64)).astype(ml_dtypes.bfloat16)
    return np.stack([high, low])


def each(count, body):
    if isinstance(count, int) and count <= UNROLL:
        for index in range(count):
            body(index)
    else:
        lax.fori_loop(0, count, lambda index, carry: (body(index), carry)[1], 0)


def total(count, term, zero):
    if isinstance(count, int) and count <= UNROLL:
        result = zero
        for index in range(count):
            result = jax.tree.map(jnp.add, result, term(index))
        return result
    return lax.fori_loop(
        0, count, lambda index, sums: jax.tree.map(jnp.add, sums, term(index)), zero
    )


def conv_kernel(
    outer, chunks, *refs
):
    part_refs, refs = refs[:chunks], refs[chunks:]
    filter_ref, taps_ref, skip_ref, fwd_ref, bwd_ref, out_ref, *refs = refs
    proj, query, inner, spec, filter_spec, product, back = refs
    blocks, streams, chans, _ = part_refs[0].shape
    rows = filter_ref.shape[2]
    inner_parts = blocks // outer
    taps_count = taps_ref.shape[1]
    lane = lax.broadcasted_iota(jnp.int32, (chans, rows), 1)

    depth = outer // chunks

    def add_up(inner_index, stream, group):
        value = jnp.zeros((chans, rows), jnp.float32)
        for part in range(outer):
            slot = (part - group) % outer
            column = slice(slot % depth * rows, (slot % depth + 1) * rows)
            source = part_refs[slot // depth]
            value = value + source[part * inner_parts + inner_index, stream, :, column].astype(jnp.float32)
        proj[1 + group * inner_parts + inner_index, stream] = value

    for group in range(outer):
        for stream in range(streams):
            each(inner_parts, functools.partial(add_up, stream=stream, group=group))

    for stream in range(streams):
        proj[0, stream] = jnp.zeros((chans, rows), jnp.float32)

    def first(index):
        filtered = []
        for stream in range(streams):
            now, past = proj[index + 1, stream], proj[index, stream]
            value = taps_ref[stream, 0] * now
            for offset in range(1, taps_count):
                moved = pltpu.roll(jnp.where(lane < rows - offset, now, past), offset, 1)
                value = value + taps_ref[stream, offset] * moved
            filtered.append(value)
        query[index] = filtered[0]
        inner[index] = filtered[1] * filtered[2]

    each(blocks, first)

    def product_of(value, table_ref):
        high = value.astype(jnp.bfloat16)
        low = (value - high.astype(jnp.float32)).astype(jnp.bfloat16)
        return (
            jnp.dot(high, table_ref[0], preferred_element_type=jnp.float32)
            + jnp.dot(low, table_ref[0], preferred_element_type=jnp.float32)
            + jnp.dot(high, table_ref[1], preferred_element_type=jnp.float32)
        )

    def apply(source, table_ref, target):
        if chans % 8 == 0:
            flat = source[...].reshape(blocks * chans, source.shape[2])
            target[...] = product_of(flat, table_ref).reshape(target.shape)
        else:

            def one(index):
                target[index] = product_of(source[index], table_ref)

            each(blocks, one)

    apply(filter_ref, fwd_ref, filter_spec)
    apply(inner, fwd_ref, spec)

    def multiply(index):
        def term(step):
            left, right = spec[step], filter_spec[index - step]
            left_real, left_imag = left[:, :rows], left[:, rows:]
            right_real, right_imag = right[:, :rows], right[:, rows:]
            return (
                left_real * right_real - left_imag * right_imag,
                left_real * right_imag + left_imag * right_real,
            )

        zero = jnp.zeros((chans, rows), jnp.float32)
        real, imag = total(index + 1, term, (zero, zero))
        product[index, :, :rows] = real
        product[index, :, rows:] = imag

    each(blocks, multiply)
    apply(product, bwd_ref, back)

    def last(index, carried):
        long_mix = back[index, :, :rows] + carried
        query[index] = query[index] * (long_mix + skip_ref[...] * inner[index])

    last(0, jnp.zeros((chans, rows), jnp.float32))
    each(blocks - 1, lambda index: last(index + 1, back[index, :, rows:]))

    tp_parts = out_ref.shape[0]
    part_rows = rows // tp_parts
    copies = out_ref.shape[1]

    def spread(inner_index):
        for part in range(tp_parts):
            for group in range(outer // tp_parts):
                packed = jnp.zeros((chans, rows), jnp.float32)
                for place in range(tp_parts):
                    block = query[(group * tp_parts + place) * inner_parts + inner_index]
                    shift = (place - part) * part_rows % rows
                    block = pltpu.roll(block, shift, 1) if shift else block
                    packed = jnp.where(lane // part_rows == place, block, packed)
                packed = packed.astype(out_ref.dtype)
                for copy in range(copies):
                    out_ref[part, copy, inner_index, :, group * rows : (group + 1) * rows] = packed

    each(inner_parts, spread)


def convolve(parts, filter_blocks, taps, skip, outer, tp_parts):
    blocks, streams, chans, _ = parts[0].shape
    rows = filter_blocks.shape[2]
    forward, backward = tables(rows)
    wide = (blocks, chans, 2 * rows)
    narrow = (blocks, chans, rows)
    vmem = pl.BlockSpec(memory_space=pltpu.VMEM)
    return pl.pallas_call(
        functools.partial(conv_kernel, outer, len(parts)),
        out_shape=jax.ShapeDtypeStruct(
            (tp_parts, outer, blocks // outer, chans, outer // tp_parts * rows), jnp.bfloat16
        ),
        in_specs=[vmem] * (5 + len(parts)),
        out_specs=vmem,
        scratch_shapes=[
            pltpu.VMEM((blocks + 1, streams, chans, rows), jnp.float32),
            pltpu.VMEM(narrow, jnp.float32),
            pltpu.VMEM(narrow, jnp.float32),
            pltpu.VMEM(wide, jnp.float32),
            pltpu.VMEM(wide, jnp.float32),
            pltpu.VMEM(wide, jnp.float32),
            pltpu.VMEM(wide, jnp.float32),
        ],
        compiler_params=pltpu.CompilerParams(vmem_limit_bytes=40 * 2**20),
        cost_estimate=pl.CostEstimate(flops=10**9, bytes_accessed=4 * 2**20, transcendentals=0),
    )(*parts, filter_blocks, taps, skip, jnp.asarray(forward), jnp.asarray(backward))


def out_kernel(block_ref, gated_ref, weight_ref, *refs):
    *out_refs, turned, left, held, sems = refs
    tp_parts = gated_ref.shape[0]
    part_rows = out_refs[0].shape[0]
    inner_parts, _, _, width = held.shape
    copies = [
        pltpu.make_async_copy(weight_ref.at[inner], held.at[inner], sems.at[inner])
        for inner in range(inner_parts)
    ]
    for copy in copies:
        copy.start()
    for part in range(tp_parts):
        turned[...] = gated_ref[part].T
        for index in range(len(out_refs)):
            begin = pl.multiple_of(block_ref[index] * part_rows, part_rows)
            left[part, index * part_rows : (index + 1) * part_rows] = turned[pl.ds(begin, part_rows)]
    for inner in range(inner_parts):
        copies[inner].wait()
        sums = jnp.zeros((left.shape[1], width), jnp.float32)
        for part in range(tp_parts):
            sums = sums + jnp.dot(left[part], held[inner, part], preferred_element_type=jnp.float32)
        for index, out_ref in enumerate(out_refs):
            out_ref[:, inner * width : (inner + 1) * width] = sums[
                index * part_rows : (index + 1) * part_rows
            ].astype(out_ref.dtype)


def project_out(gated, weight, blocks):
    tp_parts, depth, rows = gated.shape
    inner_parts, _, _, width = weight.shape
    columns = inner_parts * width
    part_rows = rows // len(blocks)
    vmem = pl.BlockSpec(memory_space=pltpu.VMEM)
    return pl.pallas_call(
        out_kernel,
        in_specs=[
            pl.BlockSpec(memory_space=pltpu.SMEM),
            vmem,
            pl.BlockSpec(memory_space=pl.ANY),
        ],
        out_specs=[vmem] * len(blocks),
        scratch_shapes=[
            pltpu.VMEM((rows, depth), jnp.bfloat16),
            pltpu.VMEM((tp_parts, rows, depth), jnp.bfloat16),
            pltpu.VMEM(weight.shape, weight.dtype),
            pltpu.SemaphoreType.DMA((inner_parts,)),
        ],
        out_shape=[jax.ShapeDtypeStruct((part_rows, columns), jnp.bfloat16)] * len(blocks),
        compiler_params=pltpu.CompilerParams(vmem_limit_bytes=52 * 2**20),
        cost_estimate=pl.CostEstimate(
            flops=2 * gated.size * columns,
            bytes_accessed=2 * (weight.size + gated.size + rows * columns),
            transcendentals=0,
        ),
    )(jnp.stack(blocks).astype(jnp.int32), gated, weight)


def per_device(features, in_proj, short_taps, long_filter, skip_gain, out_proj):
    rows = features.shape[0]
    seq_parts = lax.axis_size("seq")
    tp_parts = lax.axis_size("tp")
    outer = outer_factor(seq_parts, tp_parts)
    inner_parts = seq_parts // outer
    streams, _, chan_tp = in_proj.shape
    chans = chan_tp // seq_parts
    position = lax.axis_index("seq")
    inner_groups = [[a * inner_parts + b for b in range(inner_parts)] for a in range(outer)]
    tp_groups = [
        [index * tp_parts + tp for index in group for tp in range(tp_parts)] for group in inner_groups
    ]

    near = 2 if inner_parts % 2 == 0 else 1
    far_groups = [group[index::near] for group in inner_groups for index in range(near)]
    near_groups = [
        group[index : index + near] for group in inner_groups for index in range(0, inner_parts, near)
    ]
    weight = lax.all_gather(in_proj, "seq", axis_index_groups=far_groups)

    taps = lax.dynamic_slice_in_dim(short_taps, position * chans, chans, axis=2)
    taps = jnp.broadcast_to(taps[..., None], taps.shape + (rows,))
    skip = lax.dynamic_slice_in_dim(skip_gain, position * chans, chans, axis=0)
    skip = jnp.broadcast_to(skip[:, None], (chans, rows))
    filter_blocks = lax.all_to_all(
        long_filter.T.reshape(seq_parts, chans, rows), "seq", split_axis=0, concat_axis=0, tiled=True
    )

    held = share_columns(features, outer, inner_parts, tp_parts)
    arrived = cross_outer(held, (0, 1), outer, inner_parts, tp_parts)
    held[0], taps, skip, filter_blocks = lax.optimization_barrier((held[0], taps, skip, filter_blocks))
    if outer > 2:
        arrived |= cross_outer(held, (outer - 1,), outer, inner_parts, tp_parts)
    own = share_over_tp(arrived[0], tp_parts)
    held, arrived[1], own = lax.optimization_barrier((held, arrived[1], own))
    arrived |= cross_outer(held, range(2, outer - 1), outer, inner_parts, tp_parts)
    chunks = [own] + [share_over_tp(arrived[step], tp_parts) for step in range(1, outer)]
    last = chunks[outer // 2]
    last[0], weight = lax.optimization_barrier((last[0], weight))
    weight = lax.all_gather(weight, "seq", axis_index_groups=near_groups)

    chunks, out_proj = lax.optimization_barrier((chunks, out_proj))
    out_weight = lax.all_gather(out_proj, ("seq", "tp"), axis_index_groups=tp_groups)
    out_weight = out_weight.reshape((inner_parts, tp_parts) + out_proj.shape)

    partial = project_in(chunks, weight, seq_parts)
    parts = lax.all_to_all(partial, "seq", split_axis=0, concat_axis=0, tiled=True)

    gated = convolve([parts], filter_blocks, taps, skip, outer, tp_parts)
    gated = lax.all_to_all(
        gated.reshape((-1,) + gated.shape[3:]), ("tp", "seq"), split_axis=0, concat_axis=0, tiled=True
    )
    blocks, places = return_places(outer, inner_parts, tp_parts)
    pieces = project_out(gated.reshape(tp_parts, chan_tp, -1), out_weight, blocks)
    return return_output(pieces, places, inner_parts, tp_parts)


def solution(mesh):
    return jax.shard_map(
        per_device,
        mesh=mesh,
        in_specs=(
            P("seq", "tp"),
            P(None, "seq", "tp"),
            P(None, None, "tp"),
            P("seq", "tp"),
            P("tp"),
            P("tp", "seq"),
        ),
        out_specs=P("seq", "tp"),
        check_vma=False,
    )
```

```python
import functools
import math

import jax
import jax.numpy as jnp
import ml_dtypes
import numpy as np
from jax import lax
from jax.experimental import pallas as pl
from jax.experimental.pallas import tpu as pltpu
from jax.sharding import PartitionSpec as P

UNROLL = 16
HEAVY = 30


def outer_factor(seq_parts, tp_parts):
    outer = tp_parts
    while 4 * outer * outer <= seq_parts and seq_parts % (2 * outer) == 0:
        outer *= 2
    return outer


def assemble_kernel(place_ref, *refs):
    *piece_refs, out_ref, sems = refs
    part_rows, width = piece_refs[0].shape
    copies = []
    for index, piece_ref in enumerate(piece_refs):
        row = pl.multiple_of(place_ref[2 * index] * part_rows, part_rows)
        column = pl.multiple_of(place_ref[2 * index + 1] * width, width)
        target = out_ref.at[pl.ds(row, part_rows), pl.ds(column, width)]
        copies.append(pltpu.make_async_copy(piece_ref, target, sems.at[index]))
    for copy in copies:
        copy.start()
    for copy in copies:
        copy.wait()


def assemble(pieces, places, shape):
    return pl.pallas_call(
        assemble_kernel,
        in_specs=[pl.BlockSpec(memory_space=pltpu.SMEM)]
        + [pl.BlockSpec(memory_space=pltpu.VMEM)] * len(pieces),
        out_specs=pl.BlockSpec(memory_space=pl.ANY),
        out_shape=jax.ShapeDtypeStruct(shape, pieces[0].dtype),
        scratch_shapes=[pltpu.SemaphoreType.DMA((len(pieces),))],
        compiler_params=pltpu.CompilerParams(vmem_limit_bytes=4 * 2**20),
        cost_estimate=pl.CostEstimate(
            flops=0, bytes_accessed=4 * shape[0] * shape[1], transcendentals=0
        ),
    )(jnp.stack(places).astype(jnp.int32), *pieces)


def return_places(outer, inner_parts, tp_parts):
    per_tp = outer // tp_parts
    tp_place = lax.axis_index("tp")
    outer_place = lax.axis_index("seq") // inner_parts
    blocks, places = [], []
    for far in range(tp_parts):
        for near in range(per_tp):
            low = outer_place % per_tp
            blocks.append((tp_place + low + far) % tp_parts * per_tp + (low + near) % per_tp)
            low = (low - near + per_tp) % per_tp
            places.append((outer_place // per_tp - far - low + tp_parts + per_tp * tp_parts) % tp_parts)
            places.append(low)
    return blocks, places


def return_output(pieces, places, inner_parts, tp_parts):
    outer = len(pieces)
    part_rows, width = pieces[0].shape
    per_tp = outer // tp_parts
    arrived = []
    for index, piece in enumerate(pieces):
        far, near = divmod(index, per_tp)

        def target(seq, tp):
            src = seq // inner_parts
            low = src % per_tp
            dst = (tp + low + far) % tp_parts * per_tp + (low + near) % per_tp
            return (dst * inner_parts + seq % inner_parts) * tp_parts + src // per_tp

        pairs = [
            (seq * tp_parts + tp, target(seq, tp))
            for seq in range(outer * inner_parts)
            for tp in range(tp_parts)
        ]
        arrived.append(lax.ppermute(piece, ("seq", "tp"), pairs))
    return assemble(arrived, places, (tp_parts * part_rows, per_tp * width))


def share_columns(features, outer, inner_parts, tp_parts):
    _, cols = features.shape
    per_tp = outer // tp_parts
    width = cols // outer
    tp_place = lax.axis_index("tp")
    outer_place = lax.axis_index("seq") // inner_parts
    held = []
    for after in range(per_tp):
        group = (outer_place + 1 + after) % per_tp
        pieces = []
        for step in range(tp_parts):
            column = (group * tp_parts + (tp_place + step) % tp_parts) * width
            piece = lax.dynamic_slice_in_dim(features, column, width, axis=1)
            if step:
                pairs = [(i, (i + step) % tp_parts) for i in range(tp_parts)]
                piece = lax.ppermute(piece, "tp", pairs)
            pieces.append(piece)
        held.append(jnp.stack(pieces))
    return held


def cross_outer(held, steps, outer, inner_parts, tp_parts):
    per_tp = outer // tp_parts
    seq_parts = outer * inner_parts
    tp_place = lax.axis_index("tp")
    outer_place = lax.axis_index("seq") // inner_parts
    arrived = {}
    for step in steps:
        target = (outer_place + step) % outer
        which = (tp_place - target // per_tp + tp_parts) % tp_parts
        piece = lax.dynamic_index_in_dim(held[(step - 1) % per_tp], which, axis=0, keepdims=False)
        if step:
            far = step * inner_parts
            piece = lax.ppermute(piece, "seq", [(i, (i + far) % seq_parts) for i in range(seq_parts)])
        arrived[step] = piece
    return arrived


def share_over_tp(part, tp_parts):
    pieces = [part]
    for step in range(1, tp_parts):
        pairs = [(i, (i + step) % tp_parts) for i in range(tp_parts)]
        pieces.append(lax.ppermute(part, "tp", pairs))
    return pieces


def gather_inner(block, inner_parts):
    held, masks = [block], [0]
    bit = inner_parts // 2
    while bit:
        pairs = [(i, i ^ bit) for i in range(lax.axis_size("seq"))]
        held += [lax.ppermute(piece, "seq", pairs) for piece in held]
        masks += [mask ^ bit for mask in masks]
        bit //= 2
    return held, masks


def project_kernel(tp_parts, masks, place_ref, *refs):
    *refs, weight_ref, out_ref, held, weight_sems, shard_sems = refs
    share_refs, shard_refs = refs[: -len(masks)], refs[-len(masks) :]
    seq_parts, streams, chans, count = out_ref.shape
    gathered = weight_ref.shape[0]
    depth = shard_refs[0].shape[1]
    blocks = len(masks) // tp_parts
    copies = {stream: [] for stream in range(streams)}
    for stream in range(gathered):
        for step in range(tp_parts):
            which = lax.rem(place_ref[0] - step + tp_parts, tp_parts)
            copies[stream].append(
                pltpu.make_async_copy(
                    weight_ref.at[stream, which], held.at[stream, step], weight_sems.at[stream, step]
                )
            )
    for slot, mask in enumerate(masks):
        inner = jnp.bitwise_xor(place_ref[1], mask)
        step = lax.rem(place_ref[0] - inner // blocks + tp_parts, tp_parts)
        row = pl.multiple_of(lax.rem(inner, blocks) * depth, depth)
        for stream in range(gathered, streams):
            copies[stream].append(
                pltpu.make_async_copy(
                    shard_refs[slot].at[stream - gathered],
                    held.at[stream, step, pl.ds(row, depth)],
                    shard_sems.at[stream - gathered, slot],
                )
            )
    order = [*range(gathered, streams), *range(gathered)]
    for stream in order:
        for copy in copies[stream]:
            copy.start()
    left = [
        jnp.concatenate([share_ref[...] for share_ref in share_refs[step::tp_parts]])
        for step in range(tp_parts)
    ]
    for stream in order:
        for copy in copies[stream]:
            copy.wait()
        sums = jnp.zeros((count, seq_parts * chans), jnp.float32)
        for step in range(tp_parts):
            sums = sums + jnp.dot(
                left[step], held[stream, step], preferred_element_type=jnp.float32
            )
        turned = sums.astype(out_ref.dtype).T
        for seq in range(seq_parts):
            out_ref[seq, stream] = turned[seq * chans : (seq + 1) * chans]


def project_in(chunks, weight, shards, masks, inner_parts, seq_parts):
    tp_parts = len(chunks[0])
    rows, width = chunks[0][0].shape
    gathered, _, chan_tp = weight.shape
    weight = weight.reshape(gathered, tp_parts, width, chan_tp)
    sent = shards[0].shape[0]
    streams = gathered + sent
    chans = chan_tp // seq_parts
    pieces = [piece for chunk in chunks for piece in chunk]
    count = len(chunks) * rows
    place = jnp.stack([lax.axis_index("tp"), lax.axis_index("seq") % inner_parts]).astype(jnp.int32)
    vmem = pl.BlockSpec(memory_space=pltpu.VMEM)
    return pl.pallas_call(
        functools.partial(project_kernel, tp_parts, masks),
        in_specs=[pl.BlockSpec(memory_space=pltpu.SMEM)]
        + [vmem] * (len(pieces) + len(shards))
        + [pl.BlockSpec(memory_space=pl.ANY)],
        out_specs=vmem,
        out_shape=jax.ShapeDtypeStruct((seq_parts, streams, chans, count), jnp.bfloat16),
        scratch_shapes=[
            pltpu.VMEM((streams, tp_parts, width, chan_tp), weight.dtype),
            pltpu.SemaphoreType.DMA((gathered, tp_parts)),
            pltpu.SemaphoreType.DMA((sent, len(shards))),
        ],
        compiler_params=pltpu.CompilerParams(vmem_limit_bytes=48 * 2**20),
        cost_estimate=pl.CostEstimate(
            flops=HEAVY * 2 * count * weight.size,
            bytes_accessed=2 * (weight.size + len(pieces) * pieces[0].size)
            + 2 * streams * count * seq_parts * chans,
            transcendentals=0,
        ),
    )(place, *pieces, *shards, weight)


def tables(block):
    place = np.arange(block)
    angle = 2.0 * math.pi * np.outer(place, place + 0.5) / (2 * block)
    forward = np.concatenate([np.cos(angle), -np.sin(angle)], 1)
    place = np.arange(2 * block)
    angle = 2.0 * math.pi * np.outer(np.arange(block) + 0.5, place) / (2 * block)
    backward = np.concatenate([np.cos(angle), -np.sin(angle)], 0) / block
    return halves(forward), halves(backward)


def halves(table):
    high = table.astype(ml_dtypes.bfloat16)
    low = (table - high.astype(np.float64)).astype(ml_dtypes.bfloat16)
    return np.stack([high, low])


def each(count, body):
    if isinstance(count, int) and count <= UNROLL:
        for index in range(count):
            body(index)
    else:
        lax.fori_loop(0, count, lambda index, carry: (body(index), carry)[1], 0)


def total(count, term, zero):
    if isinstance(count, int) and count <= UNROLL:
        result = zero
        for index in range(count):
            result = jax.tree.map(jnp.add, result, term(index))
        return result
    return lax.fori_loop(
        0, count, lambda index, sums: jax.tree.map(jnp.add, sums, term(index)), zero
    )


def conv_kernel(
    outer, chunks, *refs
):
    part_refs, refs = refs[:chunks], refs[chunks:]
    filter_ref, taps_ref, skip_ref, fwd_ref, bwd_ref, out_ref, *refs = refs
    proj, query, inner, spec, filter_spec, product, back = refs
    blocks, streams, chans, _ = part_refs[0].shape
    rows = filter_ref.shape[2]
    inner_parts = blocks // outer
    taps_count = taps_ref.shape[1]
    lane = lax.broadcasted_iota(jnp.int32, (chans, rows), 1)

    depth = outer // chunks

    def add_up(inner_index, stream, group):
        value = jnp.zeros((chans, rows), jnp.float32)
        for part in range(outer):
            slot = (part - group) % outer
            column = slice(slot % depth * rows, (slot % depth + 1) * rows)
            source = part_refs[slot // depth]
            value = value + source[part * inner_parts + inner_index, stream, :, column].astype(jnp.float32)
        proj[1 + group * inner_parts + inner_index, stream] = value

    for group in range(outer):
        for stream in range(streams):
            each(inner_parts, functools.partial(add_up, stream=stream, group=group))

    for stream in range(streams):
        proj[0, stream] = jnp.zeros((chans, rows), jnp.float32)

    def first(index):
        filtered = []
        for stream in range(streams):
            now, past = proj[index + 1, stream], proj[index, stream]
            value = taps_ref[stream, 0] * now
            for offset in range(1, taps_count):
                moved = pltpu.roll(jnp.where(lane < rows - offset, now, past), offset, 1)
                value = value + taps_ref[stream, offset] * moved
            filtered.append(value)
        query[index] = filtered[0]
        inner[index] = filtered[1] * filtered[2]

    each(blocks, first)

    def product_of(value, table_ref):
        high = value.astype(jnp.bfloat16)
        low = (value - high.astype(jnp.float32)).astype(jnp.bfloat16)
        return (
            jnp.dot(high, table_ref[0], preferred_element_type=jnp.float32)
            + jnp.dot(low, table_ref[0], preferred_element_type=jnp.float32)
            + jnp.dot(high, table_ref[1], preferred_element_type=jnp.float32)
        )

    def apply(source, table_ref, target):
        if chans % 8 == 0:
            flat = source[...].reshape(blocks * chans, source.shape[2])
            target[...] = product_of(flat, table_ref).reshape(target.shape)
        else:

            def one(index):
                target[index] = product_of(source[index], table_ref)

            each(blocks, one)

    apply(filter_ref, fwd_ref, filter_spec)
    apply(inner, fwd_ref, spec)

    def multiply(index):
        def term(step):
            left, right = spec[step], filter_spec[index - step]
            left_real, left_imag = left[:, :rows], left[:, rows:]
            right_real, right_imag = right[:, :rows], right[:, rows:]
            return (
                left_real * right_real - left_imag * right_imag,
                left_real * right_imag + left_imag * right_real,
            )

        zero = jnp.zeros((chans, rows), jnp.float32)
        real, imag = total(index + 1, term, (zero, zero))
        product[index, :, :rows] = real
        product[index, :, rows:] = imag

    each(blocks, multiply)
    apply(product, bwd_ref, back)

    def last(index, carried):
        long_mix = back[index, :, :rows] + carried
        query[index] = query[index] * (long_mix + skip_ref[...] * inner[index])

    last(0, jnp.zeros((chans, rows), jnp.float32))
    each(blocks - 1, lambda index: last(index + 1, back[index, :, rows:]))

    tp_parts = out_ref.shape[0]
    part_rows = rows // tp_parts
    copies = out_ref.shape[1]

    def spread(inner_index):
        for part in range(tp_parts):
            for group in range(outer // tp_parts):
                packed = jnp.zeros((chans, rows), jnp.float32)
                for place in range(tp_parts):
                    block = query[(group * tp_parts + place) * inner_parts + inner_index]
                    shift = (place - part) * part_rows % rows
                    block = pltpu.roll(block, shift, 1) if shift else block
                    packed = jnp.where(lane // part_rows == place, block, packed)
                packed = packed.astype(out_ref.dtype)
                for copy in range(copies):
                    out_ref[part, copy, inner_index, :, group * rows : (group + 1) * rows] = packed

    each(inner_parts, spread)


def convolve(parts, filter_blocks, taps, skip, outer, tp_parts):
    blocks, streams, chans, _ = parts[0].shape
    rows = filter_blocks.shape[2]
    forward, backward = tables(rows)
    wide = (blocks, chans, 2 * rows)
    narrow = (blocks, chans, rows)
    vmem = pl.BlockSpec(memory_space=pltpu.VMEM)
    return pl.pallas_call(
        functools.partial(conv_kernel, outer, len(parts)),
        out_shape=jax.ShapeDtypeStruct(
            (tp_parts, outer, blocks // outer, chans, outer // tp_parts * rows), jnp.bfloat16
        ),
        in_specs=[vmem] * (5 + len(parts)),
        out_specs=vmem,
        scratch_shapes=[
            pltpu.VMEM((blocks + 1, streams, chans, rows), jnp.float32),
            pltpu.VMEM(narrow, jnp.float32),
            pltpu.VMEM(narrow, jnp.float32),
            pltpu.VMEM(wide, jnp.float32),
            pltpu.VMEM(wide, jnp.float32),
            pltpu.VMEM(wide, jnp.float32),
            pltpu.VMEM(wide, jnp.float32),
        ],
        compiler_params=pltpu.CompilerParams(vmem_limit_bytes=40 * 2**20),
        cost_estimate=pl.CostEstimate(flops=10**9, bytes_accessed=4 * 2**20, transcendentals=0),
    )(*parts, filter_blocks, taps, skip, jnp.asarray(forward), jnp.asarray(backward))


def out_kernel(block_ref, gated_ref, weight_ref, *refs):
    *out_refs, turned, left, held, sems = refs
    tp_parts = gated_ref.shape[0]
    part_rows = out_refs[0].shape[0]
    inner_parts, _, _, width = held.shape
    copies = [
        pltpu.make_async_copy(weight_ref.at[inner], held.at[inner], sems.at[inner])
        for inner in range(inner_parts)
    ]
    for copy in copies:
        copy.start()
    for part in range(tp_parts):
        turned[...] = gated_ref[part].T
        for index in range(len(out_refs)):
            begin = pl.multiple_of(block_ref[index] * part_rows, part_rows)
            left[part, index * part_rows : (index + 1) * part_rows] = turned[pl.ds(begin, part_rows)]
    for inner in range(inner_parts):
        copies[inner].wait()
        sums = jnp.zeros((left.shape[1], width), jnp.float32)
        for part in range(tp_parts):
            sums = sums + jnp.dot(left[part], held[inner, part], preferred_element_type=jnp.float32)
        for index, out_ref in enumerate(out_refs):
            out_ref[:, inner * width : (inner + 1) * width] = sums[
                index * part_rows : (index + 1) * part_rows
            ].astype(out_ref.dtype)


def project_out(gated, weight, blocks):
    tp_parts, depth, rows = gated.shape
    inner_parts, _, _, width = weight.shape
    columns = inner_parts * width
    part_rows = rows // len(blocks)
    vmem = pl.BlockSpec(memory_space=pltpu.VMEM)
    return pl.pallas_call(
        out_kernel,
        in_specs=[
            pl.BlockSpec(memory_space=pltpu.SMEM),
            vmem,
            pl.BlockSpec(memory_space=pl.ANY),
        ],
        out_specs=[vmem] * len(blocks),
        scratch_shapes=[
            pltpu.VMEM((rows, depth), jnp.bfloat16),
            pltpu.VMEM((tp_parts, rows, depth), jnp.bfloat16),
            pltpu.VMEM(weight.shape, weight.dtype),
            pltpu.SemaphoreType.DMA((inner_parts,)),
        ],
        out_shape=[jax.ShapeDtypeStruct((part_rows, columns), jnp.bfloat16)] * len(blocks),
        compiler_params=pltpu.CompilerParams(vmem_limit_bytes=52 * 2**20),
        cost_estimate=pl.CostEstimate(
            flops=2 * gated.size * columns,
            bytes_accessed=2 * (weight.size + gated.size + rows * columns),
            transcendentals=0,
        ),
    )(jnp.stack(blocks).astype(jnp.int32), gated, weight)


def per_device(features, in_proj, short_taps, long_filter, skip_gain, out_proj):
    rows = features.shape[0]
    seq_parts = lax.axis_size("seq")
    tp_parts = lax.axis_size("tp")
    outer = outer_factor(seq_parts, tp_parts)
    inner_parts = seq_parts // outer
    streams, _, chan_tp = in_proj.shape
    chans = chan_tp // seq_parts
    position = lax.axis_index("seq")
    inner_groups = [[a * inner_parts + b for b in range(inner_parts)] for a in range(outer)]
    tp_groups = [
        [index * tp_parts + tp for index in group for tp in range(tp_parts)] for group in inner_groups
    ]

    weight = lax.all_gather(
        in_proj[: streams - 1], "seq", axis=1, tiled=True, axis_index_groups=inner_groups
    )
    shards, masks = gather_inner(in_proj[streams - 1 :], inner_parts)

    taps = lax.dynamic_slice_in_dim(short_taps, position * chans, chans, axis=2)
    taps = jnp.broadcast_to(taps[..., None], taps.shape + (rows,))
    skip = lax.dynamic_slice_in_dim(skip_gain, position * chans, chans, axis=0)
    skip = jnp.broadcast_to(skip[:, None], (chans, rows))
    filter_blocks = lax.all_to_all(
        long_filter.T.reshape(seq_parts, chans, rows), "seq", split_axis=0, concat_axis=0, tiled=True
    )

    held = share_columns(features, outer, inner_parts, tp_parts)
    arrived = cross_outer(held, sorted({0, 1, outer - 1}), outer, inner_parts, tp_parts)
    own = share_over_tp(arrived[0], tp_parts)
    first = [arrived[step] for step in sorted({1, outer - 1})]
    held, first, own, taps, skip, filter_blocks = lax.optimization_barrier(
        (held, first, own, taps, skip, filter_blocks)
    )
    arrived |= dict(zip(sorted({1, outer - 1}), first))
    arrived |= cross_outer(held, range(2, outer - 1), outer, inner_parts, tp_parts)
    chunks = [own] + [share_over_tp(arrived[step], tp_parts) for step in range(1, outer)]
    chunks, out_proj = lax.optimization_barrier((chunks, out_proj))
    out_weight = lax.all_gather(out_proj, ("seq", "tp"), axis_index_groups=tp_groups)
    out_weight = out_weight.reshape((inner_parts, tp_parts) + out_proj.shape)

    partial = project_in(chunks, weight, shards, masks, inner_parts, seq_parts)
    parts = lax.all_to_all(partial, "seq", split_axis=0, concat_axis=0, tiled=True)

    gated = convolve([parts], filter_blocks, taps, skip, outer, tp_parts)
    gated = lax.all_to_all(
        gated.reshape((-1,) + gated.shape[3:]), ("tp", "seq"), split_axis=0, concat_axis=0, tiled=True
    )
    blocks, places = return_places(outer, inner_parts, tp_parts)
    pieces = project_out(gated.reshape(tp_parts, chan_tp, -1), out_weight, blocks)
    return return_output(pieces, places, inner_parts, tp_parts)


def solution(mesh):
    return jax.shard_map(
        per_device,
        mesh=mesh,
        in_specs=(
            P("seq", "tp"),
            P(None, "seq", "tp"),
            P(None, None, "tp"),
            P("seq", "tp"),
            P("tp"),
            P("tp", "seq"),
        ),
        out_specs=P("seq", "tp"),
        check_vma=False,
    )
```

```python
import functools
import math

import jax
import jax.numpy as jnp
import ml_dtypes
import numpy as np
from jax import lax
from jax.experimental import pallas as pl
from jax.experimental.pallas import tpu as pltpu
from jax.sharding import PartitionSpec as P

UNROLL = 16
HEAVY = 30


def outer_factor(seq_parts, tp_parts):
    outer = tp_parts
    while 4 * outer * outer <= seq_parts and seq_parts % (2 * outer) == 0:
        outer *= 2
    return outer


def assemble_kernel(place_ref, *refs):
    *piece_refs, out_ref, sems = refs
    part_rows, width = piece_refs[0].shape
    copies = []
    for index, piece_ref in enumerate(piece_refs):
        row = pl.multiple_of(place_ref[2 * index] * part_rows, part_rows)
        column = pl.multiple_of(place_ref[2 * index + 1] * width, width)
        target = out_ref.at[pl.ds(row, part_rows), pl.ds(column, width)]
        copies.append(pltpu.make_async_copy(piece_ref, target, sems.at[index]))
    for copy in copies:
        copy.start()
    for copy in copies:
        copy.wait()


def assemble(pieces, places, shape):
    return pl.pallas_call(
        assemble_kernel,
        in_specs=[pl.BlockSpec(memory_space=pltpu.SMEM)]
        + [pl.BlockSpec(memory_space=pltpu.VMEM)] * len(pieces),
        out_specs=pl.BlockSpec(memory_space=pl.ANY),
        out_shape=jax.ShapeDtypeStruct(shape, pieces[0].dtype),
        scratch_shapes=[pltpu.SemaphoreType.DMA((len(pieces),))],
        compiler_params=pltpu.CompilerParams(vmem_limit_bytes=4 * 2**20),
        cost_estimate=pl.CostEstimate(
            flops=0, bytes_accessed=4 * shape[0] * shape[1], transcendentals=0
        ),
    )(jnp.stack(places).astype(jnp.int32), *pieces)


def return_places(outer, inner_parts, tp_parts):
    per_tp = outer // tp_parts
    tp_place = lax.axis_index("tp")
    outer_place = lax.axis_index("seq") // inner_parts
    blocks, places = [], []
    for far in range(tp_parts):
        for near in range(per_tp):
            low = outer_place % per_tp
            blocks.append((tp_place + low + far) % tp_parts * per_tp + (low + near) % per_tp)
            low = (low - near + per_tp) % per_tp
            places.append((outer_place // per_tp - far - low + tp_parts + per_tp * tp_parts) % tp_parts)
            places.append(low)
    return blocks, places


def return_output(pieces, places, inner_parts, tp_parts):
    outer = len(pieces)
    part_rows, width = pieces[0].shape
    per_tp = outer // tp_parts
    arrived = []
    for index, piece in enumerate(pieces):
        far, near = divmod(index, per_tp)

        def target(seq, tp):
            src = seq // inner_parts
            low = src % per_tp
            dst = (tp + low + far) % tp_parts * per_tp + (low + near) % per_tp
            return (dst * inner_parts + seq % inner_parts) * tp_parts + src // per_tp

        pairs = [
            (seq * tp_parts + tp, target(seq, tp))
            for seq in range(outer * inner_parts)
            for tp in range(tp_parts)
        ]
        arrived.append(lax.ppermute(piece, ("seq", "tp"), pairs))
    return assemble(arrived, places, (tp_parts * part_rows, per_tp * width))


def share_columns(features, outer, inner_parts, tp_parts):
    _, cols = features.shape
    per_tp = outer // tp_parts
    width = cols // outer
    tp_place = lax.axis_index("tp")
    outer_place = lax.axis_index("seq") // inner_parts
    held = []
    for after in range(per_tp):
        group = (outer_place + 1 + after) % per_tp
        pieces = []
        for step in range(tp_parts):
            column = (group * tp_parts + (tp_place + step) % tp_parts) * width
            piece = lax.dynamic_slice_in_dim(features, column, width, axis=1)
            if step:
                pairs = [(i, (i + step) % tp_parts) for i in range(tp_parts)]
                piece = lax.ppermute(piece, "tp", pairs)
            pieces.append(piece)
        held.append(jnp.stack(pieces))
    return held


def cross_outer(held, steps, outer, inner_parts, tp_parts):
    per_tp = outer // tp_parts
    seq_parts = outer * inner_parts
    tp_place = lax.axis_index("tp")
    outer_place = lax.axis_index("seq") // inner_parts
    arrived = {}
    for step in steps:
        target = (outer_place + step) % outer
        which = (tp_place - target // per_tp + tp_parts) % tp_parts
        piece = lax.dynamic_index_in_dim(held[(step - 1) % per_tp], which, axis=0, keepdims=False)
        if step:
            far = step * inner_parts
            piece = lax.ppermute(piece, "seq", [(i, (i + far) % seq_parts) for i in range(seq_parts)])
        arrived[step] = piece
    return arrived


def share_over_tp(part, tp_parts):
    pieces = [part]
    for step in range(1, tp_parts):
        pairs = [(i, (i + step) % tp_parts) for i in range(tp_parts)]
        pieces.append(lax.ppermute(part, "tp", pairs))
    return pieces


def project_kernel(tp_parts, place_ref, *refs):
    *share_refs, weight_ref, out_ref, held, sems = refs
    seq_parts, streams, chans, count = out_ref.shape
    copies = []
    for stream in range(streams):
        for step in range(tp_parts):
            which = lax.rem(place_ref[0] - step + tp_parts, tp_parts)
            copies.append(
                pltpu.make_async_copy(
                    weight_ref.at[stream, which], held.at[stream, step], sems.at[len(copies)]
                )
            )
            copies[-1].start()
    left = [
        jnp.concatenate([share_ref[...] for share_ref in share_refs[step::tp_parts]])
        for step in range(tp_parts)
    ]
    for stream in range(streams):
        sums = jnp.zeros((count, seq_parts * chans), jnp.float32)
        for step in range(tp_parts):
            copies[stream * tp_parts + step].wait()
            sums = sums + jnp.dot(
                left[step], held[stream, step], preferred_element_type=jnp.float32
            )
        turned = sums.astype(out_ref.dtype).T
        for seq in range(seq_parts):
            out_ref[seq, stream] = turned[seq * chans : (seq + 1) * chans]


def project_in(chunks, weight, seq_parts):
    tp_parts = len(chunks[0])
    rows, width = chunks[0][0].shape
    streams, _, chan_tp = weight.shape
    weight = weight.reshape(streams, tp_parts, width, chan_tp)
    chans = chan_tp // seq_parts
    pieces = [piece for chunk in chunks for piece in chunk]
    count = len(chunks) * rows
    place = lax.axis_index("tp").astype(jnp.int32)[None]
    vmem = pl.BlockSpec(memory_space=pltpu.VMEM)
    return pl.pallas_call(
        functools.partial(project_kernel, tp_parts),
        in_specs=[pl.BlockSpec(memory_space=pltpu.SMEM)]
        + [vmem] * len(pieces)
        + [pl.BlockSpec(memory_space=pl.ANY)],
        out_specs=vmem,
        out_shape=jax.ShapeDtypeStruct((seq_parts, streams, chans, count), jnp.bfloat16),
        scratch_shapes=[
            pltpu.VMEM(weight.shape, weight.dtype),
            pltpu.SemaphoreType.DMA((streams * tp_parts,)),
        ],
        compiler_params=pltpu.CompilerParams(vmem_limit_bytes=48 * 2**20),
        cost_estimate=pl.CostEstimate(
            flops=HEAVY * 2 * count * weight.size,
            bytes_accessed=2 * (weight.size + len(pieces) * pieces[0].size)
            + 2 * streams * count * seq_parts * chans,
            transcendentals=0,
        ),
    )(place, *pieces, weight)


def tables(block):
    place = np.arange(block)
    angle = 2.0 * math.pi * np.outer(place, place + 0.5) / (2 * block)
    forward = np.concatenate([np.cos(angle), -np.sin(angle)], 1)
    place = np.arange(2 * block)
    angle = 2.0 * math.pi * np.outer(np.arange(block) + 0.5, place) / (2 * block)
    backward = np.concatenate([np.cos(angle), -np.sin(angle)], 0) / block
    return halves(forward), halves(backward)


def halves(table):
    high = table.astype(ml_dtypes.bfloat16)
    low = (table - high.astype(np.float64)).astype(ml_dtypes.bfloat16)
    return np.stack([high, low])


def each(count, body):
    if isinstance(count, int) and count <= UNROLL:
        for index in range(count):
            body(index)
    else:
        lax.fori_loop(0, count, lambda index, carry: (body(index), carry)[1], 0)


def total(count, term, zero):
    if isinstance(count, int) and count <= UNROLL:
        result = zero
        for index in range(count):
            result = jax.tree.map(jnp.add, result, term(index))
        return result
    return lax.fori_loop(
        0, count, lambda index, sums: jax.tree.map(jnp.add, sums, term(index)), zero
    )


def conv_kernel(
    outer, chunks, *refs
):
    part_refs, refs = refs[:chunks], refs[chunks:]
    filter_ref, taps_ref, skip_ref, fwd_ref, bwd_ref, out_ref, *refs = refs
    proj, query, inner, spec, filter_spec, product, back = refs
    blocks, streams, chans, _ = part_refs[0].shape
    rows = filter_ref.shape[2]
    inner_parts = blocks // outer
    taps_count = taps_ref.shape[1]
    lane = lax.broadcasted_iota(jnp.int32, (chans, rows), 1)

    depth = outer // chunks

    def add_up(inner_index, stream, group):
        value = jnp.zeros((chans, rows), jnp.float32)
        for part in range(outer):
            slot = (part - group) % outer
            column = slice(slot % depth * rows, (slot % depth + 1) * rows)
            source = part_refs[slot // depth]
            value = value + source[part * inner_parts + inner_index, stream, :, column].astype(jnp.float32)
        proj[1 + group * inner_parts + inner_index, stream] = value

    for group in range(outer):
        for stream in range(streams):
            each(inner_parts, functools.partial(add_up, stream=stream, group=group))

    for stream in range(streams):
        proj[0, stream] = jnp.zeros((chans, rows), jnp.float32)

    def first(index):
        filtered = []
        for stream in range(streams):
            now, past = proj[index + 1, stream], proj[index, stream]
            value = taps_ref[stream, 0] * now
            for offset in range(1, taps_count):
                moved = pltpu.roll(jnp.where(lane < rows - offset, now, past), offset, 1)
                value = value + taps_ref[stream, offset] * moved
            filtered.append(value)
        query[index] = filtered[0]
        inner[index] = filtered[1] * filtered[2]

    each(blocks, first)

    def product_of(value, table_ref):
        high = value.astype(jnp.bfloat16)
        low = (value - high.astype(jnp.float32)).astype(jnp.bfloat16)
        return (
            jnp.dot(high, table_ref[0], preferred_element_type=jnp.float32)
            + jnp.dot(low, table_ref[0], preferred_element_type=jnp.float32)
            + jnp.dot(high, table_ref[1], preferred_element_type=jnp.float32)
        )

    def apply(source, table_ref, target):
        if chans % 8 == 0:
            flat = source[...].reshape(blocks * chans, source.shape[2])
            target[...] = product_of(flat, table_ref).reshape(target.shape)
        else:

            def one(index):
                target[index] = product_of(source[index], table_ref)

            each(blocks, one)

    apply(filter_ref, fwd_ref, filter_spec)
    apply(inner, fwd_ref, spec)

    def multiply(index):
        def term(step):
            left, right = spec[step], filter_spec[index - step]
            left_real, left_imag = left[:, :rows], left[:, rows:]
            right_real, right_imag = right[:, :rows], right[:, rows:]
            return (
                left_real * right_real - left_imag * right_imag,
                left_real * right_imag + left_imag * right_real,
            )

        zero = jnp.zeros((chans, rows), jnp.float32)
        real, imag = total(index + 1, term, (zero, zero))
        product[index, :, :rows] = real
        product[index, :, rows:] = imag

    each(blocks, multiply)
    apply(product, bwd_ref, back)

    def last(index, carried):
        long_mix = back[index, :, :rows] + carried
        query[index] = query[index] * (long_mix + skip_ref[...] * inner[index])

    last(0, jnp.zeros((chans, rows), jnp.float32))
    each(blocks - 1, lambda index: last(index + 1, back[index, :, rows:]))

    tp_parts = out_ref.shape[0]
    part_rows = rows // tp_parts
    copies = out_ref.shape[1]

    def spread(inner_index):
        for part in range(tp_parts):
            for group in range(outer // tp_parts):
                packed = jnp.zeros((chans, rows), jnp.float32)
                for place in range(tp_parts):
                    block = query[(group * tp_parts + place) * inner_parts + inner_index]
                    shift = (place - part) * part_rows % rows
                    block = pltpu.roll(block, shift, 1) if shift else block
                    packed = jnp.where(lane // part_rows == place, block, packed)
                packed = packed.astype(out_ref.dtype)
                for copy in range(copies):
                    out_ref[part, copy, inner_index, :, group * rows : (group + 1) * rows] = packed

    each(inner_parts, spread)


def convolve(parts, filter_blocks, taps, skip, outer, tp_parts):
    blocks, streams, chans, _ = parts[0].shape
    rows = filter_blocks.shape[2]
    forward, backward = tables(rows)
    wide = (blocks, chans, 2 * rows)
    narrow = (blocks, chans, rows)
    vmem = pl.BlockSpec(memory_space=pltpu.VMEM)
    return pl.pallas_call(
        functools.partial(conv_kernel, outer, len(parts)),
        out_shape=jax.ShapeDtypeStruct(
            (tp_parts, outer, blocks // outer, chans, outer // tp_parts * rows), jnp.bfloat16
        ),
        in_specs=[vmem] * (5 + len(parts)),
        out_specs=vmem,
        scratch_shapes=[
            pltpu.VMEM((blocks + 1, streams, chans, rows), jnp.float32),
            pltpu.VMEM(narrow, jnp.float32),
            pltpu.VMEM(narrow, jnp.float32),
            pltpu.VMEM(wide, jnp.float32),
            pltpu.VMEM(wide, jnp.float32),
            pltpu.VMEM(wide, jnp.float32),
            pltpu.VMEM(wide, jnp.float32),
        ],
        compiler_params=pltpu.CompilerParams(vmem_limit_bytes=40 * 2**20),
        cost_estimate=pl.CostEstimate(flops=10**9, bytes_accessed=4 * 2**20, transcendentals=0),
    )(*parts, filter_blocks, taps, skip, jnp.asarray(forward), jnp.asarray(backward))


def out_kernel(block_ref, gated_ref, weight_ref, *refs):
    *out_refs, turned, left, held, sems = refs
    tp_parts = gated_ref.shape[0]
    part_rows = out_refs[0].shape[0]
    inner_parts, _, _, width = held.shape
    copies = [
        pltpu.make_async_copy(weight_ref.at[inner], held.at[inner], sems.at[inner])
        for inner in range(inner_parts)
    ]
    for copy in copies:
        copy.start()
    for part in range(tp_parts):
        turned[...] = gated_ref[part].T
        for index in range(len(out_refs)):
            begin = pl.multiple_of(block_ref[index] * part_rows, part_rows)
            left[part, index * part_rows : (index + 1) * part_rows] = turned[pl.ds(begin, part_rows)]
    for inner in range(inner_parts):
        copies[inner].wait()
        sums = jnp.zeros((left.shape[1], width), jnp.float32)
        for part in range(tp_parts):
            sums = sums + jnp.dot(left[part], held[inner, part], preferred_element_type=jnp.float32)
        for index, out_ref in enumerate(out_refs):
            out_ref[:, inner * width : (inner + 1) * width] = sums[
                index * part_rows : (index + 1) * part_rows
            ].astype(out_ref.dtype)


def project_out(gated, weight, blocks):
    tp_parts, depth, rows = gated.shape
    inner_parts, _, _, width = weight.shape
    columns = inner_parts * width
    part_rows = rows // len(blocks)
    vmem = pl.BlockSpec(memory_space=pltpu.VMEM)
    return pl.pallas_call(
        out_kernel,
        in_specs=[
            pl.BlockSpec(memory_space=pltpu.SMEM),
            vmem,
            pl.BlockSpec(memory_space=pl.ANY),
        ],
        out_specs=[vmem] * len(blocks),
        scratch_shapes=[
            pltpu.VMEM((rows, depth), jnp.bfloat16),
            pltpu.VMEM((tp_parts, rows, depth), jnp.bfloat16),
            pltpu.VMEM(weight.shape, weight.dtype),
            pltpu.SemaphoreType.DMA((inner_parts,)),
        ],
        out_shape=[jax.ShapeDtypeStruct((part_rows, columns), jnp.bfloat16)] * len(blocks),
        compiler_params=pltpu.CompilerParams(vmem_limit_bytes=52 * 2**20),
        cost_estimate=pl.CostEstimate(
            flops=2 * gated.size * columns,
            bytes_accessed=2 * (weight.size + gated.size + rows * columns),
            transcendentals=0,
        ),
    )(jnp.stack(blocks).astype(jnp.int32), gated, weight)


def per_device(features, in_proj, short_taps, long_filter, skip_gain, out_proj):
    rows = features.shape[0]
    seq_parts = lax.axis_size("seq")
    tp_parts = lax.axis_size("tp")
    outer = outer_factor(seq_parts, tp_parts)
    inner_parts = seq_parts // outer
    streams, _, chan_tp = in_proj.shape
    chans = chan_tp // seq_parts
    position = lax.axis_index("seq")
    inner_groups = [[a * inner_parts + b for b in range(inner_parts)] for a in range(outer)]
    tp_groups = [
        [index * tp_parts + tp for index in group for tp in range(tp_parts)] for group in inner_groups
    ]

    weight = lax.all_gather(in_proj, "seq", axis=1, tiled=True, axis_index_groups=inner_groups)

    taps = lax.dynamic_slice_in_dim(short_taps, position * chans, chans, axis=2)
    taps = jnp.broadcast_to(taps[..., None], taps.shape + (rows,))
    skip = lax.dynamic_slice_in_dim(skip_gain, position * chans, chans, axis=0)
    skip = jnp.broadcast_to(skip[:, None], (chans, rows))
    filter_blocks = lax.all_to_all(
        long_filter.T.reshape(seq_parts, chans, rows), "seq", split_axis=0, concat_axis=0, tiled=True
    )

    held = share_columns(features, outer, inner_parts, tp_parts)
    arrived = cross_outer(held, (0, 1), outer, inner_parts, tp_parts)
    held[0], taps, skip, filter_blocks = lax.optimization_barrier((held[0], taps, skip, filter_blocks))
    if outer > 2:
        arrived |= cross_outer(held, (outer - 1,), outer, inner_parts, tp_parts)
    own = share_over_tp(arrived[0], tp_parts)
    held, arrived[1], own = lax.optimization_barrier((held, arrived[1], own))
    arrived |= cross_outer(held, range(2, outer - 1), outer, inner_parts, tp_parts)
    chunks = [own] + [share_over_tp(arrived[step], tp_parts) for step in range(1, outer)]
    chunks, out_proj = lax.optimization_barrier((chunks, out_proj))
    out_weight = lax.all_gather(out_proj, ("seq", "tp"), axis_index_groups=tp_groups)
    out_weight = out_weight.reshape((inner_parts, tp_parts) + out_proj.shape)

    partial = project_in(chunks, weight, seq_parts)
    parts = lax.all_to_all(partial, "seq", split_axis=0, concat_axis=0, tiled=True)

    gated = convolve([parts], filter_blocks, taps, skip, outer, tp_parts)
    gated = lax.all_to_all(
        gated.reshape((-1,) + gated.shape[3:]), ("tp", "seq"), split_axis=0, concat_axis=0, tiled=True
    )
    blocks, places = return_places(outer, inner_parts, tp_parts)
    pieces = project_out(gated.reshape(tp_parts, chan_tp, -1), out_weight, blocks)
    return return_output(pieces, places, inner_parts, tp_parts)


def solution(mesh):
    return jax.shard_map(
        per_device,
        mesh=mesh,
        in_specs=(
            P("seq", "tp"),
            P(None, "seq", "tp"),
            P(None, None, "tp"),
            P("seq", "tp"),
            P("tp"),
            P("tp", "seq"),
        ),
        out_specs=P("seq", "tp"),
        check_vma=False,
    )
```

```python
import functools
import math

import jax
import jax.numpy as jnp
import ml_dtypes
import numpy as np
from jax import lax
from jax.experimental import pallas as pl
from jax.experimental.pallas import tpu as pltpu
from jax.sharding import PartitionSpec as P

UNROLL = 16
HEAVY = 30


def outer_factor(seq_parts, tp_parts):
    outer = tp_parts
    while 4 * outer * outer <= seq_parts and seq_parts % (2 * outer) == 0:
        outer *= 2
    return outer


def assemble_kernel(place_ref, *refs):
    *piece_refs, out_ref, sems = refs
    part_rows, width = piece_refs[0].shape
    copies = []
    for index, piece_ref in enumerate(piece_refs):
        row = pl.multiple_of(place_ref[2 * index] * part_rows, part_rows)
        column = pl.multiple_of(place_ref[2 * index + 1] * width, width)
        target = out_ref.at[pl.ds(row, part_rows), pl.ds(column, width)]
        copies.append(pltpu.make_async_copy(piece_ref, target, sems.at[index]))
    for copy in copies:
        copy.start()
    for copy in copies:
        copy.wait()


def assemble(pieces, places, shape):
    return pl.pallas_call(
        assemble_kernel,
        in_specs=[pl.BlockSpec(memory_space=pltpu.SMEM)]
        + [pl.BlockSpec(memory_space=pltpu.VMEM)] * len(pieces),
        out_specs=pl.BlockSpec(memory_space=pl.ANY),
        out_shape=jax.ShapeDtypeStruct(shape, pieces[0].dtype),
        scratch_shapes=[pltpu.SemaphoreType.DMA((len(pieces),))],
        compiler_params=pltpu.CompilerParams(vmem_limit_bytes=4 * 2**20),
        cost_estimate=pl.CostEstimate(
            flops=0, bytes_accessed=4 * shape[0] * shape[1], transcendentals=0
        ),
    )(jnp.stack(places).astype(jnp.int32), *pieces)


def return_places(outer, inner_parts, tp_parts):
    per_tp = outer // tp_parts
    tp_place = lax.axis_index("tp")
    outer_place = lax.axis_index("seq") // inner_parts
    blocks, places = [], []
    for far in range(tp_parts):
        for near in range(per_tp):
            low = outer_place % per_tp
            blocks.append((tp_place + low + far) % tp_parts * per_tp + (low + near) % per_tp)
            low = (low - near + per_tp) % per_tp
            places.append((outer_place // per_tp - far - low + tp_parts + per_tp * tp_parts) % tp_parts)
            places.append(low)
    return blocks, places


def return_output(pieces, places, inner_parts, tp_parts):
    outer = len(pieces)
    part_rows, width = pieces[0].shape
    per_tp = outer // tp_parts
    arrived = []
    for index, piece in enumerate(pieces):
        far, near = divmod(index, per_tp)

        def target(seq, tp):
            src = seq // inner_parts
            low = src % per_tp
            dst = (tp + low + far) % tp_parts * per_tp + (low + near) % per_tp
            return (dst * inner_parts + seq % inner_parts) * tp_parts + src // per_tp

        pairs = [
            (seq * tp_parts + tp, target(seq, tp))
            for seq in range(outer * inner_parts)
            for tp in range(tp_parts)
        ]
        arrived.append(lax.ppermute(piece, ("seq", "tp"), pairs))
    return assemble(arrived, places, (tp_parts * part_rows, per_tp * width))


def share_columns(features, outer, tp_parts):
    rows, cols = features.shape
    per_tp = outer // tp_parts
    tp_place = lax.axis_index("tp")
    width = cols // outer
    held = []
    for step in range(tp_parts):
        which = (tp_place + step) % tp_parts
        piece = jnp.stack(
            [
                lax.dynamic_slice_in_dim(features, (group * tp_parts + which) * width, width, axis=1)
                for group in range(per_tp)
            ]
        )
        if step:
            piece = lax.ppermute(piece, "tp", [(i, (i + step) % tp_parts) for i in range(tp_parts)])
        held.append(piece)
    return jnp.concatenate(held)


def cross_outer(held, steps, outer, inner_parts, tp_parts):
    per_tp = outer // tp_parts
    seq_parts = outer * inner_parts
    tp_place = lax.axis_index("tp")
    outer_place = lax.axis_index("seq") // inner_parts
    arrived = {}
    for step in steps:
        target = (outer_place + step) % outer
        which = (tp_place - target // per_tp + tp_parts) % tp_parts * per_tp + target % per_tp
        piece = lax.dynamic_index_in_dim(held, which, axis=0, keepdims=False)
        if step:
            far = step * inner_parts
            piece = lax.ppermute(piece, "seq", [(i, (i + far) % seq_parts) for i in range(seq_parts)])
        arrived[step] = piece
    return arrived


def share_over_tp(part, tp_parts):
    pieces = [part]
    for step in range(1, tp_parts):
        pairs = [(i, (i + step) % tp_parts) for i in range(tp_parts)]
        pieces.append(lax.ppermute(part, "tp", pairs))
    return pieces


def project_kernel(tp_parts, place_ref, *refs):
    *share_refs, weight_ref, out_ref, held, left, sems = refs
    seq_parts, streams, chans, count = out_ref.shape
    rows, width = share_refs[0].shape
    copies = []
    for stream in range(streams):
        for step in range(tp_parts):
            which = lax.rem(place_ref[0] - step + tp_parts, tp_parts)
            copies.append(
                pltpu.make_async_copy(
                    weight_ref.at[stream, which], held.at[stream, step], sems.at[len(copies)]
                )
            )
            copies[-1].start()
    for index, share_ref in enumerate(share_refs):
        chunk, step = divmod(index, tp_parts)
        left[chunk * rows : (chunk + 1) * rows, step * width : (step + 1) * width] = share_ref[...]
    for stream in range(streams):
        for copy in copies[stream * tp_parts : (stream + 1) * tp_parts]:
            copy.wait()
        sums = jnp.dot(
            left[...],
            held[stream].reshape(tp_parts * width, seq_parts * chans),
            preferred_element_type=jnp.float32,
        )
        turned = sums.astype(out_ref.dtype).T
        for seq in range(seq_parts):
            out_ref[seq, stream] = turned[seq * chans : (seq + 1) * chans]


def project_in(chunks, weight, seq_parts):
    tp_parts = len(chunks[0])
    rows, width = chunks[0][0].shape
    streams, _, chan_tp = weight.shape
    weight = weight.reshape(streams, tp_parts, width, chan_tp)
    chans = chan_tp // seq_parts
    pieces = [piece for chunk in chunks for piece in chunk]
    count = len(chunks) * rows
    place = lax.axis_index("tp").astype(jnp.int32)[None]
    vmem = pl.BlockSpec(memory_space=pltpu.VMEM)
    return pl.pallas_call(
        functools.partial(project_kernel, tp_parts),
        in_specs=[pl.BlockSpec(memory_space=pltpu.SMEM)]
        + [vmem] * len(pieces)
        + [pl.BlockSpec(memory_space=pl.ANY)],
        out_specs=vmem,
        out_shape=jax.ShapeDtypeStruct((seq_parts, streams, chans, count), jnp.bfloat16),
        scratch_shapes=[
            pltpu.VMEM(weight.shape, weight.dtype),
            pltpu.VMEM((count, tp_parts * width), jnp.bfloat16),
            pltpu.SemaphoreType.DMA((streams * tp_parts,)),
        ],
        compiler_params=pltpu.CompilerParams(vmem_limit_bytes=48 * 2**20),
        cost_estimate=pl.CostEstimate(
            flops=HEAVY * 2 * count * weight.size,
            bytes_accessed=2 * (weight.size + len(pieces) * pieces[0].size)
            + 2 * streams * count * seq_parts * chans,
            transcendentals=0,
        ),
    )(place, *pieces, weight)


def tables(block):
    place = np.arange(block)
    angle = 2.0 * math.pi * np.outer(place, place + 0.5) / (2 * block)
    forward = np.concatenate([np.cos(angle), -np.sin(angle)], 1)
    place = np.arange(2 * block)
    angle = 2.0 * math.pi * np.outer(np.arange(block) + 0.5, place) / (2 * block)
    backward = np.concatenate([np.cos(angle), -np.sin(angle)], 0) / block
    return halves(forward), halves(backward)


def halves(table):
    high = table.astype(ml_dtypes.bfloat16)
    low = (table - high.astype(np.float64)).astype(ml_dtypes.bfloat16)
    return np.stack([high, low])


def each(count, body):
    if isinstance(count, int) and count <= UNROLL:
        for index in range(count):
            body(index)
    else:
        lax.fori_loop(0, count, lambda index, carry: (body(index), carry)[1], 0)


def total(count, term, zero):
    if isinstance(count, int) and count <= UNROLL:
        result = zero
        for index in range(count):
            result = jax.tree.map(jnp.add, result, term(index))
        return result
    return lax.fori_loop(
        0, count, lambda index, sums: jax.tree.map(jnp.add, sums, term(index)), zero
    )


def conv_kernel(
    outer, chunks, *refs
):
    part_refs, refs = refs[:chunks], refs[chunks:]
    filter_ref, taps_ref, skip_ref, fwd_ref, bwd_ref, out_ref, *refs = refs
    proj, query, inner, spec, filter_spec, product, back = refs
    blocks, streams, chans, _ = part_refs[0].shape
    rows = filter_ref.shape[2]
    inner_parts = blocks // outer
    taps_count = taps_ref.shape[1]
    lane = lax.broadcasted_iota(jnp.int32, (chans, rows), 1)

    depth = outer // chunks

    def add_up(inner_index, stream, group):
        value = jnp.zeros((chans, rows), jnp.float32)
        for part in range(outer):
            slot = (part - group) % outer
            column = slice(slot % depth * rows, (slot % depth + 1) * rows)
            source = part_refs[slot // depth]
            value = value + source[part * inner_parts + inner_index, stream, :, column].astype(jnp.float32)
        proj[1 + group * inner_parts + inner_index, stream] = value

    for group in range(outer):
        for stream in range(streams):
            each(inner_parts, functools.partial(add_up, stream=stream, group=group))

    for stream in range(streams):
        proj[0, stream] = jnp.zeros((chans, rows), jnp.float32)

    def first(index):
        filtered = []
        for stream in range(streams):
            now, past = proj[index + 1, stream], proj[index, stream]
            value = taps_ref[stream, 0] * now
            for offset in range(1, taps_count):
                moved = pltpu.roll(jnp.where(lane < rows - offset, now, past), offset, 1)
                value = value + taps_ref[stream, offset] * moved
            filtered.append(value)
        query[index] = filtered[0]
        inner[index] = filtered[1] * filtered[2]

    each(blocks, first)

    def product_of(value, table_ref):
        high = value.astype(jnp.bfloat16)
        low = (value - high.astype(jnp.float32)).astype(jnp.bfloat16)
        return (
            jnp.dot(high, table_ref[0], preferred_element_type=jnp.float32)
            + jnp.dot(low, table_ref[0], preferred_element_type=jnp.float32)
            + jnp.dot(high, table_ref[1], preferred_element_type=jnp.float32)
        )

    def apply(source, table_ref, target):
        if chans % 8 == 0:
            flat = source[...].reshape(blocks * chans, source.shape[2])
            target[...] = product_of(flat, table_ref).reshape(target.shape)
        else:

            def one(index):
                target[index] = product_of(source[index], table_ref)

            each(blocks, one)

    apply(filter_ref, fwd_ref, filter_spec)
    apply(inner, fwd_ref, spec)

    def multiply(index):
        def term(step):
            left, right = spec[step], filter_spec[index - step]
            left_real, left_imag = left[:, :rows], left[:, rows:]
            right_real, right_imag = right[:, :rows], right[:, rows:]
            return (
                left_real * right_real - left_imag * right_imag,
                left_real * right_imag + left_imag * right_real,
            )

        zero = jnp.zeros((chans, rows), jnp.float32)
        real, imag = total(index + 1, term, (zero, zero))
        product[index, :, :rows] = real
        product[index, :, rows:] = imag

    each(blocks, multiply)
    apply(product, bwd_ref, back)

    def last(index, carried):
        long_mix = back[index, :, :rows] + carried
        query[index] = query[index] * (long_mix + skip_ref[...] * inner[index])

    last(0, jnp.zeros((chans, rows), jnp.float32))
    each(blocks - 1, lambda index: last(index + 1, back[index, :, rows:]))

    tp_parts = out_ref.shape[0]
    part_rows = rows // tp_parts
    copies = out_ref.shape[1]

    def spread(inner_index):
        for part in range(tp_parts):
            for group in range(outer // tp_parts):
                packed = jnp.zeros((chans, rows), jnp.float32)
                for place in range(tp_parts):
                    block = query[(group * tp_parts + place) * inner_parts + inner_index]
                    shift = (place - part) * part_rows % rows
                    block = pltpu.roll(block, shift, 1) if shift else block
                    packed = jnp.where(lane // part_rows == place, block, packed)
                packed = packed.astype(out_ref.dtype)
                for copy in range(copies):
                    out_ref[part, copy, inner_index, :, group * rows : (group + 1) * rows] = packed

    each(inner_parts, spread)


def convolve(parts, filter_blocks, taps, skip, outer, tp_parts):
    blocks, streams, chans, _ = parts[0].shape
    rows = filter_blocks.shape[2]
    forward, backward = tables(rows)
    wide = (blocks, chans, 2 * rows)
    narrow = (blocks, chans, rows)
    vmem = pl.BlockSpec(memory_space=pltpu.VMEM)
    return pl.pallas_call(
        functools.partial(conv_kernel, outer, len(parts)),
        out_shape=jax.ShapeDtypeStruct(
            (tp_parts, outer, blocks // outer, chans, outer // tp_parts * rows), jnp.bfloat16
        ),
        in_specs=[vmem] * (5 + len(parts)),
        out_specs=vmem,
        scratch_shapes=[
            pltpu.VMEM((blocks + 1, streams, chans, rows), jnp.float32),
            pltpu.VMEM(narrow, jnp.float32),
            pltpu.VMEM(narrow, jnp.float32),
            pltpu.VMEM(wide, jnp.float32),
            pltpu.VMEM(wide, jnp.float32),
            pltpu.VMEM(wide, jnp.float32),
            pltpu.VMEM(wide, jnp.float32),
        ],
        compiler_params=pltpu.CompilerParams(vmem_limit_bytes=40 * 2**20),
        cost_estimate=pl.CostEstimate(flops=10**9, bytes_accessed=4 * 2**20, transcendentals=0),
    )(*parts, filter_blocks, taps, skip, jnp.asarray(forward), jnp.asarray(backward))


def out_kernel(block_ref, gated_ref, weight_ref, *refs):
    *out_refs, turned, left, held, sems = refs
    tp_parts = gated_ref.shape[0]
    part_rows = out_refs[0].shape[0]
    inner_parts, _, depth, width = held.shape
    copies = [
        pltpu.make_async_copy(weight_ref.at[inner], held.at[inner], sems.at[inner])
        for inner in range(inner_parts)
    ]
    for copy in copies:
        copy.start()
    for part in range(tp_parts):
        turned[...] = gated_ref[part].T
        for index in range(len(out_refs)):
            begin = pl.multiple_of(block_ref[index] * part_rows, part_rows)
            left[
                index * part_rows : (index + 1) * part_rows, part * depth : (part + 1) * depth
            ] = turned[pl.ds(begin, part_rows)]
    for inner in range(inner_parts):
        copies[inner].wait()
        sums = jnp.dot(
            left[...],
            held[inner].reshape(tp_parts * depth, width),
            preferred_element_type=jnp.float32,
        )
        for index, out_ref in enumerate(out_refs):
            out_ref[:, inner * width : (inner + 1) * width] = sums[
                index * part_rows : (index + 1) * part_rows
            ].astype(out_ref.dtype)


def project_out(gated, weight, blocks):
    tp_parts, depth, rows = gated.shape
    inner_parts, _, _, width = weight.shape
    columns = inner_parts * width
    part_rows = rows // len(blocks)
    vmem = pl.BlockSpec(memory_space=pltpu.VMEM)
    return pl.pallas_call(
        out_kernel,
        in_specs=[
            pl.BlockSpec(memory_space=pltpu.SMEM),
            vmem,
            pl.BlockSpec(memory_space=pl.ANY),
        ],
        out_specs=[vmem] * len(blocks),
        scratch_shapes=[
            pltpu.VMEM((rows, depth), jnp.bfloat16),
            pltpu.VMEM((rows, tp_parts * depth), jnp.bfloat16),
            pltpu.VMEM(weight.shape, weight.dtype),
            pltpu.SemaphoreType.DMA((inner_parts,)),
        ],
        out_shape=[jax.ShapeDtypeStruct((part_rows, columns), jnp.bfloat16)] * len(blocks),
        compiler_params=pltpu.CompilerParams(vmem_limit_bytes=52 * 2**20),
        cost_estimate=pl.CostEstimate(
            flops=2 * gated.size * columns,
            bytes_accessed=2 * (weight.size + gated.size + rows * columns),
            transcendentals=0,
        ),
    )(jnp.stack(blocks).astype(jnp.int32), gated, weight)


def per_device(features, in_proj, short_taps, long_filter, skip_gain, out_proj):
    rows = features.shape[0]
    seq_parts = lax.axis_size("seq")
    tp_parts = lax.axis_size("tp")
    outer = outer_factor(seq_parts, tp_parts)
    inner_parts = seq_parts // outer
    streams, _, chan_tp = in_proj.shape
    chans = chan_tp // seq_parts
    position = lax.axis_index("seq")
    inner_groups = [[a * inner_parts + b for b in range(inner_parts)] for a in range(outer)]
    tp_groups = [
        [index * tp_parts + tp for index in group for tp in range(tp_parts)] for group in inner_groups
    ]

    weight = lax.all_gather(in_proj, "seq", axis=1, tiled=True, axis_index_groups=inner_groups)

    taps = lax.dynamic_slice_in_dim(short_taps, position * chans, chans, axis=2)
    taps = jnp.broadcast_to(taps[..., None], taps.shape + (rows,))
    skip = lax.dynamic_slice_in_dim(skip_gain, position * chans, chans, axis=0)
    skip = jnp.broadcast_to(skip[:, None], (chans, rows))
    filter_blocks = lax.all_to_all(
        long_filter.T.reshape(seq_parts, chans, rows), "seq", split_axis=0, concat_axis=0, tiled=True
    )

    held = share_columns(features, outer, tp_parts)
    arrived = cross_outer(held, (0, 1), outer, inner_parts, tp_parts)
    held, taps, skip, filter_blocks = lax.optimization_barrier((held, taps, skip, filter_blocks))
    if outer > 2:
        arrived |= cross_outer(held, (outer - 1,), outer, inner_parts, tp_parts)
    own = share_over_tp(arrived[0], tp_parts)
    held, arrived[1], own = lax.optimization_barrier((held, arrived[1], own))
    arrived |= cross_outer(held, range(2, outer - 1), outer, inner_parts, tp_parts)
    chunks = [own] + [share_over_tp(arrived[step], tp_parts) for step in range(1, outer)]
    chunks, out_proj = lax.optimization_barrier((chunks, out_proj))
    out_weight = lax.all_gather(out_proj, ("seq", "tp"), axis_index_groups=tp_groups)
    out_weight = out_weight.reshape((inner_parts, tp_parts) + out_proj.shape)

    partial = project_in(chunks, weight, seq_parts)
    parts = lax.all_to_all(partial, "seq", split_axis=0, concat_axis=0, tiled=True)

    gated = convolve([parts], filter_blocks, taps, skip, outer, tp_parts)
    gated = lax.all_to_all(
        gated.reshape((-1,) + gated.shape[3:]), ("tp", "seq"), split_axis=0, concat_axis=0, tiled=True
    )
    blocks, places = return_places(outer, inner_parts, tp_parts)
    pieces = project_out(gated.reshape(tp_parts, chan_tp, -1), out_weight, blocks)
    return return_output(pieces, places, inner_parts, tp_parts)


def solution(mesh):
    return jax.shard_map(
        per_device,
        mesh=mesh,
        in_specs=(
            P("seq", "tp"),
            P(None, "seq", "tp"),
            P(None, None, "tp"),
            P("seq", "tp"),
            P("tp"),
            P("tp", "seq"),
        ),
        out_specs=P("seq", "tp"),
        check_vma=False,
    )
```

```python
import functools
import math

import jax
import jax.numpy as jnp
import ml_dtypes
import numpy as np
from jax import lax
from jax.experimental import pallas as pl
from jax.experimental.pallas import tpu as pltpu
from jax.sharding import PartitionSpec as P

UNROLL = 16
HEAVY = 30


def outer_factor(seq_parts, tp_parts):
    outer = tp_parts
    while 4 * outer * outer <= seq_parts and seq_parts % (2 * outer) == 0:
        outer *= 2
    return outer


def assemble_kernel(place_ref, *refs):
    *piece_refs, out_ref, sems = refs
    part_rows, width = piece_refs[0].shape
    copies = []
    for index, piece_ref in enumerate(piece_refs):
        row = pl.multiple_of(place_ref[2 * index] * part_rows, part_rows)
        column = pl.multiple_of(place_ref[2 * index + 1] * width, width)
        target = out_ref.at[pl.ds(row, part_rows), pl.ds(column, width)]
        copies.append(pltpu.make_async_copy(piece_ref, target, sems.at[index]))
    for copy in copies:
        copy.start()
    for copy in copies:
        copy.wait()


def assemble(pieces, places, shape):
    return pl.pallas_call(
        assemble_kernel,
        in_specs=[pl.BlockSpec(memory_space=pltpu.SMEM)]
        + [pl.BlockSpec(memory_space=pltpu.VMEM)] * len(pieces),
        out_specs=pl.BlockSpec(memory_space=pl.ANY),
        out_shape=jax.ShapeDtypeStruct(shape, pieces[0].dtype),
        scratch_shapes=[pltpu.SemaphoreType.DMA((len(pieces),))],
        compiler_params=pltpu.CompilerParams(vmem_limit_bytes=4 * 2**20),
        cost_estimate=pl.CostEstimate(
            flops=0, bytes_accessed=4 * shape[0] * shape[1], transcendentals=0
        ),
    )(jnp.stack(places).astype(jnp.int32), *pieces)


def return_places(outer, inner_parts, tp_parts):
    per_tp = outer // tp_parts
    tp_place = lax.axis_index("tp")
    outer_place = lax.axis_index("seq") // inner_parts
    blocks, places = [], []
    for far in range(tp_parts):
        for near in range(per_tp):
            low = outer_place % per_tp
            blocks.append((tp_place + low + far) % tp_parts * per_tp + (low + near) % per_tp)
            low = (low - near + per_tp) % per_tp
            places.append((outer_place // per_tp - far - low + tp_parts + per_tp * tp_parts) % tp_parts)
            places.append(low)
    return blocks, places


def return_output(pieces, places, inner_parts, tp_parts):
    outer = len(pieces)
    part_rows, width = pieces[0].shape
    per_tp = outer // tp_parts
    arrived = []
    for index, piece in enumerate(pieces):
        far, near = divmod(index, per_tp)

        def target(seq, tp):
            src = seq // inner_parts
            low = src % per_tp
            dst = (tp + low + far) % tp_parts * per_tp + (low + near) % per_tp
            return (dst * inner_parts + seq % inner_parts) * tp_parts + src // per_tp

        pairs = [
            (seq * tp_parts + tp, target(seq, tp))
            for seq in range(outer * inner_parts)
            for tp in range(tp_parts)
        ]
        arrived.append(lax.ppermute(piece, ("seq", "tp"), pairs))
    return assemble(arrived, places, (tp_parts * part_rows, per_tp * width))


def share_columns(features, outer, tp_parts):
    rows, cols = features.shape
    per_tp = outer // tp_parts
    tp_place = lax.axis_index("tp")
    width = cols // outer
    held = []
    for step in range(tp_parts):
        which = (tp_place + step) % tp_parts
        piece = jnp.stack(
            [
                lax.dynamic_slice_in_dim(features, (group * tp_parts + which) * width, width, axis=1)
                for group in range(per_tp)
            ]
        )
        if step:
            piece = lax.ppermute(piece, "tp", [(i, (i + step) % tp_parts) for i in range(tp_parts)])
        held.append(piece)
    return jnp.concatenate(held)


def cross_outer(held, steps, outer, inner_parts, tp_parts):
    per_tp = outer // tp_parts
    seq_parts = outer * inner_parts
    tp_place = lax.axis_index("tp")
    outer_place = lax.axis_index("seq") // inner_parts
    arrived = {}
    for step in steps:
        target = (outer_place + step) % outer
        which = (tp_place - target // per_tp + tp_parts) % tp_parts * per_tp + target % per_tp
        piece = lax.dynamic_index_in_dim(held, which, axis=0, keepdims=False)
        if step:
            far = step * inner_parts
            piece = lax.ppermute(piece, "seq", [(i, (i + far) % seq_parts) for i in range(seq_parts)])
        arrived[step] = piece
    return arrived


def share_over_tp(part, tp_parts):
    pieces = [part]
    for step in range(1, tp_parts):
        pairs = [(i, (i + step) % tp_parts) for i in range(tp_parts)]
        pieces.append(lax.ppermute(part, "tp", pairs))
    return pieces


def project_kernel(tp_parts, place_ref, *refs):
    *share_refs, weight_ref, out_ref, held, left, sems = refs
    seq_parts, streams, chans, count = out_ref.shape
    rows, width = share_refs[0].shape
    copies = []
    for stream in range(streams):
        for step in range(tp_parts):
            which = lax.rem(place_ref[0] - step + tp_parts, tp_parts)
            copies.append(
                pltpu.make_async_copy(
                    weight_ref.at[stream, which], held.at[stream, step], sems.at[len(copies)]
                )
            )
            copies[-1].start()
    for index, share_ref in enumerate(share_refs):
        chunk, step = divmod(index, tp_parts)
        left[chunk * rows : (chunk + 1) * rows, step * width : (step + 1) * width] = share_ref[...]
    for stream in range(streams):
        for copy in copies[stream * tp_parts : (stream + 1) * tp_parts]:
            copy.wait()
        sums = jnp.dot(
            left[...],
            held[stream].reshape(tp_parts * width, seq_parts * chans),
            preferred_element_type=jnp.float32,
        )
        turned = sums.astype(out_ref.dtype).T
        for seq in range(seq_parts):
            out_ref[seq, stream] = turned[seq * chans : (seq + 1) * chans]


def project_in(chunks, weight, seq_parts):
    tp_parts = len(chunks[0])
    rows, width = chunks[0][0].shape
    streams, _, chan_tp = weight.shape
    weight = weight.reshape(streams, tp_parts, width, chan_tp)
    chans = chan_tp // seq_parts
    pieces = [piece for chunk in chunks for piece in chunk]
    count = len(chunks) * rows
    place = lax.axis_index("tp").astype(jnp.int32)[None]
    vmem = pl.BlockSpec(memory_space=pltpu.VMEM)
    return pl.pallas_call(
        functools.partial(project_kernel, tp_parts),
        in_specs=[pl.BlockSpec(memory_space=pltpu.SMEM)]
        + [vmem] * len(pieces)
        + [pl.BlockSpec(memory_space=pl.ANY)],
        out_specs=vmem,
        out_shape=jax.ShapeDtypeStruct((seq_parts, streams, chans, count), jnp.bfloat16),
        scratch_shapes=[
            pltpu.VMEM(weight.shape, weight.dtype),
            pltpu.VMEM((count, tp_parts * width), jnp.bfloat16),
            pltpu.SemaphoreType.DMA((streams * tp_parts,)),
        ],
        compiler_params=pltpu.CompilerParams(vmem_limit_bytes=48 * 2**20),
        cost_estimate=pl.CostEstimate(
            flops=HEAVY * 2 * count * weight.size,
            bytes_accessed=2 * (weight.size + len(pieces) * pieces[0].size)
            + 2 * streams * count * seq_parts * chans,
            transcendentals=0,
        ),
    )(place, *pieces, weight)


def tables(block):
    place = np.arange(block)
    angle = 2.0 * math.pi * np.outer(place, place + 0.5) / (2 * block)
    forward = np.concatenate([np.cos(angle), -np.sin(angle)], 1)
    place = np.arange(2 * block)
    angle = 2.0 * math.pi * np.outer(np.arange(block) + 0.5, place) / (2 * block)
    backward = np.concatenate([np.cos(angle), -np.sin(angle)], 0) / block
    return halves(forward), halves(backward)


def halves(table):
    high = table.astype(ml_dtypes.bfloat16)
    low = (table - high.astype(np.float64)).astype(ml_dtypes.bfloat16)
    return np.stack([high, low])


def each(count, body):
    if isinstance(count, int) and count <= UNROLL:
        for index in range(count):
            body(index)
    else:
        lax.fori_loop(0, count, lambda index, carry: (body(index), carry)[1], 0)


def total(count, term, zero):
    if isinstance(count, int) and count <= UNROLL:
        result = zero
        for index in range(count):
            result = jax.tree.map(jnp.add, result, term(index))
        return result
    return lax.fori_loop(
        0, count, lambda index, sums: jax.tree.map(jnp.add, sums, term(index)), zero
    )


def conv_kernel(
    outer, chunks, *refs
):
    part_refs, refs = refs[:chunks], refs[chunks:]
    filter_ref, taps_ref, skip_ref, fwd_ref, bwd_ref, out_ref, *refs = refs
    proj, query, inner, spec, filter_spec, product, back = refs
    blocks, streams, chans, _ = part_refs[0].shape
    rows = filter_ref.shape[2]
    inner_parts = blocks // outer
    taps_count = taps_ref.shape[1]
    lane = lax.broadcasted_iota(jnp.int32, (chans, rows), 1)

    depth = outer // chunks

    def add_up(inner_index, stream, group):
        value = jnp.zeros((chans, rows), jnp.float32)
        for part in range(outer):
            slot = (part - group) % outer
            column = slice(slot % depth * rows, (slot % depth + 1) * rows)
            source = part_refs[slot // depth]
            value = value + source[part * inner_parts + inner_index, stream, :, column].astype(jnp.float32)
        proj[1 + group * inner_parts + inner_index, stream] = value

    for group in range(outer):
        for stream in range(streams):
            each(inner_parts, functools.partial(add_up, stream=stream, group=group))

    for stream in range(streams):
        proj[0, stream] = jnp.zeros((chans, rows), jnp.float32)

    def first(index):
        filtered = []
        for stream in range(streams):
            now, past = proj[index + 1, stream], proj[index, stream]
            value = taps_ref[stream, 0] * now
            for offset in range(1, taps_count):
                moved = pltpu.roll(jnp.where(lane < rows - offset, now, past), offset, 1)
                value = value + taps_ref[stream, offset] * moved
            filtered.append(value)
        query[index] = filtered[0]
        inner[index] = filtered[1] * filtered[2]

    each(blocks, first)

    def product_of(value, table_ref):
        high = value.astype(jnp.bfloat16)
        low = (value - high.astype(jnp.float32)).astype(jnp.bfloat16)
        return (
            jnp.dot(high, table_ref[0], preferred_element_type=jnp.float32)
            + jnp.dot(low, table_ref[0], preferred_element_type=jnp.float32)
            + jnp.dot(high, table_ref[1], preferred_element_type=jnp.float32)
        )

    def apply(source, table_ref, target):
        if chans % 8 == 0:
            flat = source[...].reshape(blocks * chans, source.shape[2])
            target[...] = product_of(flat, table_ref).reshape(target.shape)
        else:

            def one(index):
                target[index] = product_of(source[index], table_ref)

            each(blocks, one)

    apply(filter_ref, fwd_ref, filter_spec)
    apply(inner, fwd_ref, spec)

    def multiply(index):
        def term(step):
            left, right = spec[step], filter_spec[index - step]
            left_real, left_imag = left[:, :rows], left[:, rows:]
            right_real, right_imag = right[:, :rows], right[:, rows:]
            return (
                left_real * right_real - left_imag * right_imag,
                left_real * right_imag + left_imag * right_real,
            )

        zero = jnp.zeros((chans, rows), jnp.float32)
        real, imag = total(index + 1, term, (zero, zero))
        product[index, :, :rows] = real
        product[index, :, rows:] = imag

    each(blocks, multiply)
    apply(product, bwd_ref, back)

    def last(index, carried):
        long_mix = back[index, :, :rows] + carried
        query[index] = query[index] * (long_mix + skip_ref[...] * inner[index])

    last(0, jnp.zeros((chans, rows), jnp.float32))
    each(blocks - 1, lambda index: last(index + 1, back[index, :, rows:]))

    tp_parts = out_ref.shape[0]
    part_rows = rows // tp_parts
    copies = out_ref.shape[1]

    def spread(inner_index):
        for part in range(tp_parts):
            for group in range(outer // tp_parts):
                packed = jnp.zeros((chans, rows), jnp.float32)
                for place in range(tp_parts):
                    block = query[(group * tp_parts + place) * inner_parts + inner_index]
                    shift = (place - part) * part_rows % rows
                    block = pltpu.roll(block, shift, 1) if shift else block
                    packed = jnp.where(lane // part_rows == place, block, packed)
                packed = packed.astype(out_ref.dtype)
                for copy in range(copies):
                    out_ref[part, copy, inner_index, :, group * rows : (group + 1) * rows] = packed

    each(inner_parts, spread)


def convolve(parts, filter_blocks, taps, skip, outer, tp_parts):
    blocks, streams, chans, _ = parts[0].shape
    rows = filter_blocks.shape[2]
    forward, backward = tables(rows)
    wide = (blocks, chans, 2 * rows)
    narrow = (blocks, chans, rows)
    vmem = pl.BlockSpec(memory_space=pltpu.VMEM)
    return pl.pallas_call(
        functools.partial(conv_kernel, outer, len(parts)),
        out_shape=jax.ShapeDtypeStruct(
            (tp_parts, outer, blocks // outer, chans, outer // tp_parts * rows), jnp.bfloat16
        ),
        in_specs=[vmem] * (5 + len(parts)),
        out_specs=vmem,
        scratch_shapes=[
            pltpu.VMEM((blocks + 1, streams, chans, rows), jnp.float32),
            pltpu.VMEM(narrow, jnp.float32),
            pltpu.VMEM(narrow, jnp.float32),
            pltpu.VMEM(wide, jnp.float32),
            pltpu.VMEM(wide, jnp.float32),
            pltpu.VMEM(wide, jnp.float32),
            pltpu.VMEM(wide, jnp.float32),
        ],
        compiler_params=pltpu.CompilerParams(vmem_limit_bytes=40 * 2**20),
        cost_estimate=pl.CostEstimate(flops=10**9, bytes_accessed=4 * 2**20, transcendentals=0),
    )(*parts, filter_blocks, taps, skip, jnp.asarray(forward), jnp.asarray(backward))


def out_kernel(block_ref, gated_ref, weight_ref, *refs):
    *out_refs, turned, left, held, sems = refs
    tp_parts = gated_ref.shape[0]
    part_rows = out_refs[0].shape[0]
    inner_parts, _, depth, width = held.shape
    copies = [
        pltpu.make_async_copy(weight_ref.at[inner], held.at[inner], sems.at[inner])
        for inner in range(inner_parts)
    ]
    for copy in copies:
        copy.start()
    for part in range(tp_parts):
        turned[...] = gated_ref[part].T
        for index in range(len(out_refs)):
            begin = pl.multiple_of(block_ref[index] * part_rows, part_rows)
            left[
                index * part_rows : (index + 1) * part_rows, part * depth : (part + 1) * depth
            ] = turned[pl.ds(begin, part_rows)]
    for inner in range(inner_parts):
        copies[inner].wait()
        sums = jnp.dot(
            left[...],
            held[inner].reshape(tp_parts * depth, width),
            preferred_element_type=jnp.float32,
        )
        for index, out_ref in enumerate(out_refs):
            out_ref[:, inner * width : (inner + 1) * width] = sums[
                index * part_rows : (index + 1) * part_rows
            ].astype(out_ref.dtype)


def project_out(gated, weight, blocks, part_rows):
    tp_parts, depth, rows = gated.shape
    inner_parts, _, _, width = weight.shape
    columns = inner_parts * width
    vmem = pl.BlockSpec(memory_space=pltpu.VMEM)
    return pl.pallas_call(
        out_kernel,
        in_specs=[
            pl.BlockSpec(memory_space=pltpu.SMEM),
            vmem,
            pl.BlockSpec(memory_space=pl.ANY),
        ],
        out_specs=[vmem] * len(blocks),
        scratch_shapes=[
            pltpu.VMEM((rows, depth), jnp.bfloat16),
            pltpu.VMEM((len(blocks) * part_rows, tp_parts * depth), jnp.bfloat16),
            pltpu.VMEM(weight.shape, weight.dtype),
            pltpu.SemaphoreType.DMA((inner_parts,)),
        ],
        out_shape=[jax.ShapeDtypeStruct((part_rows, columns), jnp.bfloat16)] * len(blocks),
        compiler_params=pltpu.CompilerParams(vmem_limit_bytes=52 * 2**20),
        cost_estimate=pl.CostEstimate(
            flops=2 * tp_parts * depth * len(blocks) * part_rows * columns,
            bytes_accessed=2 * (weight.size + gated.size + len(blocks) * part_rows * columns),
            transcendentals=0,
        ),
    )(jnp.stack(blocks).astype(jnp.int32), gated, weight)


def per_device(features, in_proj, short_taps, long_filter, skip_gain, out_proj):
    rows = features.shape[0]
    seq_parts = lax.axis_size("seq")
    tp_parts = lax.axis_size("tp")
    outer = outer_factor(seq_parts, tp_parts)
    inner_parts = seq_parts // outer
    streams, _, chan_tp = in_proj.shape
    chans = chan_tp // seq_parts
    position = lax.axis_index("seq")
    inner_groups = [[a * inner_parts + b for b in range(inner_parts)] for a in range(outer)]
    tp_groups = [
        [index * tp_parts + tp for index in group for tp in range(tp_parts)] for group in inner_groups
    ]

    weight = lax.all_gather(in_proj, "seq", axis=1, tiled=True, axis_index_groups=inner_groups)

    taps = lax.dynamic_slice_in_dim(short_taps, position * chans, chans, axis=2)
    taps = jnp.broadcast_to(taps[..., None], taps.shape + (rows,))
    skip = lax.dynamic_slice_in_dim(skip_gain, position * chans, chans, axis=0)
    skip = jnp.broadcast_to(skip[:, None], (chans, rows))
    filter_blocks = lax.all_to_all(
        long_filter.T.reshape(seq_parts, chans, rows), "seq", split_axis=0, concat_axis=0, tiled=True
    )

    held = share_columns(features, outer, tp_parts)
    arrived = cross_outer(held, (0, 1), outer, inner_parts, tp_parts)
    held, taps, skip, filter_blocks = lax.optimization_barrier((held, taps, skip, filter_blocks))
    if outer > 2:
        arrived |= cross_outer(held, (outer - 1,), outer, inner_parts, tp_parts)
    own = share_over_tp(arrived[0], tp_parts)
    held, arrived[1], own = lax.optimization_barrier((held, arrived[1], own))
    arrived |= cross_outer(held, range(2, outer - 1), outer, inner_parts, tp_parts)
    chunks = [own] + [share_over_tp(arrived[step], tp_parts) for step in range(1, outer)]
    chunks, out_proj = lax.optimization_barrier((chunks, out_proj))
    out_weight = lax.all_gather(out_proj, ("seq", "tp"), axis_index_groups=tp_groups)
    out_weight = out_weight.reshape((inner_parts, tp_parts) + out_proj.shape)

    partial = project_in(chunks, weight, seq_parts)
    parts = lax.all_to_all(partial, "seq", split_axis=0, concat_axis=0, tiled=True)

    gated = convolve([parts], filter_blocks, taps, skip, outer, tp_parts)
    gated = lax.all_to_all(
        gated.reshape((-1,) + gated.shape[3:]), ("tp", "seq"), split_axis=0, concat_axis=0, tiled=True
    )
    blocks, places = return_places(outer, inner_parts, tp_parts)
    gated = gated.reshape(tp_parts, chan_tp, -1)
    half = (outer + 1) // 2
    pieces = []
    for some in (blocks[:half], blocks[half:]):
        pieces += project_out(gated, out_weight, some, rows // tp_parts)
    return return_output(pieces, places, inner_parts, tp_parts)


def solution(mesh):
    return jax.shard_map(
        per_device,
        mesh=mesh,
        in_specs=(
            P("seq", "tp"),
            P(None, "seq", "tp"),
            P(None, None, "tp"),
            P("seq", "tp"),
            P("tp"),
            P("tp", "seq"),
        ),
        out_specs=P("seq", "tp"),
        check_vma=False,
    )
```

```python
import functools
import math

import jax
import jax.numpy as jnp
import ml_dtypes
import numpy as np
from jax import lax
from jax.experimental import pallas as pl
from jax.experimental.pallas import tpu as pltpu
from jax.sharding import PartitionSpec as P

UNROLL = 16
HEAVY = 30


def outer_factor(seq_parts, tp_parts):
    outer = tp_parts
    while 4 * outer * outer <= seq_parts and seq_parts % (2 * outer) == 0:
        outer *= 2
    return outer


def assemble_kernel(place_ref, *refs):
    *piece_refs, out_ref, sems = refs
    part_rows, width = piece_refs[0].shape
    copies = []
    for index, piece_ref in enumerate(piece_refs):
        row = pl.multiple_of(place_ref[2 * index] * part_rows, part_rows)
        column = pl.multiple_of(place_ref[2 * index + 1] * width, width)
        target = out_ref.at[pl.ds(row, part_rows), pl.ds(column, width)]
        copies.append(pltpu.make_async_copy(piece_ref, target, sems.at[index]))
    for copy in copies:
        copy.start()
    for copy in copies:
        copy.wait()


def assemble(pieces, places, shape):
    return pl.pallas_call(
        assemble_kernel,
        in_specs=[pl.BlockSpec(memory_space=pltpu.SMEM)]
        + [pl.BlockSpec(memory_space=pltpu.VMEM)] * len(pieces),
        out_specs=pl.BlockSpec(memory_space=pl.ANY),
        out_shape=jax.ShapeDtypeStruct(shape, pieces[0].dtype),
        scratch_shapes=[pltpu.SemaphoreType.DMA((len(pieces),))],
        compiler_params=pltpu.CompilerParams(vmem_limit_bytes=4 * 2**20),
        cost_estimate=pl.CostEstimate(
            flops=0, bytes_accessed=4 * shape[0] * shape[1], transcendentals=0
        ),
    )(jnp.stack(places).astype(jnp.int32), *pieces)


def return_places(outer, inner_parts, tp_parts):
    per_tp = outer // tp_parts
    tp_place = lax.axis_index("tp")
    outer_place = lax.axis_index("seq") // inner_parts
    blocks, places = [], []
    for far in range(tp_parts):
        for near in range(per_tp):
            low = outer_place % per_tp
            blocks.append((tp_place + low + far) % tp_parts * per_tp + (low + near) % per_tp)
            low = (low - near + per_tp) % per_tp
            places.append((outer_place // per_tp - far - low + tp_parts + per_tp * tp_parts) % tp_parts)
            places.append(low)
    return blocks, places


def return_output(pieces, places, inner_parts, tp_parts):
    outer = len(pieces)
    part_rows, width = pieces[0].shape
    per_tp = outer // tp_parts
    arrived = []
    for index, piece in enumerate(pieces):
        far, near = divmod(index, per_tp)

        def target(seq, tp):
            src = seq // inner_parts
            low = src % per_tp
            dst = (tp + low + far) % tp_parts * per_tp + (low + near) % per_tp
            return (dst * inner_parts + seq % inner_parts) * tp_parts + src // per_tp

        pairs = [
            (seq * tp_parts + tp, target(seq, tp))
            for seq in range(outer * inner_parts)
            for tp in range(tp_parts)
        ]
        arrived.append(lax.ppermute(piece, ("seq", "tp"), pairs))
    return assemble(arrived, places, (tp_parts * part_rows, per_tp * width))


def share_columns(features, outer, tp_parts):
    rows, cols = features.shape
    per_tp = outer // tp_parts
    tp_place = lax.axis_index("tp")
    width = cols // outer
    held = []
    for step in range(tp_parts):
        which = (tp_place + step) % tp_parts
        piece = jnp.stack(
            [
                lax.dynamic_slice_in_dim(features, (group * tp_parts + which) * width, width, axis=1)
                for group in range(per_tp)
            ]
        )
        if step:
            piece = lax.ppermute(piece, "tp", [(i, (i + step) % tp_parts) for i in range(tp_parts)])
        held.append(piece)
    return jnp.concatenate(held)


def cross_outer(held, steps, outer, inner_parts, tp_parts):
    per_tp = outer // tp_parts
    seq_parts = outer * inner_parts
    tp_place = lax.axis_index("tp")
    outer_place = lax.axis_index("seq") // inner_parts
    arrived = {}
    for step in steps:
        target = (outer_place + step) % outer
        which = (tp_place - target // per_tp + tp_parts) % tp_parts * per_tp + target % per_tp
        piece = lax.dynamic_index_in_dim(held, which, axis=0, keepdims=False)
        if step:
            far = step * inner_parts
            piece = lax.ppermute(piece, "seq", [(i, (i + far) % seq_parts) for i in range(seq_parts)])
        arrived[step] = piece
    return arrived


def share_over_tp(part, tp_parts):
    pieces = [part]
    for step in range(1, tp_parts):
        pairs = [(i, (i + step) % tp_parts) for i in range(tp_parts)]
        pieces.append(lax.ppermute(part, "tp", pairs))
    return pieces


def project_kernel(tp_parts, place_ref, *refs):
    *share_refs, weight_ref, out_ref, held, left, sems = refs
    seq_parts, streams, chans, count = out_ref.shape
    rows, width = share_refs[0].shape
    copies = []
    for stream in range(streams):
        for step in range(tp_parts):
            which = lax.rem(place_ref[0] - step + tp_parts, tp_parts)
            copies.append(
                pltpu.make_async_copy(
                    weight_ref.at[stream, which], held.at[stream, step], sems.at[len(copies)]
                )
            )
            copies[-1].start()
    for index, share_ref in enumerate(share_refs):
        chunk, step = divmod(index, tp_parts)
        left[chunk * rows : (chunk + 1) * rows, step * width : (step + 1) * width] = share_ref[...]
    for stream in range(streams):
        for copy in copies[stream * tp_parts : (stream + 1) * tp_parts]:
            copy.wait()
        sums = jnp.dot(
            left[...],
            held[stream].reshape(tp_parts * width, seq_parts * chans),
            preferred_element_type=jnp.float32,
        )
        turned = sums.astype(out_ref.dtype).T
        for seq in range(seq_parts):
            out_ref[seq, stream] = turned[seq * chans : (seq + 1) * chans]


def project_in(chunks, weight, seq_parts):
    tp_parts = len(chunks[0])
    rows, width = chunks[0][0].shape
    streams, _, chan_tp = weight.shape
    weight = weight.reshape(streams, tp_parts, width, chan_tp)
    chans = chan_tp // seq_parts
    pieces = [piece for chunk in chunks for piece in chunk]
    count = len(chunks) * rows
    place = lax.axis_index("tp").astype(jnp.int32)[None]
    vmem = pl.BlockSpec(memory_space=pltpu.VMEM)
    return pl.pallas_call(
        functools.partial(project_kernel, tp_parts),
        in_specs=[pl.BlockSpec(memory_space=pltpu.SMEM)]
        + [vmem] * len(pieces)
        + [pl.BlockSpec(memory_space=pl.ANY)],
        out_specs=vmem,
        out_shape=jax.ShapeDtypeStruct((seq_parts, streams, chans, count), jnp.bfloat16),
        scratch_shapes=[
            pltpu.VMEM(weight.shape, weight.dtype),
            pltpu.VMEM((count, tp_parts * width), jnp.bfloat16),
            pltpu.SemaphoreType.DMA((streams * tp_parts,)),
        ],
        compiler_params=pltpu.CompilerParams(vmem_limit_bytes=48 * 2**20),
        cost_estimate=pl.CostEstimate(
            flops=HEAVY * 2 * count * weight.size,
            bytes_accessed=2 * (weight.size + len(pieces) * pieces[0].size)
            + 2 * streams * count * seq_parts * chans,
            transcendentals=0,
        ),
    )(place, *pieces, weight)


def tables(block):
    place = np.arange(block)
    angle = 2.0 * math.pi * np.outer(place, place + 0.5) / (2 * block)
    forward = np.concatenate([np.cos(angle), -np.sin(angle)], 1)
    place = np.arange(2 * block)
    angle = 2.0 * math.pi * np.outer(np.arange(block) + 0.5, place) / (2 * block)
    backward = np.concatenate([np.cos(angle), -np.sin(angle)], 0) / block
    return halves(forward), halves(backward)


def halves(table):
    high = table.astype(ml_dtypes.bfloat16)
    low = (table - high.astype(np.float64)).astype(ml_dtypes.bfloat16)
    return np.stack([high, low])


def each(count, body):
    if isinstance(count, int) and count <= UNROLL:
        for index in range(count):
            body(index)
    else:
        lax.fori_loop(0, count, lambda index, carry: (body(index), carry)[1], 0)


def total(count, term, zero):
    if isinstance(count, int) and count <= UNROLL:
        result = zero
        for index in range(count):
            result = jax.tree.map(jnp.add, result, term(index))
        return result
    return lax.fori_loop(
        0, count, lambda index, sums: jax.tree.map(jnp.add, sums, term(index)), zero
    )


def conv_kernel(
    outer, chunks, *refs
):
    part_refs, refs = refs[:chunks], refs[chunks:]
    filter_ref, taps_ref, skip_ref, fwd_ref, bwd_ref, out_ref, *refs = refs
    proj, query, inner, spec, filter_spec, product, back = refs
    blocks, streams, chans, _ = part_refs[0].shape
    rows = filter_ref.shape[2]
    inner_parts = blocks // outer
    taps_count = taps_ref.shape[1]
    lane = lax.broadcasted_iota(jnp.int32, (chans, rows), 1)

    depth = outer // chunks

    def add_up(inner_index, stream, group):
        value = jnp.zeros((chans, rows), jnp.float32)
        for part in range(outer):
            slot = (part - group) % outer
            column = slice(slot % depth * rows, (slot % depth + 1) * rows)
            source = part_refs[slot // depth]
            value = value + source[part * inner_parts + inner_index, stream, :, column].astype(jnp.float32)
        proj[1 + group * inner_parts + inner_index, stream] = value

    for group in range(outer):
        for stream in range(streams):
            each(inner_parts, functools.partial(add_up, stream=stream, group=group))

    for stream in range(streams):
        proj[0, stream] = jnp.zeros((chans, rows), jnp.float32)

    def first(index):
        filtered = []
        for stream in range(streams):
            now, past = proj[index + 1, stream], proj[index, stream]
            value = taps_ref[stream, 0] * now
            for offset in range(1, taps_count):
                moved = pltpu.roll(jnp.where(lane < rows - offset, now, past), offset, 1)
                value = value + taps_ref[stream, offset] * moved
            filtered.append(value)
        query[index] = filtered[0]
        inner[index] = filtered[1] * filtered[2]

    each(blocks, first)

    def product_of(value, table_ref):
        high = value.astype(jnp.bfloat16)
        low = (value - high.astype(jnp.float32)).astype(jnp.bfloat16)
        return (
            jnp.dot(high, table_ref[0], preferred_element_type=jnp.float32)
            + jnp.dot(low, table_ref[0], preferred_element_type=jnp.float32)
            + jnp.dot(high, table_ref[1], preferred_element_type=jnp.float32)
        )

    def apply(source, table_ref, target):
        if chans % 8 == 0:
            flat = source[...].reshape(blocks * chans, source.shape[2])
            target[...] = product_of(flat, table_ref).reshape(target.shape)
        else:

            def one(index):
                target[index] = product_of(source[index], table_ref)

            each(blocks, one)

    apply(filter_ref, fwd_ref, filter_spec)
    apply(inner, fwd_ref, spec)

    def multiply(index):
        def term(step):
            left, right = spec[step], filter_spec[index - step]
            left_real, left_imag = left[:, :rows], left[:, rows:]
            right_real, right_imag = right[:, :rows], right[:, rows:]
            return (
                left_real * right_real - left_imag * right_imag,
                left_real * right_imag + left_imag * right_real,
            )

        zero = jnp.zeros((chans, rows), jnp.float32)
        real, imag = total(index + 1, term, (zero, zero))
        product[index, :, :rows] = real
        product[index, :, rows:] = imag

    each(blocks, multiply)
    apply(product, bwd_ref, back)

    def last(index, carried):
        long_mix = back[index, :, :rows] + carried
        query[index] = query[index] * (long_mix + skip_ref[...] * inner[index])

    last(0, jnp.zeros((chans, rows), jnp.float32))
    each(blocks - 1, lambda index: last(index + 1, back[index, :, rows:]))

    tp_parts = out_ref.shape[0]
    part_rows = rows // tp_parts
    copies = out_ref.shape[1]

    def spread(inner_index):
        for part in range(tp_parts):
            for group in range(outer // tp_parts):
                packed = jnp.zeros((chans, rows), jnp.float32)
                for place in range(tp_parts):
                    block = query[(group * tp_parts + place) * inner_parts + inner_index]
                    shift = (place - part) * part_rows % rows
                    block = pltpu.roll(block, shift, 1) if shift else block
                    packed = jnp.where(lane // part_rows == place, block, packed)
                packed = packed.astype(out_ref.dtype)
                for copy in range(copies):
                    out_ref[part, copy, inner_index, :, group * rows : (group + 1) * rows] = packed

    each(inner_parts, spread)


def convolve(parts, filter_blocks, taps, skip, outer, tp_parts):
    blocks, streams, chans, _ = parts[0].shape
    rows = filter_blocks.shape[2]
    forward, backward = tables(rows)
    wide = (blocks, chans, 2 * rows)
    narrow = (blocks, chans, rows)
    vmem = pl.BlockSpec(memory_space=pltpu.VMEM)
    return pl.pallas_call(
        functools.partial(conv_kernel, outer, len(parts)),
        out_shape=jax.ShapeDtypeStruct(
            (tp_parts, outer, blocks // outer, chans, outer // tp_parts * rows), jnp.bfloat16
        ),
        in_specs=[vmem] * (5 + len(parts)),
        out_specs=vmem,
        scratch_shapes=[
            pltpu.VMEM((blocks + 1, streams, chans, rows), jnp.float32),
            pltpu.VMEM(narrow, jnp.float32),
            pltpu.VMEM(narrow, jnp.float32),
            pltpu.VMEM(wide, jnp.float32),
            pltpu.VMEM(wide, jnp.float32),
            pltpu.VMEM(wide, jnp.float32),
            pltpu.VMEM(wide, jnp.float32),
        ],
        compiler_params=pltpu.CompilerParams(vmem_limit_bytes=40 * 2**20),
        cost_estimate=pl.CostEstimate(flops=10**9, bytes_accessed=4 * 2**20, transcendentals=0),
    )(*parts, filter_blocks, taps, skip, jnp.asarray(forward), jnp.asarray(backward))


def out_kernel(block_ref, gated_ref, weight_ref, *refs):
    *out_refs, turned, left, held, sems = refs
    tp_parts = gated_ref.shape[0]
    part_rows = out_refs[0].shape[0]
    inner_parts, _, depth, width = held.shape
    copies = [
        pltpu.make_async_copy(weight_ref.at[inner], held.at[inner], sems.at[inner])
        for inner in range(inner_parts)
    ]
    for copy in copies:
        copy.start()
    for part in range(tp_parts):
        turned[...] = gated_ref[part].T
        for index in range(len(out_refs)):
            begin = pl.multiple_of(block_ref[index] * part_rows, part_rows)
            left[
                index * part_rows : (index + 1) * part_rows, part * depth : (part + 1) * depth
            ] = turned[pl.ds(begin, part_rows)]
    for inner in range(inner_parts):
        copies[inner].wait()
        sums = jnp.dot(
            left[...],
            held[inner].reshape(tp_parts * depth, width),
            preferred_element_type=jnp.float32,
        )
        for index, out_ref in enumerate(out_refs):
            out_ref[:, inner * width : (inner + 1) * width] = sums[
                index * part_rows : (index + 1) * part_rows
            ].astype(out_ref.dtype)


def project_out(gated, weight, blocks):
    tp_parts, depth, rows = gated.shape
    inner_parts, _, _, width = weight.shape
    columns = inner_parts * width
    part_rows = rows // len(blocks)
    vmem = pl.BlockSpec(memory_space=pltpu.VMEM)
    return pl.pallas_call(
        out_kernel,
        in_specs=[
            pl.BlockSpec(memory_space=pltpu.SMEM),
            vmem,
            pl.BlockSpec(memory_space=pl.ANY),
        ],
        out_specs=[vmem] * len(blocks),
        scratch_shapes=[
            pltpu.VMEM((rows, depth), jnp.bfloat16),
            pltpu.VMEM((rows, tp_parts * depth), jnp.bfloat16),
            pltpu.VMEM(weight.shape, weight.dtype),
            pltpu.SemaphoreType.DMA((inner_parts,)),
        ],
        out_shape=[jax.ShapeDtypeStruct((part_rows, columns), jnp.bfloat16)] * len(blocks),
        compiler_params=pltpu.CompilerParams(vmem_limit_bytes=52 * 2**20),
        cost_estimate=pl.CostEstimate(
            flops=2 * gated.size * columns,
            bytes_accessed=2 * (weight.size + gated.size + rows * columns),
            transcendentals=0,
        ),
    )(jnp.stack(blocks).astype(jnp.int32), gated, weight)


def per_device(features, in_proj, short_taps, long_filter, skip_gain, out_proj):
    rows = features.shape[0]
    seq_parts = lax.axis_size("seq")
    tp_parts = lax.axis_size("tp")
    outer = outer_factor(seq_parts, tp_parts)
    inner_parts = seq_parts // outer
    streams, _, chan_tp = in_proj.shape
    chans = chan_tp // seq_parts
    position = lax.axis_index("seq")
    inner_groups = [[a * inner_parts + b for b in range(inner_parts)] for a in range(outer)]
    tp_groups = [
        [index * tp_parts + tp for index in group for tp in range(tp_parts)] for group in inner_groups
    ]

    weight = lax.all_gather(in_proj, "seq", axis=1, tiled=True, axis_index_groups=inner_groups)

    taps = lax.dynamic_slice_in_dim(short_taps, position * chans, chans, axis=2)
    taps = jnp.broadcast_to(taps[..., None], taps.shape + (rows,))
    skip = lax.dynamic_slice_in_dim(skip_gain, position * chans, chans, axis=0)
    skip = jnp.broadcast_to(skip[:, None], (chans, rows))
    filter_blocks = lax.all_to_all(
        long_filter.T.reshape(seq_parts, chans, rows), "seq", split_axis=0, concat_axis=0, tiled=True
    )

    held = share_columns(features, outer, tp_parts)
    arrived = cross_outer(held, (0, 1), outer, inner_parts, tp_parts)
    held, taps, skip = lax.optimization_barrier((held, taps, skip))
    if outer > 2:
        arrived |= cross_outer(held, (outer - 1,), outer, inner_parts, tp_parts)
    own = share_over_tp(arrived[0], tp_parts)
    held, arrived[1], own, filter_blocks = lax.optimization_barrier(
        (held, arrived[1], own, filter_blocks)
    )
    arrived |= cross_outer(held, range(2, outer - 1), outer, inner_parts, tp_parts)
    chunks = [own] + [share_over_tp(arrived[step], tp_parts) for step in range(1, outer)]
    chunks, out_proj = lax.optimization_barrier((chunks, out_proj))
    out_weight = lax.all_gather(out_proj, ("seq", "tp"), axis_index_groups=tp_groups)
    out_weight = out_weight.reshape((inner_parts, tp_parts) + out_proj.shape)

    partial = project_in(chunks, weight, seq_parts)
    parts = lax.all_to_all(partial, "seq", split_axis=0, concat_axis=0, tiled=True)

    gated = convolve([parts], filter_blocks, taps, skip, outer, tp_parts)
    gated = lax.all_to_all(
        gated.reshape((-1,) + gated.shape[3:]), ("tp", "seq"), split_axis=0, concat_axis=0, tiled=True
    )
    blocks, places = return_places(outer, inner_parts, tp_parts)
    pieces = project_out(gated.reshape(tp_parts, chan_tp, -1), out_weight, blocks)
    return return_output(pieces, places, inner_parts, tp_parts)


def solution(mesh):
    return jax.shard_map(
        per_device,
        mesh=mesh,
        in_specs=(
            P("seq", "tp"),
            P(None, "seq", "tp"),
            P(None, None, "tp"),
            P("seq", "tp"),
            P("tp"),
            P("tp", "seq"),
        ),
        out_specs=P("seq", "tp"),
        check_vma=False,
    )
```

```python
import functools
import math

import jax
import jax.numpy as jnp
import ml_dtypes
import numpy as np
from jax import lax
from jax.experimental import pallas as pl
from jax.experimental.pallas import tpu as pltpu
from jax.sharding import PartitionSpec as P

UNROLL = 16
HEAVY = 30


def outer_factor(seq_parts, tp_parts):
    outer = tp_parts
    while 4 * outer * outer <= seq_parts and seq_parts % (2 * outer) == 0:
        outer *= 2
    return outer


def assemble_kernel(place_ref, *refs):
    *piece_refs, out_ref, sems = refs
    part_rows, width = piece_refs[0].shape
    copies = []
    for index, piece_ref in enumerate(piece_refs):
        row = pl.multiple_of(place_ref[2 * index] * part_rows, part_rows)
        column = pl.multiple_of(place_ref[2 * index + 1] * width, width)
        target = out_ref.at[pl.ds(row, part_rows), pl.ds(column, width)]
        copies.append(pltpu.make_async_copy(piece_ref, target, sems.at[index]))
    for copy in copies:
        copy.start()
    for copy in copies:
        copy.wait()


def assemble(pieces, places, shape):
    return pl.pallas_call(
        assemble_kernel,
        in_specs=[pl.BlockSpec(memory_space=pltpu.SMEM)]
        + [pl.BlockSpec(memory_space=pltpu.VMEM)] * len(pieces),
        out_specs=pl.BlockSpec(memory_space=pl.ANY),
        out_shape=jax.ShapeDtypeStruct(shape, pieces[0].dtype),
        scratch_shapes=[pltpu.SemaphoreType.DMA((len(pieces),))],
        compiler_params=pltpu.CompilerParams(vmem_limit_bytes=4 * 2**20),
        cost_estimate=pl.CostEstimate(
            flops=0, bytes_accessed=4 * shape[0] * shape[1], transcendentals=0
        ),
    )(jnp.stack(places).astype(jnp.int32), *pieces)


def return_places(outer, inner_parts, tp_parts):
    per_tp = outer // tp_parts
    tp_place = lax.axis_index("tp")
    outer_place = lax.axis_index("seq") // inner_parts
    blocks, places = [], []
    for far in range(tp_parts):
        for near in range(per_tp):
            low = outer_place % per_tp
            blocks.append((tp_place + low + far) % tp_parts * per_tp + (low + near) % per_tp)
            low = (low - near + per_tp) % per_tp
            places.append((outer_place // per_tp - far - low + tp_parts + per_tp * tp_parts) % tp_parts)
            places.append(low)
    return blocks, places


def return_output(pieces, places, inner_parts, tp_parts):
    outer = len(pieces)
    part_rows, width = pieces[0].shape
    per_tp = outer // tp_parts
    arrived = []
    for index, piece in enumerate(pieces):
        far, near = divmod(index, per_tp)

        def target(seq, tp):
            src = seq // inner_parts
            low = src % per_tp
            dst = (tp + low + far) % tp_parts * per_tp + (low + near) % per_tp
            return (dst * inner_parts + seq % inner_parts) * tp_parts + src // per_tp

        pairs = [
            (seq * tp_parts + tp, target(seq, tp))
            for seq in range(outer * inner_parts)
            for tp in range(tp_parts)
        ]
        arrived.append(lax.ppermute(piece, ("seq", "tp"), pairs))
    return assemble(arrived, places, (tp_parts * part_rows, per_tp * width))


def share_columns(features, outer, tp_parts):
    rows, cols = features.shape
    per_tp = outer // tp_parts
    tp_place = lax.axis_index("tp")
    width = cols // outer
    held = []
    for step in range(tp_parts):
        which = (tp_place + step) % tp_parts
        piece = jnp.stack(
            [
                lax.dynamic_slice_in_dim(features, (group * tp_parts + which) * width, width, axis=1)
                for group in range(per_tp)
            ]
        )
        if step:
            piece = lax.ppermute(piece, "tp", [(i, (i + step) % tp_parts) for i in range(tp_parts)])
        held.append(piece)
    return jnp.concatenate(held)


def cross_outer(held, steps, outer, inner_parts, tp_parts):
    per_tp = outer // tp_parts
    seq_parts = outer * inner_parts
    tp_place = lax.axis_index("tp")
    outer_place = lax.axis_index("seq") // inner_parts
    arrived = {}
    for step in steps:
        target = (outer_place + step) % outer
        which = (tp_place - target // per_tp + tp_parts) % tp_parts * per_tp + target % per_tp
        piece = lax.dynamic_index_in_dim(held, which, axis=0, keepdims=False)
        if step:
            far = step * inner_parts
            piece = lax.ppermute(piece, "seq", [(i, (i + far) % seq_parts) for i in range(seq_parts)])
        arrived[step] = piece
    return arrived


def share_over_tp(part, tp_parts):
    pieces = [part]
    for step in range(1, tp_parts):
        pairs = [(i, (i + step) % tp_parts) for i in range(tp_parts)]
        pieces.append(lax.ppermute(part, "tp", pairs))
    return pieces


def project_kernel(tp_parts, place_ref, *refs):
    *share_refs, weight_ref, out_ref, held, left, sems = refs
    seq_parts, streams, chans, count = out_ref.shape
    rows, width = share_refs[0].shape
    copies = []
    for stream in range(streams):
        for step in range(tp_parts):
            which = lax.rem(place_ref[0] - step + tp_parts, tp_parts)
            copies.append(
                pltpu.make_async_copy(
                    weight_ref.at[stream, which], held.at[stream, step], sems.at[len(copies)]
                )
            )
            copies[-1].start()
    for index, share_ref in enumerate(share_refs):
        chunk, step = divmod(index, tp_parts)
        left[chunk * rows : (chunk + 1) * rows, step * width : (step + 1) * width] = share_ref[...]
    for stream in range(streams):
        for copy in copies[stream * tp_parts : (stream + 1) * tp_parts]:
            copy.wait()
        sums = jnp.dot(
            left[...],
            held[stream].reshape(tp_parts * width, seq_parts * chans),
            preferred_element_type=jnp.float32,
        )
        turned = sums.astype(out_ref.dtype).T
        for seq in range(seq_parts):
            out_ref[seq, stream] = turned[seq * chans : (seq + 1) * chans]


def project_in(chunks, weight, seq_parts):
    tp_parts = len(chunks[0])
    rows, width = chunks[0][0].shape
    streams, _, chan_tp = weight.shape
    weight = weight.reshape(streams, tp_parts, width, chan_tp)
    chans = chan_tp // seq_parts
    pieces = [piece for chunk in chunks for piece in chunk]
    count = len(chunks) * rows
    place = lax.axis_index("tp").astype(jnp.int32)[None]
    vmem = pl.BlockSpec(memory_space=pltpu.VMEM)
    return pl.pallas_call(
        functools.partial(project_kernel, tp_parts),
        in_specs=[pl.BlockSpec(memory_space=pltpu.SMEM)]
        + [vmem] * len(pieces)
        + [pl.BlockSpec(memory_space=pl.ANY)],
        out_specs=vmem,
        out_shape=jax.ShapeDtypeStruct((seq_parts, streams, chans, count), jnp.bfloat16),
        scratch_shapes=[
            pltpu.VMEM(weight.shape, weight.dtype),
            pltpu.VMEM((count, tp_parts * width), jnp.bfloat16),
            pltpu.SemaphoreType.DMA((streams * tp_parts,)),
        ],
        compiler_params=pltpu.CompilerParams(vmem_limit_bytes=48 * 2**20),
        cost_estimate=pl.CostEstimate(
            flops=HEAVY * 2 * count * weight.size,
            bytes_accessed=2 * (weight.size + len(pieces) * pieces[0].size)
            + 2 * streams * count * seq_parts * chans,
            transcendentals=0,
        ),
    )(place, *pieces, weight)


def tables(block):
    place = np.arange(block)
    angle = 2.0 * math.pi * np.outer(place, place + 0.5) / (2 * block)
    forward = np.concatenate([np.cos(angle), -np.sin(angle)], 1)
    place = np.arange(2 * block)
    angle = 2.0 * math.pi * np.outer(np.arange(block) + 0.5, place) / (2 * block)
    backward = np.concatenate([np.cos(angle), -np.sin(angle)], 0) / block
    return halves(forward), halves(backward)


def halves(table):
    high = table.astype(ml_dtypes.bfloat16)
    low = (table - high.astype(np.float64)).astype(ml_dtypes.bfloat16)
    return np.stack([high, low])


def each(count, body):
    if isinstance(count, int) and count <= UNROLL:
        for index in range(count):
            body(index)
    else:
        lax.fori_loop(0, count, lambda index, carry: (body(index), carry)[1], 0)


def total(count, term, zero):
    if isinstance(count, int) and count <= UNROLL:
        result = zero
        for index in range(count):
            result = jax.tree.map(jnp.add, result, term(index))
        return result
    return lax.fori_loop(
        0, count, lambda index, sums: jax.tree.map(jnp.add, sums, term(index)), zero
    )


def conv_kernel(
    outer, chunks, *refs
):
    part_refs, refs = refs[:chunks], refs[chunks:]
    filter_ref, taps_ref, skip_ref, fwd_ref, bwd_ref, out_ref, *refs = refs
    proj, query, inner, spec, filter_spec, product, back = refs
    blocks, streams, chans, _ = part_refs[0].shape
    rows = filter_ref.shape[2]
    inner_parts = blocks // outer
    taps_count = taps_ref.shape[1]
    lane = lax.broadcasted_iota(jnp.int32, (chans, rows), 1)

    depth = outer // chunks

    def add_up(inner_index, stream, group):
        value = jnp.zeros((chans, rows), jnp.float32)
        for part in range(outer):
            slot = (part - group) % outer
            column = slice(slot % depth * rows, (slot % depth + 1) * rows)
            source = part_refs[slot // depth]
            value = value + source[part * inner_parts + inner_index, stream, :, column].astype(jnp.float32)
        proj[1 + group * inner_parts + inner_index, stream] = value

    for group in range(outer):
        for stream in range(streams):
            each(inner_parts, functools.partial(add_up, stream=stream, group=group))

    for stream in range(streams):
        proj[0, stream] = jnp.zeros((chans, rows), jnp.float32)

    def first(index):
        filtered = []
        for stream in range(streams):
            now, past = proj[index + 1, stream], proj[index, stream]
            value = taps_ref[stream, 0] * now
            for offset in range(1, taps_count):
                moved = pltpu.roll(jnp.where(lane < rows - offset, now, past), offset, 1)
                value = value + taps_ref[stream, offset] * moved
            filtered.append(value)
        query[index] = filtered[0]
        inner[index] = filtered[1] * filtered[2]

    each(blocks, first)

    def product_of(value, table_ref):
        high = value.astype(jnp.bfloat16)
        low = (value - high.astype(jnp.float32)).astype(jnp.bfloat16)
        return (
            jnp.dot(high, table_ref[0], preferred_element_type=jnp.float32)
            + jnp.dot(low, table_ref[0], preferred_element_type=jnp.float32)
            + jnp.dot(high, table_ref[1], preferred_element_type=jnp.float32)
        )

    def apply(source, table_ref, target):
        if chans % 8 == 0:
            flat = source[...].reshape(blocks * chans, source.shape[2])
            target[...] = product_of(flat, table_ref).reshape(target.shape)
        else:

            def one(index):
                target[index] = product_of(source[index], table_ref)

            each(blocks, one)

    apply(filter_ref, fwd_ref, filter_spec)
    apply(inner, fwd_ref, spec)

    def multiply(index):
        def term(step):
            left, right = spec[step], filter_spec[index - step]
            left_real, left_imag = left[:, :rows], left[:, rows:]
            right_real, right_imag = right[:, :rows], right[:, rows:]
            return (
                left_real * right_real - left_imag * right_imag,
                left_real * right_imag + left_imag * right_real,
            )

        zero = jnp.zeros((chans, rows), jnp.float32)
        real, imag = total(index + 1, term, (zero, zero))
        product[index, :, :rows] = real
        product[index, :, rows:] = imag

    each(blocks, multiply)
    apply(product, bwd_ref, back)

    def last(index, carried):
        long_mix = back[index, :, :rows] + carried
        query[index] = query[index] * (long_mix + skip_ref[...] * inner[index])

    last(0, jnp.zeros((chans, rows), jnp.float32))
    each(blocks - 1, lambda index: last(index + 1, back[index, :, rows:]))

    tp_parts = out_ref.shape[0]
    part_rows = rows // tp_parts
    copies = out_ref.shape[1]

    def spread(inner_index):
        for part in range(tp_parts):
            for group in range(outer // tp_parts):
                packed = jnp.zeros((chans, rows), jnp.float32)
                for place in range(tp_parts):
                    block = query[(group * tp_parts + place) * inner_parts + inner_index]
                    shift = (place - part) * part_rows % rows
                    block = pltpu.roll(block, shift, 1) if shift else block
                    packed = jnp.where(lane // part_rows == place, block, packed)
                packed = packed.astype(out_ref.dtype)
                for copy in range(copies):
                    out_ref[part, copy, inner_index, :, group * rows : (group + 1) * rows] = packed

    each(inner_parts, spread)


def convolve(parts, filter_blocks, taps, skip, outer, tp_parts):
    blocks, streams, chans, _ = parts[0].shape
    rows = filter_blocks.shape[2]
    forward, backward = tables(rows)
    wide = (blocks, chans, 2 * rows)
    narrow = (blocks, chans, rows)
    vmem = pl.BlockSpec(memory_space=pltpu.VMEM)
    return pl.pallas_call(
        functools.partial(conv_kernel, outer, len(parts)),
        out_shape=jax.ShapeDtypeStruct(
            (tp_parts, outer, blocks // outer, chans, outer // tp_parts * rows), jnp.bfloat16
        ),
        in_specs=[vmem] * (5 + len(parts)),
        out_specs=vmem,
        scratch_shapes=[
            pltpu.VMEM((blocks + 1, streams, chans, rows), jnp.float32),
            pltpu.VMEM(narrow, jnp.float32),
            pltpu.VMEM(narrow, jnp.float32),
            pltpu.VMEM(wide, jnp.float32),
            pltpu.VMEM(wide, jnp.float32),
            pltpu.VMEM(wide, jnp.float32),
            pltpu.VMEM(wide, jnp.float32),
        ],
        compiler_params=pltpu.CompilerParams(vmem_limit_bytes=40 * 2**20),
        cost_estimate=pl.CostEstimate(flops=10**9, bytes_accessed=4 * 2**20, transcendentals=0),
    )(*parts, filter_blocks, taps, skip, jnp.asarray(forward), jnp.asarray(backward))


def out_kernel(block_ref, gated_ref, weight_ref, *refs):
    *out_refs, turned, left, held, sems = refs
    tp_parts = gated_ref.shape[0]
    part_rows = out_refs[0].shape[0]
    inner_parts, _, depth, width = held.shape
    copies = [
        pltpu.make_async_copy(weight_ref.at[inner], held.at[inner], sems.at[inner])
        for inner in range(inner_parts)
    ]
    for copy in copies:
        copy.start()
    for part in range(tp_parts):
        turned[...] = gated_ref[part].T
        for index in range(len(out_refs)):
            begin = pl.multiple_of(block_ref[index] * part_rows, part_rows)
            left[
                index * part_rows : (index + 1) * part_rows, part * depth : (part + 1) * depth
            ] = turned[pl.ds(begin, part_rows)]
    for inner in range(inner_parts):
        copies[inner].wait()
        sums = jnp.dot(
            left[...],
            held[inner].reshape(tp_parts * depth, width),
            preferred_element_type=jnp.float32,
        )
        for index, out_ref in enumerate(out_refs):
            out_ref[:, inner * width : (inner + 1) * width] = sums[
                index * part_rows : (index + 1) * part_rows
            ].astype(out_ref.dtype)


def project_out(gated, weight, blocks):
    tp_parts, depth, rows = gated.shape
    inner_parts, _, _, width = weight.shape
    columns = inner_parts * width
    part_rows = rows // len(blocks)
    vmem = pl.BlockSpec(memory_space=pltpu.VMEM)
    return pl.pallas_call(
        out_kernel,
        in_specs=[
            pl.BlockSpec(memory_space=pltpu.SMEM),
            vmem,
            pl.BlockSpec(memory_space=pl.ANY),
        ],
        out_specs=[vmem] * len(blocks),
        scratch_shapes=[
            pltpu.VMEM((rows, depth), jnp.bfloat16),
            pltpu.VMEM((rows, tp_parts * depth), jnp.bfloat16),
            pltpu.VMEM(weight.shape, weight.dtype),
            pltpu.SemaphoreType.DMA((inner_parts,)),
        ],
        out_shape=[jax.ShapeDtypeStruct((part_rows, columns), jnp.bfloat16)] * len(blocks),
        compiler_params=pltpu.CompilerParams(vmem_limit_bytes=52 * 2**20),
        cost_estimate=pl.CostEstimate(
            flops=2 * gated.size * columns,
            bytes_accessed=2 * (weight.size + gated.size + rows * columns),
            transcendentals=0,
        ),
    )(jnp.stack(blocks).astype(jnp.int32), gated, weight)


def per_device(features, in_proj, short_taps, long_filter, skip_gain, out_proj):
    rows = features.shape[0]
    seq_parts = lax.axis_size("seq")
    tp_parts = lax.axis_size("tp")
    outer = outer_factor(seq_parts, tp_parts)
    inner_parts = seq_parts // outer
    streams, _, chan_tp = in_proj.shape
    chans = chan_tp // seq_parts
    position = lax.axis_index("seq")
    inner_groups = [[a * inner_parts + b for b in range(inner_parts)] for a in range(outer)]
    tp_groups = [
        [index * tp_parts + tp for index in group for tp in range(tp_parts)] for group in inner_groups
    ]

    weight = lax.all_gather(in_proj, "seq", axis=1, tiled=True, axis_index_groups=inner_groups)

    taps = lax.dynamic_slice_in_dim(short_taps, position * chans, chans, axis=2)
    taps = jnp.broadcast_to(taps[..., None], taps.shape + (rows,))
    skip = lax.dynamic_slice_in_dim(skip_gain, position * chans, chans, axis=0)
    skip = jnp.broadcast_to(skip[:, None], (chans, rows))
    filter_blocks = lax.all_to_all(
        long_filter.T.astype(jnp.bfloat16).reshape(seq_parts, chans, rows), "seq", split_axis=0, concat_axis=0, tiled=True
    )

    held = share_columns(features, outer, tp_parts)
    arrived = cross_outer(held, (0, 1), outer, inner_parts, tp_parts)
    held, taps, skip = lax.optimization_barrier((held, taps, skip))
    if outer > 2:
        arrived |= cross_outer(held, (outer - 1,), outer, inner_parts, tp_parts)
    own = share_over_tp(arrived[0], tp_parts)
    held, arrived[1], own, filter_blocks = lax.optimization_barrier(
        (held, arrived[1], own, filter_blocks)
    )
    arrived |= cross_outer(held, range(2, outer - 1), outer, inner_parts, tp_parts)
    chunks = [own] + [share_over_tp(arrived[step], tp_parts) for step in range(1, outer)]
    chunks, out_proj = lax.optimization_barrier((chunks, out_proj))
    out_weight = lax.all_gather(out_proj, ("seq", "tp"), axis_index_groups=tp_groups)
    out_weight = out_weight.reshape((inner_parts, tp_parts) + out_proj.shape)

    partial = project_in(chunks, weight, seq_parts)
    parts = lax.all_to_all(partial, "seq", split_axis=0, concat_axis=0, tiled=True)

    gated = convolve([parts], filter_blocks, taps, skip, outer, tp_parts)
    gated = lax.all_to_all(
        gated.reshape((-1,) + gated.shape[3:]), ("tp", "seq"), split_axis=0, concat_axis=0, tiled=True
    )
    blocks, places = return_places(outer, inner_parts, tp_parts)
    pieces = project_out(gated.reshape(tp_parts, chan_tp, -1), out_weight, blocks)
    return return_output(pieces, places, inner_parts, tp_parts)


def solution(mesh):
    return jax.shard_map(
        per_device,
        mesh=mesh,
        in_specs=(
            P("seq", "tp"),
            P(None, "seq", "tp"),
            P(None, None, "tp"),
            P("seq", "tp"),
            P("tp"),
            P("tp", "seq"),
        ),
        out_specs=P("seq", "tp"),
        check_vma=False,
    )
```
